32 devices in a mesh: dev: 8 (over z, x), ha: 2 (over y), wa: 2 (over core).
Axes of the slice: x: 2, y: 2, z: 4, core: 2. Of those that a mesh axis runs over, the one named last changes fastest.
Arguments:
- tokens: bfloat16 [2352, 768], P(('dev', 'ha'), 'wa'), may hold values from -6 to 6
- cotangent: bfloat16 [2352, 768], P(('dev', 'ha'), 'wa'), may hold values from -6 to 6
- conv_taps: float32 [2, 9, 768], P(None, None, 'wa'), may hold values from -2 to 2
- norm_gain: float32 [4, 768], P(None, 'wa'), may hold values from 0.1 to 1.9
- norm_shift: float32 [4, 768], P(None, 'wa'), may hold values from -2 to 2
- w_qkv: bfloat16 [2, 768, 3, 768], P(None, 'wa', None, 'ha'), may hold values from -0.21875 to 0.21875
- w_proj: bfloat16 [2, 768, 768], P(None, 'ha', 'wa'), may hold values from -0.625 to 0.625
- w_up: bfloat16 [2, 768, 3072], P(None, 'wa', 'ha'), may hold values from -0.21875 to 0.21875
- w_down: bfloat16 [2, 3072, 768], P(None, 'ha', 'wa'), may hold values from -0.109375 to 0.109375
- valid: int32 [48, 49], P('dev'), may hold values from 0 to 1, as said below
Outputs:
- output: float32 [2352, 768], P(('dev', 'ha'), 'wa')
- grad_tokens: float32 [2352, 768], P(('dev', 'ha'), 'wa')
- grad_taps: float32 [2, 9, 768], P(None, None, 'wa')
- grad_gain: float32 [4, 768], P(None, 'wa')
- grad_shift: float32 [4, 768], P(None, 'wa')
- grad_qkv: float32 [2, 768, 3, 768], P(None, 'wa', None, ('ha', 'dev'))
- grad_proj: float32 [2, 768, 768], P(None, 'ha', ('wa', 'dev'))
- grad_up: float32 [2, 768, 3072], P(None, 'wa', ('ha', 'dev'))
- grad_down: float32 [2, 3072, 768], P(None, 'ha', ('wa', 'dev'))
The draws below stay inside these ranges and needn't reach their ends.
Inputs may be any that keep to these rules, and one draw needn't show every extreme that they name: For each image the patches with valid = 1 form the top-left rectangle of its 7 x 7 grid, of height and width each from 3 to 7.
All inputs are finite; a program needn't handle non-finite values.
Results may differ from the reference program's by a relative error of at most 0.02.
Values may be sent and summed in bfloat16 or wider, within the bound.
No kernel may reach another device: no remote copies, remote signals or barrier semaphores. Data moves between devices by JAX's collectives and lax.ppermute only.
A program may use at most 128 MiB of HBM per device.

```python
from functools import partial
import jax
import jax.numpy as jnp
from jax import lax

D = 768
HEADS = 24
F = 3072
WIN = 7
IMG_DEV = 6
HEAD_DIM = 32
PATCHES = 49
IMAGES = 48
TOKENS = 2352
N_DEV = 8


def draw_valid(key, part):
    key = jax.random.fold_in(key, 11)
    high_key, wide_key = jax.random.split(key)
    heights = jax.random.randint(high_key, (IMAGES, 1), 3, WIN + 1)
    widths = jax.random.randint(wide_key, (IMAGES, 1), 3, WIN + 1)
    patch_index = jnp.arange(PATCHES)[None, :]
    inside = (patch_index // WIN < heights) & (patch_index % WIN < widths)
    return inside.astype(jnp.int32)


def raised(values, key, source, target, blocks, factor):
    owner, partner = [(jnp.arange(values.shape[dim]) // (values.shape[dim] // blocks)).reshape([-1 if axis == dim else 1 for axis in range(values.ndim)]) for dim in (source, target)]
    chosen = jax.random.permutation(key, blocks)[partner]
    strong = (owner == chosen) | (owner == (partner + blocks // 2) % blocks)
    return jnp.where(strong, factor * values, values)


def block_scale(rng, extent, cuts, low, top_value):
    def one(dim, shards_of):
        steps = jax.random.uniform(jax.random.fold_in(jax.random.fold_in(rng, 6), dim), (shards_of,), jnp.float32, low / len(cuts), top_value / len(cuts))
        return jnp.repeat(jnp.exp(steps), extent[dim] // shards_of).reshape((-1,) + (1,) * (len(extent) - dim - 1))

    factor_of = one(*cuts[0])
    for cut in cuts[1:]:
        factor_of = factor_of * one(*cut)
    return factor_of


def gaussian(stream_key, shape, width, limit, shards=(), dtype=jnp.bfloat16):
    loudness = block_scale(stream_key, shape, shards, -0.22, 0.18) if shards else 1.0
    entries = jax.random.normal(stream_key, shape, jnp.float32) * width * loudness
    return jnp.minimum(jnp.maximum(entries, -limit), limit).astype(dtype)


def noise_with(rng, extent, width, reach, cuts, heavy, held_as=jnp.bfloat16):
    drawn = width * jax.random.normal(rng, extent, jnp.float32)
    if cuts:
        drawn = drawn * block_scale(rng, extent, cuts, -0.22, 0.18)
    return jnp.clip(raised(drawn, jax.random.fold_in(rng, 3), *heavy), -reach, reach).astype(held_as)


def setup_inputs(seed: int = 0) -> dict:
    keys = jax.random.split(jax.random.key(seed), 11)
    tokens = gaussian(keys[0], (TOKENS, D), 1.0, 6.0, ((0, 16), (1, 2)))
    cotangent = noise_with(keys[1], (TOKENS, D), 1.0, 6.0, ((0, 16), (1, 2)), (0, 1, 16, 2.0))
    conv_taps = gaussian(keys[2], (2, 9, D), 9 ** -0.5, 2.0, ((2, 2),), jnp.float32)
    norm_gain = jnp.clip(1.0 + 0.18 * jax.random.normal(keys[3], (4, D), jnp.float32), 0.1, 1.9)
    norm_shift = gaussian(keys[4], (4, D), 0.3, 2.0, ((1, 2),), jnp.float32)
    w_qkv = gaussian(keys[5], (2, D, 3, D), D ** -0.5, 0.21875, ((1, 2), (3, 2)))
    w_proj = gaussian(keys[6], (2, D, D), (D // 8) ** -0.5, 0.625, ((1, 2), (2, 2)))
    w_up = gaussian(keys[7], (2, D, F), D ** -0.5, 0.21875, ((1, 2), (2, 2)))
    w_down = gaussian(keys[8], (2, F, D), F ** -0.5, 0.109375, ((1, 2), (2, 2)))
    valid = draw_valid(jax.random.fold_in(keys[10], 71), 0)
    return {"tokens": tokens, "cotangent": cotangent, "conv_taps": conv_taps, "norm_gain": norm_gain, "norm_shift": norm_shift, "w_qkv": w_qkv, "w_proj": w_proj, "w_up": w_up, "w_down": w_down, "valid": valid}


@jax.custom_vjp
def low(v):
    return lax.optimization_barrier(v.astype(jnp.bfloat16)).astype(jnp.float32)

@jax.custom_vjp
def low_back(v):
    return v

def low_keep(v):
    return (low(v), None)

def low_pass(kept, grad):
    return (grad,)

def back_keep(v):
    return (v, None)

def back_low(kept, grad):
    return (low(grad),)
low.defvjp(low_keep, low_pass)
low_back.defvjp(back_keep, back_low)
EPS = 1e-05
HIGH = lax.Precision.HIGHEST

def layer_norm(stream, gain, shift):
    center = lax.optimization_barrier(jnp.mean(stream, axis=-1, keepdims=True))
    variance = lax.optimization_barrier(jnp.mean(jnp.square(stream - center), axis=-1, keepdims=True))
    return (stream - center) * lax.rsqrt(variance + EPS) * gain + shift

def conv_embed(stream, taps):
    images = stream.reshape(stream.shape[0], WIN, WIN, stream.shape[-1])
    padded = jnp.pad(images, ((0, 0), (1, 1), (1, 1), (0, 0)))
    result = images
    for tap_row in range(3):
        for tap_col in range(3):
            result = result + padded[:, tap_row:tap_row + WIN, tap_col:tap_col + WIN, :] * taps[tap_row * 3 + tap_col]
    return result.reshape(stream.shape)

def split_heads(packed):
    count = packed.shape[0]
    parts = packed.reshape(count, PATCHES, 3, HEADS, HEAD_DIM)
    return (parts[:, :, 0], parts[:, :, 1], parts[:, :, 2])

def window_mix(packed):
    queries, key_rows, value_rows = split_heads(packed)
    scores = jnp.einsum('iqhd,ikhd->ihqk', queries, key_rows, precision=HIGH) * HEAD_DIM ** (-0.5)
    scores = low_back(scores)
    probs = low(jax.nn.softmax(scores, axis=-1))
    mixed = jnp.einsum('ihqk,ikhd->iqhd', probs, value_rows, precision=HIGH)
    return mixed.reshape(packed.shape[0], PATCHES, D)

def channel_mix(packed, mask):
    queries, key_rows, value_rows = split_heads(packed)
    masked = queries * mask[:, :, None, None]
    scores = jnp.einsum('ingc,ingd->igcd', masked, key_rows, precision=HIGH) * HEAD_DIM ** (-0.5)
    scores = low_back(scores)
    probs = low(jax.nn.softmax(scores, axis=-1))
    mixed = jnp.einsum('ingd,igcd->ingc', value_rows, probs, precision=HIGH)
    return mixed.reshape(packed.shape[0], PATCHES, D)

def attention_branch(stream, gain, shift, w_in, w_out, mixer):
    normed = low(layer_norm(stream, gain, shift))
    packed = low_back(low(jnp.einsum('ipd,dte->ipte', normed, w_in, precision=HIGH)))
    mixed = low_back(low(mixer(packed)))
    return stream + low_back(jnp.einsum('ipc,cd->ipd', mixed, w_out, precision=HIGH))

def mlp_branch(stream, gain, shift, w_in, w_out):
    normed = low(layer_norm(stream, gain, shift))
    pre_act = low_back(jnp.einsum('ipd,df->ipf', normed, w_in, precision=HIGH))
    hidden = low_back(low(jax.nn.gelu(pre_act, approximate=False)))
    return stream + low_back(jnp.einsum('ipf,fd->ipd', hidden, w_out, precision=HIGH))

def forward(stream, taps, gains, shifts, w_qkv, w_proj, w_up, w_down, mask):
    mixers = (window_mix, partial(channel_mix, mask=mask))
    for section in range(2):
        stream = conv_embed(stream, taps[section])
        stream = attention_branch(stream, gains[2 * section], shifts[2 * section], w_qkv[section], w_proj[section], mixers[section])
        stream = mlp_branch(stream, gains[2 * section + 1], shifts[2 * section + 1], w_up[section], w_down[section])
    return stream

def reference(tokens, cotangent, conv_taps, norm_gain, norm_shift, w_qkv, w_proj, w_up, w_down, valid):
    streams = tokens.astype(jnp.float32).reshape(N_DEV, IMG_DEV, PATCHES, D)
    grads_in = cotangent.astype(jnp.float32).reshape(N_DEV, IMG_DEV, PATCHES, D)
    masks = valid.astype(jnp.float32).reshape(N_DEV, IMG_DEV, PATCHES)
    params = (conv_taps.astype(jnp.float32), norm_gain.astype(jnp.float32), norm_shift.astype(jnp.float32), w_qkv.astype(jnp.float32), w_proj.astype(jnp.float32), w_up.astype(jnp.float32), w_down.astype(jnp.float32))

    def group_step(totals, group):
        stream, grad_out, mask = group

        def apply(stream_in, *weights):
            return forward(stream_in, *weights, mask)
        result, pull = jax.vjp(apply, stream, *params)
        grads = pull(grad_out)
        totals = tuple((acc + new for acc, new in zip(totals, grads[1:])))
        return (totals, (result, grads[0]))
    start_totals = tuple((jnp.zeros_like(value) for value in params))
    totals, (results, grad_rows) = lax.scan(group_step, start_totals, (streams, grads_in, masks))
    return (results.reshape(TOKENS, D), grad_rows.reshape(TOKENS, D), totals[0], totals[1], totals[2], totals[3], totals[4], totals[5], totals[6])
```

```python
from functools import partial

import jax
import jax.numpy as jnp
import numpy as np
from jax import lax
from jax.experimental import pallas as pl
from jax.experimental.pallas import tpu as pltpu
from jax.sharding import PartitionSpec as P

WIN = 7
GRID_COLS = 8
PATCHES = 49
PADDED = WIN * GRID_COLS
HEAD_DIM = 32
LANES = 128
HEADS_TILE = LANES // HEAD_DIM
EPS = 1e-05
NEG = -1e30
BF16 = jnp.bfloat16
F32 = jnp.float32
VMEM_LIMIT = 40 * 2**20


def mm(left, right, left_dim, right_dim):
    return lax.dot_general(
        left, right, (((left_dim,), (right_dim,)), ((), ())), preferred_element_type=F32
    )


def kernel_call(body, name, ins, outs, scratch=(), flops=0):
    specs, arrays = [], []
    for item in ins:
        if isinstance(item, tuple):
            array, section = item
            specs.append(
                pl.BlockSpec(
                    (None,) + array.shape[1:],
                    lambda step, section=section, rest=array.ndim - 1: (section,) + (0,) * rest,
                )
            )
        else:
            array = item
            if array.dtype == jnp.int32:
                specs.append(pl.BlockSpec(memory_space=pltpu.SMEM))
            else:
                specs.append(
                    pl.BlockSpec(array.shape, lambda step, rest=array.ndim: (0,) * rest)
                )
        arrays.append(array)
    moved = sum(int(np.prod(o.shape)) * o.dtype.itemsize for o in outs) + sum(
        int(np.prod(a.shape)) * a.dtype.itemsize for a in arrays
    )
    return pl.pallas_call(
        body,
        grid=(1,),
        in_specs=specs,
        out_specs=[pl.BlockSpec(o.shape, lambda step, rest=len(o.shape): (0,) * rest) for o in outs],
        out_shape=list(outs),
        scratch_shapes=list(scratch),
        compiler_params=pltpu.CompilerParams(vmem_limit_bytes=VMEM_LIMIT),
        cost_estimate=pl.CostEstimate(flops=flops, bytes_accessed=moved, transcendentals=0),
        name=name,
    )(*arrays)


def sds(shape, dtype=F32):
    return jax.ShapeDtypeStruct(shape, dtype)


def column_mask(rows):
    return (lax.broadcasted_iota(jnp.int32, (rows, 1), 0) % GRID_COLS) < WIN


def side_shifts(values):
    rows = values.shape[0]
    return (pltpu.roll(values, 1, 0), values, pltpu.roll(values, rows - 1, 0))


def as_grid(values):
    return values.reshape(-1, WIN, GRID_COLS, values.shape[-1])


def move_rows(values, step):
    grid = as_grid(values)
    zeros = jnp.zeros_like(grid[:, :1])
    if step > 0:
        moved = jnp.concatenate([zeros, grid[:, :-1]], axis=1)
    else:
        moved = jnp.concatenate([grid[:, 1:], zeros], axis=1)
    return moved.reshape(values.shape)


def conv_cols(values, taps, keep):
    shifted = side_shifts(values)
    line = [
        sum(shifted[col] * taps[3 * row + col] for col in range(3)) for row in range(3)
    ]
    total = values + line[1] + move_rows(line[0], 1) + move_rows(line[2], -1)
    return jnp.where(keep, total, 0.0)


def tap_sums(grads, values):
    shifted = side_shifts(values)
    grad_grid = as_grid(grads)
    sums = []
    for row in range(3):
        for col in range(3):
            moved = as_grid(shifted[col])
            if row == 0:
                prod = grad_grid[:, 1:] * moved[:, :-1]
            elif row == 1:
                prod = grad_grid * moved
            else:
                prod = grad_grid[:, :-1] * moved[:, 1:]
            flat = prod.reshape(-1, GRID_COLS, prod.shape[-1])
            sums.append(jnp.sum(jnp.sum(flat, axis=0), axis=0, keepdims=True))
    return sums


def norm_stats(stream):
    width = stream.shape[1]
    center = jnp.sum(stream, axis=1, keepdims=True) * (1.0 / width)
    moved = stream - center
    inv_std = lax.rsqrt(jnp.sum(moved * moved, axis=1, keepdims=True) * (1.0 / width) + EPS)
    return moved * inv_std, inv_std


def norm_back(upstream, units, inv_std, gain):
    width = upstream.shape[1]
    scaled = upstream * gain
    first = jnp.sum(scaled, axis=1, keepdims=True) * (1.0 / width)
    second = jnp.sum(scaled * units, axis=1, keepdims=True) * (1.0 / width)
    return inv_std * (scaled - first - units * second)


def gelu_parts(values):
    z = jnp.abs(values) * (0.5**0.5)
    t = 1.0 / (1.0 + 0.3275911 * z)
    bell = jnp.exp(-z * z)
    poly = t * (
        0.254829592
        + t * (-0.284496736 + t * (1.421413741 + t * (-1.453152027 + t * 1.061405429)))
    )
    tail = 0.5 * poly * bell
    return jnp.where(values < 0, tail, 1.0 - tail), bell * float(1.0 / np.sqrt(2.0 * np.pi))


def head_mask(index):
    return (lax.broadcasted_iota(jnp.int32, (1, LANES), 1) // HEAD_DIM) == index


def spread_heads(tile):
    return jnp.concatenate(
        [jnp.where(head_mask(j), tile, 0.0) for j in range(HEADS_TILE)], axis=0
    ).astype(BF16)


def gather_heads(stacked):
    rows = stacked.shape[0] // HEADS_TILE
    total = jnp.where(head_mask(0), stacked[:rows], 0.0)
    for j in range(1, HEADS_TILE):
        total = jnp.where(head_mask(j), stacked[j * rows : (j + 1) * rows], total)
    return total


def softmax_rows(scores):
    top = jnp.max(scores, axis=0, keepdims=True)
    weights = jnp.exp(scores - top)
    return weights / jnp.sum(weights, axis=0, keepdims=True)


SCALE = HEAD_DIM**-0.5


def window_tile(q, k, v):
    keys_ok = column_mask(PADDED)
    scores = mm(k.astype(BF16), spread_heads(q), 1, 1) * SCALE
    probs = softmax_rows(jnp.where(keys_ok, scores, NEG))
    return probs, gather_heads(mm(probs.astype(BF16), v.astype(BF16), 0, 0))


def window_tile_back(q, k, v, probs, grad):
    low = probs.astype(BF16)
    q_big, g_big = spread_heads(q), spread_heads(grad)
    grad_probs = mm(v.astype(BF16), g_big, 1, 1)
    grad_v = mm(low, g_big, 1, 0)
    grad_scores = (
        probs * (grad_probs - jnp.sum(grad_probs * probs, axis=0, keepdims=True))
    ).astype(BF16)
    grad_k = mm(grad_scores, q_big, 1, 0) * SCALE
    grad_q = gather_heads(mm(grad_scores, k.astype(BF16), 0, 0)) * SCALE
    return grad_q, grad_k, grad_v


def same_head():
    first = lax.broadcasted_iota(jnp.int32, (LANES, LANES), 0) // HEAD_DIM
    second = lax.broadcasted_iota(jnp.int32, (LANES, LANES), 1) // HEAD_DIM
    return first == second


def channel_tile(q, k, v, mask):
    scores = mm(k.astype(BF16), (q * mask).astype(BF16), 0, 0) * SCALE
    probs = softmax_rows(jnp.where(same_head(), scores, NEG))
    return probs, mm(v.astype(BF16), probs.astype(BF16), 1, 0)


def channel_tile_back(q, k, v, probs, grad, mask):
    low = probs.astype(BF16)
    grad_low = grad.astype(BF16)
    grad_probs = mm(v.astype(BF16), grad_low, 0, 0)
    grad_v = mm(grad_low, low, 1, 1)
    grad_scores = (
        probs * (grad_probs - jnp.sum(grad_probs * probs, axis=0, keepdims=True))
    ).astype(BF16)
    grad_q = mm(k.astype(BF16), grad_scores, 1, 0) * SCALE * mask
    grad_k = mm((q * mask).astype(BF16), grad_scores, 1, 1) * SCALE
    return grad_q, grad_k, grad_v


def solution(mesh):
    n_dev = mesh.shape["dev"]
    bits = n_dev.bit_length() - 1
    assert n_dev == 1 << bits and mesh.shape["ha"] == 2 and mesh.shape["wa"] == 2

    swap = [(0, 1), (1, 0)]
    pair = ("ha", "wa")
    near_in = [(0, 2), (3, 1), (1, 0), (2, 3)]
    near_out = [(2, 0), (1, 3), (0, 1), (3, 2)]
    cross = [(1, 2), (2, 1)]

    def over_ha(values):
        return lax.ppermute(values, "ha", swap)

    def over_wa(values):
        return lax.ppermute(values, "wa", swap)

    def over_dev(values, bit):
        return lax.ppermute(values, "dev", [(i, i ^ (1 << bit)) for i in range(n_dev)])

    def reverse_bits(value):
        return sum(((value >> b) & 1) << (bits - 1 - b) for b in range(bits))

    def on_device(
        tokens, cotangent, conv_taps, norm_gain, norm_shift, w_qkv, w_proj, w_up, w_down, valid
    ):
        rows_in, half = tokens.shape
        images = rows_in // PATCHES
        rows = images * PADDED
        width = 2 * half
        heads_width = w_qkv.shape[3]
        hidden = w_up.shape[2]
        tiles = heads_width // LANES
        dev, ha, wa = (lax.axis_index(name) for name in ("dev", "ha", "wa"))
        flag = (ha == wa).astype(jnp.int32).reshape(1)
        first_ha = (ha == 0).astype(jnp.int32).reshape(1)
        chunk_at = jnp.stack([reverse_bits(p) ^ dev for p in range(n_dev)]).astype(jnp.int32)

        place = np.zeros((rows, rows_in), np.float32)
        for image in range(images):
            for patch in range(PATCHES):
                place[
                    image * PADDED + (patch // WIN) * GRID_COLS + patch % WIN,
                    image * PATCHES + patch,
                ] = 1.0
        spread = jnp.asarray(place, BF16)
        compact = jnp.asarray(place.T, BF16)

        wq_own = jnp.transpose(w_qkv, (0, 2, 1, 3))
        small = jnp.concatenate(
            [conv_taps.reshape(18, half), norm_gain, norm_shift], axis=0
        )
        near_tokens = lax.ppermute(tokens, pair, near_in)
        cross_tokens = lax.ppermute(tokens, pair, cross)
        params = jnp.concatenate([small, over_wa(small)], axis=1)
        wq_oth, wp_oth = over_wa(wq_own), over_wa(w_proj)
        wu_oth, wd_oth = over_wa(w_up), over_wa(w_down)
        near_cot = lax.ppermute(cotangent, pair, near_in)
        cross_cot = lax.ppermute(cotangent, pair, cross)

        mask = lax.dynamic_slice_in_dim(valid, wa * images, images, 0).reshape(images, WIN, WIN)
        mask = jnp.pad(mask, ((0, 0), (0, 0), (0, GRID_COLS - WIN))).reshape(rows, 1).astype(F32)

        def row(ref, index):
            return ref[index : index + 1, :]

        def unpack(flag_ref, mine, near, far, spread_ref):
            same = flag_ref[0] == 1
            own = jnp.where(same, mine[...], near[...])
            oth = jnp.where(same, near[...], far[...])
            return mm(spread_ref[...], jnp.concatenate([own, oth], axis=1), 1, 0)

        def project_in(normed, own_ref, oth_ref):
            return mm(normed[:, :half], own_ref, 1, 0) + mm(normed[:, half:], oth_ref, 1, 0)

        def to_normed(stream, params_ref, branch):
            units, _ = norm_stats(stream)
            return (units * row(params_ref, 18 + branch) + row(params_ref, 22 + branch)).astype(
                BF16
            )

        def attention_part(window, normed, mask_ref, wq_a, wq_b, qkv_ref, probs_ref):
            packed = [project_in(normed, wq_a[part], wq_b[part]).astype(BF16) for part in range(3)]
            for part in range(3):
                qkv_ref[part] = packed[part]
            wide = [part.astype(F32) for part in packed]
            mixed = []
            for image in range(images):
                line = []
                for tile in range(tiles):
                    q, k, v = (
                        part[
                            image * PADDED : (image + 1) * PADDED,
                            tile * LANES : (tile + 1) * LANES,
                        ]
                        for part in wide
                    )
                    if window:
                        probs, out = window_tile(q, k, v)
                    else:
                        valid_rows = mask_ref[image * PADDED : (image + 1) * PADDED, :]
                        probs, out = channel_tile(q, k, v, valid_rows)
                    probs_ref[image * tiles + tile] = probs
                    line.append(out)
                mixed.append(jnp.concatenate(line, axis=1))
            return jnp.concatenate(mixed, axis=0).astype(BF16)

        def attention_part_back(window, grad_mixed, mask_ref, qkv_ref, probs_ref, dpk_ref):
            wide = [qkv_ref[part].astype(F32) for part in range(3)]
            grad = grad_mixed.astype(F32)
            found = [[], [], []]
            for image in range(images):
                lines = [[], [], []]
                for tile in range(tiles):
                    rows_at = slice(image * PADDED, (image + 1) * PADDED)
                    lanes_at = slice(tile * LANES, (tile + 1) * LANES)
                    q, k, v = (part[rows_at, lanes_at] for part in wide)
                    probs = probs_ref[image * tiles + tile]
                    if window:
                        parts = window_tile_back(q, k, v, probs, grad[rows_at, lanes_at])
                    else:
                        parts = channel_tile_back(
                            q, k, v, probs, grad[rows_at, lanes_at], mask_ref[rows_at, :]
                        )
                    for line, part in zip(lines, parts):
                        line.append(part)
                for part in range(3):
                    found[part].append(jnp.concatenate(lines[part], axis=1))
            packed = [jnp.concatenate(part, axis=0).astype(BF16) for part in found]
            for part in range(3):
                dpk_ref[part] = packed[part]
            return packed

        def put_both(own_ref, oth_ref, values):
            own_ref[...] = values[:, :half]
            oth_ref[...] = values[:, half:]

        def mul_out(left, own_ref, oth_ref, out_ref):
            out_ref[:, :half] = mm(left, own_ref[...], 1, 0).astype(BF16)
            out_ref[:, half:] = mm(left, oth_ref[...], 1, 0).astype(BF16)

        def both_nt(values, own_ref, oth_ref):
            return mm(values[:, :half], own_ref[...], 1, 1) + mm(
                values[:, half:], oth_ref[...], 1, 1
            )

        def conv_into(out_ref, values, taps_at, params_ref, keep):
            for col in range(0, width, LANES):
                taps = [params_ref[taps_at + t : taps_at + t + 1, col : col + LANES] for t in range(9)]
                out_ref[:, col : col + LANES] = conv_cols(values[:, col : col + LANES], taps, keep)

        def conv_back_into(out_ref, sums_ref, sums_at, grads, values, taps_at, params_ref, keep):
            for col in range(0, width, LANES):
                lanes_at = slice(col, col + LANES)
                taps = [
                    params_ref[taps_at + 8 - t : taps_at + 9 - t, lanes_at] for t in range(9)
                ]
                for t, total in enumerate(tap_sums(grads[:, lanes_at], values[:, lanes_at])):
                    sums_ref[sums_at + t : sums_at + t + 1, lanes_at] = total
                out_ref[:, lanes_at] = conv_cols(grads[:, lanes_at], taps, keep)

        probs_shape = {
            True: (images * tiles, PADDED, HEADS_TILE * PADDED),
            False: (images * tiles, LANES, LANES),
        }
        full, full_low = sds((rows, width)), sds((rows, width), BF16)
        half_low = sds((rows, half), BF16)
        hid_low = sds((rows, hidden), BF16)
        qkv_low = sds((3, rows, heads_width), BF16)
        mixed_low = sds((rows, heads_width), BF16)

        def first_body(
            flag_ref, mine, near, far, spread_ref, params_ref, wq_a, wq_b, wp_a, wp_b,
            x_ref, s_ref, n_own, n_oth, qkv_ref, probs_ref, mixed_ref, part_ref,
        ):
            keep = column_mask(rows)
            stream = unpack(flag_ref, mine, near, far, spread_ref)
            x_ref[...] = stream.astype(BF16)
            conv_into(s_ref, stream, 0, params_ref, keep)
            normed = to_normed(s_ref[...], params_ref, 0)
            put_both(n_own, n_oth, normed)
            mixed = attention_part(True, normed, None, wq_a, wq_b, qkv_ref, probs_ref)
            mixed_ref[...] = mixed
            mul_out(mixed, wp_a, wp_b, part_ref)

        attn_flops = 2 * rows * (4 * width * heads_width)
        mlp_flops = 2 * rows * (2 * width * hidden)
        (x0, s1, n0_own, n0_oth, qkv0, probs0, mixed0, part0) = kernel_call(
            first_body, "attn_a",
            [flag, tokens, near_tokens, cross_tokens, spread, params,
             (wq_own, 0), (wq_oth, 0), (w_proj, 0), (wp_oth, 0)],
            [full_low, full, half_low, half_low, qkv_low, sds(probs_shape[True]), mixed_low, full_low],
            flops=attn_flops,
        )
        far0 = over_ha(part0)

        def mlp_body(
            s_in, part_a, part_b, params_ref, wu_a, wu_b, wd_a, wd_b,
            s_ref, n_own, n_oth, hid_ref, slope_ref, part_ref,
        ):
            s_ref[...] = s_in[...] + part_a[...].astype(F32) + part_b[...].astype(F32)
            normed = to_normed(s_ref[...], params_ref, 1)
            put_both(n_own, n_oth, normed)
            pre = project_in(normed, wu_a[...], wu_b[...])
            below, bell = gelu_parts(pre)
            hid = (pre * below).astype(BF16)
            hid_ref[...] = hid
            slope_ref[...] = below + pre * bell
            mul_out(hid, wd_a, wd_b, part_ref)

        (s2, n1_own, n1_oth, hid1, slope1, part1) = kernel_call(
            mlp_body, "mlp_b",
            [s1, part0, far0, params, (w_up, 0), (wu_oth, 0), (w_down, 0), (wd_oth, 0)],
            [full, half_low, half_low, hid_low, sds((rows, hidden)), full_low],
            flops=mlp_flops,
        )
        far1 = over_ha(part1)

        def channel_body(
            s_in, part_a, part_b, params_ref, mask_ref, wq_a, wq_b, wp_a, wp_b,
            s_before, s_ref, n_own, n_oth, qkv_ref, probs_ref, mixed_ref, part_ref,
        ):
            keep = column_mask(rows)
            total = s_in[...] + part_a[...].astype(F32) + part_b[...].astype(F32)
            s_before[...] = jnp.where(keep, total, 0.0)
            conv_into(s_ref, s_before, 9, params_ref, keep)
            normed = to_normed(s_ref[...], params_ref, 2)
            put_both(n_own, n_oth, normed)
            mixed = attention_part(False, normed, mask_ref, wq_a, wq_b, qkv_ref, probs_ref)
            mixed_ref[...] = mixed
            mul_out(mixed, wp_a, wp_b, part_ref)

        (s3, s4, n2_own, n2_oth, qkv2, probs2, mixed2, part2) = kernel_call(
            channel_body, "attn_c",
            [s2, part1, far1, params, mask, (wq_own, 1), (wq_oth, 1), (w_proj, 1), (wp_oth, 1)],
            [full, full, half_low, half_low, qkv_low, sds(probs_shape[False]), mixed_low, full_low],
            flops=attn_flops,
        )
        far2 = over_ha(part2)

        def cot_body(flag_ref, mine, near, far, spread_ref, wd_a, wd_b, g_own, g_oth, dhid_ref):
            grad = unpack(flag_ref, mine, near, far, spread_ref).astype(BF16)
            put_both(g_own, g_oth, grad)
            dhid_ref[...] = both_nt(grad, wd_a, wd_b).astype(BF16)

        g3_own, g3_oth, dhid3 = kernel_call(
            cot_body, "cot_d",
            [flag, cotangent, near_cot, cross_cot, spread, (w_down, 1), (wd_oth, 1)],
            [half_low, half_low, hid_low],
            flops=mlp_flops // 2,
        )

        def last_body(
            s_in, part_a, part_b, params_ref, dhid_ref, wu_a, wu_b,
            s_ref, n_own, n_oth, hid_ref, dpre_ref, part_ref,
        ):
            s_ref[...] = s_in[...] + part_a[...].astype(F32) + part_b[...].astype(F32)
            normed = to_normed(s_ref[...], params_ref, 3)
            put_both(n_own, n_oth, normed)
            pre = project_in(normed, wu_a[...], wu_b[...])
            below, bell = gelu_parts(pre)
            hid_ref[...] = (pre * below).astype(BF16)
            dpre = (dhid_ref[...].astype(F32) * (below + pre * bell)).astype(BF16)
            dpre_ref[...] = dpre
            part_ref[:, :half] = mm(dpre, wu_a[...], 1, 1).astype(BF16)
            part_ref[:, half:] = mm(dpre, wu_b[...], 1, 1).astype(BF16)

        (s5, n3_own, n3_oth, hid3, dpre3, back3) = kernel_call(
            last_body, "mlp_d",
            [s4, part2, far2, params, dhid3, (w_up, 1), (wu_oth, 1)],
            [full, half_low, half_low, hid_low, hid_low, full_low],
            flops=mlp_flops,
        )
        far_back3 = over_ha(back3)

        def ship(flag_ref, total, compact_ref, kept, sent, crossed):
            packed = mm(compact_ref[...], total.astype(BF16), 1, 0).astype(BF16)
            own, oth = packed[:, :half], packed[:, half:]
            kept[...] = own
            sent[...] = jnp.where(flag_ref[0] == 1, oth, own)
            crossed[...] = oth

        shipped = [sds((rows_in, half), BF16)] * 3

        def join(flag_ref, kept, near, far, out_ref):
            mine = jnp.where(flag_ref[0] == 1, kept[...], far[...])
            out_ref[...] = near[...].astype(F32) + mine.astype(F32)

        def deliver(kept, sent, crossed, name):
            near = lax.ppermute(sent, pair, near_out)
            far = lax.ppermute(crossed, pair, cross)
            return kernel_call(join, name, [flag, kept, near, far], [sds((rows_in, half))])[0]

        def out_body(flag_ref, ha_ref, s_in, hid_ref, wd_a, wd_b, compact_ref, kept, sent, crossed):
            hid = hid_ref[...]
            base = jnp.where(ha_ref[0] == 1, s_in[...], 0.0)
            branch = jnp.concatenate(
                [mm(hid, wd_a[...], 1, 0), mm(hid, wd_b[...], 1, 0)], axis=1
            )
            ship(flag_ref, base + branch, compact_ref, kept, sent, crossed)

        output_parts = kernel_call(
            out_body, "out_d",
            [flag, first_ha, s5, hid3, (w_down, 1), (wd_oth, 1), compact],
            shipped, flops=mlp_flops // 2,
        )
        output = deliver(*output_parts, "join_out")

        def reduce_chunks(kept, sent):
            for bit in range(bits):
                received = over_dev(sent, bit)
                total = kept.astype(F32) + received.astype(F32)
                if bit == bits - 1:
                    return total[0]
                total = total.astype(BF16)
                cut = total.shape[0] // 2
                kept, sent = total[:cut], total[cut:]

        def scatter_chunks(scratch, chunk_ref, kept, sent):
            cut = n_dev // 2
            for position in range(n_dev):
                target = kept if position < cut else sent
                target[position % cut] = scratch[chunk_ref[position]].astype(BF16)

        up_rows, down_rows = hidden // n_dev, half // n_dev
        folds = hidden // half
        mlp_rows = up_rows + folds * down_rows

        def mlp_weights_body(
            chunk_ref, dpre_a, dpre_b, n_a, n_b, g_a, g_b, hid_a, hid_b, kept, sent, scratch
        ):
            up = mm(dpre_a[...], n_a[...], 0, 0) + mm(dpre_b[...], n_b[...], 0, 0)
            for chunk in range(n_dev):
                scratch[chunk, :up_rows, :] = up[chunk * up_rows : (chunk + 1) * up_rows]
            down = mm(g_a[...], hid_a[...], 0, 0) + mm(g_b[...], hid_b[...], 0, 0)
            for chunk in range(n_dev):
                for fold in range(folds):
                    at = up_rows + fold * down_rows
                    scratch[chunk, at : at + down_rows, :] = down[
                        chunk * down_rows : (chunk + 1) * down_rows,
                        fold * half : (fold + 1) * half,
                    ]
            scatter_chunks(scratch, chunk_ref, kept, sent)

        def mlp_weights(dpre, n_own, n_oth, g_own, g_oth, hid, name):
            kept, sent = kernel_call(
                mlp_weights_body, name,
                [chunk_at, dpre, over_wa(dpre), n_own, over_wa(n_oth),
                 g_own, over_wa(g_oth), hid, over_wa(hid)],
                [sds((n_dev // 2, mlp_rows, half), BF16)] * 2,
                scratch=[pltpu.VMEM((n_dev, mlp_rows, half), F32)],
                flops=2 * 4 * rows * half * hidden,
            )
            total = reduce_chunks(kept, sent)
            up = total[:up_rows]
            down = total[up_rows:].reshape(folds, down_rows, half)
            return up, jnp.transpose(down, (1, 0, 2)).reshape(down_rows, hidden)

        qkv_rows, proj_rows = heads_width // n_dev, half // n_dev
        attn_rows = 3 * qkv_rows + proj_rows
        assert heads_width == half

        def attn_weights_body(
            chunk_ref, dpk_a, dpk_b, n_a, n_b, g_a, g_b, mix_a, mix_b, kept, sent, scratch
        ):
            for part in range(3):
                qkv = mm(dpk_a[part], n_a[...], 0, 0) + mm(dpk_b[part], n_b[...], 0, 0)
                for chunk in range(n_dev):
                    scratch[chunk, part * qkv_rows : (part + 1) * qkv_rows, :] = qkv[
                        chunk * qkv_rows : (chunk + 1) * qkv_rows
                    ]
            proj = mm(g_a[...], mix_a[...], 0, 0) + mm(g_b[...], mix_b[...], 0, 0)
            for chunk in range(n_dev):
                scratch[chunk, 3 * qkv_rows :, :] = proj[
                    chunk * proj_rows : (chunk + 1) * proj_rows
                ]
            scatter_chunks(scratch, chunk_ref, kept, sent)

        def attn_weights(dpk, n_own, n_oth, g_own, g_oth, mixed, name):
            kept, sent = kernel_call(
                attn_weights_body, name,
                [chunk_at, dpk, over_wa(dpk), n_own, over_wa(n_oth),
                 g_own, over_wa(g_oth), mixed, over_wa(mixed)],
                [sds((n_dev // 2, attn_rows, half), BF16)] * 2,
                scratch=[pltpu.VMEM((n_dev, attn_rows, half), F32)],
                flops=2 * 2 * rows * half * 4 * heads_width,
            )
            total = reduce_chunks(kept, sent)
            return total[: 3 * qkv_rows].reshape(3, qkv_rows, half), total[3 * qkv_rows :]

        def add_norm_back(grad, part_a, part_b, stream, params_ref, branch, sums_ref):
            upstream = part_a[...].astype(F32) + part_b[...].astype(F32)
            units, inv_std = norm_stats(stream)
            sums_ref[0:1, :] = jnp.sum(upstream * units, axis=0, keepdims=True)
            sums_ref[1:2, :] = jnp.sum(upstream, axis=0, keepdims=True)
            return grad + norm_back(upstream, units, inv_std, row(params_ref, 18 + branch))

        def qkv_back(packed, wq_a, wq_b):
            return [
                sum(mm(packed[part], ref[part], 1, 1) for part in range(3)) for ref in (wq_a, wq_b)
            ]

        def channel_back_body(
            g_in_own, g_in_oth, part_a, part_b, s_in, params_ref, mask_ref, qkv_ref, probs_ref,
            wp_a, wp_b, wq_a, wq_b, g_ref, g_own, g_oth, dpk_ref, part_ref, sums_ref,
        ):
            grad = jnp.concatenate([g_in_own[...], g_in_oth[...]], axis=1).astype(F32)
            grad = add_norm_back(grad, part_a, part_b, s_in[...], params_ref, 3, sums_ref)
            g_ref[...] = grad
            low = grad.astype(BF16)
            put_both(g_own, g_oth, low)
            grad_mixed = both_nt(low, wp_a, wp_b).astype(BF16)
            packed = attention_part_back(False, grad_mixed, mask_ref, qkv_ref, probs_ref, dpk_ref)
            own, oth = qkv_back(packed, wq_a, wq_b)
            part_ref[:, :half] = own.astype(BF16)
            part_ref[:, half:] = oth.astype(BF16)

        (g2, g2_own, g2_oth, dpk2, back2, sums3) = kernel_call(
            channel_back_body, "back_c",
            [g3_own, g3_oth, back3, far_back3, s5, params, mask, qkv2, probs2,
             (w_proj, 1), (wp_oth, 1), (wq_own, 1), (wq_oth, 1)],
            [full, half_low, half_low, qkv_low, full_low, sds((2, width))],
            flops=attn_flops,
        )
        far_back2 = over_ha(back2)
        up_one, down_one = mlp_weights(dpre3, n3_own, n3_oth, g3_own, g3_oth, hid3, "wgrad_d")

        def mlp_back_body(
            g_in, part_a, part_b, s_in, s_before, params_ref, slope_ref, wd_a, wd_b, wu_a, wu_b,
            g_ref, g_own, g_oth, dpre_ref, part_ref, sums_ref,
        ):
            keep = column_mask(rows)
            grad = add_norm_back(g_in[...], part_a, part_b, s_in[...], params_ref, 2, sums_ref)
            conv_back_into(g_ref, sums_ref, 2, grad, s_before[...], 9, params_ref, keep)
            low = g_ref[...].astype(BF16)
            put_both(g_own, g_oth, low)
            dhid = both_nt(low, wd_a, wd_b).astype(BF16).astype(F32)
            dpre = (dhid * slope_ref[...]).astype(BF16)
            dpre_ref[...] = dpre
            part_ref[:, :half] = mm(dpre, wu_a[...], 1, 1).astype(BF16)
            part_ref[:, half:] = mm(dpre, wu_b[...], 1, 1).astype(BF16)

        (g1, g1_own, g1_oth, dpre1, back1, sums2) = kernel_call(
            mlp_back_body, "back_b",
            [g2, back2, far_back2, s4, s3, params, slope1,
             (w_down, 0), (wd_oth, 0), (w_up, 0), (wu_oth, 0)],
            [full, half_low, half_low, hid_low, full_low, sds((11, width))],
            flops=mlp_flops,
        )
        far_back1 = over_ha(back1)
        qkv_one, proj_one = attn_weights(dpk2, n2_own, n2_oth, g2_own, g2_oth, mixed2, "wgrad_c")

        def window_back_body(
            g_in, part_a, part_b, s_in, params_ref, qkv_ref, probs_ref, wp_a, wp_b,
            g_ref, g_own, g_oth, dpk_ref, sums_ref,
        ):
            grad = add_norm_back(g_in[...], part_a, part_b, s_in[...], params_ref, 1, sums_ref)
            g_ref[...] = grad
            low = grad.astype(BF16)
            put_both(g_own, g_oth, low)
            grad_mixed = both_nt(low, wp_a, wp_b).astype(BF16)
            attention_part_back(True, grad_mixed, None, qkv_ref, probs_ref, dpk_ref)

        (g0, g0_own, g0_oth, dpk0, sums1) = kernel_call(
            window_back_body, "back_a",
            [g1, back1, far_back1, s2, params, qkv0, probs0, (w_proj, 0), (wp_oth, 0)],
            [full, half_low, half_low, qkv_low, sds((2, width))],
            flops=attn_flops,
        )
        up_zero, down_zero = mlp_weights(dpre1, n1_own, n1_oth, g1_own, g1_oth, hid1, "wgrad_b")
        qkv_zero, proj_zero = attn_weights(dpk0, n0_own, n0_oth, g0_own, g0_oth, mixed0, "wgrad_a")

        def first_back_body(
            flag_ref, ha_ref, g_in, dpk_ref, s_in, x_ref, params_ref, wq_a, wq_b, compact_ref,
            kept, sent, crossed, sums_ref, scratch,
        ):
            keep = column_mask(rows)
            packed = [dpk_ref[part] for part in range(3)]
            upstream = jnp.concatenate(qkv_back(packed, wq_a, wq_b), axis=1)
            units, inv_std = norm_stats(s_in[...])
            sums_ref[0:1, :] = jnp.sum(upstream * units, axis=0, keepdims=True)
            sums_ref[1:2, :] = jnp.sum(upstream, axis=0, keepdims=True)
            grad = jnp.where(ha_ref[0] == 1, g_in[...], 0.0)
            grad = grad + norm_back(upstream, units, inv_std, row(params_ref, 18))
            conv_back_into(
                scratch, sums_ref, 2, grad, x_ref[...].astype(F32), 0, params_ref, keep
            )
            ship(flag_ref, scratch[...], compact_ref, kept, sent, crossed)

        *token_parts, sums0 = kernel_call(
            first_back_body, "back_0",
            [flag, first_ha, g0, dpk0, s1, x0, params, (wq_own, 0), (wq_oth, 0), compact],
            shipped + [sds((11, width))],
            scratch=[pltpu.VMEM((rows, width), F32)],
            flops=attn_flops * 3 // 4,
        )
        grad_tokens = deliver(*token_parts, "join_tokens")

        sums = jnp.concatenate([sums0, 0.5 * sums1, 0.5 * sums2, 0.5 * sums3], axis=0)
        total = sums[:, :half] + over_wa(sums[:, half:])
        total = total + over_ha(total)
        for bit in range(bits):
            total = total + over_dev(total, bit)
        gain_at, shift_at = (0, 11, 13, 24), (1, 12, 14, 25)
        grad_gain = jnp.stack([total[at] for at in gain_at])
        grad_shift = jnp.stack([total[at] for at in shift_at])
        grad_taps = jnp.stack([total[2:11], total[15:24]])

        grad_qkv = jnp.transpose(jnp.stack([qkv_zero, qkv_one]), (0, 3, 1, 2))
        grad_proj = jnp.transpose(jnp.stack([proj_zero, proj_one]), (0, 2, 1))
        grad_up = jnp.transpose(jnp.stack([up_zero, up_one]), (0, 2, 1))
        grad_down = jnp.transpose(jnp.stack([down_zero, down_one]), (0, 2, 1))
        return (
            output,
            grad_tokens,
            grad_taps,
            grad_gain,
            grad_shift,
            grad_qkv,
            grad_proj,
            grad_up,
            grad_down,
        )

    placed = (
        P(("dev", "ha"), "wa"),
        P(("dev", "ha"), "wa"),
        P(None, None, "wa"),
        P(None, "wa"),
        P(None, "wa"),
        P(None, "wa", None, "ha"),
        P(None, "ha", "wa"),
        P(None, "wa", "ha"),
        P(None, "ha", "wa"),
        P("dev", None),
    )
    return jax.shard_map(
        on_device,
        mesh=mesh,
        in_specs=placed,
        out_specs=(
            P(("dev", "ha"), "wa"),
            P(("dev", "ha"), "wa"),
            P(None, None, "wa"),
            P(None, "wa"),
            P(None, "wa"),
            P(None, "wa", None, ("ha", "dev")),
            P(None, "ha", ("wa", "dev")),
            P(None, "wa", ("ha", "dev")),
            P(None, "ha", ("wa", "dev")),
        ),
        check_vma=False,
    )
```

```python
from functools import partial

import jax
import jax.numpy as jnp
import numpy as np
from jax import lax
from jax.experimental import pallas as pl
from jax.experimental.pallas import tpu as pltpu
from jax.sharding import PartitionSpec as P

WIN = 7
GRID_COLS = 8
PATCHES = 49
PADDED = WIN * GRID_COLS
HEAD_DIM = 32
LANES = 128
HEADS_TILE = LANES // HEAD_DIM
EPS = 1e-05
NEG = -1e30
BF16 = jnp.bfloat16
F32 = jnp.float32
VMEM_LIMIT = 16 * 2**20


def mm(left, right, left_dim, right_dim):
    return lax.dot_general(
        left, right, (((left_dim,), (right_dim,)), ((), ())), preferred_element_type=F32
    )


class Order:
    def __init__(self):
        self.last = None


def kernel_call(body, name, ins, outs, order, scratch=(), flops=0, hold=()):
    arrays = list(ins) + list(hold) + ([] if order.last is None else [order.last])
    specs = [
        pl.BlockSpec(
            memory_space=pltpu.SMEM if a.dtype == jnp.int32 and a.ndim == 1 else pltpu.VMEM
        )
        for a in arrays
    ]
    outs = list(outs) + [sds((8, LANES))]

    def wrapped(*refs):
        given = refs[: len(ins)] + refs[len(arrays) : len(arrays) + len(outs) - 1]
        body(*given, *refs[len(arrays) + len(outs) :])
        mark = refs[len(arrays) + len(outs) - 1]
        mark[...] = jnp.zeros_like(mark)

    moved = sum(int(np.prod(o.shape)) * o.dtype.itemsize for o in outs) + sum(
        int(np.prod(a.shape)) * a.dtype.itemsize for a in ins
    )
    *results, order.last = pl.pallas_call(
        wrapped,
        in_specs=specs,
        out_specs=[pl.BlockSpec(memory_space=pltpu.VMEM)] * len(outs),
        out_shape=outs,
        scratch_shapes=list(scratch),
        compiler_params=pltpu.CompilerParams(vmem_limit_bytes=VMEM_LIMIT),
        cost_estimate=pl.CostEstimate(flops=0, bytes_accessed=0, transcendentals=0),
        name=name,
    )(*arrays)
    return results


def sds(shape, dtype=F32):
    return jax.ShapeDtypeStruct(shape, dtype)


def column_mask(rows):
    return (lax.broadcasted_iota(jnp.int32, (rows, 1), 0) % GRID_COLS) < WIN


def placement(images, transposed):
    padded, plain = images * PADDED, images * PATCHES
    shape = (plain, padded) if transposed else (padded, plain)
    at = lax.broadcasted_iota(jnp.int32, shape, 1 if transposed else 0)
    image = sum((at >= i * PADDED).astype(jnp.int32) for i in range(1, images))
    inside = at - image * PADDED
    source = image * PATCHES + (inside >> 3) * WIN + (inside & 7)
    other = lax.broadcasted_iota(jnp.int32, shape, 0 if transposed else 1)
    return (((inside & 7) < WIN) & (source == other)).astype(F32).astype(BF16)


def side_shifts(values):
    rows = values.shape[0]
    return (pltpu.roll(values, 1, 0), values, pltpu.roll(values, rows - 1, 0))


def as_grid(values):
    return values.reshape(-1, WIN, GRID_COLS, values.shape[-1])


def move_rows(values, step):
    grid = as_grid(values)
    zeros = jnp.zeros_like(grid[:, :1])
    if step > 0:
        moved = jnp.concatenate([zeros, grid[:, :-1]], axis=1)
    else:
        moved = jnp.concatenate([grid[:, 1:], zeros], axis=1)
    return moved.reshape(values.shape)


def conv_cols(values, taps, keep):
    shifted = side_shifts(values)
    line = [
        sum(shifted[col] * taps[3 * row + col] for col in range(3)) for row in range(3)
    ]
    total = values + line[1] + move_rows(line[0], 1) + move_rows(line[2], -1)
    return jnp.where(keep, total, 0.0)


def tap_sums(grads, values):
    shifted = side_shifts(values)
    grad_grid = as_grid(grads)
    sums = []
    for row in range(3):
        for col in range(3):
            moved = as_grid(shifted[col])
            if row == 0:
                prod = grad_grid[:, 1:] * moved[:, :-1]
            elif row == 1:
                prod = grad_grid * moved
            else:
                prod = grad_grid[:, :-1] * moved[:, 1:]
            flat = prod.reshape(-1, GRID_COLS, prod.shape[-1])
            sums.append(jnp.sum(jnp.sum(flat, axis=0), axis=0, keepdims=True))
    return sums


def norm_stats(stream):
    width = stream.shape[1]
    center = jnp.sum(stream, axis=1, keepdims=True) * (1.0 / width)
    moved = stream - center
    inv_std = lax.rsqrt(jnp.sum(moved * moved, axis=1, keepdims=True) * (1.0 / width) + EPS)
    return moved * inv_std, inv_std


def norm_back(upstream, units, inv_std, gain):
    width = upstream.shape[1]
    scaled = upstream * gain
    first = jnp.sum(scaled, axis=1, keepdims=True) * (1.0 / width)
    second = jnp.sum(scaled * units, axis=1, keepdims=True) * (1.0 / width)
    return inv_std * (scaled - first - units * second)


def gelu_parts(values):
    z = jnp.abs(values) * (0.5**0.5)
    t = 1.0 / (1.0 + 0.3275911 * z)
    bell = jnp.exp(-z * z)
    poly = t * (
        0.254829592
        + t * (-0.284496736 + t * (1.421413741 + t * (-1.453152027 + t * 1.061405429)))
    )
    tail = 0.5 * poly * bell
    return jnp.where(values < 0, tail, 1.0 - tail), bell * float(1.0 / np.sqrt(2.0 * np.pi))


def head_mask(index):
    return (lax.broadcasted_iota(jnp.int32, (1, LANES), 1) // HEAD_DIM) == index


def spread_heads(tile):
    return jnp.concatenate(
        [jnp.where(head_mask(j), tile, 0.0) for j in range(HEADS_TILE)], axis=0
    ).astype(BF16)


def gather_heads(stacked):
    rows = stacked.shape[0] // HEADS_TILE
    total = jnp.where(head_mask(0), stacked[:rows], 0.0)
    for j in range(1, HEADS_TILE):
        total = jnp.where(head_mask(j), stacked[j * rows : (j + 1) * rows], total)
    return total


def softmax_rows(scores):
    top = jnp.max(scores, axis=0, keepdims=True)
    weights = jnp.exp(scores - top)
    return weights / jnp.sum(weights, axis=0, keepdims=True)


SCALE = HEAD_DIM**-0.5


def window_tile(q, k, v):
    keys_ok = column_mask(PADDED)
    scores = mm(k.astype(BF16), spread_heads(q), 1, 1) * SCALE
    probs = softmax_rows(jnp.where(keys_ok, scores, NEG))
    return probs, gather_heads(mm(probs.astype(BF16), v.astype(BF16), 0, 0))


def window_tile_back(q, k, v, probs, grad):
    low = probs.astype(BF16)
    q_big, g_big = spread_heads(q), spread_heads(grad)
    grad_probs = mm(v.astype(BF16), g_big, 1, 1)
    grad_v = mm(low, g_big, 1, 0)
    grad_scores = (
        probs * (grad_probs - jnp.sum(grad_probs * probs, axis=0, keepdims=True))
    ).astype(BF16)
    grad_k = mm(grad_scores, q_big, 1, 0) * SCALE
    grad_q = gather_heads(mm(grad_scores, k.astype(BF16), 0, 0)) * SCALE
    return grad_q, grad_k, grad_v


def same_head():
    first = lax.broadcasted_iota(jnp.int32, (LANES, LANES), 0) // HEAD_DIM
    second = lax.broadcasted_iota(jnp.int32, (LANES, LANES), 1) // HEAD_DIM
    return first == second


def channel_tile(q, k, v, mask):
    scores = mm(k.astype(BF16), (q * mask).astype(BF16), 0, 0) * SCALE
    probs = softmax_rows(jnp.where(same_head(), scores, NEG))
    return probs, mm(v.astype(BF16), probs.astype(BF16), 1, 0)


def channel_tile_back(q, k, v, probs, grad, mask):
    low = probs.astype(BF16)
    grad_low = grad.astype(BF16)
    grad_probs = mm(v.astype(BF16), grad_low, 0, 0)
    grad_v = mm(grad_low, low, 1, 1)
    grad_scores = (
        probs * (grad_probs - jnp.sum(grad_probs * probs, axis=0, keepdims=True))
    ).astype(BF16)
    grad_q = mm(k.astype(BF16), grad_scores, 1, 0) * SCALE * mask
    grad_k = mm((q * mask).astype(BF16), grad_scores, 1, 1) * SCALE
    return grad_q, grad_k, grad_v


def solution(mesh):
    n_dev = mesh.shape["dev"]
    bits = n_dev.bit_length() - 1
    assert n_dev == 1 << bits and mesh.shape["ha"] == 2 and mesh.shape["wa"] == 2

    swap = [(0, 1), (1, 0)]

    def over_ha(values):
        return lax.ppermute(values, "ha", swap)

    def over_wa(values):
        return lax.ppermute(values, "wa", swap)

    def over_dev(values, bit):
        return lax.ppermute(values, "dev", [(i, i ^ (1 << bit)) for i in range(n_dev)])

    def on_device(
        tokens, cotangent, conv_taps, norm_gain, norm_shift, w_qkv, w_proj, w_up, w_down, valid
    ):
        rows_in, half = tokens.shape
        images = rows_in // PATCHES
        rows = images * PADDED
        width = 2 * half
        heads_width = w_qkv.shape[3]
        hidden = w_up.shape[2]
        tiles = heads_width // LANES
        assert heads_width == half
        dev, ha, wa = (lax.axis_index(name) for name in ("dev", "ha", "wa"))
        orders = [list(range(bits)), [1, 0, *range(2, bits)]]

        def chunk_of(place, order):
            found = 0
            for step, bit in enumerate(order):
                found |= ((place >> (bits - 1 - step)) & 1) << bit
            return found ^ dev

        where = jnp.stack(
            [(ha == wa).astype(jnp.int32), (ha == 0).astype(jnp.int32), wa]
            + [chunk_of(place, order) for order in orders for place in range(n_dev)]
        ).astype(jnp.int32)

        order = Order()
        call = partial(kernel_call, order=order)

        def spread_rows(values):
            received = over_ha(values)
            oth = over_wa(jnp.where(ha == wa, received, values))
            return values, received, oth

        def later(values, event):
            return lax.optimization_barrier((values, event))[0]

        token_parts = spread_rows(tokens)
        small_own = jnp.concatenate([conv_taps.reshape(18, half), norm_gain, norm_shift], axis=0)
        small = (small_own, over_wa(small_own))

        def both_cores(values, event):
            return values, over_wa(later(values, event))

        wq_all = jnp.transpose(w_qkv, (0, 2, 1, 3))
        wq = [both_cores(wq_all[0], small[1])]
        wp = [both_cores(w_proj[0], small[1])]

        def unpack(where_ref, mine, received, oth):
            own = jnp.where(where_ref[0] == 1, mine[...], received[...])
            values = jnp.concatenate([own, oth[...]], axis=1)
            return mm(placement(images, False), values, 1, 0)

        def gain_row(refs, branch):
            return jnp.concatenate([ref[18 + branch : 19 + branch, :] for ref in refs], axis=1)

        def shift_row(refs, branch):
            return jnp.concatenate([ref[22 + branch : 23 + branch, :] for ref in refs], axis=1)

        def tap_rows(small_refs, section, col, flipped):
            ref = small_refs[col // half]
            at = col % half
            found = [
                ref[9 * section + t : 9 * section + t + 1, at : at + LANES] for t in range(9)
            ]
            return found[::-1] if flipped else found

        def project_in(normed, first, second):
            return mm(normed[:, :half], first, 1, 0) + mm(normed[:, half:], second, 1, 0)

        def project_back(values, first, second):
            return mm(values[:, :half], first, 1, 1) + mm(values[:, half:], second, 1, 1)

        def to_normed(stream, small_refs, branch):
            units, _ = norm_stats(stream)
            return (units * gain_row(small_refs, branch) + shift_row(small_refs, branch)).astype(
                BF16
            )

        def put_both(own_ref, oth_ref, values):
            own_ref[...] = values[:, :half]
            oth_ref[...] = values[:, half:]

        def add_parts(stream, part_a, part_b):
            return stream[...] + part_a[...].astype(F32) + part_b[...].astype(F32)

        def attention_part(window, normed, valid_rows, wq_a, wq_b, qkv_ref, probs_ref):
            packed = [
                project_in(normed, wq_a[part], wq_b[part]).astype(BF16)
                for part in range(3)
            ]
            for part in range(3):
                qkv_ref[part] = packed[part]
            wide = [part.astype(F32) for part in packed]
            mixed = []
            for image in range(images):
                line = []
                rows_at = slice(image * PADDED, (image + 1) * PADDED)
                for tile in range(tiles):
                    lanes_at = slice(tile * LANES, (tile + 1) * LANES)
                    q, k, v = (part[rows_at, lanes_at] for part in wide)
                    if window:
                        probs, out = window_tile(q, k, v)
                    else:
                        probs, out = channel_tile(q, k, v, valid_rows[image])
                    probs_ref[image * tiles + tile] = probs
                    line.append(out)
                mixed.append(jnp.concatenate(line, axis=1))
            return jnp.concatenate(mixed, axis=0).astype(BF16)

        def attention_part_back(window, grad_mixed, mask_ref, qkv_ref, probs_ref, dpk_ref):
            wide = [qkv_ref[part].astype(F32) for part in range(3)]
            grad = grad_mixed.astype(F32)
            found = [[], [], []]
            for image in range(images):
                lines = [[], [], []]
                for tile in range(tiles):
                    rows_at = slice(image * PADDED, (image + 1) * PADDED)
                    lanes_at = slice(tile * LANES, (tile + 1) * LANES)
                    q, k, v = (part[rows_at, lanes_at] for part in wide)
                    probs = probs_ref[image * tiles + tile]
                    if window:
                        parts = window_tile_back(q, k, v, probs, grad[rows_at, lanes_at])
                    else:
                        parts = channel_tile_back(
                            q, k, v, probs, grad[rows_at, lanes_at], mask_ref[rows_at, :]
                        )
                    for line, part in zip(lines, parts):
                        line.append(part)
                for part in range(3):
                    found[part].append(jnp.concatenate(lines[part], axis=1))
            packed = [jnp.concatenate(part, axis=0).astype(BF16) for part in found]
            for part in range(3):
                dpk_ref[part] = packed[part]
            return packed

        def mul_out(left, own_ref, oth_ref, out_ref):
            out_ref[:, :half] = mm(left, own_ref[...], 1, 0).astype(BF16)
            out_ref[:, half:] = mm(left, oth_ref[...], 1, 0).astype(BF16)

        def conv_into(out_ref, values, small_refs, section, keep):
            for col in range(0, width, LANES):
                taps = tap_rows(small_refs, section, col, False)
                out_ref[:, col : col + LANES] = conv_cols(values[:, col : col + LANES], taps, keep)

        def conv_back_into(out_ref, sums_ref, sums_at, grads, values, small_refs, section, keep):
            for col in range(0, width, LANES):
                lanes_at = slice(col, col + LANES)
                taps = tap_rows(small_refs, section, col, True)
                for t, total in enumerate(tap_sums(grads[:, lanes_at], values[:, lanes_at])):
                    sums_ref[sums_at + t : sums_at + t + 1, lanes_at] = total
                out_ref[:, lanes_at] = conv_cols(grads[:, lanes_at], taps, keep)

        window_probs = sds((images * tiles, PADDED, HEADS_TILE * PADDED))
        channel_probs = sds((images * tiles, LANES, LANES))
        full, full_low = sds((rows, width)), sds((rows, width), BF16)
        half_low = sds((rows, half), BF16)
        hid_low = sds((rows, hidden), BF16)
        qkv_low = sds((3, rows, heads_width), BF16)
        attn_flops = 2 * rows * (4 * width * heads_width)
        mlp_flops = 2 * rows * (2 * width * hidden)

        def first_body(
            where_ref, mine, received, far, small_a, small_b, wq_a, wq_b, wp_a, wp_b,
            x_ref, s_ref, n_own, n_oth, qkv_ref, probs_ref, mixed_ref, part_ref, keep_a, keep_b,
        ):
            keep_a[...], keep_b[...] = small_a[...], small_b[...]
            keep = column_mask(rows)
            stream = unpack(where_ref, mine, received, far)
            x_ref[...] = stream.astype(BF16)
            conv_into(s_ref, stream, (small_a, small_b), 0, keep)
            normed = to_normed(s_ref[...], (small_a, small_b), 0)
            put_both(n_own, n_oth, normed)
            mixed = attention_part(True, normed, None, wq_a, wq_b, qkv_ref, probs_ref)
            mixed_ref[...] = mixed
            mul_out(mixed, wp_a, wp_b, part_ref)

        (x0, s1, n0_own, n0_oth, qkv0, probs0, mixed0, part0, *small) = call(
            first_body, "attn_a",
            [where, *token_parts, *small, *wq[0], *wp[0]],
            [full_low, full, half_low, half_low, qkv_low, window_probs, half_low, full_low]
            + [sds((26, half))] * 2,
            flops=attn_flops,
        )
        far0 = over_ha(part0)
        wq.append(both_cores(later(wq_all[1], part0), part0))
        wp.append(both_cores(later(w_proj[1], part0), part0))
        wu = [both_cores(later(w_up[at], part0), part0) for at in range(2)]
        wd = [both_cores(later(w_down[at], part0), part0) for at in range(2)]
        cot_parts = spread_rows(later(cotangent, part0))
        keep_a = [x0, n0_own, n0_oth, qkv0, probs0, mixed0, s1]

        def mlp_body(
            s_in, part_a, part_b, small_a, small_b, wu_a, wu_b, wd_a, wd_b,
            s_ref, n_own, n_oth, hid_ref, slope_ref, part_ref,
        ):
            s_ref[...] = add_parts(s_in, part_a, part_b)
            normed = to_normed(s_ref[...], (small_a, small_b), 1)
            put_both(n_own, n_oth, normed)
            pre = project_in(normed, wu_a[...], wu_b[...])
            below, bell = gelu_parts(pre)
            hid = (pre * below).astype(BF16)
            hid_ref[...] = hid
            slope_ref[...] = below + pre * bell
            mul_out(hid, wd_a, wd_b, part_ref)

        (s2, n1_own, n1_oth, hid1, slope1, part1) = call(
            mlp_body, "mlp_b",
            [s1, part0, far0, *small, *wu[0], *wd[0]],
            [full, half_low, half_low, hid_low, sds((rows, hidden)), full_low],
            flops=mlp_flops, hold=[*keep_a, *wq[0], *wp[0]],
        )
        far1 = over_ha(part1)
        keep_b = [s2, n1_own, n1_oth, hid1, slope1]
        weights0 = [*wq[0], *wp[0], *wu[0], *wd[0]]

        def cot_body(where_ref, mine, received, far, wd_a, wd_b, g_own, g_oth, dhid_ref):
            grad = unpack(where_ref, mine, received, far).astype(BF16)
            put_both(g_own, g_oth, grad)
            dhid_ref[...] = project_back(grad, wd_a[...], wd_b[...]).astype(BF16)

        g3_own, g3_oth, dhid3 = call(
            cot_body, "cot_d",
            [where, *cot_parts, *wd[1]],
            [half_low, half_low, hid_low],
            flops=mlp_flops // 2, hold=[*keep_a, *keep_b, *small, *weights0],
        )

        def channel_body(
            where_ref, s_in, part_a, part_b, valid_ref, small_a, small_b,
            wq_a, wq_b, wp_a, wp_b,
            s_before, s_ref, n_own, n_oth, qkv_ref, probs_ref, mixed_ref, part_ref, mask_ref,
        ):
            keep = column_mask(rows)
            s_before[...] = jnp.where(keep, add_parts(s_in, part_a, part_b), 0.0)
            conv_into(s_ref, s_before, (small_a, small_b), 1, keep)
            normed = to_normed(s_ref[...], (small_a, small_b), 2)
            put_both(n_own, n_oth, normed)
            one_image = placement(1, False).astype(F32)
            valid_rows = []
            for image in range(images):
                line = jnp.where(
                    where_ref[2] == 0,
                    valid_ref[image : image + 1, :],
                    valid_ref[images + image : images + image + 1, :],
                ).astype(F32)
                valid_rows.append(jnp.sum(one_image * line, axis=1, keepdims=True))
                mask_ref[image * PADDED : (image + 1) * PADDED, :] = valid_rows[image]
            mixed = attention_part(False, normed, valid_rows, wq_a, wq_b, qkv_ref, probs_ref)
            mixed_ref[...] = mixed
            mul_out(mixed, wp_a, wp_b, part_ref)

        (s3, s4, n2_own, n2_oth, qkv2, probs2, mixed2, part2, mask) = call(
            channel_body, "attn_c",
            [where, s2, part1, far1, valid, *small, *wq[1], *wp[1]],
            [full, full, half_low, half_low, qkv_low, channel_probs, half_low, full_low,
             sds((rows, 1))],
            flops=attn_flops,
            hold=[*keep_a, *keep_b, g3_own, g3_oth, dhid3, *weights0, *wd[1]],
        )
        far2 = over_ha(part2)
        keep_c = [s3, s4, n2_own, n2_oth, qkv2, probs2, mixed2, mask]
        weights = [*weights0, *wq[1], *wp[1], *wu[1], *wd[1]]

        def last_body(
            s_in, part_a, part_b, small_a, small_b, dhid_ref, wu_a, wu_b,
            s_ref, n_own, n_oth, hid_ref, dpre_ref, part_ref,
        ):
            s_ref[...] = add_parts(s_in, part_a, part_b)
            normed = to_normed(s_ref[...], (small_a, small_b), 3)
            put_both(n_own, n_oth, normed)
            pre = project_in(normed, wu_a[...], wu_b[...])
            below, bell = gelu_parts(pre)
            hid_ref[...] = (pre * below).astype(BF16)
            dpre = (dhid_ref[...].astype(F32) * (below + pre * bell)).astype(BF16)
            dpre_ref[...] = dpre
            part_ref[:, :half] = mm(dpre, wu_a[...], 1, 1).astype(BF16)
            part_ref[:, half:] = mm(dpre, wu_b[...], 1, 1).astype(BF16)

        (s5, n3_own, n3_oth, hid3, dpre3, back3) = call(
            last_body, "mlp_d",
            [s4, part2, far2, *small, dhid3, *wu[1]],
            [full, half_low, half_low, hid_low, hid_low, full_low],
            flops=mlp_flops,
            hold=[*keep_a, *keep_b, *keep_c, g3_own, g3_oth, *weights0, *wq[1], *wp[1], *wd[1]],
        )
        far_back3 = over_ha(back3)

        def halve(kept, received, name, hold=()):
            cut = kept.shape[0] // 2

            def last_sum(kept_ref, received_ref, out_ref):
                out_ref[...] = kept_ref[0].astype(F32) + received_ref[0].astype(F32)

            def half_sum(kept_ref, received_ref, stay_ref, go_ref):
                for at in range(2 * cut):
                    total = (kept_ref[at].astype(F32) + received_ref[at].astype(F32)).astype(BF16)
                    (stay_ref if at < cut else go_ref)[at % cut] = total

            if cut == 0:
                return call(
                    last_sum, name, [kept, received], [sds(kept.shape[1:])], hold=hold
                )[0]
            return call(
                half_sum, name, [kept, received], [sds((cut,) + kept.shape[1:], BF16)] * 2, hold=hold
            )

        def scatter_chunks(scratch, where_ref, which, kept, sent):
            cut = n_dev // 2
            for at in range(n_dev):
                target = kept if at < cut else sent
                target[at % cut] = scratch[where_ref[3 + which * n_dev + at]].astype(BF16)

        up_rows, down_rows = hidden // n_dev, half // n_dev
        folds = hidden // half
        mlp_rows = up_rows + folds * down_rows

        def mlp_weights_body(
            where_ref, dpre_a, dpre_b, n_a, n_b, g_a, g_b, hid_a, hid_b, kept, sent, scratch
        ):
            up = mm(dpre_a[...], n_a[...], 0, 0) + mm(dpre_b[...], n_b[...], 0, 0)
            for chunk in range(n_dev):
                scratch[chunk, :up_rows, :] = up[chunk * up_rows : (chunk + 1) * up_rows]
            down = mm(g_a[...], hid_a[...], 0, 0) + mm(g_b[...], hid_b[...], 0, 0)
            for chunk in range(n_dev):
                for fold in range(folds):
                    at = up_rows + fold * down_rows
                    scratch[chunk, at : at + down_rows, :] = down[
                        chunk * down_rows : (chunk + 1) * down_rows,
                        fold * half : (fold + 1) * half,
                    ]
            scatter_chunks(scratch, where_ref, 0, kept, sent)

        def mlp_weights(dpre, n_own, n_oth, g_own, g_oth, hid, name, hold):
            return call(
                mlp_weights_body, name,
                [where, dpre, over_wa(dpre), n_own, over_wa(n_oth),
                 g_own, over_wa(g_oth), hid, over_wa(hid)],
                [sds((n_dev // 2, mlp_rows, half), BF16)] * 2,
                scratch=[pltpu.VMEM((n_dev, mlp_rows, half), F32)],
                flops=2 * 4 * rows * half * hidden, hold=hold,
            )

        qkv_rows, proj_rows = heads_width // n_dev, half // n_dev
        attn_rows = 3 * qkv_rows + proj_rows

        def attn_weights_body(
            where_ref, dpk_a, dpk_b, n_a, n_b, g_a, g_b, mix_a, mix_b, kept, sent, scratch
        ):
            for part in range(3):
                qkv = mm(dpk_a[part], n_a[...], 0, 0) + mm(dpk_b[part], n_b[...], 0, 0)
                for chunk in range(n_dev):
                    scratch[chunk, part * qkv_rows : (part + 1) * qkv_rows, :] = qkv[
                        chunk * qkv_rows : (chunk + 1) * qkv_rows
                    ]
            proj = mm(g_a[...], mix_a[...], 0, 0) + mm(g_b[...], mix_b[...], 0, 0)
            for chunk in range(n_dev):
                scratch[chunk, 3 * qkv_rows :, :] = proj[
                    chunk * proj_rows : (chunk + 1) * proj_rows
                ]
            scatter_chunks(scratch, where_ref, 1, kept, sent)

        def attn_weights(dpk, n_own, n_oth, g_own, g_oth, mixed, name, hold):
            return call(
                attn_weights_body, name,
                [where, dpk, over_wa(dpk), n_own, over_wa(n_oth),
                 g_own, over_wa(g_oth), mixed, over_wa(mixed)],
                [sds((n_dev // 2, attn_rows, half), BF16)] * 2,
                scratch=[pltpu.VMEM((n_dev, attn_rows, half), F32)],
                flops=2 * 2 * rows * half * 4 * heads_width, hold=hold,
            )

        def send(values, which, step):
            return over_dev(values, orders[which][step])

        def ship(total, kept, sent):
            packed = mm(placement(images, True), total.astype(BF16), 1, 0).astype(BF16)
            kept[...] = packed[:, :half]
            sent[...] = packed[:, half:]

        shipped = [sds((rows_in, half), BF16)] * 2

        def fold(where_ref, kept, received, stay, go):
            same = where_ref[0] == 1
            stay[...] = jnp.where(same, kept[...], received[...])
            go[...] = jnp.where(same, received[...], kept[...])

        def join(stay, received, out_ref):
            out_ref[...] = stay[...].astype(F32) + received[...].astype(F32)

        def out_body(where_ref, s_in, hid_ref, wd_a, wd_b, kept, sent):
            hid = hid_ref[...]
            base = jnp.where(where_ref[1] == 1, s_in[...], 0.0)
            branch = jnp.concatenate([mm(hid, wd_a[...], 1, 0), mm(hid, wd_b[...], 1, 0)], axis=1)
            ship(base + branch, kept, sent)

        kept_d, sent_d = mlp_weights(
            dpre3, n3_own, n3_oth, g3_own, g3_oth, hid3, "wgrad_d",
            [*keep_a, *keep_b, *keep_c, *small, *weights, s5],
        )
        got_d = send(sent_d, 0, 0)

        def add_norm_back(grad, part_a, part_b, stream, gain, sums_ref):
            upstream = part_a[...].astype(F32) + part_b[...].astype(F32)
            units, inv_std = norm_stats(stream)
            sums_ref[0:1, :] = jnp.sum(upstream * units, axis=0, keepdims=True)
            sums_ref[1:2, :] = jnp.sum(upstream, axis=0, keepdims=True)
            return grad + norm_back(upstream, units, inv_std, gain)

        def qkv_back(packed, wq_a, wq_b):
            return [
                sum(mm(packed[part], ref[part], 1, 1) for part in range(3)) for ref in (wq_a, wq_b)
            ]

        def channel_back_body(
            g_in_own, g_in_oth, part_a, part_b, s_in, small_a, small_b, mask_ref, qkv_ref,
            probs_ref, wp_a, wp_b, wq_a, wq_b, g_ref, g_own, g_oth, dpk_ref, part_ref, sums_ref,
        ):
            grad = jnp.concatenate([g_in_own[...], g_in_oth[...]], axis=1).astype(F32)
            gain = gain_row((small_a, small_b), 3)
            grad = add_norm_back(grad, part_a, part_b, s_in[...], gain, sums_ref)
            g_ref[...] = grad
            low = grad.astype(BF16)
            put_both(g_own, g_oth, low)
            grad_mixed = project_back(low, wp_a[...], wp_b[...]).astype(BF16)
            packed = attention_part_back(False, grad_mixed, mask_ref, qkv_ref, probs_ref, dpk_ref)
            own, oth = qkv_back(packed, wq_a, wq_b)
            part_ref[:, :half] = own.astype(BF16)
            part_ref[:, half:] = oth.astype(BF16)

        late = [hid3, *wd[1], s5]
        (g2, g2_own, g2_oth, dpk2, back2, sums3) = call(
            channel_back_body, "back_c",
            [g3_own, g3_oth, back3, far_back3, s5, *small, mask, qkv2, probs2, *wp[1], *wq[1]],
            [full, half_low, half_low, qkv_low, full_low, sds((2, width))],
            flops=attn_flops,
            hold=[*keep_a, *keep_b, s3, s4, n2_own, n2_oth, mixed2, *weights0, hid3, *wd[1]],
        )
        far_back2 = over_ha(back2)
        kept_c, sent_c = attn_weights(
            dpk2, n2_own, n2_oth, g2_own, g2_oth, mixed2, "wgrad_c",
            [*keep_a, *keep_b, s3, s4, *small, *weights0, g2, *late],
        )
        got_c = send(sent_c, 1, 0)

        def mlp_back_body(
            g_in, part_a, part_b, s_in, s_before, small_a, small_b, slope_ref,
            wd_a, wd_b, wu_a, wu_b, g_ref, g_own, g_oth, dpre_ref, part_ref, sums_ref,
        ):
            keep = column_mask(rows)
            gain = gain_row((small_a, small_b), 2)
            grad = add_norm_back(g_in[...], part_a, part_b, s_in[...], gain, sums_ref)
            conv_back_into(g_ref, sums_ref, 2, grad, s_before[...], (small_a, small_b), 1, keep)
            low = g_ref[...].astype(BF16)
            put_both(g_own, g_oth, low)
            dhid = project_back(low, wd_a[...], wd_b[...]).astype(BF16).astype(F32)
            dpre = (dhid * slope_ref[...]).astype(BF16)
            dpre_ref[...] = dpre
            part_ref[:, :half] = mm(dpre, wu_a[...], 1, 1).astype(BF16)
            part_ref[:, half:] = mm(dpre, wu_b[...], 1, 1).astype(BF16)

        (g1, g1_own, g1_oth, dpre1, back1, sums2) = call(
            mlp_back_body, "back_b",
            [g2, back2, far_back2, s4, s3, *small, slope1, *wd[0], *wu[0]],
            [full, half_low, half_low, hid_low, full_low, sds((11, width))],
            flops=mlp_flops, hold=[*keep_a, s2, n1_own, n1_oth, hid1, *wq[0], *wp[0], *late],
        )
        far_back1 = over_ha(back1)
        kept_b, sent_b = mlp_weights(
            dpre1, n1_own, n1_oth, g1_own, g1_oth, hid1, "wgrad_b",
            [*keep_a, s2, *small, *wq[0], *wp[0], g1, *late],
        )
        got_b = send(sent_b, 0, 0)

        def window_back_body(
            g_in, part_a, part_b, s_in, small_a, small_b, qkv_ref, probs_ref, wp_a, wp_b,
            g_ref, g_own, g_oth, dpk_ref, sums_ref,
        ):
            gain = gain_row((small_a, small_b), 1)
            grad = add_norm_back(g_in[...], part_a, part_b, s_in[...], gain, sums_ref)
            g_ref[...] = grad
            low = grad.astype(BF16)
            put_both(g_own, g_oth, low)
            grad_mixed = project_back(low, wp_a[...], wp_b[...]).astype(BF16)
            attention_part_back(True, grad_mixed, None, qkv_ref, probs_ref, dpk_ref)

        (g0, g0_own, g0_oth, dpk0, sums1) = call(
            window_back_body, "back_a",
            [g1, back1, far_back1, s2, *small, qkv0, probs0, *wp[0]],
            [full, half_low, half_low, qkv_low, sds((2, width))],
            flops=attn_flops, hold=[x0, n0_own, n0_oth, mixed0, s1, *wq[0], *late],
        )

        def first_back_body(
            where_ref, g_in, dpk_ref, s_in, x_ref, small_a, small_b, wq_a, wq_b,
            kept, sent, sums_ref, scratch,
        ):
            keep = column_mask(rows)
            packed = [dpk_ref[part] for part in range(3)]
            upstream = jnp.concatenate(qkv_back(packed, wq_a, wq_b), axis=1)
            units, inv_std = norm_stats(s_in[...])
            sums_ref[0:1, :] = jnp.sum(upstream * units, axis=0, keepdims=True)
            sums_ref[1:2, :] = jnp.sum(upstream, axis=0, keepdims=True)
            grad = jnp.where(where_ref[1] == 1, g_in[...], 0.0)
            grad = grad + norm_back(upstream, units, inv_std, gain_row((small_a, small_b), 0))
            conv_back_into(
                scratch, sums_ref, 2, grad, x_ref[...].astype(F32), (small_a, small_b), 0, keep
            )
            ship(scratch[...], kept, sent)

        token_kept, token_sent, sums0 = call(
            first_back_body, "back_0",
            [where, g0, dpk0, s1, x0, *small, *wq[0]],
            shipped + [sds((11, width))],
            scratch=[pltpu.VMEM((rows, width), F32)],
            flops=attn_flops * 3 // 4,
            hold=[n0_own, n0_oth, mixed0, g0_own, g0_oth, *late],
        )
        kept_a, sent_a = attn_weights(
            dpk0, n0_own, n0_oth, g0_own, g0_oth, mixed0, "wgrad_a", late
        )
        got_a = send(sent_a, 1, 0)
        token_stay, token_go = call(
            fold, "fold_tokens", [where, token_kept, over_wa(token_sent)], shipped, hold=late
        )
        token_got = over_ha(token_go)
        out_kept, out_sent = call(
            out_body, "out_d", [where, s5, hid3, *wd[1]], shipped, flops=mlp_flops // 2
        )
        out_stay, out_go = call(fold, "fold_out", [where, out_kept, over_wa(out_sent)], shipped)
        out_got = over_ha(out_go)

        sums = jnp.concatenate([sums0, 0.5 * sums1, 0.5 * sums2, 0.5 * sums3], axis=0)
        total = sums[:, :half] + over_wa(sums[:, half:])
        total = total + over_ha(total)

        kept_c, sent_c = halve(kept_c, got_c, "halve_c1")
        got_c = send(sent_c, 1, 1)
        kept_d, sent_d = halve(kept_d, got_d, "halve_d1")
        got_d = send(sent_d, 0, 1)
        owned = [sds((rows_in, half))]
        grad_tokens = call(join, "join_tokens", [token_stay, token_got], owned)[0]
        output = call(join, "join_out", [out_stay, out_got], owned)[0]
        kept_c, sent_c = halve(kept_c, got_c, "halve_c2")
        got_c = send(sent_c, 1, 2)
        kept_d, sent_d = halve(kept_d, got_d, "halve_d2")
        got_d = send(sent_d, 0, 2)
        kept_a, sent_a = halve(kept_a, got_a, "halve_a1")
        got_a = send(sent_a, 1, 1)
        kept_b, sent_b = halve(kept_b, got_b, "halve_b1")
        got_b = send(sent_b, 0, 1)
        kept_a, sent_a = halve(kept_a, got_a, "halve_a2")
        got_a = send(sent_a, 1, 2)
        kept_b, sent_b = halve(kept_b, got_b, "halve_b2")
        got_b = send(sent_b, 0, 2)
        for step in range(3, bits):
            kept_c, sent_c = halve(kept_c, got_c, f"halve_c{step}")
            got_c = send(sent_c, 1, step)
            kept_d, sent_d = halve(kept_d, got_d, f"halve_d{step}")
            got_d = send(sent_d, 0, step)
            kept_a, sent_a = halve(kept_a, got_a, f"halve_a{step}")
            got_a = send(sent_a, 1, step)
            kept_b, sent_b = halve(kept_b, got_b, f"halve_b{step}")
            got_b = send(sent_b, 0, step)
        sum_c = halve(kept_c, got_c, "halve_c")
        sum_d = halve(kept_d, got_d, "halve_d")
        sum_a = halve(kept_a, got_a, "halve_a")
        sum_b = halve(kept_b, got_b, "halve_b")

        for bit in range(bits):
            total = total + over_dev(total, bit)
        gain_at, shift_at = (0, 11, 13, 24), (1, 12, 14, 25)
        grad_gain = jnp.stack([total[at] for at in gain_at])
        grad_shift = jnp.stack([total[at] for at in shift_at])
        grad_taps = jnp.stack([total[2:11], total[15:24]])

        def down_of(total):
            down = total[up_rows:].reshape(folds, down_rows, half)
            return jnp.transpose(down, (1, 0, 2)).reshape(down_rows, hidden)

        def qkv_of(total):
            return total[: 3 * qkv_rows].reshape(3, qkv_rows, half)

        grad_qkv = jnp.transpose(jnp.stack([qkv_of(sum_a), qkv_of(sum_c)]), (0, 3, 1, 2))
        grad_proj = jnp.transpose(
            jnp.stack([sum_a[3 * qkv_rows :], sum_c[3 * qkv_rows :]]), (0, 2, 1)
        )
        grad_up = jnp.transpose(jnp.stack([sum_b[:up_rows], sum_d[:up_rows]]), (0, 2, 1))
        grad_down = jnp.transpose(jnp.stack([down_of(sum_b), down_of(sum_d)]), (0, 2, 1))
        return (
            output,
            grad_tokens,
            grad_taps,
            grad_gain,
            grad_shift,
            grad_qkv,
            grad_proj,
            grad_up,
            grad_down,
        )

    placed = (
        P(("dev", "ha"), "wa"),
        P(("dev", "ha"), "wa"),
        P(None, None, "wa"),
        P(None, "wa"),
        P(None, "wa"),
        P(None, "wa", None, "ha"),
        P(None, "ha", "wa"),
        P(None, "wa", "ha"),
        P(None, "ha", "wa"),
        P("dev", None),
    )
    return jax.shard_map(
        on_device,
        mesh=mesh,
        in_specs=placed,
        out_specs=(
            P(("dev", "ha"), "wa"),
            P(("dev", "ha"), "wa"),
            P(None, None, "wa"),
            P(None, "wa"),
            P(None, "wa"),
            P(None, "wa", None, ("ha", "dev")),
            P(None, "ha", ("wa", "dev")),
            P(None, "wa", ("ha", "dev")),
            P(None, "ha", ("wa", "dev")),
        ),
        check_vma=False,
    )
```

```python
from functools import partial

import jax
import jax.numpy as jnp
import numpy as np
from jax import lax
from jax.experimental import pallas as pl
from jax.experimental.pallas import tpu as pltpu
from jax.sharding import PartitionSpec as P

WIN = 7
GRID_COLS = 8
PATCHES = 49
PADDED = WIN * GRID_COLS
HEAD_DIM = 32
LANES = 128
HEADS_TILE = LANES // HEAD_DIM
EPS = 1e-05
NEG = -1e30
SPLIT_D, SPLIT_C, SPLIT_B, SPLIT_A = 0, 2, 1, 3
BF16 = jnp.bfloat16
F32 = jnp.float32
VMEM_LIMIT = 16 * 2**20


def mm(left, right, left_dim, right_dim):
    return lax.dot_general(
        left, right, (((left_dim,), (right_dim,)), ((), ())), preferred_element_type=F32
    )


class Order:
    def __init__(self):
        self.last = None


def kernel_call(body, name, ins, outs, order, scratch=(), flops=0, hold=(), far=0):
    arrays = list(ins) + list(hold) + ([] if order.last is None else [order.last])
    specs = [
        pl.BlockSpec(
            memory_space=pltpu.SMEM if a.dtype == jnp.int32 and a.ndim == 1 else pltpu.VMEM
        )
        for a in arrays
    ]
    for at in range(len(ins) - far, len(ins)):
        specs[at] = pl.BlockSpec(memory_space=pltpu.HBM)
    outs = list(outs) + [sds((8, LANES))]

    def wrapped(*refs):
        given = refs[: len(ins)] + refs[len(arrays) : len(arrays) + len(outs) - 1]
        body(*given, *refs[len(arrays) + len(outs) :])
        mark = refs[len(arrays) + len(outs) - 1]
        mark[...] = jnp.zeros_like(mark)

    moved = sum(int(np.prod(o.shape)) * o.dtype.itemsize for o in outs) + sum(
        int(np.prod(a.shape)) * a.dtype.itemsize for a in ins
    )
    *results, order.last = pl.pallas_call(
        wrapped,
        in_specs=specs,
        out_specs=[pl.BlockSpec(memory_space=pltpu.VMEM)] * len(outs),
        out_shape=outs,
        scratch_shapes=list(scratch),
        compiler_params=pltpu.CompilerParams(vmem_limit_bytes=VMEM_LIMIT),
        cost_estimate=pl.CostEstimate(flops=0, bytes_accessed=0, transcendentals=0),
        name=name,
    )(*arrays)
    return results


def sds(shape, dtype=F32):
    return jax.ShapeDtypeStruct(shape, dtype)


def column_mask(rows):
    return (lax.broadcasted_iota(jnp.int32, (rows, 1), 0) % GRID_COLS) < WIN


def placement(images, transposed):
    padded, plain = images * PADDED, images * PATCHES
    shape = (plain, padded) if transposed else (padded, plain)
    at = lax.broadcasted_iota(jnp.int32, shape, 1 if transposed else 0)
    image = sum((at >= i * PADDED).astype(jnp.int32) for i in range(1, images))
    inside = at - image * PADDED
    source = image * PATCHES + (inside >> 3) * WIN + (inside & 7)
    other = lax.broadcasted_iota(jnp.int32, shape, 0 if transposed else 1)
    return (((inside & 7) < WIN) & (source == other)).astype(F32).astype(BF16)


def side_shifts(values):
    rows = values.shape[0]
    return (pltpu.roll(values, 1, 0), values, pltpu.roll(values, rows - 1, 0))


def as_grid(values):
    return values.reshape(-1, WIN, GRID_COLS, values.shape[-1])


def move_rows(values, step):
    grid = as_grid(values)
    zeros = jnp.zeros_like(grid[:, :1])
    if step > 0:
        moved = jnp.concatenate([zeros, grid[:, :-1]], axis=1)
    else:
        moved = jnp.concatenate([grid[:, 1:], zeros], axis=1)
    return moved.reshape(values.shape)


def conv_cols(values, taps, keep):
    shifted = side_shifts(values)
    line = [
        sum(shifted[col] * taps[3 * row + col] for col in range(3)) for row in range(3)
    ]
    total = values + line[1] + move_rows(line[0], 1) + move_rows(line[2], -1)
    return jnp.where(keep, total, 0.0)


def tap_sums(grads, values):
    shifted = side_shifts(values)
    grad_grid = as_grid(grads)
    sums = []
    for row in range(3):
        for col in range(3):
            moved = as_grid(shifted[col])
            if row == 0:
                prod = grad_grid[:, 1:] * moved[:, :-1]
            elif row == 1:
                prod = grad_grid * moved
            else:
                prod = grad_grid[:, :-1] * moved[:, 1:]
            flat = prod.reshape(-1, GRID_COLS, prod.shape[-1])
            sums.append(jnp.sum(jnp.sum(flat, axis=0), axis=0, keepdims=True))
    return sums


def norm_stats(stream):
    width = stream.shape[1]
    center = jnp.sum(stream, axis=1, keepdims=True) * (1.0 / width)
    moved = stream - center
    inv_std = lax.rsqrt(jnp.sum(moved * moved, axis=1, keepdims=True) * (1.0 / width) + EPS)
    return moved * inv_std, inv_std


def norm_back(upstream, units, inv_std, gain):
    width = upstream.shape[1]
    scaled = upstream * gain
    first = jnp.sum(scaled, axis=1, keepdims=True) * (1.0 / width)
    second = jnp.sum(scaled * units, axis=1, keepdims=True) * (1.0 / width)
    return inv_std * (scaled - first - units * second)


def gelu_parts(values):
    z = jnp.abs(values) * (0.5**0.5)
    t = 1.0 / (1.0 + 0.3275911 * z)
    bell = jnp.exp(-z * z)
    poly = t * (
        0.254829592
        + t * (-0.284496736 + t * (1.421413741 + t * (-1.453152027 + t * 1.061405429)))
    )
    tail = 0.5 * poly * bell
    return jnp.where(values < 0, tail, 1.0 - tail), bell * float(1.0 / np.sqrt(2.0 * np.pi))


def head_mask(index):
    return (lax.broadcasted_iota(jnp.int32, (1, LANES), 1) // HEAD_DIM) == index


def spread_heads(tile):
    return jnp.concatenate(
        [jnp.where(head_mask(j), tile, 0.0) for j in range(HEADS_TILE)], axis=0
    ).astype(BF16)


def gather_heads(stacked):
    rows = stacked.shape[0] // HEADS_TILE
    total = jnp.where(head_mask(0), stacked[:rows], 0.0)
    for j in range(1, HEADS_TILE):
        total = jnp.where(head_mask(j), stacked[j * rows : (j + 1) * rows], total)
    return total


def softmax_rows(scores):
    top = jnp.max(scores, axis=0, keepdims=True)
    weights = jnp.exp(scores - top)
    return weights / jnp.sum(weights, axis=0, keepdims=True)


SCALE = HEAD_DIM**-0.5


def window_tile(q, k, v):
    keys_ok = column_mask(PADDED)
    scores = mm(k.astype(BF16), spread_heads(q), 1, 1) * SCALE
    probs = softmax_rows(jnp.where(keys_ok, scores, NEG))
    return probs, gather_heads(mm(probs.astype(BF16), v.astype(BF16), 0, 0))


def window_tile_back(q, k, v, probs, grad):
    low = probs.astype(BF16)
    q_big, g_big = spread_heads(q), spread_heads(grad)
    grad_probs = mm(v.astype(BF16), g_big, 1, 1)
    grad_v = mm(low, g_big, 1, 0)
    grad_scores = (
        probs * (grad_probs - jnp.sum(grad_probs * probs, axis=0, keepdims=True))
    ).astype(BF16)
    grad_k = mm(grad_scores, q_big, 1, 0) * SCALE
    grad_q = gather_heads(mm(grad_scores, k.astype(BF16), 0, 0)) * SCALE
    return grad_q, grad_k, grad_v


def same_head():
    first = lax.broadcasted_iota(jnp.int32, (LANES, LANES), 0) // HEAD_DIM
    second = lax.broadcasted_iota(jnp.int32, (LANES, LANES), 1) // HEAD_DIM
    return first == second


def channel_tile(q, k, v, mask):
    scores = mm(k.astype(BF16), (q * mask).astype(BF16), 0, 0) * SCALE
    probs = softmax_rows(jnp.where(same_head(), scores, NEG))
    return probs, mm(v.astype(BF16), probs.astype(BF16), 1, 0)


def channel_tile_back(q, k, v, probs, grad, mask):
    low = probs.astype(BF16)
    grad_low = grad.astype(BF16)
    grad_probs = mm(v.astype(BF16), grad_low, 0, 0)
    grad_v = mm(grad_low, low, 1, 1)
    grad_scores = (
        probs * (grad_probs - jnp.sum(grad_probs * probs, axis=0, keepdims=True))
    ).astype(BF16)
    grad_q = mm(k.astype(BF16), grad_scores, 1, 0) * SCALE * mask
    grad_k = mm((q * mask).astype(BF16), grad_scores, 1, 1) * SCALE
    return grad_q, grad_k, grad_v


def solution(mesh):
    n_dev = mesh.shape["dev"]
    bits = n_dev.bit_length() - 1
    assert n_dev == 1 << bits and mesh.shape["ha"] == 2 and mesh.shape["wa"] == 2

    swap = [(0, 1), (1, 0)]

    def over_ha(values):
        return lax.ppermute(values, "ha", swap)

    def over_wa(values):
        return lax.ppermute(values, "wa", swap)

    def over_dev(values, bit):
        return lax.ppermute(values, "dev", [(i, i ^ (1 << bit)) for i in range(n_dev)])

    def on_device(
        tokens, cotangent, conv_taps, norm_gain, norm_shift, w_qkv, w_proj, w_up, w_down, valid
    ):
        rows_in, half = tokens.shape
        images = rows_in // PATCHES
        rows = images * PADDED
        width = 2 * half
        heads_width = w_qkv.shape[3]
        hidden = w_up.shape[2]
        tiles = heads_width // LANES
        assert heads_width == half
        orders = [list(range(bits)), [1, 0, *range(2, bits)]]

        def here(name):
            return lax.axis_index(name)

        def chunk_at(place, which):
            found = 0
            for step, bit in enumerate(orders[which]):
                found |= ((place >> (bits - 1 - step)) & 1) << bit
            return found ^ here("dev")

        order = Order()
        call = partial(kernel_call, order=order)

        def later(values, event):
            return lax.optimization_barrier((values, event))[0]

        def pack_small(taps_ref, gain_ref, shift_ref, out_ref):
            for section in range(2):
                for t in range(9):
                    at = 9 * section + t
                    out_ref[at : at + 1, :] = taps_ref[t, section : section + 1, :]
            out_ref[18:22, :] = gain_ref[...]
            out_ref[22:26, :] = shift_ref[...]

        def choose(mine, received, own, other):
            same = here("ha") == here("wa")
            own[...] = jnp.where(same, mine[...], received[...])
            other[...] = jnp.where(same, received[...], mine[...])

        wq_own = jnp.transpose(w_qkv, (0, 2, 1, 3))
        wq, wp = (wq_own, over_wa(wq_own)), (w_proj, over_wa(w_proj))
        tokens_in = over_ha(tokens)
        small_own = call(
            pack_small, "pack_small",
            [jnp.transpose(conv_taps, (1, 0, 2)), norm_gain, norm_shift], [sds((26, half))],
            hold=[wq_own, w_proj, tokens],
        )[0]
        small = (small_own, over_wa(small_own))
        chosen = [sds((rows_in, half), BF16)] * 2
        tokens_own, tokens_oth = call(
            choose, "choose_tokens", [tokens, tokens_in], chosen, hold=[*wq, *wp, small_own]
        )
        token_parts = (tokens_own, over_wa(tokens_oth))
        arrived = (token_parts[1], small[1])
        wu, wd = ((values, over_wa(later(values, arrived))) for values in (w_up, w_down))

        def unpack(own, oth):
            values = jnp.concatenate([own[...], oth[...]], axis=1)
            return mm(placement(images, False), values, 1, 0)

        def gain_row(refs, branch):
            return jnp.concatenate([ref[18 + branch : 19 + branch, :] for ref in refs], axis=1)

        def shift_row(refs, branch):
            return jnp.concatenate([ref[22 + branch : 23 + branch, :] for ref in refs], axis=1)

        def tap_rows(small_refs, section, col, flipped):
            ref = small_refs[col // half]
            at = col % half
            found = [
                ref[9 * section + t : 9 * section + t + 1, at : at + LANES] for t in range(9)
            ]
            return found[::-1] if flipped else found

        def project_in(normed, first, second):
            return mm(normed[:, :half], first, 1, 0) + mm(normed[:, half:], second, 1, 0)

        def project_back(values, first, second):
            return mm(values[:, :half], first, 1, 1) + mm(values[:, half:], second, 1, 1)

        def to_normed(stream, small_refs, branch):
            units, _ = norm_stats(stream)
            return (units * gain_row(small_refs, branch) + shift_row(small_refs, branch)).astype(
                BF16
            )

        def put_both(own_ref, oth_ref, values):
            own_ref[...] = values[:, :half]
            oth_ref[...] = values[:, half:]

        def add_parts(stream, part_a, part_b):
            return stream[...] + part_a[...].astype(F32) + part_b[...].astype(F32)

        def attention_part(window, section, normed, valid_rows, wq_a, wq_b, qkv_ref, probs_ref):
            packed = [
                project_in(normed, wq_a[section, part], wq_b[section, part]).astype(BF16)
                for part in range(3)
            ]
            for part in range(3):
                qkv_ref[part] = packed[part]
            wide = [part.astype(F32) for part in packed]
            mixed = []
            for image in range(images):
                line = []
                rows_at = slice(image * PADDED, (image + 1) * PADDED)
                for tile in range(tiles):
                    lanes_at = slice(tile * LANES, (tile + 1) * LANES)
                    q, k, v = (part[rows_at, lanes_at] for part in wide)
                    if window:
                        probs, out = window_tile(q, k, v)
                    else:
                        probs, out = channel_tile(q, k, v, valid_rows[image])
                    probs_ref[image * tiles + tile] = probs
                    line.append(out)
                mixed.append(jnp.concatenate(line, axis=1))
            return jnp.concatenate(mixed, axis=0).astype(BF16)

        def attention_part_back(window, grad_mixed, mask_ref, qkv_ref, probs_ref, dpk_ref):
            wide = [qkv_ref[part].astype(F32) for part in range(3)]
            grad = grad_mixed.astype(F32)
            found = [[], [], []]
            for image in range(images):
                lines = [[], [], []]
                for tile in range(tiles):
                    rows_at = slice(image * PADDED, (image + 1) * PADDED)
                    lanes_at = slice(tile * LANES, (tile + 1) * LANES)
                    q, k, v = (part[rows_at, lanes_at] for part in wide)
                    probs = probs_ref[image * tiles + tile]
                    if window:
                        parts = window_tile_back(q, k, v, probs, grad[rows_at, lanes_at])
                    else:
                        parts = channel_tile_back(
                            q, k, v, probs, grad[rows_at, lanes_at], mask_ref[rows_at, :]
                        )
                    for line, part in zip(lines, parts):
                        line.append(part)
                for part in range(3):
                    found[part].append(jnp.concatenate(lines[part], axis=1))
            packed = [jnp.concatenate(part, axis=0).astype(BF16) for part in found]
            for part in range(3):
                dpk_ref[part] = packed[part]
            return packed

        def mul_out(left, section, own_ref, oth_ref, out_ref):
            out_ref[:, :half] = mm(left, own_ref[section], 1, 0).astype(BF16)
            out_ref[:, half:] = mm(left, oth_ref[section], 1, 0).astype(BF16)

        def conv_into(out_ref, values, small_refs, section, keep):
            for col in range(0, width, LANES):
                taps = tap_rows(small_refs, section, col, False)
                out_ref[:, col : col + LANES] = conv_cols(values[:, col : col + LANES], taps, keep)

        def conv_back_into(out_ref, sums_ref, sums_at, grads, values, small_refs, section, keep):
            for col in range(0, width, LANES):
                lanes_at = slice(col, col + LANES)
                taps = tap_rows(small_refs, section, col, True)
                for t, total in enumerate(tap_sums(grads[:, lanes_at], values[:, lanes_at])):
                    sums_ref[sums_at + t : sums_at + t + 1, lanes_at] = total
                out_ref[:, lanes_at] = conv_cols(grads[:, lanes_at], taps, keep)

        window_probs = sds((images * tiles, PADDED, HEADS_TILE * PADDED))
        channel_probs = sds((images * tiles, LANES, LANES))
        full, full_low = sds((rows, width)), sds((rows, width), BF16)
        half_low = sds((rows, half), BF16)
        hid_low = sds((rows, hidden), BF16)
        qkv_low = sds((3, rows, heads_width), BF16)
        attn_flops = 2 * rows * (4 * width * heads_width)
        mlp_flops = 2 * rows * (2 * width * hidden)

        def first_body(
            tokens_a, tokens_b, small_a, small_b, wq_a, wq_b, wp_a, wp_b,
            x_ref, s_ref, n_own, n_oth, qkv_ref, probs_ref, mixed_ref, part_ref, keep_a, keep_b,
        ):
            keep_a[...], keep_b[...] = small_a[...], small_b[...]
            keep = column_mask(rows)
            stream = unpack(tokens_a, tokens_b)
            x_ref[...] = stream.astype(BF16)
            conv_into(s_ref, stream, (small_a, small_b), 0, keep)
            normed = to_normed(s_ref[...], (small_a, small_b), 0)
            put_both(n_own, n_oth, normed)
            mixed = attention_part(True, 0, normed, None, wq_a, wq_b, qkv_ref, probs_ref)
            mixed_ref[...] = mixed
            mul_out(mixed, 0, wp_a, wp_b, part_ref)

        (x0, s1, n0_own, n0_oth, qkv0, probs0, mixed0, part0, *small) = call(
            first_body, "attn_a",
            [*token_parts, *small, *wq, *wp],
            [full_low, full, half_low, half_low, qkv_low, window_probs, half_low, full_low]
            + [sds((26, half))] * 2,
            flops=attn_flops,
        )
        far0 = over_ha(part0)
        keep_a = [x0, n0_own, n0_oth, qkv0, probs0, mixed0, s1]

        def mlp_body(
            s_in, part_a, part_b, small_a, small_b, wu_a, wu_b, wd_a, wd_b,
            s_ref, n_own, n_oth, hid_ref, slope_ref, part_ref,
        ):
            s_ref[...] = add_parts(s_in, part_a, part_b)
            normed = to_normed(s_ref[...], (small_a, small_b), 1)
            put_both(n_own, n_oth, normed)
            pre = project_in(normed, wu_a[0], wu_b[0])
            below, bell = gelu_parts(pre)
            hid = (pre * below).astype(BF16)
            hid_ref[...] = hid
            slope_ref[...] = below + pre * bell
            mul_out(hid, 0, wd_a, wd_b, part_ref)

        (s2, n1_own, n1_oth, hid1, slope1, part1) = call(
            mlp_body, "mlp_b",
            [s1, part0, far0, *small, *wu, *wd],
            [full, half_low, half_low, hid_low, sds((rows, hidden)), full_low],
            flops=mlp_flops, hold=[*keep_a, *wq, *wp],
        )
        far1 = over_ha(part1)
        keep_b = [s2, n1_own, n1_oth, hid1, slope1]
        weights = [*wq, *wp, *wu, *wd]


        cot_in = over_ha(later(cotangent, part1))

        def channel_body(
            s_in, part_a, part_b, valid_ref, small_a, small_b,
            wq_a, wq_b, wp_a, wp_b,
            s_before, s_ref, n_own, n_oth, qkv_ref, probs_ref, mixed_ref, part_ref, mask_ref,
        ):
            keep = column_mask(rows)
            s_before[...] = jnp.where(keep, add_parts(s_in, part_a, part_b), 0.0)
            conv_into(s_ref, s_before, (small_a, small_b), 1, keep)
            normed = to_normed(s_ref[...], (small_a, small_b), 2)
            put_both(n_own, n_oth, normed)
            one_image = placement(1, False).astype(F32)
            valid_rows = []
            for image in range(images):
                line = jnp.where(
                    here("wa") == 0,
                    valid_ref[image : image + 1, :],
                    valid_ref[images + image : images + image + 1, :],
                ).astype(F32)
                valid_rows.append(jnp.sum(one_image * line, axis=1, keepdims=True))
                mask_ref[image * PADDED : (image + 1) * PADDED, :] = valid_rows[image]
            mixed = attention_part(False, 1, normed, valid_rows, wq_a, wq_b, qkv_ref, probs_ref)
            mixed_ref[...] = mixed
            mul_out(mixed, 1, wp_a, wp_b, part_ref)

        (s3, s4, n2_own, n2_oth, qkv2, probs2, mixed2, part2, mask) = call(
            channel_body, "attn_c",
            [s2, part1, far1, valid, *small, *wq, *wp],
            [full, full, half_low, half_low, qkv_low, channel_probs, half_low, full_low,
             sds((rows, 1))],
            flops=attn_flops,
            hold=[*keep_a, *keep_b, *wu, *wd, cot_in],
        )
        far2 = over_ha(part2)
        keep_c = [s3, s4, n2_own, n2_oth, qkv2, probs2, mixed2, mask]

        cot_own, cot_oth = call(
            choose, "choose_cot", [cotangent, cot_in], chosen,
            hold=[*keep_a, *keep_b, *keep_c, *small, *wq, *wp, *wu, *wd],
        )
        cot_parts = (cot_own, over_wa(cot_oth))

        def cot_body(cot_a, cot_b, wd_a, wd_b, g_own, g_oth, dhid_ref):
            grad = unpack(cot_a, cot_b).astype(BF16)
            put_both(g_own, g_oth, grad)
            dhid_ref[...] = project_back(grad, wd_a[1], wd_b[1]).astype(BF16)

        g3_own, g3_oth, dhid3 = call(
            cot_body, "cot_d",
            [*cot_parts, *wd],
            [half_low, half_low, hid_low],
            flops=mlp_flops // 2, hold=[*keep_a, *keep_b, *keep_c, *small, *wq, *wp, *wu],
        )

        def last_body(
            s_in, part_a, part_b, small_a, small_b, dhid_ref, wu_a, wu_b,
            s_ref, n_own, n_oth, hid_ref, dpre_ref, part_ref,
        ):
            s_ref[...] = add_parts(s_in, part_a, part_b)
            normed = to_normed(s_ref[...], (small_a, small_b), 3)
            put_both(n_own, n_oth, normed)
            pre = project_in(normed, wu_a[1], wu_b[1])
            below, bell = gelu_parts(pre)
            hid_ref[...] = (pre * below).astype(BF16)
            dpre = (dhid_ref[...].astype(F32) * (below + pre * bell)).astype(BF16)
            dpre_ref[...] = dpre
            part_ref[:, :half] = mm(dpre, wu_a[1], 1, 1).astype(BF16)
            part_ref[:, half:] = mm(dpre, wu_b[1], 1, 1).astype(BF16)

        (s5, n3_own, n3_oth, hid3, dpre3, back3) = call(
            last_body, "mlp_d",
            [s4, part2, far2, *small, dhid3, *wu],
            [full, half_low, half_low, hid_low, hid_low, full_low],
            flops=mlp_flops,
            hold=[*keep_a, *keep_b, *keep_c, g3_own, g3_oth, *wq, *wp, *wd],
        )
        far_back3 = over_ha(back3)

        up_rows, down_rows = hidden // n_dev, half // n_dev
        qkv_rows, proj_rows = heads_width // n_dev, half // n_dev
        folds = hidden // half
        cut = n_dev // 2
        sum_rows = 32

        class Stream:
            def __init__(self, which, pieces):
                self.bits, self.which, self.pieces = orders[which], which, pieces
                self.chunk_rows = sum(piece_rows(piece) for piece in pieces)
                self.step, self.kept, self.got, self.at, self.final = 0, None, None, 0, None

        def piece_rows(piece):
            return {"up": up_rows, "q": qkv_rows, "k": qkv_rows, "v": qkv_rows}.get(
                piece, down_rows
            )

        downs = [("down", fold) for fold in range(folds)]

        def mlp_streams(first):
            return [Stream(0, ["up", *downs[:first]]), Stream(1, downs[first:])]

        def attn_streams(first):
            parts = ["q", "k", "v", "proj"]
            return [Stream(0, parts[:first]), Stream(1, parts[first:])]

        def write_pieces(values, streams, scratches):
            for stream, scratch in zip(streams, scratches):
                at = 0
                for piece in stream.pieces:
                    size = piece_rows(piece)
                    for chunk in range(n_dev):
                        rows_at = slice(chunk * size, (chunk + 1) * size)
                        if isinstance(piece, tuple):
                            columns = slice(piece[1] * half, (piece[1] + 1) * half)
                            part = values["down"][rows_at, columns]
                        else:
                            part = values[piece][rows_at]
                        scratch[chunk, at : at + size, :] = part
                    at += size

        def write_mlp(refs, streams, scratches):
            dpre_a, dpre_b, n_a, n_b, g_a, g_b, hid_a, hid_b = refs
            up = mm(dpre_a[...], n_a[...], 0, 0) + mm(dpre_b[...], n_b[...], 0, 0)
            down = mm(g_a[...], hid_a[...], 0, 0) + mm(g_b[...], hid_b[...], 0, 0)
            write_pieces({"up": up, "down": down}, streams, scratches)

        def write_attn(refs, streams, scratches):
            dpk_a, dpk_b, n_a, n_b, g_a, g_b, mix_a, mix_b = refs
            values = {
                name: mm(dpk_a[part], n_a[...], 0, 0) + mm(dpk_b[part], n_b[...], 0, 0)
                for part, name in enumerate(("q", "k", "v"))
            }
            values["proj"] = mm(g_a[...], mix_a[...], 0, 0) + mm(g_b[...], mix_b[...], 0, 0)
            write_pieces(values, streams, scratches)

        def split_low(values):
            high = values.astype(BF16)
            return high, (values - high.astype(F32)).astype(BF16)

        def joined(ref, at):
            high = ref[at : at + sum_rows, :].astype(F32)
            return high + ref[at + sum_rows : at + 2 * sum_rows, :].astype(F32)

        def last_sum(stream, kept, got):
            return kept[...].astype(F32) + got[
                stream.at : stream.at + stream.chunk_rows, :
            ].astype(F32)

        def slot(
            name, write=None, fresh=(), sources=(), moving=(), ending=(), sums=None, hold=()
        ):
            ins, outs, sizes = list(sources), [], {}
            plan_fresh, plan_moving = [], []

            def room(bit, size):
                at = sizes.get(bit, 0)
                sizes[bit] = at + size
                return at

            for stream in fresh:
                size = cut * stream.chunk_rows
                plan_fresh.append((len(outs), stream.bits[0], room(stream.bits[0], size)))
                outs.append(sds((size, half), BF16))
            got_places = {}

            def place_of(array):
                for at, known in enumerate(ins):
                    if known is array:
                        return at
                ins.append(array)
                return len(ins) - 1

            for stream in moving:
                size = stream.kept.shape[0] // 2
                bit = stream.bits[stream.step]
                plan_moving.append(
                    (place_of(stream.kept), place_of(stream.got), stream.at, size,
                     len(outs), bit, room(bit, size))
                )
                outs.append(sds((size, half), BF16))
            plan_ending = []
            for stream in ending:
                plan_ending.append(
                    (stream, place_of(stream.kept), place_of(stream.got), len(outs))
                )
                outs.append(sds((stream.chunk_rows, half)))
            if sums is not None:
                total_at = place_of(sums[0])
                sums_got = None if sums[1] is None else place_of(sums[1])
                sums_room = room(sums[3], 2 * sum_rows)
                sums_out = len(outs)
                outs.append(sds((sum_rows, half)))
            bits_used = sorted(sizes)
            buffer_at = {bit: len(outs) + at for at, bit in enumerate(bits_used)}
            outs += [sds((sizes[bit], half), BF16) for bit in bits_used]
            scratch = [pltpu.VMEM((n_dev, stream.chunk_rows, half), F32) for stream in fresh]

            def body(*refs):
                in_refs, out_refs = refs[: len(ins)], refs[len(ins) : len(ins) + len(outs)]
                scratches = refs[len(ins) + len(outs) :]
                if fresh:
                    write(in_refs[: len(sources)], fresh, scratches)
                for stream, held, (kept_at, bit, at) in zip(fresh, scratches, plan_fresh):
                    size = stream.chunk_rows
                    for place in range(n_dev):
                        chunk = held[chunk_at(place, stream.which)].astype(BF16)
                        if place < cut:
                            out_refs[kept_at][place * size : (place + 1) * size, :] = chunk
                        else:
                            to = at + (place - cut) * size
                            out_refs[buffer_at[bit]][to : to + size, :] = chunk
                for kept_in, got_in, got_row, size, kept_at, bit, at in plan_moving:
                    kept, got = in_refs[kept_in], in_refs[got_in]
                    out_refs[kept_at][...] = (
                        kept[:size, :].astype(F32) + got[got_row : got_row + size, :].astype(F32)
                    ).astype(BF16)
                    out_refs[buffer_at[bit]][at : at + size, :] = (
                        kept[size:, :].astype(F32)
                        + got[got_row + size : got_row + 2 * size, :].astype(F32)
                    ).astype(BF16)
                for stream, kept_in, got_in, out_at in plan_ending:
                    out_refs[out_at][...] = last_sum(stream, in_refs[kept_in], in_refs[got_in])
                if sums is not None:
                    total = in_refs[total_at][...]
                    if sums_got is not None:
                        total = total + joined(in_refs[sums_got], sums[2])
                    high, low = split_low(total)
                    out_refs[sums_out][...] = high.astype(F32) + low.astype(F32)
                    buffer = out_refs[buffer_at[sums[3]]]
                    buffer[sums_room : sums_room + sum_rows, :] = high
                    buffer[sums_room + sum_rows : sums_room + 2 * sum_rows, :] = low

            results = call(body, name, ins, outs, scratch=scratch, hold=hold)
            received = {bit: over_dev(results[buffer_at[bit]], bit) for bit in bits_used}
            for stream, (kept_at, bit, at) in zip(fresh, plan_fresh):
                stream.kept, stream.got, stream.at = results[kept_at], received[bit], at
                stream.step = 1
            for stream, _, _, out_at in plan_ending:
                stream.final = results[out_at]
            for stream, (_, _, _, _, kept_at, bit, at) in zip(moving, plan_moving):
                stream.kept, stream.got, stream.at = results[kept_at], received[bit], at
                stream.step += 1
            if sums is not None:
                sums[:3] = results[sums_out], received[sums[3]], sums_room

        def gradient_sources(left, n_own, n_oth, g_own, g_oth, right):
            return [left, over_wa(left), n_own, over_wa(n_oth),
                    g_own, over_wa(g_oth), right, over_wa(right)]

        def ship(total, kept, sent):
            packed = mm(placement(images, True), total.astype(BF16), 1, 0).astype(BF16)
            kept[...] = packed[:, :half]
            sent[...] = packed[:, half:]

        shipped = [sds((rows_in, half), BF16)] * 2

        def fold(kept, received, stay, go):
            same = here("ha") == here("wa")
            stay[...] = jnp.where(same, kept[...], received[...])
            go[:rows_in, :] = jnp.where(same, received[...], kept[...])

        def join(stay, received, out_ref):
            out_ref[...] = stay[...].astype(F32) + received[:rows_in, :].astype(F32)

        def out_body(s_in, hid_ref, wd_a, wd_b, kept, sent):
            hid = hid_ref[...]
            base = jnp.where(here("ha") == 0, s_in[...], 0.0)
            branch = jnp.concatenate([mm(hid, wd_a[1], 1, 0), mm(hid, wd_b[1], 1, 0)], axis=1)
            ship(base + branch, kept, sent)

        streams_d = mlp_streams(SPLIT_D)
        slot(
            "wgrad_d", write_mlp, streams_d,
            gradient_sources(dpre3, n3_own, n3_oth, g3_own, g3_oth, hid3),
            hold=[*keep_a, *keep_b, *keep_c, *small, *weights, s5],
        )

        def add_norm_back(grad, part_a, part_b, stream, gain, sums_ref):
            upstream = part_a[...].astype(F32) + part_b[...].astype(F32)
            units, inv_std = norm_stats(stream)
            sums_ref[0:1, :] = jnp.sum(upstream * units, axis=0, keepdims=True)
            sums_ref[1:2, :] = jnp.sum(upstream, axis=0, keepdims=True)
            return grad + norm_back(upstream, units, inv_std, gain)

        def qkv_back(packed, section, wq_a, wq_b):
            return [
                sum(mm(packed[part], ref[section, part], 1, 1) for part in range(3))
                for ref in (wq_a, wq_b)
            ]

        def channel_back_body(
            g_in_own, g_in_oth, part_a, part_b, s_in, small_a, small_b, mask_ref, qkv_ref,
            probs_ref, wp_a, wp_b, wq_a, wq_b, g_ref, g_own, g_oth, dpk_ref, part_ref, sums_ref,
        ):
            grad = jnp.concatenate([g_in_own[...], g_in_oth[...]], axis=1).astype(F32)
            gain = gain_row((small_a, small_b), 3)
            grad = add_norm_back(grad, part_a, part_b, s_in[...], gain, sums_ref)
            g_ref[...] = grad
            low = grad.astype(BF16)
            put_both(g_own, g_oth, low)
            grad_mixed = project_back(low, wp_a[1], wp_b[1]).astype(BF16)
            packed = attention_part_back(False, grad_mixed, mask_ref, qkv_ref, probs_ref, dpk_ref)
            own, oth = qkv_back(packed, 1, wq_a, wq_b)
            part_ref[:, :half] = own.astype(BF16)
            part_ref[:, half:] = oth.astype(BF16)

        late = [hid3, *wd, s5]
        (g2, g2_own, g2_oth, dpk2, back2, sums3) = call(
            channel_back_body, "back_c",
            [g3_own, g3_oth, back3, far_back3, s5, *small, mask, qkv2, probs2, *wp, *wq],
            [full, half_low, half_low, qkv_low, full_low, sds((2, width))],
            flops=attn_flops,
            hold=[*keep_a, *keep_b, s3, s4, n2_own, n2_oth, mixed2, *wu, *wd, hid3],
        )
        far_back2 = over_ha(back2)
        streams_c = attn_streams(SPLIT_C)
        slot(
            "wgrad_c", write_attn, streams_c,
            gradient_sources(dpk2, n2_own, n2_oth, g2_own, g2_oth, mixed2),
            moving=streams_d,
            hold=[*keep_a, *keep_b, s3, s4, *small, *weights, g2, *late, sums3, back2, far_back2],
        )

        def mlp_back_body(
            g_in, part_a, part_b, s_in, s_before, small_a, small_b, slope_ref,
            wd_a, wd_b, wu_a, wu_b, g_ref, g_own, g_oth, dpre_ref, part_ref, sums_ref,
        ):
            keep = column_mask(rows)
            gain = gain_row((small_a, small_b), 2)
            grad = add_norm_back(g_in[...], part_a, part_b, s_in[...], gain, sums_ref)
            conv_back_into(g_ref, sums_ref, 2, grad, s_before[...], (small_a, small_b), 1, keep)
            low = g_ref[...].astype(BF16)
            put_both(g_own, g_oth, low)
            dhid = project_back(low, wd_a[0], wd_b[0]).astype(BF16).astype(F32)
            dpre = (dhid * slope_ref[...]).astype(BF16)
            dpre_ref[...] = dpre
            part_ref[:, :half] = mm(dpre, wu_a[0], 1, 1).astype(BF16)
            part_ref[:, half:] = mm(dpre, wu_b[0], 1, 1).astype(BF16)

        (g1, g1_own, g1_oth, dpre1, back1, sums2) = call(
            mlp_back_body, "back_b",
            [g2, back2, far_back2, s4, s3, *small, slope1, *wd, *wu],
            [full, half_low, half_low, hid_low, full_low, sds((11, width))],
            flops=mlp_flops, hold=[*keep_a, s2, n1_own, n1_oth, hid1, *wq, *wp, hid3, s5, sums3],
        )
        far_back1 = over_ha(back1)
        streams_b = mlp_streams(SPLIT_B)
        slot(
            "wgrad_b", write_mlp, streams_b,
            gradient_sources(dpre1, n1_own, n1_oth, g1_own, g1_oth, hid1),
            moving=[*streams_d, *streams_c],
            hold=[*keep_a, s2, *small, *wq, *wp, g1, *late, sums3, sums2, back1, far_back1],
        )

        def window_back_body(
            g_in, part_a, part_b, s_in, small_a, small_b, qkv_ref, probs_ref, wp_a, wp_b,
            g_ref, g_own, g_oth, dpk_ref, sums_ref,
        ):
            gain = gain_row((small_a, small_b), 1)
            grad = add_norm_back(g_in[...], part_a, part_b, s_in[...], gain, sums_ref)
            g_ref[...] = grad
            low = grad.astype(BF16)
            put_both(g_own, g_oth, low)
            grad_mixed = project_back(low, wp_a[0], wp_b[0]).astype(BF16)
            attention_part_back(True, grad_mixed, None, qkv_ref, probs_ref, dpk_ref)

        (g0, g0_own, g0_oth, dpk0, sums1) = call(
            window_back_body, "back_a",
            [g1, back1, far_back1, s2, *small, qkv0, probs0, *wp],
            [full, half_low, half_low, qkv_low, sds((2, width))],
            flops=attn_flops, hold=[x0, n0_own, n0_oth, mixed0, s1, *wq, *late, sums3, sums2],
        )

        def first_back_body(
            g_in, dpk_ref, s_in, x_ref, small_a, small_b, wq_a, wq_b,
            sums_one, sums_two, sums_three, kept, sent, sums_own, sums_oth, scratch, sums_ref,
        ):
            keep = column_mask(rows)
            packed = [dpk_ref[part] for part in range(3)]
            upstream = jnp.concatenate(qkv_back(packed, 0, wq_a, wq_b), axis=1)
            units, inv_std = norm_stats(s_in[...])
            sums_ref[0:1, :] = jnp.sum(upstream * units, axis=0, keepdims=True)
            sums_ref[1:2, :] = jnp.sum(upstream, axis=0, keepdims=True)
            grad = jnp.where(here("ha") == 0, g_in[...], 0.0)
            grad = grad + norm_back(upstream, units, inv_std, gain_row((small_a, small_b), 0))
            conv_back_into(
                scratch, sums_ref, 2, grad, x_ref[...].astype(F32), (small_a, small_b), 0, keep
            )
            ship(scratch[...], kept, sent)
            sums_ref[11:13, :] = 0.5 * sums_one[...]
            sums_ref[13:24, :] = 0.5 * sums_two[...]
            sums_ref[24:26, :] = 0.5 * sums_three[...]
            sums_ref[26:, :] = jnp.zeros((sum_rows - 26, width), F32)
            put_both(sums_own, sums_oth, sums_ref[...])

        sums_half = sds((sum_rows, half))
        token_kept, token_sent, sums_own, sums_oth = call(
            first_back_body, "back_0",
            [g0, dpk0, s1, x0, *small, *wq, sums1, sums2, sums3],
            shipped + [sums_half] * 2,
            scratch=[pltpu.VMEM((rows, width), F32), pltpu.VMEM((sum_rows, width), F32)],
            flops=attn_flops * 3 // 4,
            hold=[n0_own, n0_oth, mixed0, g0_own, g0_oth, *late],
        )
        keep_wgrad = [dpk0, n0_own, n0_oth, g0_own, g0_oth, mixed0]

        sums_at = -(-rows_in // 16) * 16

        def fold_tokens(kept, received, sums_a, sums_b, stay, go, sums_ref):
            fold(kept, received, stay, go)
            high, low = split_low(sums_a[...] + sums_b[...])
            sums_ref[...] = high.astype(F32) + low.astype(F32)
            go[sums_at : sums_at + sum_rows, :] = high
            go[sums_at + sum_rows :, :] = low

        token_stay, token_go, sums_chip = call(
            fold_tokens, "fold_tokens",
            [token_kept, over_wa(token_sent), sums_own, over_wa(sums_oth)],
            [shipped[0], sds((sums_at + 2 * sum_rows, half), BF16), sums_half],
            hold=[*late, *keep_wgrad],
        )
        token_got = over_ha(token_go)
        out_kept, out_sent = call(
            out_body, "out_d", [s5, hid3, *wd], shipped, flops=mlp_flops // 2,
            hold=[*keep_wgrad, token_stay, sums_chip],
        )
        out_stay, out_go = call(
            fold, "fold_out", [out_kept, over_wa(out_sent)], shipped,
            hold=[*keep_wgrad, token_stay, sums_chip],
        )
        out_got = over_ha(out_go)

        def join_tokens(stay, received, sums_chip, out_ref, sums_ref):
            join(stay, received, out_ref)
            sums_ref[...] = sums_chip[...] + joined(received, sums_at)

        earlier = [*streams_d, *streams_c, *streams_b]
        slot(
            "halve_bc", moving=[s for s in earlier if s.step < bits],
            ending=[s for s in earlier if s.step == bits],
            hold=[*keep_wgrad, token_stay, sums_chip, out_stay],
        )
        streams_a = attn_streams(SPLIT_A)
        slot(
            "wgrad_a", write_attn, streams_a,
            gradient_sources(dpk0, n0_own, n0_oth, g0_own, g0_oth, mixed0),
            hold=[token_stay, sums_chip, out_stay],
        )
        owned = sds((rows_in, half))
        grad_tokens, sums_ha = call(
            join_tokens, "join_tokens", [token_stay, token_got, sums_chip], [owned, sums_half],
            hold=[out_stay],
        )
        left_bits = list(range(bits))
        sums = [sums_ha, None, 0, left_bits.pop(0)]
        turn = 0
        while left_bits or any(stream.step < bits for stream in [*earlier, *streams_a]):
            turn += 1
            moving = [s for s in earlier if s.step < bits]
            arrived = [s for s in earlier if s.step == bits and s.final is None]
            if moving:
                slot(f"halve_{turn}", moving=moving, sums=sums if turn == 1 else None)
            if turn == 1:
                output = call(join, "join_out", [out_stay, out_got], [owned])[0]
            now = None
            if left_bits:
                sums[3] = left_bits.pop(0)
                now = sums
            slot(
                f"halve_a{turn}", moving=[s for s in streams_a if s.step < bits],
                ending=arrived, sums=now,
            )

        def finish_body(*refs):
            (up, down, qkv, proj, taps_ref, gain_ref, shift_ref) = refs[-7:]
            at = iter(refs)
            total = next(at)[...] + joined(next(at), sums[2])
            for branch, row in enumerate((0, 11, 13, 24)):
                gain_ref[branch : branch + 1, :] = total[row : row + 1]
                shift_ref[branch : branch + 1, :] = total[row + 1 : row + 2]
            for section, row in enumerate((2, 15)):
                for t in range(9):
                    taps_ref[t, section : section + 1, :] = total[row + t : row + t + 1]

            def finished(stream):
                if stream.final is not None:
                    return next(at)[...]
                return last_sum(stream, next(at), next(at))

            for section, streams in enumerate(
                ((*streams_a, *streams_b), (*streams_c, *streams_d))
            ):
                for stream in streams:
                    values, row = finished(stream), 0
                    for piece in stream.pieces:
                        part = values[row : row + piece_rows(piece)]
                        row += piece_rows(piece)
                        if piece == "up":
                            up[section] = part
                        elif piece == "proj":
                            proj[section] = part
                        elif isinstance(piece, tuple):
                            down[section, :, piece[1] * half : (piece[1] + 1) * half] = part
                        else:
                            qkv[section, ("q", "k", "v").index(piece)] = part

        ends = []
        for stream in (*streams_a, *streams_b, *streams_c, *streams_d):
            ends += [stream.kept, stream.got] if stream.final is None else [stream.final]
        up, down, qkv, proj, grad_taps, grad_gain, grad_shift = call(
            finish_body, "finish", [*sums[:2], *ends],
            [sds((2, up_rows, half)), sds((2, down_rows, hidden)), sds((2, 3, qkv_rows, half)),
             sds((2, proj_rows, half)), sds((9, 2, half)), sds((4, half)), sds((4, half))],
        )
        grad_taps = jnp.transpose(grad_taps, (1, 0, 2))
        grad_qkv = jnp.transpose(qkv, (0, 3, 1, 2))
        grad_proj, grad_up, grad_down = (
            jnp.transpose(values, (0, 2, 1)) for values in (proj, up, down)
        )
        return (
            output,
            grad_tokens,
            grad_taps,
            grad_gain,
            grad_shift,
            grad_qkv,
            grad_proj,
            grad_up,
            grad_down,
        )

    placed = (
        P(("dev", "ha"), "wa"),
        P(("dev", "ha"), "wa"),
        P(None, None, "wa"),
        P(None, "wa"),
        P(None, "wa"),
        P(None, "wa", None, "ha"),
        P(None, "ha", "wa"),
        P(None, "wa", "ha"),
        P(None, "ha", "wa"),
        P("dev", None),
    )
    return jax.shard_map(
        on_device,
        mesh=mesh,
        in_specs=placed,
        out_specs=(
            P(("dev", "ha"), "wa"),
            P(("dev", "ha"), "wa"),
            P(None, None, "wa"),
            P(None, "wa"),
            P(None, "wa"),
            P(None, "wa", None, ("ha", "dev")),
            P(None, "ha", ("wa", "dev")),
            P(None, "wa", ("ha", "dev")),
            P(None, "ha", ("wa", "dev")),
        ),
        check_vma=False,
    )
```

```python
from functools import partial

import jax
import jax.numpy as jnp
import numpy as np
from jax import lax
from jax.experimental import pallas as pl
from jax.experimental.pallas import tpu as pltpu
from jax.sharding import PartitionSpec as P

WIN = 7
GRID_COLS = 8
PATCHES = 49
PADDED = WIN * GRID_COLS
HEAD_DIM = 32
LANES = 128
HEADS_TILE = LANES // HEAD_DIM
EPS = 1e-05
NEG = -1e30
SPLIT_D, SPLIT_C, SPLIT_B, SPLIT_A = 0, 2, 0, 4
BF16 = jnp.bfloat16
F32 = jnp.float32
VMEM_LIMIT = 16 * 2**20
TIMES = {"pack_small": 5.0, "choose": 5.0}


def mm(left, right, left_dim, right_dim):
    return lax.dot_general(
        left, right, (((left_dim,), (right_dim,)), ((), ())), preferred_element_type=F32
    )


class Order:
    def __init__(self):
        self.last = None


def kernel_call(body, name, ins, outs, order, scratch=(), flops=0, hold=(), far=0):
    arrays = list(ins) + list(hold) + ([] if order.last is None else [order.last])
    specs = [
        pl.BlockSpec(
            memory_space=pltpu.SMEM if a.dtype == jnp.int32 and a.ndim == 1 else pltpu.VMEM
        )
        for a in arrays
    ]
    for at in range(len(ins) - far, len(ins)):
        specs[at] = pl.BlockSpec(memory_space=pltpu.HBM)
    outs = list(outs) + [sds((8, LANES))]

    def wrapped(*refs):
        given = refs[: len(ins)] + refs[len(arrays) : len(arrays) + len(outs) - 1]
        body(*given, *refs[len(arrays) + len(outs) :])
        mark = refs[len(arrays) + len(outs) - 1]
        mark[...] = jnp.zeros_like(mark)

    moved = sum(int(np.prod(o.shape)) * o.dtype.itemsize for o in outs) + sum(
        int(np.prod(a.shape)) * a.dtype.itemsize for a in ins
    )
    *results, order.last = pl.pallas_call(
        wrapped,
        in_specs=specs,
        out_specs=[pl.BlockSpec(memory_space=pltpu.VMEM)] * len(outs),
        out_shape=outs,
        scratch_shapes=list(scratch),
        compiler_params=pltpu.CompilerParams(vmem_limit_bytes=VMEM_LIMIT),
        cost_estimate=pl.CostEstimate(
            flops=int(TIMES.get(name, 0) * 1.15e9), bytes_accessed=0, transcendentals=0
        ),
        name=name,
    )(*arrays)
    return results


def sds(shape, dtype=F32):
    return jax.ShapeDtypeStruct(shape, dtype)


def column_mask(rows):
    return (lax.broadcasted_iota(jnp.int32, (rows, 1), 0) % GRID_COLS) < WIN


def placement(images, transposed):
    padded, plain = images * PADDED, images * PATCHES
    shape = (plain, padded) if transposed else (padded, plain)
    at = lax.broadcasted_iota(jnp.int32, shape, 1 if transposed else 0)
    image = sum((at >= i * PADDED).astype(jnp.int32) for i in range(1, images))
    inside = at - image * PADDED
    source = image * PATCHES + (inside >> 3) * WIN + (inside & 7)
    other = lax.broadcasted_iota(jnp.int32, shape, 0 if transposed else 1)
    return (((inside & 7) < WIN) & (source == other)).astype(F32).astype(BF16)


def side_shifts(values):
    rows = values.shape[0]
    return (pltpu.roll(values, 1, 0), values, pltpu.roll(values, rows - 1, 0))


def as_grid(values):
    return values.reshape(-1, WIN, GRID_COLS, values.shape[-1])


def move_rows(values, step):
    grid = as_grid(values)
    zeros = jnp.zeros_like(grid[:, :1])
    if step > 0:
        moved = jnp.concatenate([zeros, grid[:, :-1]], axis=1)
    else:
        moved = jnp.concatenate([grid[:, 1:], zeros], axis=1)
    return moved.reshape(values.shape)


def conv_cols(values, taps, keep):
    shifted = side_shifts(values)
    line = [
        sum(shifted[col] * taps[3 * row + col] for col in range(3)) for row in range(3)
    ]
    total = values + line[1] + move_rows(line[0], 1) + move_rows(line[2], -1)
    return jnp.where(keep, total, 0.0)


def tap_sums(grads, values):
    shifted = side_shifts(values)
    grad_grid = as_grid(grads)
    sums = []
    for row in range(3):
        for col in range(3):
            moved = as_grid(shifted[col])
            if row == 0:
                prod = grad_grid[:, 1:] * moved[:, :-1]
            elif row == 1:
                prod = grad_grid * moved
            else:
                prod = grad_grid[:, :-1] * moved[:, 1:]
            flat = prod.reshape(-1, GRID_COLS, prod.shape[-1])
            sums.append(jnp.sum(jnp.sum(flat, axis=0), axis=0, keepdims=True))
    return sums


def norm_stats(stream):
    width = stream.shape[1]
    center = jnp.sum(stream, axis=1, keepdims=True) * (1.0 / width)
    moved = stream - center
    inv_std = lax.rsqrt(jnp.sum(moved * moved, axis=1, keepdims=True) * (1.0 / width) + EPS)
    return moved * inv_std, inv_std


def norm_back(upstream, units, inv_std, gain):
    width = upstream.shape[1]
    scaled = upstream * gain
    first = jnp.sum(scaled, axis=1, keepdims=True) * (1.0 / width)
    second = jnp.sum(scaled * units, axis=1, keepdims=True) * (1.0 / width)
    return inv_std * (scaled - first - units * second)


def gelu_parts(values):
    z = jnp.abs(values) * (0.5**0.5)
    t = 1.0 / (1.0 + 0.3275911 * z)
    bell = jnp.exp(-z * z)
    poly = t * (
        0.254829592
        + t * (-0.284496736 + t * (1.421413741 + t * (-1.453152027 + t * 1.061405429)))
    )
    tail = 0.5 * poly * bell
    return jnp.where(values < 0, tail, 1.0 - tail), bell * float(1.0 / np.sqrt(2.0 * np.pi))


def head_mask(index):
    return (lax.broadcasted_iota(jnp.int32, (1, LANES), 1) // HEAD_DIM) == index


def spread_heads(tile):
    return jnp.concatenate(
        [jnp.where(head_mask(j), tile, 0.0) for j in range(HEADS_TILE)], axis=0
    ).astype(BF16)


def gather_heads(stacked):
    rows = stacked.shape[0] // HEADS_TILE
    total = jnp.where(head_mask(0), stacked[:rows], 0.0)
    for j in range(1, HEADS_TILE):
        total = jnp.where(head_mask(j), stacked[j * rows : (j + 1) * rows], total)
    return total


def softmax_rows(scores):
    top = jnp.max(scores, axis=0, keepdims=True)
    weights = jnp.exp(scores - top)
    return weights / jnp.sum(weights, axis=0, keepdims=True)


SCALE = HEAD_DIM**-0.5


def window_tile(q, k, v):
    keys_ok = column_mask(PADDED)
    scores = mm(k.astype(BF16), spread_heads(q), 1, 1) * SCALE
    probs = softmax_rows(jnp.where(keys_ok, scores, NEG))
    return probs, gather_heads(mm(probs.astype(BF16), v.astype(BF16), 0, 0))


def window_tile_back(q, k, v, probs, grad):
    low = probs.astype(BF16)
    q_big, g_big = spread_heads(q), spread_heads(grad)
    grad_probs = mm(v.astype(BF16), g_big, 1, 1)
    grad_v = mm(low, g_big, 1, 0)
    grad_scores = (
        probs * (grad_probs - jnp.sum(grad_probs * probs, axis=0, keepdims=True))
    ).astype(BF16)
    grad_k = mm(grad_scores, q_big, 1, 0) * SCALE
    grad_q = gather_heads(mm(grad_scores, k.astype(BF16), 0, 0)) * SCALE
    return grad_q, grad_k, grad_v


def same_head():
    first = lax.broadcasted_iota(jnp.int32, (LANES, LANES), 0) // HEAD_DIM
    second = lax.broadcasted_iota(jnp.int32, (LANES, LANES), 1) // HEAD_DIM
    return first == second


def channel_tile(q, k, v, mask):
    scores = mm(k.astype(BF16), (q * mask).astype(BF16), 0, 0) * SCALE
    probs = softmax_rows(jnp.where(same_head(), scores, NEG))
    return probs, mm(v.astype(BF16), probs.astype(BF16), 1, 0)


def channel_tile_back(q, k, v, probs, grad, mask):
    low = probs.astype(BF16)
    grad_low = grad.astype(BF16)
    grad_probs = mm(v.astype(BF16), grad_low, 0, 0)
    grad_v = mm(grad_low, low, 1, 1)
    grad_scores = (
        probs * (grad_probs - jnp.sum(grad_probs * probs, axis=0, keepdims=True))
    ).astype(BF16)
    grad_q = mm(k.astype(BF16), grad_scores, 1, 0) * SCALE * mask
    grad_k = mm((q * mask).astype(BF16), grad_scores, 1, 1) * SCALE
    return grad_q, grad_k, grad_v


def solution(mesh):
    n_dev = mesh.shape["dev"]
    bits = n_dev.bit_length() - 1
    assert n_dev == 1 << bits and mesh.shape["ha"] == 2 and mesh.shape["wa"] == 2

    swap = [(0, 1), (1, 0)]

    def over_ha(values):
        return lax.ppermute(values, "ha", swap)

    def over_wa(values):
        return lax.ppermute(values, "wa", swap)

    def over_dev(values, bit):
        return lax.ppermute(values, "dev", [(i, i ^ (1 << bit)) for i in range(n_dev)])

    def on_device(
        tokens, cotangent, conv_taps, norm_gain, norm_shift, w_qkv, w_proj, w_up, w_down, valid
    ):
        rows_in, half = tokens.shape
        images = rows_in // PATCHES
        rows = images * PADDED
        width = 2 * half
        heads_width = w_qkv.shape[3]
        hidden = w_up.shape[2]
        tiles = heads_width // LANES
        assert heads_width == half
        rest = list(range(3, bits))
        orders = [[0, 1, 2, *rest], [1, 0, 2, *rest], [0, 2, 1, *rest], [1, 2, 0, *rest]]

        def here(name):
            return lax.axis_index(name)

        def chunk_at(place, which):
            found = 0
            for step, bit in enumerate(orders[which]):
                found |= ((place >> (bits - 1 - step)) & 1) << bit
            return found ^ here("dev")

        order = Order()
        call = partial(kernel_call, order=order)

        def later(values, event):
            return lax.optimization_barrier((values, event))[0]

        def pack_small(taps_ref, gain_ref, shift_ref, out_ref):
            for section in range(2):
                for t in range(9):
                    at = 9 * section + t
                    out_ref[at : at + 1, :] = taps_ref[t, section : section + 1, :]
            out_ref[18:22, :] = gain_ref[...]
            out_ref[22:26, :] = shift_ref[...]

        def choose(mine, received, cot, cot_received, own, other, cot_own, cot_other):
            same = here("ha") == here("wa")
            own[...] = jnp.where(same, mine[...], received[...])
            other[...] = jnp.where(same, received[...], mine[...])
            cot_own[...] = jnp.where(same, cot[...], cot_received[...])
            cot_other[...] = jnp.where(same, cot_received[...], cot[...])

        wq_own = jnp.transpose(w_qkv, (0, 2, 1, 3))
        wq, wp = (wq_own, over_wa(wq_own)), (w_proj, over_wa(w_proj))
        tokens_in, cot_in = over_ha(tokens), over_ha(cotangent)
        small_own = call(
            pack_small, "pack_small",
            [jnp.transpose(conv_taps, (1, 0, 2)), norm_gain, norm_shift], [sds((26, half))],
            hold=[tokens],
        )[0]
        small = (small_own, over_wa(small_own))
        tokens_own, tokens_oth, cot_own, cot_oth = call(
            choose, "choose", [tokens, tokens_in, cotangent, cot_in],
            [sds((rows_in, half), BF16)] * 4, hold=[wq[1], wp[1], small_own],
        )
        token_parts = (tokens_own, over_wa(tokens_oth))
        arrived = (token_parts[1], small[1])
        cot_parts = (cot_own, over_wa(later(cot_oth, arrived)))
        wu, wd = ((values, over_wa(later(values, arrived))) for values in (w_up, w_down))

        def unpack(own, oth):
            values = jnp.concatenate([own[...], oth[...]], axis=1)
            return mm(placement(images, False), values, 1, 0)

        def gain_row(refs, branch):
            return jnp.concatenate([ref[18 + branch : 19 + branch, :] for ref in refs], axis=1)

        def shift_row(refs, branch):
            return jnp.concatenate([ref[22 + branch : 23 + branch, :] for ref in refs], axis=1)

        def tap_rows(small_refs, section, col, flipped):
            ref = small_refs[col // half]
            at = col % half
            found = [
                ref[9 * section + t : 9 * section + t + 1, at : at + LANES] for t in range(9)
            ]
            return found[::-1] if flipped else found

        def project_in(normed, first, second):
            return mm(normed[:, :half], first, 1, 0) + mm(normed[:, half:], second, 1, 0)

        def project_back(values, first, second):
            return mm(values[:, :half], first, 1, 1) + mm(values[:, half:], second, 1, 1)

        def to_normed(stream, small_refs, branch):
            units, _ = norm_stats(stream)
            return (units * gain_row(small_refs, branch) + shift_row(small_refs, branch)).astype(
                BF16
            )

        def both_rear(pieces):
            return pieces, [over_wa(piece) for piece in pieces]

        def put_both(own_ref, oth_ref, values):
            own_ref[...] = values[:, :half]
            oth_ref[:, :half] = values[:, half:]

        def add_parts(stream, part_a, part_b):
            return stream[...] + part_a[...].astype(F32) + part_b[...].astype(F32)

        def attention_part(window, section, normed, valid_rows, wq_a, wq_b, qkv_ref, probs_ref):
            packed = [
                project_in(normed, wq_a[section, part], wq_b[section, part]).astype(BF16)
                for part in range(3)
            ]
            for part in range(3):
                qkv_ref[part] = packed[part]
            wide = [part.astype(F32) for part in packed]
            mixed = []
            for image in range(images):
                line = []
                rows_at = slice(image * PADDED, (image + 1) * PADDED)
                for tile in range(tiles):
                    lanes_at = slice(tile * LANES, (tile + 1) * LANES)
                    q, k, v = (part[rows_at, lanes_at] for part in wide)
                    if window:
                        probs, out = window_tile(q, k, v)
                    else:
                        probs, out = channel_tile(q, k, v, valid_rows[image])
                    probs_ref[image * tiles + tile] = probs
                    line.append(out)
                mixed.append(jnp.concatenate(line, axis=1))
            return jnp.concatenate(mixed, axis=0).astype(BF16)

        def attention_part_back(window, grad_mixed, mask_ref, qkv_ref, probs_ref, rear_refs):
            wide = [qkv_ref[part].astype(F32) for part in range(3)]
            grad = grad_mixed.astype(F32)
            found = [[], [], []]
            for image in range(images):
                lines = [[], [], []]
                for tile in range(tiles):
                    rows_at = slice(image * PADDED, (image + 1) * PADDED)
                    lanes_at = slice(tile * LANES, (tile + 1) * LANES)
                    q, k, v = (part[rows_at, lanes_at] for part in wide)
                    probs = probs_ref[image * tiles + tile]
                    if window:
                        parts = window_tile_back(q, k, v, probs, grad[rows_at, lanes_at])
                    else:
                        parts = channel_tile_back(
                            q, k, v, probs, grad[rows_at, lanes_at], mask_ref[rows_at, :]
                        )
                    for line, part in zip(lines, parts):
                        line.append(part)
                for part in range(3):
                    found[part].append(jnp.concatenate(lines[part], axis=1))
            packed = [jnp.concatenate(part, axis=0).astype(BF16) for part in found]
            for part in range(3):
                put_rear(rear_refs, half + part * heads_width, packed[part])
            return packed

        def mul_out(left, section, own_ref, oth_ref, out_ref):
            out_ref[:, :half] = mm(left, own_ref[section], 1, 0).astype(BF16)
            out_ref[:, half:] = mm(left, oth_ref[section], 1, 0).astype(BF16)

        def conv_into(out_ref, values, small_refs, section, keep):
            for col in range(0, width, LANES):
                taps = tap_rows(small_refs, section, col, False)
                out_ref[:, col : col + LANES] = conv_cols(values[:, col : col + LANES], taps, keep)

        def conv_back_into(out_ref, sums_ref, sums_at, grads, values, small_refs, section, keep):
            for col in range(0, width, LANES):
                lanes_at = slice(col, col + LANES)
                taps = tap_rows(small_refs, section, col, True)
                for t, total in enumerate(tap_sums(grads[:, lanes_at], values[:, lanes_at])):
                    sums_ref[sums_at + t : sums_at + t + 1, lanes_at] = total
                out_ref[:, lanes_at] = conv_cols(grads[:, lanes_at], taps, keep)

        window_probs = sds((images * tiles, PADDED, HEADS_TILE * PADDED))
        channel_probs = sds((images * tiles, LANES, LANES))
        full, full_low = sds((rows, width)), sds((rows, width), BF16)
        half_low = sds((rows, half), BF16)
        hid_low = sds((rows, hidden), BF16)
        qkv_low = sds((3, rows, heads_width), BF16)
        fore_attn, fore_mlp = (
            sds((rows, half + heads_width), BF16),
            sds((rows, half + hidden), BF16),
        )
        def cuts(total, count):
            tiles_all = total // LANES
            return [LANES * (-(-tiles_all * (at + 1) // count)) for at in range(count)]

        def rear_shapes(total, count):
            ends = cuts(total, count)
            return [sds((rows, e - b), BF16) for b, e in zip([0, *ends], ends)]

        def rear_ranges(refs, at, size):
            begin = 0
            for ref in refs:
                end = begin + ref.shape[1]
                low, high = max(begin, at), min(end, at + size)
                if low < high:
                    yield ref, low - begin, high - begin, low - at
                begin = end

        def put_rear(refs, at, values):
            for ref, low, high, source in rear_ranges(refs, at, values.shape[1]):
                ref[:, low:high] = values[:, source : source + high - low]

        def get_rear(refs, at, size):
            parts = [ref[:, low:high] for ref, low, high, _ in rear_ranges(refs, at, size)]
            return parts[0] if len(parts) == 1 else jnp.concatenate(parts, axis=1)

        rear_width_attn, rear_width_mlp = half + 3 * heads_width, half + hidden
        attn_flops = 2 * rows * (4 * width * heads_width)
        mlp_flops = 2 * rows * (2 * width * hidden)

        def first_body(
            tokens_a, tokens_b, small_a, small_b, wq_a, wq_b, wp_a, wp_b,
            x_ref, s_ref, n_own, fore_ref, qkv_ref, probs_ref, part_ref, keep_a, keep_b,
        ):
            keep_a[...], keep_b[...] = small_a[...], small_b[...]
            keep = column_mask(rows)
            stream = unpack(tokens_a, tokens_b)
            x_ref[...] = stream.astype(BF16)
            conv_into(s_ref, stream, (small_a, small_b), 0, keep)
            normed = to_normed(s_ref[...], (small_a, small_b), 0)
            put_both(n_own, fore_ref, normed)
            mixed = attention_part(True, 0, normed, None, wq_a, wq_b, qkv_ref, probs_ref)
            fore_ref[:, half:] = mixed
            mul_out(mixed, 0, wp_a, wp_b, part_ref)

        (x0, s1, n0_own, fore0, qkv0, probs0, part0, *small) = call(
            first_body, "attn_a",
            [*token_parts, *small, *wq, *wp],
            [full_low, full, half_low, fore_attn, qkv_low, window_probs, full_low]
            + [sds((26, half))] * 2,
            flops=attn_flops, hold=[cot_own],
        )
        far0 = over_ha(part0)
        fore0 = (fore0, over_wa(fore0))
        keep_a = [x0, n0_own, *fore0, qkv0, probs0, s1]

        def mlp_body(
            s_in, part_a, part_b, small_a, small_b, wu_a, wu_b, wd_a, wd_b,
            s_ref, n_own, fore_ref, slope_ref, part_ref,
        ):
            s_ref[...] = add_parts(s_in, part_a, part_b)
            normed = to_normed(s_ref[...], (small_a, small_b), 1)
            put_both(n_own, fore_ref, normed)
            pre = project_in(normed, wu_a[0], wu_b[0])
            below, bell = gelu_parts(pre)
            hid = (pre * below).astype(BF16)
            fore_ref[:, half:] = hid
            slope_ref[...] = below + pre * bell
            mul_out(hid, 0, wd_a, wd_b, part_ref)

        (s2, n1_own, fore1, slope1, part1) = call(
            mlp_body, "mlp_b",
            [s1, part0, far0, *small, *wu, *wd],
            [full, half_low, fore_mlp, sds((rows, hidden)), full_low],
            flops=mlp_flops, hold=[*keep_a, *wq, *wp, *cot_parts],
        )
        far1 = over_ha(part1)
        fore1 = (fore1, over_wa(fore1))
        keep_b = [s2, n1_own, *fore1, slope1]
        weights = [*wq, *wp, *wu, *wd]


        def cot_body(cot_a, cot_b, wd_a, wd_b, g_own, g_oth, dhid_ref):
            grad = unpack(cot_a, cot_b).astype(BF16)
            put_both(g_own, g_oth, grad)
            dhid_ref[...] = project_back(grad, wd_a[1], wd_b[1]).astype(BF16)

        g3_own, g3_oth, dhid3 = call(
            cot_body, "cot_d",
            [*cot_parts, *wd],
            [half_low, half_low, hid_low],
            flops=mlp_flops // 2, hold=[*keep_a, *keep_b, *small, *wq, *wp, *wu],
        )

        def channel_body(
            s_in, part_a, part_b, valid_ref, small_a, small_b,
            wq_a, wq_b, wp_a, wp_b,
            s_before, s_ref, n_own, fore_ref, qkv_ref, probs_ref, part_ref, mask_ref,
        ):
            keep = column_mask(rows)
            s_before[...] = jnp.where(keep, add_parts(s_in, part_a, part_b), 0.0)
            conv_into(s_ref, s_before, (small_a, small_b), 1, keep)
            normed = to_normed(s_ref[...], (small_a, small_b), 2)
            put_both(n_own, fore_ref, normed)
            one_image = placement(1, False).astype(F32)
            valid_rows = []
            for image in range(images):
                line = jnp.where(
                    here("wa") == 0,
                    valid_ref[image : image + 1, :],
                    valid_ref[images + image : images + image + 1, :],
                ).astype(F32)
                valid_rows.append(jnp.sum(one_image * line, axis=1, keepdims=True))
                mask_ref[image * PADDED : (image + 1) * PADDED, :] = valid_rows[image]
            mixed = attention_part(False, 1, normed, valid_rows, wq_a, wq_b, qkv_ref, probs_ref)
            fore_ref[:, half:] = mixed
            mul_out(mixed, 1, wp_a, wp_b, part_ref)

        (s3, s4, n2_own, fore2, qkv2, probs2, part2, mask) = call(
            channel_body, "attn_c",
            [s2, part1, far1, valid, *small, *wq, *wp],
            [full, full, half_low, fore_attn, qkv_low, channel_probs, full_low,
             sds((rows, 1))],
            flops=attn_flops,
            hold=[*keep_a, *keep_b, *wu, *wd, g3_own, g3_oth, dhid3],
        )
        far2 = over_ha(part2)
        fore2 = (fore2, over_wa(fore2))
        keep_c = [s3, s4, n2_own, *fore2, qkv2, probs2, mask]

        def last_body(
            s_in, part_a, part_b, small_a, small_b, dhid_ref, g_oth, wu_a, wu_b,
            s_ref, n_own, fore_ref, part_ref, *rear_refs,
        ):
            s_ref[...] = add_parts(s_in, part_a, part_b)
            normed = to_normed(s_ref[...], (small_a, small_b), 3)
            put_both(n_own, fore_ref, normed)
            pre = project_in(normed, wu_a[1], wu_b[1])
            below, bell = gelu_parts(pre)
            fore_ref[:, half:] = (pre * below).astype(BF16)
            dpre = (dhid_ref[...].astype(F32) * (below + pre * bell)).astype(BF16)
            put_rear(rear_refs, 0, g_oth[...])
            put_rear(rear_refs, half, dpre)
            part_ref[:, :half] = mm(dpre, wu_a[1], 1, 1).astype(BF16)
            part_ref[:, half:] = mm(dpre, wu_b[1], 1, 1).astype(BF16)

        (s5, n3_own, fore3, back3, *rear3) = call(
            last_body, "mlp_d",
            [s4, part2, far2, *small, dhid3, g3_oth, *wu],
            [full, half_low, fore_mlp, full_low, *rear_shapes(rear_width_mlp, 2)],
            flops=mlp_flops,
            hold=[*keep_a, *keep_b, *keep_c, g3_own, g3_oth, *wq, *wp, *wd],
        )
        far_back3 = over_ha(back3)
        fore3 = (fore3, over_wa(fore3))
        rear3 = both_rear(rear3)

        up_rows, down_rows = hidden // n_dev, half // n_dev
        qkv_rows, proj_rows = heads_width // n_dev, half // n_dev
        folds = hidden // half
        cut = n_dev // 2
        sum_rows = 32

        class Stream:
            def __init__(self, which, pieces):
                self.bits, self.which, self.pieces = orders[which], which, pieces
                self.chunk_rows = sum(piece_rows(piece) for piece in pieces)
                self.step, self.kept, self.got, self.at, self.final = 0, None, None, 0, None

        def piece_rows(piece):
            return {"up": up_rows, "q": qkv_rows, "k": qkv_rows, "v": qkv_rows}.get(
                piece, down_rows
            )

        downs = [("down", fold) for fold in range(folds)]

        def two_streams(parts, first, which):
            streams = [Stream(which, parts[:first]), Stream(which + 1, parts[first:])]
            return [stream for stream in streams if stream.pieces]

        def mlp_streams(first, which):
            return two_streams(["up", *downs], 1 + first, which)

        def attn_streams(first, which):
            return two_streams(["q", "k", "v", "proj"], first, which)

        def write_pieces(values, streams, scratches):
            for stream, scratch in zip(streams, scratches):
                at = 0
                for piece in stream.pieces:
                    size = piece_rows(piece)
                    for chunk in range(n_dev):
                        rows_at = slice(chunk * size, (chunk + 1) * size)
                        if isinstance(piece, tuple):
                            columns = slice(piece[1] * half, (piece[1] + 1) * half)
                            part = values["down"][rows_at, columns]
                        else:
                            part = values[piece][rows_at]
                        scratch[chunk, at : at + size, :] = part
                    at += size

        def both_sums(n_own, g_own, fore_a, fore_b, rear_a, rear_b):
            def left(at, size):
                return mm(get_rear(rear_a, at, size), n_own[...], 0, 0) + mm(
                    get_rear(rear_b, at, size), fore_b[:, :half], 0, 0
                )

            right = mm(g_own[...], fore_a[:, half:], 0, 0) + mm(
                get_rear(rear_b, 0, half), fore_b[:, half:], 0, 0
            )
            return left, right

        def write_mlp(*refs):
            left, right = both_sums(*refs)
            return {"up": left(half, hidden), "down": right}

        def write_attn(*refs):
            left, right = both_sums(*refs)
            values = {
                name: left(half + part * heads_width, heads_width)
                for part, name in enumerate(("q", "k", "v"))
            }
            return {**values, "proj": right}

        def make(name, write, streams, n_own, g_own, fore, rear, hold):
            outs = [sds((cut * s.chunk_rows, half), BF16) for s in streams for _ in range(2)]
            count = len(rear[0])

            def body(n_ref, g_ref, fore_a, fore_b, *refs):
                rear_a, rear_b, refs = refs[:count], refs[count : 2 * count], refs[2 * count :]
                out_refs, scratches = refs[: len(outs)], refs[len(outs) :]
                values = write(n_ref, g_ref, fore_a, fore_b, rear_a, rear_b)
                write_pieces(values, streams, scratches)
                for at, (stream, scratch) in enumerate(zip(streams, scratches)):
                    size = stream.chunk_rows
                    for place in range(n_dev):
                        chunk = scratch[chunk_at(place, stream.which)].astype(BF16)
                        to = (place % cut) * size
                        out_refs[2 * at + place // cut][to : to + size, :] = chunk

            results = call(
                body, name, [n_own, g_own, *fore, *rear[0], *rear[1]], outs, hold=hold,
                scratch=[pltpu.VMEM((n_dev, s.chunk_rows, half), F32) for s in streams],
            )
            for at, stream in enumerate(streams):
                stream.kept, stream.sent = results[2 * at], results[2 * at + 1]

        def send_first(streams):
            for stream in streams:
                stream.got, stream.step = over_dev(stream.sent, stream.bits[0]), 1

        def split_low(values):
            high = values.astype(BF16)
            return high, (values - high.astype(F32)).astype(BF16)

        def joined(ref, at):
            high = ref[at : at + sum_rows, :].astype(F32)
            return high + ref[at + sum_rows : at + 2 * sum_rows, :].astype(F32)

        def last_sum(stream, kept, got):
            return kept[...].astype(F32) + got[
                stream.at : stream.at + stream.chunk_rows, :
            ].astype(F32)

        def slot(name, fresh=(), moving=(), ending=(), sums=None, hold=()):
            ins, outs, sizes = [], [], {}
            plan_fresh, plan_moving = [], []

            def room(bit, size):
                at = sizes.get(bit, 0)
                sizes[bit] = at + size
                return at

            def place_of(array):
                for at, known in enumerate(ins):
                    if known is array:
                        return at
                ins.append(array)
                return len(ins) - 1

            for stream in fresh:
                size, bit = stream.sent.shape[0], stream.bits[0]
                plan_fresh.append((place_of(stream.sent), size, bit, room(bit, size)))
            for stream in moving:
                size = stream.kept.shape[0] // 2
                bit = stream.bits[stream.step]
                plan_moving.append(
                    (place_of(stream.kept), place_of(stream.got), stream.at, size,
                     len(outs), bit, room(bit, size))
                )
                outs.append(sds((size, half), BF16))
            plan_ending = []
            for stream in ending:
                plan_ending.append(
                    (stream, place_of(stream.kept), place_of(stream.got), len(outs))
                )
                outs.append(sds((stream.chunk_rows, half)))
            if sums is not None:
                total_at = place_of(sums[0])
                sums_got = None if sums[1] is None else place_of(sums[1])
                sums_room = room(sums[3], 2 * sum_rows)
                sums_out = len(outs)
                outs.append(sds((sum_rows, half)))
            bits_used = sorted(sizes)
            buffer_at = {bit: len(outs) + at for at, bit in enumerate(bits_used)}
            outs += [sds((sizes[bit], half), BF16) for bit in bits_used]

            def body(*refs):
                in_refs, out_refs = refs[: len(ins)], refs[len(ins) :]
                for sent_in, size, bit, at in plan_fresh:
                    out_refs[buffer_at[bit]][at : at + size, :] = in_refs[sent_in][...]
                for kept_in, got_in, got_row, size, kept_at, bit, at in plan_moving:
                    kept, got = in_refs[kept_in], in_refs[got_in]
                    out_refs[kept_at][...] = (
                        kept[:size, :].astype(F32) + got[got_row : got_row + size, :].astype(F32)
                    ).astype(BF16)
                    out_refs[buffer_at[bit]][at : at + size, :] = (
                        kept[size:, :].astype(F32)
                        + got[got_row + size : got_row + 2 * size, :].astype(F32)
                    ).astype(BF16)
                for stream, kept_in, got_in, out_at in plan_ending:
                    out_refs[out_at][...] = last_sum(stream, in_refs[kept_in], in_refs[got_in])
                if sums is not None:
                    total = in_refs[total_at][...]
                    if sums_got is not None:
                        total = total + joined(in_refs[sums_got], sums[2])
                    high, low = split_low(total)
                    out_refs[sums_out][...] = high.astype(F32) + low.astype(F32)
                    buffer = out_refs[buffer_at[sums[3]]]
                    buffer[sums_room : sums_room + sum_rows, :] = high
                    buffer[sums_room + sum_rows : sums_room + 2 * sum_rows, :] = low

            results = call(body, name, ins, outs, hold=hold)
            received = {bit: over_dev(results[buffer_at[bit]], bit) for bit in bits_used}
            for stream, (_, _, bit, at) in zip(fresh, plan_fresh):
                stream.got, stream.at, stream.step = received[bit], at, 1
            for stream, _, _, out_at in plan_ending:
                stream.final = results[out_at]
            for stream, (_, _, _, _, kept_at, bit, at) in zip(moving, plan_moving):
                stream.kept, stream.got, stream.at = results[kept_at], received[bit], at
                stream.step += 1
            if sums is not None:
                sums[:3] = results[sums_out], received[sums[3]], sums_room

        def ship(total, kept, sent):
            packed = mm(placement(images, True), total.astype(BF16), 1, 0).astype(BF16)
            kept[...] = packed[:, :half]
            sent[...] = packed[:, half:]

        shipped = [sds((rows_in, half), BF16)] * 2

        def fold(kept, received, stay, go):
            same = here("ha") == here("wa")
            stay[...] = jnp.where(same, kept[...], received[...])
            go[:rows_in, :] = jnp.where(same, received[...], kept[...])

        def join(stay, received, out_ref):
            out_ref[...] = stay[...].astype(F32) + received[:rows_in, :].astype(F32)

        def out_body(s_in, fore_ref, wd_a, wd_b, kept, sent):
            hid = fore_ref[:, half:]
            base = jnp.where(here("ha") == 0, s_in[...], 0.0)
            branch = jnp.concatenate([mm(hid, wd_a[1], 1, 0), mm(hid, wd_b[1], 1, 0)], axis=1)
            ship(base + branch, kept, sent)

        streams_d = mlp_streams(SPLIT_D, 0)
        make(
            "wgrad_d", write_mlp, streams_d, n3_own, g3_own, fore3, rear3,
            [*keep_a, *keep_b, *keep_c, *small, *weights, s5],
        )
        send_first(streams_d)

        def add_norm_back(grad, part_a, part_b, stream, gain, sums_ref):
            upstream = part_a[...].astype(F32) + part_b[...].astype(F32)
            units, inv_std = norm_stats(stream)
            sums_ref[0:1, :] = jnp.sum(upstream * units, axis=0, keepdims=True)
            sums_ref[1:2, :] = jnp.sum(upstream, axis=0, keepdims=True)
            return grad + norm_back(upstream, units, inv_std, gain)

        def qkv_back(packed, section, wq_a, wq_b):
            return [
                sum(mm(packed[part], ref[section, part], 1, 1) for part in range(3))
                for ref in (wq_a, wq_b)
            ]

        def channel_back_body(
            g_in_own, g_in_oth, part_a, part_b, s_in, small_a, small_b, mask_ref, qkv_ref,
            probs_ref, wp_a, wp_b, wq_a, wq_b,
            g_ref, g_own, part_ref, sums_ref, *rear_refs,
        ):
            grad = jnp.concatenate([g_in_own[...], g_in_oth[...]], axis=1).astype(F32)
            gain = gain_row((small_a, small_b), 3)
            grad = add_norm_back(grad, part_a, part_b, s_in[...], gain, sums_ref)
            g_ref[...] = grad
            low = grad.astype(BF16)
            g_own[...] = low[:, :half]
            put_rear(rear_refs, 0, low[:, half:])
            grad_mixed = project_back(low, wp_a[1], wp_b[1]).astype(BF16)
            packed = attention_part_back(
                False, grad_mixed, mask_ref, qkv_ref, probs_ref, rear_refs
            )
            own, oth = qkv_back(packed, 1, wq_a, wq_b)
            part_ref[:, :half] = own.astype(BF16)
            part_ref[:, half:] = oth.astype(BF16)

        late = [fore3[0], *wd, s5]
        (g2, g2_own, back2, sums3, *rear2) = call(
            channel_back_body, "back_c",
            [g3_own, g3_oth, back3, far_back3, s5, *small, mask, qkv2, probs2, *wp, *wq],
            [full, half_low, full_low, sds((2, width)), *rear_shapes(rear_width_attn, 1)],
            flops=attn_flops,
            hold=[*keep_a, *keep_b, s3, s4, n2_own, *fore2, *wu, *wd, fore3[0]],
        )
        far_back2 = over_ha(back2)
        rear2 = both_rear(rear2)
        streams_c = attn_streams(SPLIT_C, 2)
        kept_c = [*keep_a, *keep_b, s3, s4, *small, *weights, g2, *late, sums3]
        make("wgrad_c", write_attn, streams_c, n2_own, g2_own, fore2, rear2, kept_c)
        slot(
            "slot_c", fresh=streams_c, moving=streams_d, hold=[*kept_c, back2, far_back2],
        )

        def mlp_back_body(
            g_in, part_a, part_b, s_in, s_before, small_a, small_b, slope_ref,
            wd_a, wd_b, wu_a, wu_b, g_ref, g_own, part_ref, sums_ref, *rear_refs,
        ):
            keep = column_mask(rows)
            gain = gain_row((small_a, small_b), 2)
            grad = add_norm_back(g_in[...], part_a, part_b, s_in[...], gain, sums_ref)
            conv_back_into(g_ref, sums_ref, 2, grad, s_before[...], (small_a, small_b), 1, keep)
            low = g_ref[...].astype(BF16)
            g_own[...] = low[:, :half]
            put_rear(rear_refs, 0, low[:, half:])
            dhid = project_back(low, wd_a[0], wd_b[0]).astype(BF16).astype(F32)
            dpre = (dhid * slope_ref[...]).astype(BF16)
            put_rear(rear_refs, half, dpre)
            part_ref[:, :half] = mm(dpre, wu_a[0], 1, 1).astype(BF16)
            part_ref[:, half:] = mm(dpre, wu_b[0], 1, 1).astype(BF16)

        (g1, g1_own, back1, sums2, *rear1) = call(
            mlp_back_body, "back_b",
            [g2, back2, far_back2, s4, s3, *small, slope1, *wd, *wu],
            [full, half_low, full_low, sds((11, width)), *rear_shapes(rear_width_mlp, 2)],
            flops=mlp_flops,
            hold=[*keep_a, s2, n1_own, *fore1, *wq, *wp, fore3[0], s5, sums3],
        )
        far_back1 = over_ha(back1)
        rear1 = both_rear(rear1)
        streams_b = mlp_streams(SPLIT_B, 0)
        make(
            "wgrad_b", write_mlp, streams_b, n1_own, g1_own, fore1, rear1,
            [*keep_a, s2, *small, *wq, *wp, g1, *late, sums3, sums2],
        )

        def window_back_body(
            g_in, part_a, part_b, s_in, small_a, small_b, qkv_ref, probs_ref, wp_a, wp_b,
            g_ref, g_own, sums_ref, *rear_refs,
        ):
            gain = gain_row((small_a, small_b), 1)
            grad = add_norm_back(g_in[...], part_a, part_b, s_in[...], gain, sums_ref)
            g_ref[...] = grad
            low = grad.astype(BF16)
            g_own[...] = low[:, :half]
            put_rear(rear_refs, 0, low[:, half:])
            grad_mixed = project_back(low, wp_a[0], wp_b[0]).astype(BF16)
            attention_part_back(True, grad_mixed, None, qkv_ref, probs_ref, rear_refs)

        (g0, g0_own, sums1, *rear0) = call(
            window_back_body, "back_a",
            [g1, back1, far_back1, s2, *small, qkv0, probs0, *wp],
            [full, half_low, sds((2, width)), *rear_shapes(rear_width_attn, 3)],
            flops=attn_flops, hold=[x0, n0_own, *fore0, s1, *wq, *late, sums3, sums2],
        )
        rear0 = both_rear(rear0)

        keep_0 = [g0, s1, x0, *small, *wq, sums1, sums2, sums3, *rear0[0]]
        streams_a = attn_streams(SPLIT_A, 2)
        make("wgrad_a", write_attn, streams_a, n0_own, g0_own, fore0, rear0, [*late, *keep_0])
        every = [*streams_d, *streams_c, *streams_b, *streams_a]
        slot(
            "slot_ab", fresh=[*streams_b, *streams_a], moving=[*streams_d, *streams_c],
            hold=[*late, *keep_0],
        )

        def first_back_body(
            g_in, s_in, x_ref, small_a, small_b, wq_a, wq_b, sums_one, sums_two, sums_three, *refs
        ):
            rear_refs, (kept, sent, sums_own, sums_oth, scratch, sums_ref) = refs[:-6], refs[-6:]
            keep = column_mask(rows)
            packed = [
                get_rear(rear_refs, half + part * heads_width, heads_width) for part in range(3)
            ]
            upstream = jnp.concatenate(qkv_back(packed, 0, wq_a, wq_b), axis=1)
            units, inv_std = norm_stats(s_in[...])
            sums_ref[0:1, :] = jnp.sum(upstream * units, axis=0, keepdims=True)
            sums_ref[1:2, :] = jnp.sum(upstream, axis=0, keepdims=True)
            grad = jnp.where(here("ha") == 0, g_in[...], 0.0)
            grad = grad + norm_back(upstream, units, inv_std, gain_row((small_a, small_b), 0))
            conv_back_into(
                scratch, sums_ref, 2, grad, x_ref[...].astype(F32), (small_a, small_b), 0, keep
            )
            ship(scratch[...], kept, sent)
            sums_ref[11:13, :] = 0.5 * sums_one[...]
            sums_ref[13:24, :] = 0.5 * sums_two[...]
            sums_ref[24:26, :] = 0.5 * sums_three[...]
            sums_ref[26:, :] = jnp.zeros((sum_rows - 26, width), F32)
            put_both(sums_own, sums_oth, sums_ref[...])

        sums_half = sds((sum_rows, half))
        token_kept, token_sent, sums_own, sums_oth = call(
            first_back_body, "back_0",
            [g0, s1, x0, *small, *wq, sums1, sums2, sums3, *rear0[0]],
            shipped + [sds((sum_rows, half))] * 2,
            scratch=[pltpu.VMEM((rows, width), F32), pltpu.VMEM((sum_rows, width), F32)],
            flops=attn_flops * 3 // 4, hold=late,
        )
        sums_at = -(-rows_in // 16) * 16
        sums_half = sds((sum_rows, half))

        def fold_tokens(kept, received, sums_a, sums_b, stay, go, sums_ref):
            fold(kept, received, stay, go)
            high, low = split_low(sums_a[...] + sums_b[...])
            sums_ref[...] = high.astype(F32) + low.astype(F32)
            go[sums_at : sums_at + sum_rows, :] = high
            go[sums_at + sum_rows :, :] = low

        token_stay, token_go, sums_chip = call(
            fold_tokens, "fold_tokens",
            [token_kept, over_wa(token_sent), sums_own, over_wa(sums_oth)],
            [shipped[0], sds((sums_at + 2 * sum_rows, half), BF16), sums_half], hold=late,
        )
        token_got = over_ha(token_go)

        def join_tokens(stay, received, sums_chip, out_ref, sums_ref):
            join(stay, received, out_ref)
            sums_ref[...] = sums_chip[...] + joined(received, sums_at)

        owned = sds((rows_in, half))
        grad_tokens, sums_ha = call(
            join_tokens, "join_tokens", [token_stay, token_got, sums_chip], [owned, sums_half],
            hold=late,
        )
        left_bits = [2, 0, 1, *range(3, bits)]
        sums = [sums_ha, None, 0, left_bits.pop(0)]
        slot("sums_z", sums=sums, hold=late)
        turn = 0
        while left_bits or any(stream.step < bits for stream in every):
            turn += 1
            now = None
            if left_bits:
                sums[3] = left_bits.pop(0)
                now = sums
            slot(
                f"slot_{turn}", moving=[s for s in every if s.step < bits], sums=now,
                ending=[s for s in every if s.step == bits and s.final is None],
                hold=late if turn == 1 else [],
            )
            if turn == 1:
                out_kept, out_sent = call(
                    out_body, "out_d", [s5, fore3[0], *wd], shipped, flops=mlp_flops // 2
                )
                out_stay, out_go = call(fold, "fold_out", [out_kept, over_wa(out_sent)], shipped)
                out_got = over_ha(out_go)
        output = call(join, "join_out", [out_stay, out_got], [owned])[0]

        def finish_body(*refs):
            (up, down, qkv, proj, taps_ref, gain_ref, shift_ref) = refs[-7:]
            at = iter(refs)
            total = next(at)[...] + joined(next(at), sums[2])
            for branch, row in enumerate((0, 11, 13, 24)):
                gain_ref[branch : branch + 1, :] = total[row : row + 1]
                shift_ref[branch : branch + 1, :] = total[row + 1 : row + 2]
            for section, row in enumerate((2, 15)):
                for t in range(9):
                    taps_ref[t, section : section + 1, :] = total[row + t : row + t + 1]

            def finished(stream):
                if stream.final is not None:
                    return next(at)[...]
                return last_sum(stream, next(at), next(at))

            for section, streams in enumerate(
                ((*streams_a, *streams_b), (*streams_c, *streams_d))
            ):
                for stream in streams:
                    values, row = finished(stream), 0
                    for piece in stream.pieces:
                        part = values[row : row + piece_rows(piece)]
                        row += piece_rows(piece)
                        if piece == "up":
                            up[section] = part
                        elif piece == "proj":
                            proj[section] = part
                        elif isinstance(piece, tuple):
                            down[section, :, piece[1] * half : (piece[1] + 1) * half] = part
                        else:
                            qkv[section, ("q", "k", "v").index(piece)] = part

        ends = []
        for stream in (*streams_a, *streams_b, *streams_c, *streams_d):
            ends += [stream.kept, stream.got] if stream.final is None else [stream.final]
        up, down, qkv, proj, grad_taps, grad_gain, grad_shift = call(
            finish_body, "finish", [*sums[:2], *ends],
            [sds((2, up_rows, half)), sds((2, down_rows, hidden)), sds((2, 3, qkv_rows, half)),
             sds((2, proj_rows, half)), sds((9, 2, half)), sds((4, half)), sds((4, half))],
        )
        grad_taps = jnp.transpose(grad_taps, (1, 0, 2))
        grad_qkv = jnp.transpose(qkv, (0, 3, 1, 2))
        grad_proj, grad_up, grad_down = (
            jnp.transpose(values, (0, 2, 1)) for values in (proj, up, down)
        )
        return (
            output,
            grad_tokens,
            grad_taps,
            grad_gain,
            grad_shift,
            grad_qkv,
            grad_proj,
            grad_up,
            grad_down,
        )

    placed = (
        P(("dev", "ha"), "wa"),
        P(("dev", "ha"), "wa"),
        P(None, None, "wa"),
        P(None, "wa"),
        P(None, "wa"),
        P(None, "wa", None, "ha"),
        P(None, "ha", "wa"),
        P(None, "wa", "ha"),
        P(None, "ha", "wa"),
        P("dev", None),
    )
    return jax.shard_map(
        on_device,
        mesh=mesh,
        in_specs=placed,
        out_specs=(
            P(("dev", "ha"), "wa"),
            P(("dev", "ha"), "wa"),
            P(None, None, "wa"),
            P(None, "wa"),
            P(None, "wa"),
            P(None, "wa", None, ("ha", "dev")),
            P(None, "ha", ("wa", "dev")),
            P(None, "wa", ("ha", "dev")),
            P(None, "ha", ("wa", "dev")),
        ),
        check_vma=False,
    )
```

```python
from functools import partial

import jax
import jax.numpy as jnp
import numpy as np
from jax import lax
from jax.experimental import pallas as pl
from jax.experimental.pallas import tpu as pltpu
from jax.sharding import PartitionSpec as P

WIN = 7
GRID_COLS = 8
PATCHES = 49
PADDED = WIN * GRID_COLS
HEAD_DIM = 32
LANES = 128
HEADS_TILE = LANES // HEAD_DIM
EPS = 1e-05
NEG = -1e30
SPLIT_D, SPLIT_C, SPLIT_B, SPLIT_A = 0, 2, 0, 4
BF16 = jnp.bfloat16
F32 = jnp.float32
VMEM_LIMIT = 16 * 2**20
TIMES = {"pack_small": 5.0, "choose": 5.0}


def mm(left, right, left_dim, right_dim):
    return lax.dot_general(
        left, right, (((left_dim,), (right_dim,)), ((), ())), preferred_element_type=F32
    )


class Order:
    def __init__(self):
        self.last = None


def kernel_call(body, name, ins, outs, order, scratch=(), flops=0, hold=(), far=0):
    arrays = list(ins) + list(hold) + ([] if order.last is None else [order.last])
    specs = [
        pl.BlockSpec(
            memory_space=pltpu.SMEM if a.dtype == jnp.int32 and a.ndim == 1 else pltpu.VMEM
        )
        for a in arrays
    ]
    for at in range(len(ins) - far, len(ins)):
        specs[at] = pl.BlockSpec(memory_space=pltpu.HBM)
    outs = list(outs) + [sds((8, LANES))]

    def wrapped(*refs):
        given = refs[: len(ins)] + refs[len(arrays) : len(arrays) + len(outs) - 1]
        body(*given, *refs[len(arrays) + len(outs) :])
        mark = refs[len(arrays) + len(outs) - 1]
        mark[...] = jnp.zeros_like(mark)

    moved = sum(int(np.prod(o.shape)) * o.dtype.itemsize for o in outs) + sum(
        int(np.prod(a.shape)) * a.dtype.itemsize for a in ins
    )
    *results, order.last = pl.pallas_call(
        wrapped,
        in_specs=specs,
        out_specs=[pl.BlockSpec(memory_space=pltpu.VMEM)] * len(outs),
        out_shape=outs,
        scratch_shapes=list(scratch),
        compiler_params=pltpu.CompilerParams(vmem_limit_bytes=VMEM_LIMIT),
        cost_estimate=pl.CostEstimate(
            flops=int(TIMES.get(name, 0) * 1.15e9), bytes_accessed=0, transcendentals=0
        ),
        name=name,
    )(*arrays)
    return results


def sds(shape, dtype=F32):
    return jax.ShapeDtypeStruct(shape, dtype)


def column_mask(rows):
    return (lax.broadcasted_iota(jnp.int32, (rows, 1), 0) % GRID_COLS) < WIN


def placement(images, transposed):
    padded, plain = images * PADDED, images * PATCHES
    shape = (plain, padded) if transposed else (padded, plain)
    at = lax.broadcasted_iota(jnp.int32, shape, 1 if transposed else 0)
    image = sum((at >= i * PADDED).astype(jnp.int32) for i in range(1, images))
    inside = at - image * PADDED
    source = image * PATCHES + (inside >> 3) * WIN + (inside & 7)
    other = lax.broadcasted_iota(jnp.int32, shape, 0 if transposed else 1)
    return (((inside & 7) < WIN) & (source == other)).astype(F32).astype(BF16)


def side_shifts(values):
    rows = values.shape[0]
    return (pltpu.roll(values, 1, 0), values, pltpu.roll(values, rows - 1, 0))


def as_grid(values):
    return values.reshape(-1, WIN, GRID_COLS, values.shape[-1])


def move_rows(values, step):
    grid = as_grid(values)
    zeros = jnp.zeros_like(grid[:, :1])
    if step > 0:
        moved = jnp.concatenate([zeros, grid[:, :-1]], axis=1)
    else:
        moved = jnp.concatenate([grid[:, 1:], zeros], axis=1)
    return moved.reshape(values.shape)


def conv_cols(values, taps, keep):
    shifted = side_shifts(values)
    line = [
        sum(shifted[col] * taps[3 * row + col] for col in range(3)) for row in range(3)
    ]
    total = values + line[1] + move_rows(line[0], 1) + move_rows(line[2], -1)
    return jnp.where(keep, total, 0.0)


def tap_sums(grads, values):
    shifted = side_shifts(values)
    grad_grid = as_grid(grads)
    sums = []
    for row in range(3):
        for col in range(3):
            moved = as_grid(shifted[col])
            if row == 0:
                prod = grad_grid[:, 1:] * moved[:, :-1]
            elif row == 1:
                prod = grad_grid * moved
            else:
                prod = grad_grid[:, :-1] * moved[:, 1:]
            flat = prod.reshape(-1, GRID_COLS, prod.shape[-1])
            sums.append(jnp.sum(jnp.sum(flat, axis=0), axis=0, keepdims=True))
    return sums


def norm_stats(stream):
    width = stream.shape[1]
    center = jnp.sum(stream, axis=1, keepdims=True) * (1.0 / width)
    moved = stream - center
    inv_std = lax.rsqrt(jnp.sum(moved * moved, axis=1, keepdims=True) * (1.0 / width) + EPS)
    return moved * inv_std, inv_std


def norm_back(upstream, units, inv_std, gain):
    width = upstream.shape[1]
    scaled = upstream * gain
    first = jnp.sum(scaled, axis=1, keepdims=True) * (1.0 / width)
    second = jnp.sum(scaled * units, axis=1, keepdims=True) * (1.0 / width)
    return inv_std * (scaled - first - units * second)


def gelu_parts(values):
    z = jnp.abs(values) * (0.5**0.5)
    t = 1.0 / (1.0 + 0.3275911 * z)
    bell = jnp.exp(-z * z)
    poly = t * (
        0.254829592
        + t * (-0.284496736 + t * (1.421413741 + t * (-1.453152027 + t * 1.061405429)))
    )
    tail = 0.5 * poly * bell
    return jnp.where(values < 0, tail, 1.0 - tail), bell * float(1.0 / np.sqrt(2.0 * np.pi))


def head_mask(index):
    return (lax.broadcasted_iota(jnp.int32, (1, LANES), 1) // HEAD_DIM) == index


def spread_heads(tile):
    return jnp.concatenate(
        [jnp.where(head_mask(j), tile, 0.0) for j in range(HEADS_TILE)], axis=0
    ).astype(BF16)


def gather_heads(stacked):
    rows = stacked.shape[0] // HEADS_TILE
    total = jnp.where(head_mask(0), stacked[:rows], 0.0)
    for j in range(1, HEADS_TILE):
        total = jnp.where(head_mask(j), stacked[j * rows : (j + 1) * rows], total)
    return total


def softmax_rows(scores):
    top = jnp.max(scores, axis=0, keepdims=True)
    weights = jnp.exp(scores - top)
    return weights / jnp.sum(weights, axis=0, keepdims=True)


SCALE = HEAD_DIM**-0.5


def window_tile(q, k, v):
    keys_ok = column_mask(PADDED)
    scores = mm(k.astype(BF16), spread_heads(q), 1, 1) * SCALE
    probs = softmax_rows(jnp.where(keys_ok, scores, NEG))
    return probs, gather_heads(mm(probs.astype(BF16), v.astype(BF16), 0, 0))


def window_tile_back(q, k, v, probs, grad):
    low = probs.astype(BF16)
    q_big, g_big = spread_heads(q), spread_heads(grad)
    grad_probs = mm(v.astype(BF16), g_big, 1, 1)
    grad_v = mm(low, g_big, 1, 0)
    grad_scores = (
        probs * (grad_probs - jnp.sum(grad_probs * probs, axis=0, keepdims=True))
    ).astype(BF16)
    grad_k = mm(grad_scores, q_big, 1, 0) * SCALE
    grad_q = gather_heads(mm(grad_scores, k.astype(BF16), 0, 0)) * SCALE
    return grad_q, grad_k, grad_v


def same_head():
    first = lax.broadcasted_iota(jnp.int32, (LANES, LANES), 0) // HEAD_DIM
    second = lax.broadcasted_iota(jnp.int32, (LANES, LANES), 1) // HEAD_DIM
    return first == second


def channel_tile(q, k, v, mask):
    scores = mm(k.astype(BF16), (q * mask).astype(BF16), 0, 0) * SCALE
    probs = softmax_rows(jnp.where(same_head(), scores, NEG))
    return probs, mm(v.astype(BF16), probs.astype(BF16), 1, 0)


def channel_tile_back(q, k, v, probs, grad, mask):
    low = probs.astype(BF16)
    grad_low = grad.astype(BF16)
    grad_probs = mm(v.astype(BF16), grad_low, 0, 0)
    grad_v = mm(grad_low, low, 1, 1)
    grad_scores = (
        probs * (grad_probs - jnp.sum(grad_probs * probs, axis=0, keepdims=True))
    ).astype(BF16)
    grad_q = mm(k.astype(BF16), grad_scores, 1, 0) * SCALE * mask
    grad_k = mm((q * mask).astype(BF16), grad_scores, 1, 1) * SCALE
    return grad_q, grad_k, grad_v


def solution(mesh):
    n_dev = mesh.shape["dev"]
    bits = n_dev.bit_length() - 1
    assert n_dev == 1 << bits and mesh.shape["ha"] == 2 and mesh.shape["wa"] == 2

    swap = [(0, 1), (1, 0)]

    def over_ha(values):
        return lax.ppermute(values, "ha", swap)

    def over_wa(values):
        return lax.ppermute(values, "wa", swap)

    def over_dev(values, bit):
        return lax.ppermute(values, "dev", [(i, i ^ (1 << bit)) for i in range(n_dev)])

    def on_device(
        tokens, cotangent, conv_taps, norm_gain, norm_shift, w_qkv, w_proj, w_up, w_down, valid
    ):
        rows_in, half = tokens.shape
        images = rows_in // PATCHES
        rows = images * PADDED
        width = 2 * half
        heads_width = w_qkv.shape[3]
        hidden = w_up.shape[2]
        tiles = heads_width // LANES
        assert heads_width == half
        rest = list(range(3, bits))
        orders = [[0, 1, 2, *rest], [1, 0, 2, *rest], [0, 2, 1, *rest], [1, 2, 0, *rest]]

        def here(name):
            return lax.axis_index(name)

        def chunk_at(place, which):
            found = 0
            for step, bit in enumerate(orders[which]):
                found |= ((place >> (bits - 1 - step)) & 1) << bit
            return found ^ here("dev")

        order = Order()
        call = partial(kernel_call, order=order)

        def later(values, event):
            return lax.optimization_barrier((values, event))[0]

        def pack_small(taps_ref, gain_ref, shift_ref, out_ref):
            for section in range(2):
                for t in range(9):
                    at = 9 * section + t
                    out_ref[at : at + 1, :] = taps_ref[t, section : section + 1, :]
            out_ref[18:22, :] = gain_ref[...]
            out_ref[22:26, :] = shift_ref[...]

        def choose(mine, received, cot, cot_received, own, other, cot_own, cot_other):
            same = here("ha") == here("wa")
            own[...] = jnp.where(same, mine[...], received[...])
            other[...] = jnp.where(same, received[...], mine[...])
            cot_own[...] = jnp.where(same, cot[...], cot_received[...])
            cot_other[...] = jnp.where(same, cot_received[...], cot[...])

        wq_own = jnp.transpose(w_qkv, (0, 2, 1, 3))
        wq, wp = (wq_own, over_wa(wq_own)), (w_proj, over_wa(w_proj))
        tokens_in, cot_in = over_ha(tokens), over_ha(cotangent)
        small_own = call(
            pack_small, "pack_small",
            [jnp.transpose(conv_taps, (1, 0, 2)), norm_gain, norm_shift], [sds((26, half))],
            hold=[tokens],
        )[0]
        small = (small_own, over_wa(small_own))
        tokens_own, tokens_oth, cot_own, cot_oth = call(
            choose, "choose", [tokens, tokens_in, cotangent, cot_in],
            [sds((rows_in, half), BF16)] * 4, hold=[wq[1], wp[1], small_own],
        )
        token_parts = (tokens_own, over_wa(tokens_oth))
        arrived = (token_parts[1], small[1])
        cot_parts = (cot_own, over_wa(later(cot_oth, arrived)))
        wu, wd = ((values, over_wa(later(values, arrived))) for values in (w_up, w_down))

        def unpack(own, oth):
            values = jnp.concatenate([own[...], oth[...]], axis=1)
            return mm(placement(images, False), values, 1, 0)

        def gain_row(refs, branch):
            return jnp.concatenate([ref[18 + branch : 19 + branch, :] for ref in refs], axis=1)

        def shift_row(refs, branch):
            return jnp.concatenate([ref[22 + branch : 23 + branch, :] for ref in refs], axis=1)

        def tap_rows(small_refs, section, col, flipped):
            ref = small_refs[col // half]
            at = col % half
            found = [
                ref[9 * section + t : 9 * section + t + 1, at : at + LANES] for t in range(9)
            ]
            return found[::-1] if flipped else found

        def project_in(normed, first, second):
            return mm(normed[:, :half], first, 1, 0) + mm(normed[:, half:], second, 1, 0)

        def project_back(values, first, second):
            return mm(values[:, :half], first, 1, 1) + mm(values[:, half:], second, 1, 1)

        def to_normed(stream, small_refs, branch):
            units, _ = norm_stats(stream)
            return (units * gain_row(small_refs, branch) + shift_row(small_refs, branch)).astype(
                BF16
            )

        def both_rear(pieces, gather=True):
            pieces = list(pieces)
            if gather:
                return pieces, [lax.all_gather(piece, "wa") for piece in pieces]
            return pieces, [over_wa(piece) for piece in pieces]

        def other_core(ref):
            return ref.at[1 - here("wa")] if len(ref.shape) == 3 else ref

        def put_both(own_ref, oth_ref, values):
            own_ref[...] = values[:, :half]
            oth_ref[:, :half] = values[:, half:]

        def add_parts(stream, part_a, part_b):
            return stream[...] + part_a[...].astype(F32) + part_b[...].astype(F32)

        def attention_part(window, section, normed, valid_rows, wq_a, wq_b, qkv_ref, probs_ref):
            packed = [
                project_in(normed, wq_a[section, part], wq_b[section, part]).astype(BF16)
                for part in range(3)
            ]
            for part in range(3):
                qkv_ref[part] = packed[part]
            wide = [part.astype(F32) for part in packed]
            mixed = []
            for image in range(images):
                line = []
                rows_at = slice(image * PADDED, (image + 1) * PADDED)
                for tile in range(tiles):
                    lanes_at = slice(tile * LANES, (tile + 1) * LANES)
                    q, k, v = (part[rows_at, lanes_at] for part in wide)
                    if window:
                        probs, out = window_tile(q, k, v)
                    else:
                        probs, out = channel_tile(q, k, v, valid_rows[image])
                    probs_ref[image * tiles + tile] = probs
                    line.append(out)
                mixed.append(jnp.concatenate(line, axis=1))
            return jnp.concatenate(mixed, axis=0).astype(BF16)

        def attention_part_back(window, grad_mixed, mask_ref, qkv_ref, probs_ref, rear_refs):
            wide = [qkv_ref[part].astype(F32) for part in range(3)]
            grad = grad_mixed.astype(F32)
            found = [[], [], []]
            for image in range(images):
                lines = [[], [], []]
                for tile in range(tiles):
                    rows_at = slice(image * PADDED, (image + 1) * PADDED)
                    lanes_at = slice(tile * LANES, (tile + 1) * LANES)
                    q, k, v = (part[rows_at, lanes_at] for part in wide)
                    probs = probs_ref[image * tiles + tile]
                    if window:
                        parts = window_tile_back(q, k, v, probs, grad[rows_at, lanes_at])
                    else:
                        parts = channel_tile_back(
                            q, k, v, probs, grad[rows_at, lanes_at], mask_ref[rows_at, :]
                        )
                    for line, part in zip(lines, parts):
                        line.append(part)
                for part in range(3):
                    found[part].append(jnp.concatenate(lines[part], axis=1))
            packed = [jnp.concatenate(part, axis=0).astype(BF16) for part in found]
            for part in range(3):
                put_rear(rear_refs, half + part * heads_width, packed[part])
            return packed

        def mul_out(left, section, own_ref, oth_ref, out_ref):
            out_ref[:, :half] = mm(left, own_ref[section], 1, 0).astype(BF16)
            out_ref[:, half:] = mm(left, oth_ref[section], 1, 0).astype(BF16)

        def conv_into(out_ref, values, small_refs, section, keep):
            for col in range(0, width, LANES):
                taps = tap_rows(small_refs, section, col, False)
                out_ref[:, col : col + LANES] = conv_cols(values[:, col : col + LANES], taps, keep)

        def conv_back_into(out_ref, sums_ref, sums_at, grads, values, small_refs, section, keep):
            for col in range(0, width, LANES):
                lanes_at = slice(col, col + LANES)
                taps = tap_rows(small_refs, section, col, True)
                for t, total in enumerate(tap_sums(grads[:, lanes_at], values[:, lanes_at])):
                    sums_ref[sums_at + t : sums_at + t + 1, lanes_at] = total
                out_ref[:, lanes_at] = conv_cols(grads[:, lanes_at], taps, keep)

        window_probs = sds((images * tiles, PADDED, HEADS_TILE * PADDED))
        channel_probs = sds((images * tiles, LANES, LANES))
        full, full_low = sds((rows, width)), sds((rows, width), BF16)
        half_low = sds((rows, half), BF16)
        hid_low = sds((rows, hidden), BF16)
        qkv_low = sds((3, rows, heads_width), BF16)
        fore_attn, fore_mlp = (
            sds((rows, half + heads_width), BF16),
            sds((rows, half + hidden), BF16),
        )
        def cuts(total, count):
            tiles_all = total // LANES
            return [LANES * (-(-tiles_all * (at + 1) // count)) for at in range(count)]

        def rear_shapes(total, count):
            ends = cuts(total, count)
            return [sds((rows, e - b), BF16) for b, e in zip([0, *ends], ends)]

        def rear_ranges(refs, at, size):
            begin = 0
            for ref in refs:
                end = begin + ref.shape[1]
                low, high = max(begin, at), min(end, at + size)
                if low < high:
                    yield ref, low - begin, high - begin, low - at
                begin = end

        def put_rear(refs, at, values):
            for ref, low, high, source in rear_ranges(refs, at, values.shape[1]):
                ref[:, low:high] = values[:, source : source + high - low]

        def get_rear(refs, at, size):
            parts = [ref[:, low:high] for ref, low, high, _ in rear_ranges(refs, at, size)]
            return parts[0] if len(parts) == 1 else jnp.concatenate(parts, axis=1)

        rear_width_attn, rear_width_mlp = half + 3 * heads_width, half + hidden
        attn_flops = 2 * rows * (4 * width * heads_width)
        mlp_flops = 2 * rows * (2 * width * hidden)

        def first_body(
            tokens_a, tokens_b, small_a, small_b, wq_a, wq_b, wp_a, wp_b,
            x_ref, s_ref, n_own, fore_ref, qkv_ref, probs_ref, part_ref, keep_a, keep_b,
        ):
            keep_a[...], keep_b[...] = small_a[...], small_b[...]
            keep = column_mask(rows)
            stream = unpack(tokens_a, tokens_b)
            x_ref[...] = stream.astype(BF16)
            conv_into(s_ref, stream, (small_a, small_b), 0, keep)
            normed = to_normed(s_ref[...], (small_a, small_b), 0)
            put_both(n_own, fore_ref, normed)
            mixed = attention_part(True, 0, normed, None, wq_a, wq_b, qkv_ref, probs_ref)
            fore_ref[:, half:] = mixed
            mul_out(mixed, 0, wp_a, wp_b, part_ref)

        (x0, s1, n0_own, fore0, qkv0, probs0, part0, *small) = call(
            first_body, "attn_a",
            [*token_parts, *small, *wq, *wp],
            [full_low, full, half_low, fore_attn, qkv_low, window_probs, full_low]
            + [sds((26, half))] * 2,
            flops=attn_flops, hold=[cot_own],
        )
        far0 = over_ha(part0)
        fore0 = (fore0, over_wa(fore0))
        keep_a = [x0, n0_own, *fore0, qkv0, probs0, s1]

        def mlp_body(
            s_in, part_a, part_b, small_a, small_b, wu_a, wu_b, wd_a, wd_b,
            s_ref, n_own, fore_ref, slope_ref, part_ref,
        ):
            s_ref[...] = add_parts(s_in, part_a, part_b)
            normed = to_normed(s_ref[...], (small_a, small_b), 1)
            put_both(n_own, fore_ref, normed)
            pre = project_in(normed, wu_a[0], wu_b[0])
            below, bell = gelu_parts(pre)
            hid = (pre * below).astype(BF16)
            fore_ref[:, half:] = hid
            slope_ref[...] = below + pre * bell
            mul_out(hid, 0, wd_a, wd_b, part_ref)

        (s2, n1_own, fore1, slope1, part1) = call(
            mlp_body, "mlp_b",
            [s1, part0, far0, *small, *wu, *wd],
            [full, half_low, fore_mlp, sds((rows, hidden)), full_low],
            flops=mlp_flops, hold=[*keep_a, *wq, *wp, *cot_parts],
        )
        far1 = over_ha(part1)
        fore1 = (fore1, over_wa(fore1))
        keep_b = [s2, n1_own, *fore1, slope1]
        weights = [*wq, *wp, *wu, *wd]


        def cot_body(cot_a, cot_b, wd_a, wd_b, g_own, g_oth, dhid_ref):
            grad = unpack(cot_a, cot_b).astype(BF16)
            put_both(g_own, g_oth, grad)
            dhid_ref[...] = project_back(grad, wd_a[1], wd_b[1]).astype(BF16)

        g3_own, g3_oth, dhid3 = call(
            cot_body, "cot_d",
            [*cot_parts, *wd],
            [half_low, half_low, hid_low],
            flops=mlp_flops // 2, hold=[*keep_a, *keep_b, *small, *wq, *wp, *wu],
        )

        def channel_body(
            s_in, part_a, part_b, valid_ref, small_a, small_b,
            wq_a, wq_b, wp_a, wp_b,
            s_before, s_ref, n_own, fore_ref, qkv_ref, probs_ref, part_ref, mask_ref,
        ):
            keep = column_mask(rows)
            s_before[...] = jnp.where(keep, add_parts(s_in, part_a, part_b), 0.0)
            conv_into(s_ref, s_before, (small_a, small_b), 1, keep)
            normed = to_normed(s_ref[...], (small_a, small_b), 2)
            put_both(n_own, fore_ref, normed)
            one_image = placement(1, False).astype(F32)
            valid_rows = []
            for image in range(images):
                line = jnp.where(
                    here("wa") == 0,
                    valid_ref[image : image + 1, :],
                    valid_ref[images + image : images + image + 1, :],
                ).astype(F32)
                valid_rows.append(jnp.sum(one_image * line, axis=1, keepdims=True))
                mask_ref[image * PADDED : (image + 1) * PADDED, :] = valid_rows[image]
            mixed = attention_part(False, 1, normed, valid_rows, wq_a, wq_b, qkv_ref, probs_ref)
            fore_ref[:, half:] = mixed
            mul_out(mixed, 1, wp_a, wp_b, part_ref)

        (s3, s4, n2_own, fore2, qkv2, probs2, part2, mask) = call(
            channel_body, "attn_c",
            [s2, part1, far1, valid, *small, *wq, *wp],
            [full, full, half_low, fore_attn, qkv_low, channel_probs, full_low,
             sds((rows, 1))],
            flops=attn_flops,
            hold=[*keep_a, *keep_b, *wu, *wd, g3_own, g3_oth, dhid3],
        )
        far2 = over_ha(part2)
        fore2 = (fore2, over_wa(fore2))
        keep_c = [s3, s4, n2_own, *fore2, qkv2, probs2, mask]

        def last_body(
            s_in, part_a, part_b, small_a, small_b, dhid_ref, g_oth, wu_a, wu_b,
            s_ref, n_own, fore_ref, part_ref, *rear_refs,
        ):
            s_ref[...] = add_parts(s_in, part_a, part_b)
            normed = to_normed(s_ref[...], (small_a, small_b), 3)
            put_both(n_own, fore_ref, normed)
            pre = project_in(normed, wu_a[1], wu_b[1])
            below, bell = gelu_parts(pre)
            fore_ref[:, half:] = (pre * below).astype(BF16)
            dpre = (dhid_ref[...].astype(F32) * (below + pre * bell)).astype(BF16)
            put_rear(rear_refs, 0, g_oth[...])
            put_rear(rear_refs, half, dpre)
            part_ref[:, :half] = mm(dpre, wu_a[1], 1, 1).astype(BF16)
            part_ref[:, half:] = mm(dpre, wu_b[1], 1, 1).astype(BF16)

        (s5, n3_own, fore3, back3, *rear3) = call(
            last_body, "mlp_d",
            [s4, part2, far2, *small, dhid3, g3_oth, *wu],
            [full, half_low, fore_mlp, full_low, *rear_shapes(rear_width_mlp, 2)],
            flops=mlp_flops,
            hold=[*keep_a, *keep_b, *keep_c, g3_own, g3_oth, *wq, *wp, *wd],
        )
        far_back3 = over_ha(back3)
        fore3 = (fore3, over_wa(fore3))
        rear3 = both_rear(rear3, False)

        up_rows, down_rows = hidden // n_dev, half // n_dev
        qkv_rows, proj_rows = heads_width // n_dev, half // n_dev
        folds = hidden // half
        cut = n_dev // 2
        sum_rows = 32

        class Stream:
            def __init__(self, which, pieces):
                self.bits, self.which, self.pieces = orders[which], which, pieces
                self.chunk_rows = sum(piece_rows(piece) for piece in pieces)
                self.step, self.kept, self.got, self.at, self.final = 0, None, None, 0, None

        def piece_rows(piece):
            return {"up": up_rows, "q": qkv_rows, "k": qkv_rows, "v": qkv_rows}.get(
                piece, down_rows
            )

        downs = [("down", fold) for fold in range(folds)]

        def two_streams(parts, first, which):
            streams = [Stream(which, parts[:first]), Stream(which + 1, parts[first:])]
            return [stream for stream in streams if stream.pieces]

        def mlp_streams(first, which):
            return two_streams(["up", *downs], 1 + first, which)

        def attn_streams(first, which):
            return two_streams(["q", "k", "v", "proj"], first, which)

        def write_pieces(values, streams, scratches):
            for stream, scratch in zip(streams, scratches):
                at = 0
                for piece in stream.pieces:
                    size = piece_rows(piece)
                    for chunk in range(n_dev):
                        rows_at = slice(chunk * size, (chunk + 1) * size)
                        if isinstance(piece, tuple):
                            columns = slice(piece[1] * half, (piece[1] + 1) * half)
                            part = values["down"][rows_at, columns]
                        else:
                            part = values[piece][rows_at]
                        scratch[chunk, at : at + size, :] = part
                    at += size

        def both_sums(n_own, g_own, fore_a, fore_b, rear_a, rear_b):
            def left(at, size):
                return mm(get_rear(rear_a, at, size), n_own[...], 0, 0) + mm(
                    get_rear(rear_b, at, size), fore_b[:, :half], 0, 0
                )

            right = mm(g_own[...], fore_a[:, half:], 0, 0) + mm(
                get_rear(rear_b, 0, half), fore_b[:, half:], 0, 0
            )
            return left, right

        def write_mlp(*refs):
            left, right = both_sums(*refs)
            return {"up": left(half, hidden), "down": right}

        def write_attn(*refs):
            left, right = both_sums(*refs)
            values = {
                name: left(half + part * heads_width, heads_width)
                for part, name in enumerate(("q", "k", "v"))
            }
            return {**values, "proj": right}

        def make(name, write, streams, n_own, g_own, fore, rear, hold):
            outs = [sds((cut * s.chunk_rows, half), BF16) for s in streams for _ in range(2)]
            count = len(rear[0])

            def body(n_ref, g_ref, fore_a, fore_b, *refs):
                rear_a, rear_b, refs = refs[:count], refs[count : 2 * count], refs[2 * count :]
                rear_b = [other_core(ref) for ref in rear_b]
                out_refs, scratches = refs[: len(outs)], refs[len(outs) :]
                values = write(n_ref, g_ref, fore_a, fore_b, rear_a, rear_b)
                write_pieces(values, streams, scratches)
                for at, (stream, scratch) in enumerate(zip(streams, scratches)):
                    size = stream.chunk_rows
                    for place in range(n_dev):
                        chunk = scratch[chunk_at(place, stream.which)].astype(BF16)
                        to = (place % cut) * size
                        out_refs[2 * at + place // cut][to : to + size, :] = chunk

            results = call(
                body, name, [n_own, g_own, *fore, *rear[0], *rear[1]], outs, hold=hold,
                scratch=[pltpu.VMEM((n_dev, s.chunk_rows, half), F32) for s in streams],
            )
            for at, stream in enumerate(streams):
                stream.kept, stream.sent = results[2 * at], results[2 * at + 1]

        def send_first(streams):
            for stream in streams:
                stream.got, stream.step = over_dev(stream.sent, stream.bits[0]), 1

        def split_low(values):
            high = values.astype(BF16)
            return high, (values - high.astype(F32)).astype(BF16)

        def joined(ref, at):
            high = ref[at : at + sum_rows, :].astype(F32)
            return high + ref[at + sum_rows : at + 2 * sum_rows, :].astype(F32)

        def last_sum(stream, kept, got):
            return kept[...].astype(F32) + got[
                stream.at : stream.at + stream.chunk_rows, :
            ].astype(F32)

        def slot(name, fresh=(), moving=(), ending=(), sums=None, hold=()):
            ins, outs, sizes = [], [], {}
            plan_fresh, plan_moving = [], []

            def room(bit, size):
                at = sizes.get(bit, 0)
                sizes[bit] = at + size
                return at

            def place_of(array):
                for at, known in enumerate(ins):
                    if known is array:
                        return at
                ins.append(array)
                return len(ins) - 1

            for stream in fresh:
                size, bit = stream.sent.shape[0], stream.bits[0]
                plan_fresh.append((place_of(stream.sent), size, bit, room(bit, size)))
            for stream in moving:
                size = stream.kept.shape[0] // 2
                bit = stream.bits[stream.step]
                plan_moving.append(
                    (place_of(stream.kept), place_of(stream.got), stream.at, size,
                     len(outs), bit, room(bit, size))
                )
                outs.append(sds((size, half), BF16))
            plan_ending = []
            for stream in ending:
                plan_ending.append(
                    (stream, place_of(stream.kept), place_of(stream.got), len(outs))
                )
                outs.append(sds((stream.chunk_rows, half)))
            if sums is not None:
                total_at = place_of(sums[0])
                sums_got = None if sums[1] is None else place_of(sums[1])
                sums_room = room(sums[3], 2 * sum_rows)
                sums_out = len(outs)
                outs.append(sds((sum_rows, half)))
            bits_used = sorted(sizes)
            buffer_at = {bit: len(outs) + at for at, bit in enumerate(bits_used)}
            outs += [sds((sizes[bit], half), BF16) for bit in bits_used]

            def body(*refs):
                in_refs, out_refs = refs[: len(ins)], refs[len(ins) :]
                for sent_in, size, bit, at in plan_fresh:
                    out_refs[buffer_at[bit]][at : at + size, :] = in_refs[sent_in][...]
                for kept_in, got_in, got_row, size, kept_at, bit, at in plan_moving:
                    kept, got = in_refs[kept_in], in_refs[got_in]
                    out_refs[kept_at][...] = (
                        kept[:size, :].astype(F32) + got[got_row : got_row + size, :].astype(F32)
                    ).astype(BF16)
                    out_refs[buffer_at[bit]][at : at + size, :] = (
                        kept[size:, :].astype(F32)
                        + got[got_row + size : got_row + 2 * size, :].astype(F32)
                    ).astype(BF16)
                for stream, kept_in, got_in, out_at in plan_ending:
                    out_refs[out_at][...] = last_sum(stream, in_refs[kept_in], in_refs[got_in])
                if sums is not None:
                    total = in_refs[total_at][...]
                    if sums_got is not None:
                        total = total + joined(in_refs[sums_got], sums[2])
                    high, low = split_low(total)
                    out_refs[sums_out][...] = high.astype(F32) + low.astype(F32)
                    buffer = out_refs[buffer_at[sums[3]]]
                    buffer[sums_room : sums_room + sum_rows, :] = high
                    buffer[sums_room + sum_rows : sums_room + 2 * sum_rows, :] = low

            results = call(body, name, ins, outs, hold=hold)
            received = {bit: over_dev(results[buffer_at[bit]], bit) for bit in bits_used}
            for stream, (_, _, bit, at) in zip(fresh, plan_fresh):
                stream.got, stream.at, stream.step = received[bit], at, 1
            for stream, _, _, out_at in plan_ending:
                stream.final = results[out_at]
            for stream, (_, _, _, _, kept_at, bit, at) in zip(moving, plan_moving):
                stream.kept, stream.got, stream.at = results[kept_at], received[bit], at
                stream.step += 1
            if sums is not None:
                sums[:3] = results[sums_out], received[sums[3]], sums_room

        def ship(total, kept, sent):
            packed = mm(placement(images, True), total.astype(BF16), 1, 0).astype(BF16)
            kept[...] = packed[:, :half]
            sent[:rows_in, :] = packed[:, half:]

        shipped = [sds((rows_in, half), BF16)] * 2

        def fold(kept, received, stay, go):
            same = here("ha") == here("wa")
            theirs = received[:rows_in, :]
            stay[...] = jnp.where(same, kept[...], theirs)
            go[:rows_in, :] = jnp.where(same, theirs, kept[...])

        def join(stay, received, out_ref):
            out_ref[...] = stay[...].astype(F32) + received[:rows_in, :].astype(F32)

        def out_body(s_in, fore_ref, wd_a, wd_b, kept, sent):
            hid = fore_ref[:, half:]
            base = jnp.where(here("ha") == 0, s_in[...], 0.0)
            branch = jnp.concatenate([mm(hid, wd_a[1], 1, 0), mm(hid, wd_b[1], 1, 0)], axis=1)
            ship(base + branch, kept, sent)

        streams_d = mlp_streams(SPLIT_D, 0)
        make(
            "wgrad_d", write_mlp, streams_d, n3_own, g3_own, fore3, rear3,
            [*keep_a, *keep_b, *keep_c, *small, *weights, s5],
        )
        send_first(streams_d)

        def add_norm_back(grad, part_a, part_b, stream, gain, sums_ref):
            upstream = part_a[...].astype(F32) + part_b[...].astype(F32)
            units, inv_std = norm_stats(stream)
            sums_ref[0:1, :] = jnp.sum(upstream * units, axis=0, keepdims=True)
            sums_ref[1:2, :] = jnp.sum(upstream, axis=0, keepdims=True)
            return grad + norm_back(upstream, units, inv_std, gain)

        def qkv_back(packed, section, wq_a, wq_b):
            return [
                sum(mm(packed[part], ref[section, part], 1, 1) for part in range(3))
                for ref in (wq_a, wq_b)
            ]

        def channel_back_body(
            g_in_own, g_in_oth, part_a, part_b, s_in, small_a, small_b, mask_ref, qkv_ref,
            probs_ref, wp_a, wp_b, wq_a, wq_b,
            g_ref, g_own, part_ref, sums_ref, *rear_refs,
        ):
            grad = jnp.concatenate([g_in_own[...], g_in_oth[...]], axis=1).astype(F32)
            gain = gain_row((small_a, small_b), 3)
            grad = add_norm_back(grad, part_a, part_b, s_in[...], gain, sums_ref)
            g_ref[...] = grad
            low = grad.astype(BF16)
            g_own[...] = low[:, :half]
            put_rear(rear_refs, 0, low[:, half:])
            grad_mixed = project_back(low, wp_a[1], wp_b[1]).astype(BF16)
            packed = attention_part_back(
                False, grad_mixed, mask_ref, qkv_ref, probs_ref, rear_refs
            )
            own, oth = qkv_back(packed, 1, wq_a, wq_b)
            part_ref[:, :half] = own.astype(BF16)
            part_ref[:, half:] = oth.astype(BF16)

        late = [fore3[0], *wd, s5]
        (g2, g2_own, back2, sums3, *rear2) = call(
            channel_back_body, "back_c",
            [g3_own, g3_oth, back3, far_back3, s5, *small, mask, qkv2, probs2, *wp, *wq],
            [full, half_low, full_low, sds((2, width)), *rear_shapes(rear_width_attn, 1)],
            flops=attn_flops,
            hold=[*keep_a, *keep_b, s3, s4, n2_own, *fore2, *wu, *wd, fore3[0]],
        )
        far_back2 = over_ha(back2)
        rear2 = both_rear(rear2, False)
        streams_c = attn_streams(SPLIT_C, 2)
        kept_c = [*keep_a, *keep_b, s3, s4, *small, *weights, g2, *late, sums3]
        make("wgrad_c", write_attn, streams_c, n2_own, g2_own, fore2, rear2, kept_c)
        slot(
            "slot_c", fresh=streams_c, moving=streams_d, hold=[*kept_c, back2, far_back2],
        )

        def mlp_back_body(
            g_in, part_a, part_b, s_in, s_before, small_a, small_b, slope_ref,
            wd_a, wd_b, wu_a, wu_b, g_ref, g_own, part_ref, sums_ref, *rear_refs,
        ):
            keep = column_mask(rows)
            gain = gain_row((small_a, small_b), 2)
            grad = add_norm_back(g_in[...], part_a, part_b, s_in[...], gain, sums_ref)
            conv_back_into(g_ref, sums_ref, 2, grad, s_before[...], (small_a, small_b), 1, keep)
            low = g_ref[...].astype(BF16)
            g_own[...] = low[:, :half]
            put_rear(rear_refs, 0, low[:, half:])
            dhid = project_back(low, wd_a[0], wd_b[0]).astype(BF16).astype(F32)
            dpre = (dhid * slope_ref[...]).astype(BF16)
            put_rear(rear_refs, half, dpre)
            part_ref[:, :half] = mm(dpre, wu_a[0], 1, 1).astype(BF16)
            part_ref[:, half:] = mm(dpre, wu_b[0], 1, 1).astype(BF16)

        (g1, g1_own, back1, sums2, *rear1) = call(
            mlp_back_body, "back_b",
            [g2, back2, far_back2, s4, s3, *small, slope1, *wd, *wu],
            [full, half_low, full_low, sds((11, width)), *rear_shapes(rear_width_mlp, 2)],
            flops=mlp_flops,
            hold=[*keep_a, s2, n1_own, *fore1, *wq, *wp, fore3[0], s5, sums3],
        )
        far_back1 = over_ha(back1)
        rear1 = both_rear(rear1)
        streams_b = mlp_streams(SPLIT_B, 0)
        make(
            "wgrad_b", write_mlp, streams_b, n1_own, g1_own, fore1, rear1,
            [*keep_a, s2, *small, *wq, *wp, g1, *late, sums3, sums2],
        )
        send_first(streams_b)

        def window_back_body(
            g_in, part_a, part_b, s_in, small_a, small_b, qkv_ref, probs_ref, wp_a, wp_b,
            g_ref, g_own, sums_ref, *rear_refs,
        ):
            gain = gain_row((small_a, small_b), 1)
            grad = add_norm_back(g_in[...], part_a, part_b, s_in[...], gain, sums_ref)
            g_ref[...] = grad
            low = grad.astype(BF16)
            g_own[...] = low[:, :half]
            put_rear(rear_refs, 0, low[:, half:])
            grad_mixed = project_back(low, wp_a[0], wp_b[0]).astype(BF16)
            attention_part_back(True, grad_mixed, None, qkv_ref, probs_ref, rear_refs)

        (g0, g0_own, sums1, *rear0) = call(
            window_back_body, "back_a",
            [g1, back1, far_back1, s2, *small, qkv0, probs0, *wp],
            [full, half_low, sds((2, width)), *rear_shapes(rear_width_attn, 1)],
            flops=attn_flops, hold=[x0, n0_own, *fore0, s1, *wq, *late, sums3, sums2],
        )
        rear0 = both_rear(rear0)

        keep_0 = [g0, s1, x0, *small, *wq, sums1, sums2, sums3, *rear0[0]]
        streams_a = attn_streams(SPLIT_A, 0)
        make("wgrad_a", write_attn, streams_a, n0_own, g0_own, fore0, rear0, [*late, *keep_0])
        every = [*streams_d, *streams_c, *streams_b, *streams_a]
        slot(
            "slot_a", fresh=streams_a, moving=[*streams_d, *streams_c],
            hold=[*late, *keep_0],
        )

        sums_at = -(-rows_in // 16) * 16
        sums_half = sds((sum_rows, half))
        with_sums = sds((sums_at + 2 * sum_rows, half), BF16)

        def put_sums(ref, total):
            high, low = split_low(total)
            ref[sums_at : sums_at + sum_rows, :] = high
            ref[sums_at + sum_rows :, :] = low

        def first_back_body(
            g_in, s_in, x_ref, small_a, small_b, wq_a, wq_b, sums_one, sums_two, sums_three, *refs
        ):
            rear_refs, (kept, sent, sums_own, scratch, sums_ref) = refs[:-5], refs[-5:]
            keep = column_mask(rows)
            packed = [
                get_rear(rear_refs, half + part * heads_width, heads_width) for part in range(3)
            ]
            upstream = jnp.concatenate(qkv_back(packed, 0, wq_a, wq_b), axis=1)
            units, inv_std = norm_stats(s_in[...])
            sums_ref[0:1, :] = jnp.sum(upstream * units, axis=0, keepdims=True)
            sums_ref[1:2, :] = jnp.sum(upstream, axis=0, keepdims=True)
            grad = jnp.where(here("ha") == 0, g_in[...], 0.0)
            grad = grad + norm_back(upstream, units, inv_std, gain_row((small_a, small_b), 0))
            conv_back_into(
                scratch, sums_ref, 2, grad, x_ref[...].astype(F32), (small_a, small_b), 0, keep
            )
            ship(scratch[...], kept, sent)
            sums_ref[11:13, :] = 0.5 * sums_one[...]
            sums_ref[13:24, :] = 0.5 * sums_two[...]
            sums_ref[24:26, :] = 0.5 * sums_three[...]
            sums_ref[26:, :] = jnp.zeros((sum_rows - 26, width), F32)
            sums_own[...] = sums_ref[:, :half]
            put_sums(sent, sums_ref[:, half:])

        token_kept, token_sent, sums_own = call(
            first_back_body, "back_0",
            [g0, s1, x0, *small, *wq, sums1, sums2, sums3, *rear0[0]],
            [shipped[0], with_sums, sums_half],
            scratch=[pltpu.VMEM((rows, width), F32), pltpu.VMEM((sum_rows, width), F32)],
            flops=attn_flops * 3 // 4, hold=late,
        )

        def fold_tokens(kept, both, sums_a, stay, go, sums_ref):
            received = other_core(both)
            fold(kept, received, stay, go)
            total = sums_a[...] + joined(received, sums_at)
            put_sums(go, total)
            sums_ref[...] = joined(go, sums_at)

        token_stay, token_go, sums_chip = call(
            fold_tokens, "fold_tokens",
            [token_kept, lax.all_gather(token_sent, "wa"), sums_own],
            [shipped[0], with_sums, sums_half], hold=late,
        )
        token_got = over_ha(token_go)

        def join_tokens(stay, received, sums_chip, out_ref, sums_ref):
            join(stay, received, out_ref)
            sums_ref[...] = sums_chip[...] + joined(received, sums_at)

        owned = sds((rows_in, half))
        grad_tokens, sums_ha = call(
            join_tokens, "join_tokens", [token_stay, token_got, sums_chip], [owned, sums_half],
            hold=late,
        )
        left_bits = list(range(bits))
        sums = [sums_ha, None, 0, left_bits.pop(0)]
        slot("sums_x", sums=sums, hold=late)
        out_kept, out_sent = call(
            out_body, "out_d", [s5, fore3[0], *wd], shipped, flops=mlp_flops // 2
        )
        out_both = lax.all_gather(out_sent, "wa")

        def hop():
            if not left_bits:
                return None
            sums[3] = left_bits.pop(0)
            return sums

        turn = 0
        while left_bits or any(stream.step < bits for stream in every):
            turn += 1
            arrived = [s for s in every if s.step == bits and s.final is None]
            first = [*streams_b, streams_c[1]] if turn > 1 else streams_b
            slot(f"slot_b{turn}", moving=[s for s in first if s.step < bits])
            second = [s for s in every if s.step < bits and s not in (*streams_b, streams_c[1])]
            slot(
                f"slot_ac{turn}", moving=second, ending=arrived, sums=hop() if turn == 1 else None
            )
            if turn > 1 and left_bits:
                slot(f"sums_{turn}", sums=hop())
            if turn == 1:
                out_stay, out_go = call(
                    lambda kept, both, *refs: fold(kept, other_core(both), *refs),
                    "fold_out", [out_kept, out_both], shipped,
                )
                out_got = over_ha(out_go)
        output = call(join, "join_out", [out_stay, out_got], [owned])[0]

        def finish_body(*refs):
            (up, down, qkv, proj, taps_ref, gain_ref, shift_ref) = refs[-7:]
            at = iter(refs)
            total = next(at)[...] + joined(next(at), sums[2])
            for branch, row in enumerate((0, 11, 13, 24)):
                gain_ref[branch : branch + 1, :] = total[row : row + 1]
                shift_ref[branch : branch + 1, :] = total[row + 1 : row + 2]
            for section, row in enumerate((2, 15)):
                for t in range(9):
                    taps_ref[t, section : section + 1, :] = total[row + t : row + t + 1]

            def finished(stream):
                if stream.final is not None:
                    return next(at)[...]
                return last_sum(stream, next(at), next(at))

            for section, streams in enumerate(
                ((*streams_a, *streams_b), (*streams_c, *streams_d))
            ):
                for stream in streams:
                    values, row = finished(stream), 0
                    for piece in stream.pieces:
                        part = values[row : row + piece_rows(piece)]
                        row += piece_rows(piece)
                        if piece == "up":
                            up[section] = part
                        elif piece == "proj":
                            proj[section] = part
                        elif isinstance(piece, tuple):
                            down[section, :, piece[1] * half : (piece[1] + 1) * half] = part
                        else:
                            qkv[section, ("q", "k", "v").index(piece)] = part

        ends = []
        for stream in (*streams_a, *streams_b, *streams_c, *streams_d):
            ends += [stream.kept, stream.got] if stream.final is None else [stream.final]
        up, down, qkv, proj, grad_taps, grad_gain, grad_shift = call(
            finish_body, "finish", [*sums[:2], *ends],
            [sds((2, up_rows, half)), sds((2, down_rows, hidden)), sds((2, 3, qkv_rows, half)),
             sds((2, proj_rows, half)), sds((9, 2, half)), sds((4, half)), sds((4, half))],
        )
        grad_taps = jnp.transpose(grad_taps, (1, 0, 2))
        grad_qkv = jnp.transpose(qkv, (0, 3, 1, 2))
        grad_proj, grad_up, grad_down = (
            jnp.transpose(values, (0, 2, 1)) for values in (proj, up, down)
        )
        return (
            output,
            grad_tokens,
            grad_taps,
            grad_gain,
            grad_shift,
            grad_qkv,
            grad_proj,
            grad_up,
            grad_down,
        )

    placed = (
        P(("dev", "ha"), "wa"),
        P(("dev", "ha"), "wa"),
        P(None, None, "wa"),
        P(None, "wa"),
        P(None, "wa"),
        P(None, "wa", None, "ha"),
        P(None, "ha", "wa"),
        P(None, "wa", "ha"),
        P(None, "ha", "wa"),
        P("dev", None),
    )
    return jax.shard_map(
        on_device,
        mesh=mesh,
        in_specs=placed,
        out_specs=(
            P(("dev", "ha"), "wa"),
            P(("dev", "ha"), "wa"),
            P(None, None, "wa"),
            P(None, "wa"),
            P(None, "wa"),
            P(None, "wa", None, ("ha", "dev")),
            P(None, "ha", ("wa", "dev")),
            P(None, "wa", ("ha", "dev")),
            P(None, "ha", ("wa", "dev")),
        ),
        check_vma=False,
    )
```

```python
from functools import partial

import jax
import jax.numpy as jnp
import numpy as np
from jax import lax
from jax.experimental import pallas as pl
from jax.experimental.pallas import tpu as pltpu
from jax.sharding import PartitionSpec as P

WIN = 7
GRID_COLS = 8
PATCHES = 49
PADDED = WIN * GRID_COLS
HEAD_DIM = 32
LANES = 128
HEADS_TILE = LANES // HEAD_DIM
EPS = 1e-05
NEG = -1e30
SPLIT_D, SPLIT_C, SPLIT_B, SPLIT_A = 0, 2, 0, 4
BF16 = jnp.bfloat16
F32 = jnp.float32
VMEM_LIMIT = 16 * 2**20
TIMES = {"pack_small": 5.0, "choose": 5.0}


def mm(left, right, left_dim, right_dim):
    return lax.dot_general(
        left, right, (((left_dim,), (right_dim,)), ((), ())), preferred_element_type=F32
    )


class Order:
    def __init__(self):
        self.last = None


def kernel_call(
    body, name, ins, outs, order, scratch=(), flops=0, hold=(), reuse=None, carry=None
):
    reuse = reuse or {}
    arrays = list(ins) + list(hold) + ([] if order.last is None else [order.last])
    first_reused = len(arrays)
    aliases = {first_reused + at: out for at, out in enumerate(reuse)}
    arrays += list(reuse.values())
    outs = list(outs) + [sds((8, LANES))]

    def wrapped(*refs):
        out_refs = refs[len(arrays) : len(arrays) + len(outs)]
        for at, out in aliases.items():
            carry(refs[at], out_refs[out])
        body(*refs[: len(ins)], *out_refs[:-1], *refs[len(arrays) + len(outs) :])
        out_refs[-1][...] = jnp.zeros_like(out_refs[-1])

    *results, order.last = pl.pallas_call(
        wrapped,
        in_specs=[pl.BlockSpec(memory_space=pltpu.VMEM)] * len(arrays),
        out_specs=[pl.BlockSpec(memory_space=pltpu.VMEM)] * len(outs),
        out_shape=outs,
        scratch_shapes=list(scratch),
        input_output_aliases=aliases,
        compiler_params=pltpu.CompilerParams(vmem_limit_bytes=VMEM_LIMIT),
        cost_estimate=pl.CostEstimate(
            flops=int(TIMES.get(name, 0) * 1.15e9), bytes_accessed=0, transcendentals=0
        ),
        name=name,
    )(*arrays)
    return results


def sds(shape, dtype=F32):
    return jax.ShapeDtypeStruct(shape, dtype)


def column_mask(rows):
    return (lax.broadcasted_iota(jnp.int32, (rows, 1), 0) % GRID_COLS) < WIN


def placement(images, transposed, begin=0, count=None):
    padded, plain = count or images * PADDED, images * PATCHES
    shape = (plain, padded) if transposed else (padded, plain)
    at = lax.broadcasted_iota(jnp.int32, shape, 1 if transposed else 0) + begin
    image = sum((at >= i * PADDED).astype(jnp.int32) for i in range(1, images))
    inside = at - image * PADDED
    source = image * PATCHES + (inside >> 3) * WIN + (inside & 7)
    other = lax.broadcasted_iota(jnp.int32, shape, 0 if transposed else 1)
    return (((inside & 7) < WIN) & (source == other)).astype(F32).astype(BF16)


def side_shifts(values):
    rows = values.shape[0]
    return (pltpu.roll(values, 1, 0), values, pltpu.roll(values, rows - 1, 0))


def as_grid(values):
    return values.reshape(-1, WIN, GRID_COLS, values.shape[-1])


def move_rows(values, step):
    grid = as_grid(values)
    zeros = jnp.zeros_like(grid[:, :1])
    if step > 0:
        moved = jnp.concatenate([zeros, grid[:, :-1]], axis=1)
    else:
        moved = jnp.concatenate([grid[:, 1:], zeros], axis=1)
    return moved.reshape(values.shape)


def conv_cols(values, taps, keep):
    shifted = side_shifts(values)
    line = [
        sum(shifted[col] * taps[3 * row + col] for col in range(3)) for row in range(3)
    ]
    total = values + line[1] + move_rows(line[0], 1) + move_rows(line[2], -1)
    return jnp.where(keep, total, 0.0)


def tap_sums(grads, values):
    shifted = side_shifts(values)
    grad_grid = as_grid(grads)
    sums = []
    for row in range(3):
        for col in range(3):
            moved = as_grid(shifted[col])
            if row == 0:
                prod = grad_grid[:, 1:] * moved[:, :-1]
            elif row == 1:
                prod = grad_grid * moved
            else:
                prod = grad_grid[:, :-1] * moved[:, 1:]
            flat = prod.reshape(-1, GRID_COLS, prod.shape[-1])
            sums.append(jnp.sum(jnp.sum(flat, axis=0), axis=0, keepdims=True))
    return sums


def norm_stats(stream):
    width = stream.shape[1]
    center = jnp.sum(stream, axis=1, keepdims=True) * (1.0 / width)
    moved = stream - center
    inv_std = lax.rsqrt(jnp.sum(moved * moved, axis=1, keepdims=True) * (1.0 / width) + EPS)
    return moved * inv_std, inv_std


def norm_back(upstream, units, inv_std, gain):
    width = upstream.shape[1]
    scaled = upstream * gain
    first = jnp.sum(scaled, axis=1, keepdims=True) * (1.0 / width)
    second = jnp.sum(scaled * units, axis=1, keepdims=True) * (1.0 / width)
    return inv_std * (scaled - first - units * second)


def gelu_parts(values):
    below = 0.5 + 0.5 * lax.erf(values * float(0.5**0.5))
    bell = jnp.exp2(values * values * float(-0.5 * np.log2(np.e)))
    return below, bell * float(1.0 / np.sqrt(2.0 * np.pi))


def head_mask(index):
    return (lax.broadcasted_iota(jnp.int32, (1, LANES), 1) // HEAD_DIM) == index


def spread_heads(tile):
    return jnp.concatenate(
        [jnp.where(head_mask(j), tile, 0.0) for j in range(HEADS_TILE)], axis=0
    ).astype(BF16)


def gather_heads(stacked):
    rows = stacked.shape[0] // HEADS_TILE
    total = jnp.where(head_mask(0), stacked[:rows], 0.0)
    for j in range(1, HEADS_TILE):
        total = jnp.where(head_mask(j), stacked[j * rows : (j + 1) * rows], total)
    return total


def softmax_rows(scores):
    top = jnp.max(scores, axis=0, keepdims=True)
    weights = jnp.exp(scores - top)
    return weights * (1.0 / jnp.sum(weights, axis=0, keepdims=True))


SCALE = HEAD_DIM**-0.5


def low(tiles):
    return [tile.astype(BF16) for tile in tiles]


def minus_row_sums(probs, grads):
    return [
        (p * (g - jnp.sum(g * p, axis=0, keepdims=True))).astype(BF16)
        for p, g in zip(probs, grads)
    ]


def window_tiles(queries, keys, values):
    keys_ok = column_mask(PADDED)
    scores = [
        mm(k, spread_heads(q), 1, 1) * SCALE for q, k in zip(queries, low(keys))
    ]
    probs = [softmax_rows(jnp.where(keys_ok, score, NEG)) for score in scores]
    mixed = [mm(p, v, 0, 0) for p, v in zip(low(probs), low(values))]
    return probs, [gather_heads(tile) for tile in mixed]


def window_tiles_back(queries, keys, values, probs, grads):
    q_big, g_big = ([spread_heads(tile) for tile in tiles] for tiles in (queries, grads))
    grad_probs = [mm(v, g, 1, 1) for v, g in zip(low(values), g_big)]
    grad_v = [mm(p, g, 1, 0) for p, g in zip(low(probs), g_big)]
    grad_scores = minus_row_sums(probs, grad_probs)
    grad_k = [mm(d, q, 1, 0) * SCALE for d, q in zip(grad_scores, q_big)]
    grad_q = [mm(d, k, 0, 0) for d, k in zip(grad_scores, low(keys))]
    return [gather_heads(tile) * SCALE for tile in grad_q], grad_k, grad_v


def same_head():
    first = lax.broadcasted_iota(jnp.int32, (LANES, LANES), 0) // HEAD_DIM
    second = lax.broadcasted_iota(jnp.int32, (LANES, LANES), 1) // HEAD_DIM
    return first == second


def channel_tiles(queries, keys, values, masks):
    own_head = same_head()
    masked = low([q * mask for q, mask in zip(queries, masks)])
    scores = [mm(k, q, 0, 0) * SCALE for q, k in zip(masked, low(keys))]
    probs = [softmax_rows(jnp.where(own_head, score, NEG)) for score in scores]
    return probs, [mm(v, p, 1, 0) for p, v in zip(low(probs), low(values))]


def channel_tiles_back(queries, keys, values, probs, grads, masks):
    masked = low([q * mask for q, mask in zip(queries, masks)])
    grads = low(grads)
    grad_probs = [mm(v, g, 0, 0) for v, g in zip(low(values), grads)]
    grad_v = [mm(g, p, 1, 1) for g, p in zip(grads, low(probs))]
    grad_scores = minus_row_sums(probs, grad_probs)
    grad_q = [mm(k, d, 1, 0) * SCALE * m for k, d, m in zip(low(keys), grad_scores, masks)]
    grad_k = [mm(q, d, 1, 1) * SCALE for q, d in zip(masked, grad_scores)]
    return grad_q, grad_k, grad_v


def cut_tiles(values, images, tiles):
    return [
        values[image * PADDED : (image + 1) * PADDED, tile * LANES : (tile + 1) * LANES]
        for image in range(images)
        for tile in range(tiles)
    ]


def paste_tiles(parts, images, tiles):
    lines = [
        jnp.concatenate(parts[image * tiles : (image + 1) * tiles], axis=1)
        for image in range(images)
    ]
    return jnp.concatenate(lines, axis=0).astype(BF16)


def solution(mesh):
    n_dev = mesh.shape["dev"]
    bits = n_dev.bit_length() - 1
    assert n_dev == 1 << bits and mesh.shape["ha"] == 2 and mesh.shape["wa"] == 2

    swap = [(0, 1), (1, 0)]

    def over_ha(values):
        return lax.ppermute(values, "ha", swap)

    def over_wa(values):
        return lax.ppermute(values, "wa", swap)

    def over_dev(values, bit):
        return lax.ppermute(values, "dev", [(i, i ^ (1 << bit)) for i in range(n_dev)])

    def on_device(
        tokens, cotangent, conv_taps, norm_gain, norm_shift, w_qkv, w_proj, w_up, w_down, valid
    ):
        rows_in, half = tokens.shape
        images = rows_in // PATCHES
        rows = images * PADDED
        width = 2 * half
        heads_width = w_qkv.shape[3]
        hidden = w_up.shape[2]
        tiles = heads_width // LANES
        assert heads_width == half
        rest = list(range(3, bits))
        orders = [[0, 1, 2, *rest], [1, 0, 2, *rest], [0, 2, 1, *rest], [1, 2, 0, *rest]]

        def here(name):
            return lax.axis_index(name)

        def chunk_at(place, which):
            found = 0
            for step, bit in enumerate(orders[which]):
                found |= ((place >> (bits - 1 - step)) & 1) << bit
            return found ^ here("dev")

        order = Order()
        call = partial(kernel_call, order=order)

        def later(values, event):
            return lax.optimization_barrier((values, event))[0]

        def pack_small(taps_ref, gain_ref, shift_ref, out_ref):
            for section in range(2):
                for t in range(9):
                    at = 9 * section + t
                    out_ref[at : at + 1, :] = taps_ref[t, section : section + 1, :]
            out_ref[18:22, :] = gain_ref[...]
            out_ref[22:26, :] = shift_ref[...]

        def choose(mine, received, own, *others):
            same = here("ha") == here("wa")
            own[...] = jnp.where(same, mine[...], received[...])
            other, at = jnp.where(same, received[...], mine[...]), 0
            for ref in others:
                ref[...] = other[:, at : at + ref.shape[1]]
                at += ref.shape[1]

        wq_own = jnp.transpose(w_qkv, (0, 2, 1, 3))
        wq, wp = (wq_own, over_wa(wq_own)), (w_proj, over_wa(w_proj))
        tokens_in, cot_in = over_ha(tokens), over_ha(cotangent)
        small_own = call(
            pack_small, "pack_small",
            [jnp.transpose(conv_taps, (1, 0, 2)), norm_gain, norm_shift], [sds((26, half))],
            hold=[tokens],
        )[0]
        small = (small_own, over_wa(small_own))
        chosen = [sds((rows_in, columns), BF16) for columns in (half, LANES, half - LANES)]
        tokens_own, *tokens_oth = call(
            choose, "choose", [tokens, tokens_in], chosen, hold=[wq[1], wp[1], small_own]
        )
        token_parts = (tokens_own, *[over_wa(values) for values in tokens_oth])

        def arrive(out_ref):
            out_ref[...] = jnp.zeros_like(out_ref)

        arrived = call(
            arrive, "arrive", [], [sds((8, LANES))],
            hold=[*token_parts, small[1], cot_in, small_own, wq[1], wp[1]],
        )[0]
        wu, wd = ((values, over_wa(later(values, arrived))) for values in (w_up, w_down))

        def unpack(parts, begin=0, count=None):
            values = jnp.concatenate([part[...] for part in parts], axis=1)
            return mm(placement(images, False, begin, count), values, 1, 0)

        def gain_row(refs, branch):
            return jnp.concatenate([ref[18 + branch : 19 + branch, :] for ref in refs], axis=1)

        def shift_row(refs, branch):
            return jnp.concatenate([ref[22 + branch : 23 + branch, :] for ref in refs], axis=1)

        def tap_rows(small_refs, section, col, flipped):
            ref = small_refs[col // half]
            at = col % half
            found = [
                ref[9 * section + t : 9 * section + t + 1, at : at + LANES] for t in range(9)
            ]
            return found[::-1] if flipped else found

        def project_in(normed, first, second):
            return mm(normed[:, :half], first, 1, 0) + mm(normed[:, half:], second, 1, 0)

        def project_back(values, first, second):
            return mm(values[:, :half], first, 1, 1) + mm(values[:, half:], second, 1, 1)

        def to_normed(stream, small_refs, branch):
            units, _ = norm_stats(stream)
            return (units * gain_row(small_refs, branch) + shift_row(small_refs, branch)).astype(
                BF16
            )

        def both_rear(pieces, gather=True):
            pieces = list(pieces)
            if gather:
                return pieces, [lax.all_gather(piece, "wa") for piece in pieces]
            return pieces, [over_wa(piece) for piece in pieces]

        def other_core(ref):
            return ref.at[1 - here("wa")] if len(ref.shape) == 3 else ref

        def put_both(own_ref, oth_ref, values):
            own_ref[...] = values[:, :half]
            oth_ref[:, :half] = values[:, half:]

        def add_parts(stream, part_a, part_b):
            return stream + part_a[...].astype(F32) + part_b[...].astype(F32)

        def attention_part(
            window, section, normed, valid_rows, wq_a, wq_b, qkv_ref, probs_ref, first_image
        ):
            count = normed.shape[0] // PADDED
            packed = [
                project_in(normed, wq_a[section, part], wq_b[section, part]).astype(BF16)
                for part in range(3)
            ]
            begin = first_image * PADDED
            for part in range(3):
                qkv_ref[part, begin : begin + count * PADDED, :] = packed[part]
            q, k, v = (cut_tiles(part.astype(F32), count, tiles) for part in packed)
            if window:
                probs, mixed = window_tiles(q, k, v)
            else:
                masks = [mask for mask in valid_rows for _ in range(tiles)]
                probs, mixed = channel_tiles(q, k, v, masks)
            for at, tile in enumerate(probs):
                probs_ref[first_image * tiles + at] = tile
            return paste_tiles(mixed, count, tiles)

        def attention_part_back(window, grad_mixed, mask_ref, qkv_ref, probs_ref, rear_refs):
            q, k, v = (
                cut_tiles(qkv_ref[part].astype(F32), images, tiles) for part in range(3)
            )
            grads = cut_tiles(grad_mixed.astype(F32), images, tiles)
            probs = [probs_ref[at] for at in range(images * tiles)]
            if window:
                found = window_tiles_back(q, k, v, probs, grads)
            else:
                masks = [
                    mask_ref[image * PADDED : (image + 1) * PADDED, :]
                    for image in range(images)
                    for _ in range(tiles)
                ]
                found = channel_tiles_back(q, k, v, probs, grads, masks)
            packed = [paste_tiles(part, images, tiles) for part in found]
            for part in range(3):
                put_rear(rear_refs, half + part * heads_width, packed[part])
            return packed

        def mul_out(left, section, own_ref, oth_ref, out_ref):
            out_ref[:, :half] = mm(left, own_ref[section], 1, 0).astype(BF16)
            out_ref[:, half:] = mm(left, oth_ref[section], 1, 0).astype(BF16)

        def conv_into(out_ref, rows_at, values, small_refs, section, keep):
            for col in range(0, width, LANES):
                taps = tap_rows(small_refs, section, col, False)
                out_ref[rows_at, col : col + LANES] = conv_cols(
                    values[:, col : col + LANES], taps, keep
                )

        def conv_back_into(out_ref, sums_ref, sums_at, grads, values, small_refs, section, keep):
            for col in range(0, width, LANES):
                lanes_at = slice(col, col + LANES)
                taps = tap_rows(small_refs, section, col, True)
                for t, total in enumerate(tap_sums(grads[:, lanes_at], values[:, lanes_at])):
                    sums_ref[sums_at + t : sums_at + t + 1, lanes_at] = total
                out_ref[:, lanes_at] = conv_cols(grads[:, lanes_at], taps, keep)

        window_probs = sds((images * tiles, PADDED, HEADS_TILE * PADDED))
        channel_probs = sds((images * tiles, LANES, LANES))
        full, full_low = sds((rows, width)), sds((rows, width), BF16)
        half_low = sds((rows, half), BF16)
        hid_low = sds((rows, hidden), BF16)
        qkv_low = sds((3, rows, heads_width), BF16)
        fore_attn = sds((rows, half + heads_width), BF16)
        def cuts(total, count):
            tiles_all = total // LANES
            return [LANES * (-(-tiles_all * (at + 1) // count)) for at in range(count)]

        def rear_shapes(total, count):
            ends = cuts(total, count)
            return [sds((rows, e - b), BF16) for b, e in zip([0, *ends], ends)]

        def rear_ranges(refs, at, size):
            begin = 0
            for ref in refs:
                end = begin + ref.shape[1]
                low, high = max(begin, at), min(end, at + size)
                if low < high:
                    yield ref, low - begin, high - begin, low - at
                begin = end

        def put_rear(refs, at, values, span=slice(None)):
            for ref, low, high, source in rear_ranges(refs, at, values.shape[1]):
                ref[span, low:high] = values[:, source : source + high - low]

        def get_rear(refs, at, size):
            parts = [ref[:, low:high] for ref, low, high, _ in rear_ranges(refs, at, size)]
            return parts[0] if len(parts) == 1 else jnp.concatenate(parts, axis=1)

        rear_width_attn, rear_width_mlp = half + 3 * heads_width, half + hidden
        fore_mlp = sds((rows, rear_width_mlp), BF16)
        attn_flops = 2 * rows * (4 * width * heads_width)
        mlp_flops = 2 * rows * (2 * width * hidden)

        split = (images + 1) // 2
        chunks = [(0, split), (split, images)] if split < images else [(0, images)]
        spans = [slice(begin * PADDED, end * PADDED) for begin, end in chunks]

        def chunk_rows(span):
            return span.stop - span.start

        def part_shape(span):
            return sds((chunk_rows(span), width), BF16)

        def put_normed(own_ref, fore_refs, span, normed):
            own_ref[span, :] = normed[:, :half]
            put_rear(fore_refs, 0, normed[:, half:], span)

        def first_body(chunk, span):
            def body(
                tokens_a, tokens_b, tokens_c, small_a, small_b, wq_a, wq_b, wp_a, wp_b,
                x_ref, s_ref, n_own, fore_ref, qkv_ref, probs_ref, part_ref, *copies,
            ):
                if copies:
                    copies[0][...], copies[1][...] = small_a[...], small_b[...]
                keep = column_mask(chunk_rows(span))
                stream = unpack((tokens_a, tokens_b, tokens_c), span.start, chunk_rows(span))
                x_ref[span, :] = stream.astype(BF16)
                conv_into(s_ref, span, stream, (small_a, small_b), 0, keep)
                normed = to_normed(s_ref[span, :], (small_a, small_b), 0)
                put_normed(n_own, [fore_ref], span, normed)
                mixed = attention_part(
                    True, 0, normed, None, wq_a, wq_b, qkv_ref, probs_ref, chunk[0]
                )
                fore_ref[span, half:] = mixed
                mul_out(mixed, 0, wp_a, wp_b, part_ref)

            return body

        def carry_spans(upto):
            def carry(old, new):
                for chunk, span in zip(chunks[:upto], spans[:upto]):
                    if old.shape[0] == rows:
                        new[span, :] = old[span, :]
                    elif old.shape[1] == rows:
                        new[:, span, :] = old[:, span, :]
                    else:
                        per_image = old.shape[0] // images
                        held = slice(chunk[0] * per_image, chunk[1] * per_image)
                        new[held] = old[held]

            return carry

        def in_chunks(name, make_body, ins, shapes, hold, extra=(), between=None):
            arrays, parts, fars, more = None, [], [], []
            for at, (chunk, span) in enumerate(zip(chunks, spans)):
                results = call(
                    make_body(chunk, span), f"{name}{at}", ins(at),
                    [*shapes, part_shape(span), *(extra if at == 0 else ())],
                    hold=[*hold, *more, *parts],
                    reuse=None if arrays is None else dict(enumerate(arrays)),
                    carry=carry_spans(at),
                )
                arrays, part = results[: len(shapes)], results[len(shapes)]
                more = more or results[len(shapes) + 1 :]
                parts.append(part)
                fars.append(over_ha(part))
                if at == 0 and between is not None:
                    between(arrays, more)
            return arrays, parts, fars, more

        small_in, cot_parts = small, []

        def choose_cot(arrays, more):
            own, *others = call(
                choose, "choose_cot", [cotangent, cot_in], chosen,
                hold=[*arrays, *more, *wq, *wp],
            )
            cot_parts.extend([own, *others])

        (x0, s1, n0_own, fore0, qkv0, probs0), part0, far0, small = in_chunks(
            "attn_a", first_body, lambda at: [*token_parts, *small_in, *wq, *wp],
            [full_low, full, half_low, fore_attn, qkv_low, window_probs], [cot_in, arrived],
            [sds((26, half))] * 2, choose_cot,
        )
        keep_a = [x0, n0_own, fore0, qkv0, probs0, s1]

        def mlp_body(chunk, span):
            def body(
                s_in, part_a, part_b, small_a, small_b, wu_a, wu_b, wd_a, wd_b,
                s_ref, n_own, slope_ref, *refs,
            ):
                *fore_refs, part_ref = refs
                s_ref[span, :] = add_parts(s_in[span, :], part_a, part_b)
                normed = to_normed(s_ref[span, :], (small_a, small_b), 1)
                put_normed(n_own, fore_refs, span, normed)
                pre = project_in(normed, wu_a[0], wu_b[0])
                below, bell = gelu_parts(pre)
                hid = (pre * below).astype(BF16)
                put_rear(fore_refs, half, hid, span)
                slope_ref[span, :] = below + pre * bell
                mul_out(hid, 0, wd_a, wd_b, part_ref)

            return body

        (s2, n1_own, slope1, *fore1), part1, far1, _ = in_chunks(
            "mlp_b", mlp_body, lambda at: [s1, part0[at], far0[at], *small, *wu, *wd],
            [full, half_low, sds((rows, hidden)), half_low, hid_low],
            [*keep_a, *wq, *wp, *cot_parts],
        )
        n1_got = over_wa(fore1[0])
        cot_parts[1:] = [over_wa(later(values, part1[0])) for values in cot_parts[1:]]
        keep_b = [s2, n1_own, *fore1, slope1, n1_got]
        weights = [*wq, *wp, *wu, *wd]

        def channel_body(chunk, span):
            def body(
                s_in, part_a, part_b, valid_ref, small_a, small_b, wq_a, wq_b, wp_a, wp_b,
                s_before, s_ref, n_own, qkv_ref, probs_ref, mask_ref, *refs,
            ):
                *fore_refs, part_ref = refs
                keep = column_mask(chunk_rows(span))
                stream = jnp.where(keep, add_parts(s_in[span, :], part_a, part_b), 0.0)
                s_before[span, :] = stream
                conv_into(s_ref, span, stream, (small_a, small_b), 1, keep)
                normed = to_normed(s_ref[span, :], (small_a, small_b), 2)
                put_normed(n_own, fore_refs, span, normed)
                one_image = placement(1, False).astype(F32)
                valid_rows = []
                for image in range(*chunk):
                    line = jnp.where(
                        here("wa") == 0,
                        valid_ref[image : image + 1, :],
                        valid_ref[images + image : images + image + 1, :],
                    ).astype(F32)
                    valid_rows.append(jnp.sum(one_image * line, axis=1, keepdims=True))
                    mask_ref[image * PADDED : (image + 1) * PADDED, :] = valid_rows[-1]
                mixed = attention_part(
                    False, 1, normed, valid_rows, wq_a, wq_b, qkv_ref, probs_ref, chunk[0]
                )
                put_rear(fore_refs, half, mixed, span)
                mul_out(mixed, 1, wp_a, wp_b, part_ref)

            return body

        (s3, s4, n2_own, qkv2, probs2, mask, *fore2), part2, far2, _ = in_chunks(
            "attn_c", channel_body,
            lambda at: [s2, part1[at], far1[at], valid, *small, *wq, *wp],
            [full, full, half_low, qkv_low, channel_probs, sds((rows, 1)), half_low, half_low],
            [*keep_a, *keep_b, *wu, *wd, *cot_parts],
        )
        fore2 = both_rear(fore2, False)
        keep_c = [s3, s4, n2_own, *fore2[0], qkv2, probs2, mask]

        def cot_body(cot_a, cot_b, cot_c, wd_a, wd_b, g_own, g_oth, dhid_ref):
            grad = unpack((cot_a, cot_b, cot_c)).astype(BF16)
            put_both(g_own, g_oth, grad)
            dhid_ref[...] = project_back(grad, wd_a[1], wd_b[1]).astype(BF16)

        g3_own, g3_oth, dhid3 = call(
            cot_body, "cot_d",
            [*cot_parts, *wd],
            [half_low, half_low, hid_low],
            flops=mlp_flops // 2,
            hold=[*keep_a, *keep_b, *keep_c, *small, *wq, *wp, *wu],
        )


        def last_body(chunk, span):
            def body(
                s_in, part_a, part_b, small_a, small_b, dhid_ref, g_oth, wu_a, wu_b,
                s_ref, n_own, fore_ref, *refs,
            ):
                *rear_refs, part_ref = refs
                s_ref[span, :] = add_parts(s_in[span, :], part_a, part_b)
                normed = to_normed(s_ref[span, :], (small_a, small_b), 3)
                put_normed(n_own, [fore_ref], span, normed)
                pre = project_in(normed, wu_a[1], wu_b[1])
                below, bell = gelu_parts(pre)
                fore_ref[span, half:] = (pre * below).astype(BF16)
                dpre = (dhid_ref[span, :].astype(F32) * (below + pre * bell)).astype(BF16)
                put_rear(rear_refs, 0, g_oth[span, :], span)
                put_rear(rear_refs, half, dpre, span)
                part_ref[:, :half] = mm(dpre, wu_a[1], 1, 1).astype(BF16)
                part_ref[:, half:] = mm(dpre, wu_b[1], 1, 1).astype(BF16)

            return body

        (s5, n3_own, fore3, *rear3), back3, far_back3, _ = in_chunks(
            "mlp_d", last_body,
            lambda at: [s4, part2[at], far2[at], *small, dhid3, g3_oth, *wu],
            [full, half_low, fore_mlp, *rear_shapes(rear_width_mlp, 2)],
            [*keep_a, *keep_b, *keep_c, *fore2[1], g3_own, *wq, *wp, *wd],
        )
        fore3 = both_rear([fore3], False)
        keep_c += fore2[1]
        rear3 = both_rear(rear3, False)

        up_rows, down_rows = hidden // n_dev, half // n_dev
        qkv_rows, proj_rows = heads_width // n_dev, half // n_dev
        folds = hidden // half
        cut = n_dev // 2
        sum_rows = 32

        class Stream:
            def __init__(self, which, pieces):
                self.bits, self.which, self.pieces = orders[which], which, pieces
                self.chunk_rows = sum(piece_rows(piece) for piece in pieces)
                self.step, self.kept, self.got, self.at, self.final = 0, None, None, 0, None

        def piece_rows(piece):
            return {"up": up_rows, "q": qkv_rows, "k": qkv_rows, "v": qkv_rows}.get(
                piece, down_rows
            )

        downs = [("down", fold) for fold in range(folds)]

        def two_streams(parts, first, which):
            streams = [Stream(which, parts[:first]), Stream(which + 1, parts[first:])]
            return [stream for stream in streams if stream.pieces]

        def mlp_streams(first, which):
            return two_streams(["up", *downs], 1 + first, which)

        def attn_streams(first, which):
            return two_streams(["q", "k", "v", "proj"], first, which)

        def write_pieces(values, streams, scratches):
            for stream, scratch in zip(streams, scratches):
                at = 0
                for piece in stream.pieces:
                    size = piece_rows(piece)
                    for chunk in range(n_dev):
                        rows_at = slice(chunk * size, (chunk + 1) * size)
                        if isinstance(piece, tuple):
                            columns = slice(piece[1] * half, (piece[1] + 1) * half)
                            part = values["down"][rows_at, columns]
                        else:
                            part = values[piece][rows_at]
                        scratch[chunk, at : at + size, :] = part.astype(BF16)
                    at += size

        def both_sums(n_own, g_own, fore_a, fore_b, rear_a, rear_b):
            def left(at, size):
                return mm(get_rear(rear_a, at, size), n_own[...], 0, 0) + mm(
                    get_rear(rear_b, at, size), get_rear(fore_b, 0, half), 0, 0
                )

            size = sum(ref.shape[1] for ref in fore_a) - half
            right = mm(g_own[...], get_rear(fore_a, half, size), 0, 0) + mm(
                get_rear(rear_b, 0, half), get_rear(fore_b, half, size), 0, 0
            )
            return left, right

        def write_mlp(*refs):
            left, right = both_sums(*refs)
            return {"up": left(half, hidden), "down": right}

        def write_attn(*refs):
            left, right = both_sums(*refs)
            values = {
                name: left(half + part * heads_width, heads_width)
                for part, name in enumerate(("q", "k", "v"))
            }
            return {**values, "proj": right}

        def make(name, write, streams, n_own, g_own, fore, rear, hold):
            outs = [sds((cut * s.chunk_rows, half), BF16) for s in streams for _ in range(2)]
            count = len(rear[0])

            pieces = len(fore[0])

            def body(n_ref, g_ref, *refs):
                fore_a, fore_b, refs = refs[:pieces], refs[pieces : 2 * pieces], refs[2 * pieces :]
                fore_b = [other_core(ref) for ref in fore_b]
                rear_a, rear_b, refs = refs[:count], refs[count : 2 * count], refs[2 * count :]
                rear_b = [other_core(ref) for ref in rear_b]
                out_refs, scratches = refs[: len(outs)], refs[len(outs) :]
                values = write(n_ref, g_ref, fore_a, fore_b, rear_a, rear_b)
                write_pieces(values, streams, scratches)
                for at, (stream, scratch) in enumerate(zip(streams, scratches)):
                    size = stream.chunk_rows
                    for place in range(n_dev):
                        chunk = scratch[chunk_at(place, stream.which)]
                        to = (place % cut) * size
                        out_refs[2 * at + place // cut][to : to + size, :] = chunk

            results = call(
                body, name, [n_own, g_own, *fore[0], *fore[1], *rear[0], *rear[1]], outs, hold=hold,
                scratch=[pltpu.VMEM((n_dev, s.chunk_rows, half), BF16) for s in streams],
            )
            for at, stream in enumerate(streams):
                stream.kept, stream.sent = results[2 * at], results[2 * at + 1]

        def send_first(streams):
            for stream in streams:
                stream.got, stream.step = over_dev(stream.sent, stream.bits[0]), 1

        def split_low(values):
            high = values.astype(BF16)
            return high, (values - high.astype(F32)).astype(BF16)

        def joined(ref, at):
            high = ref[at : at + sum_rows, :].astype(F32)
            return high + ref[at + sum_rows : at + 2 * sum_rows, :].astype(F32)

        def last_sum(stream, kept, got):
            return kept[...].astype(F32) + got[
                stream.at : stream.at + stream.chunk_rows, :
            ].astype(F32)

        def slot(*args, **kwargs):
            prepare_slot(*args, **kwargs)()

        def prepare_slot(
            name, fresh=(), moving=(), ending=(), sums=None, hold=(), spare=None
        ):
            ins, outs, sizes = [], [], {}
            plan_fresh, plan_moving = [], []

            def room(bit, size):
                at = sizes.get(bit, 0)
                sizes[bit] = at + size
                return at

            def place_of(array):
                for at, known in enumerate(ins):
                    if known is array:
                        return at
                ins.append(array)
                return len(ins) - 1

            for stream in fresh:
                size, bit = stream.sent.shape[0], stream.bits[0]
                plan_fresh.append((place_of(stream.sent), size, bit, room(bit, size)))
            for stream in moving:
                size = stream.kept.shape[0] // 2
                bit = stream.bits[stream.step]
                plan_moving.append(
                    (place_of(stream.kept), place_of(stream.got), stream.at, size,
                     len(outs), bit, room(bit, size))
                )
                outs.append(sds((size, half), BF16))
            plan_ending = []
            for stream in ending:
                plan_ending.append(
                    (stream, place_of(stream.kept), place_of(stream.got), len(outs))
                )
                outs.append(sds((stream.chunk_rows, half)))
            if sums is not None:
                total_at = place_of(sums[0])
                sums_got = None if sums[1] is None else place_of(sums[1])
                sums_room = room(sums[3], 2 * sum_rows)
                sums_out = len(outs)
                outs.append(sds((sum_rows, half)))
            if spare is not None:
                spare_at = room(spare, 16)
            bits_used = sorted(sizes)
            buffer_at = {bit: len(outs) + at for at, bit in enumerate(bits_used)}
            outs += [sds((sizes[bit], half), BF16) for bit in bits_used]

            def body(*refs):
                in_refs, out_refs = refs[: len(ins)], refs[len(ins) :]
                for sent_in, size, bit, at in plan_fresh:
                    out_refs[buffer_at[bit]][at : at + size, :] = in_refs[sent_in][...]
                for kept_in, got_in, got_row, size, kept_at, bit, at in plan_moving:
                    kept, got = in_refs[kept_in], in_refs[got_in]
                    out_refs[kept_at][...] = (
                        kept[:size, :].astype(F32) + got[got_row : got_row + size, :].astype(F32)
                    ).astype(BF16)
                    out_refs[buffer_at[bit]][at : at + size, :] = (
                        kept[size:, :].astype(F32)
                        + got[got_row + size : got_row + 2 * size, :].astype(F32)
                    ).astype(BF16)
                if spare is not None:
                    out_refs[buffer_at[spare]][spare_at:, :] = jnp.zeros((16, half), BF16)
                for stream, kept_in, got_in, out_at in plan_ending:
                    out_refs[out_at][...] = last_sum(stream, in_refs[kept_in], in_refs[got_in])
                if sums is not None:
                    total = in_refs[total_at][...]
                    if sums_got is not None:
                        total = total + joined(in_refs[sums_got], sums[2])
                    high, low = split_low(total)
                    out_refs[sums_out][...] = high.astype(F32) + low.astype(F32)
                    buffer = out_refs[buffer_at[sums[3]]]
                    buffer[sums_room : sums_room + sum_rows, :] = high
                    buffer[sums_room + sum_rows : sums_room + 2 * sum_rows, :] = low

            results = call(body, name, ins, outs, hold=hold)
            for stream, _, _, out_at in plan_ending:
                stream.final = results[out_at]
            for stream, (_, _, _, _, kept_at, _, _) in zip(moving, plan_moving):
                stream.kept = results[kept_at]

            def depart():
                received = {bit: over_dev(results[buffer_at[bit]], bit) for bit in bits_used}
                for stream, (_, _, bit, at) in zip(fresh, plan_fresh):
                    stream.got, stream.at, stream.step = received[bit], at, 1
                for stream, (_, _, _, _, _, bit, at) in zip(moving, plan_moving):
                    stream.got, stream.at = received[bit], at
                    stream.step += 1
                if sums is not None:
                    sums[:3] = results[sums_out], received[sums[3]], sums_room

            return depart

        def ship(total, kept, sent):
            packed = mm(placement(images, True), total.astype(BF16), 1, 0).astype(BF16)
            kept[...] = packed[:, :half]
            sent[:rows_in, :] = packed[:, half:]

        shipped = [sds((rows_in, half), BF16)] * 2

        def fold(kept, received, stay, go):
            same = here("ha") == here("wa")
            theirs = received[:rows_in, :]
            stay[...] = jnp.where(same, kept[...], theirs)
            go[:rows_in, :] = jnp.where(same, theirs, kept[...])

        def join(stay, received, out_ref):
            out_ref[...] = stay[...].astype(F32) + received[:rows_in, :].astype(F32)

        def out_body(s_in, fore_ref, wd_a, wd_b, kept, sent):
            hid = fore_ref[:, half:]
            base = jnp.where(here("ha") == 0, s_in[...], 0.0)
            branch = jnp.concatenate([mm(hid, wd_a[1], 1, 0), mm(hid, wd_b[1], 1, 0)], axis=1)
            ship(base + branch, kept, sent)

        streams_d = mlp_streams(SPLIT_D, 0)
        make(
            "wgrad_d", write_mlp, streams_d, n3_own, g3_own, fore3, rear3,
            [*keep_a, *keep_b, *keep_c, *small, *weights, s5],
        )
        send_first(streams_d)

        def add_norm_back(grad, part_a, part_b, stream, gain, sums_ref):
            upstream = part_a[...].astype(F32) + part_b[...].astype(F32)
            units, inv_std = norm_stats(stream)
            sums_ref[0:1, :] = jnp.sum(upstream * units, axis=0, keepdims=True)
            sums_ref[1:2, :] = jnp.sum(upstream, axis=0, keepdims=True)
            return grad + norm_back(upstream, units, inv_std, gain)

        def qkv_back(packed, section, wq_a, wq_b):
            return [
                sum(mm(packed[part], ref[section, part], 1, 1) for part in range(3))
                for ref in (wq_a, wq_b)
            ]

        def channel_back_body(
            g_in_own, g_in_oth, s_in, small_a, small_b, mask_ref, qkv_ref, probs_ref,
            wp_a, wp_b, wq_a, wq_b, *refs,
        ):
            count = len(chunks)
            part_a, part_b = (
                jnp.concatenate([ref[...] for ref in refs[at : at + count]], axis=0)
                for at in (0, count)
            )
            g_ref, g_own, part_ref, sums_ref, *rear_refs = refs[2 * count :]
            grad = jnp.concatenate([g_in_own[...], g_in_oth[...]], axis=1).astype(F32)
            gain = gain_row((small_a, small_b), 3)
            grad = add_norm_back(grad, part_a, part_b, s_in[...], gain, sums_ref)
            g_ref[...] = grad
            low = grad.astype(BF16)
            g_own[...] = low[:, :half]
            put_rear(rear_refs, 0, low[:, half:])
            grad_mixed = project_back(low, wp_a[1], wp_b[1]).astype(BF16)
            packed = attention_part_back(
                False, grad_mixed, mask_ref, qkv_ref, probs_ref, rear_refs
            )
            own, oth = qkv_back(packed, 1, wq_a, wq_b)
            part_ref[:, :half] = own.astype(BF16)
            part_ref[:, half:] = oth.astype(BF16)

        late = [*fore3[0], *wd, s5]
        (g2, g2_own, back2, sums3, *rear2) = call(
            channel_back_body, "back_c",
            [g3_own, g3_oth, s5, *small, mask, qkv2, probs2, *wp, *wq, *back3, *far_back3],
            [full, half_low, full_low, sds((2, width)), *rear_shapes(rear_width_attn, 1)],
            flops=attn_flops,
            hold=[*keep_a, *keep_b, s3, s4, n2_own, *fore2[0], *fore2[1], *wu, *wd, *fore3[0]],
        )
        far_back2 = over_ha(back2)
        rear2 = both_rear(rear2, False)
        hid_got, fore0_got = (
            lax.all_gather(later(values, g2), "wa") for values in (fore1[1], fore0)
        )
        fore1, fore0 = (fore1, [n1_got, hid_got]), ([fore0], [fore0_got])
        keep_a.append(fore0_got)
        keep_b.append(hid_got)
        streams_c = attn_streams(SPLIT_C, 2)
        kept_c = [*keep_a, *keep_b, s3, s4, *small, *weights, g2, *late, sums3]
        make("wgrad_c", write_attn, streams_c, n2_own, g2_own, fore2, rear2, kept_c)
        slot(
            "slot_c", fresh=streams_c, moving=streams_d, hold=[*kept_c, back2, far_back2],
        )

        def mlp_back_body(
            g_in, part_a, part_b, s_in, s_before, small_a, small_b, slope_ref,
            wd_a, wd_b, wu_a, wu_b, g_ref, g_own, part_ref, sums_ref, *rear_refs,
        ):
            keep = column_mask(rows)
            gain = gain_row((small_a, small_b), 2)
            grad = add_norm_back(g_in[...], part_a, part_b, s_in[...], gain, sums_ref)
            conv_back_into(g_ref, sums_ref, 2, grad, s_before[...], (small_a, small_b), 1, keep)
            low = g_ref[...].astype(BF16)
            g_own[...] = low[:, :half]
            put_rear(rear_refs, 0, low[:, half:])
            dhid = project_back(low, wd_a[0], wd_b[0]).astype(BF16).astype(F32)
            dpre = (dhid * slope_ref[...]).astype(BF16)
            put_rear(rear_refs, half, dpre)
            part_ref[:, :half] = mm(dpre, wu_a[0], 1, 1).astype(BF16)
            part_ref[:, half:] = mm(dpre, wu_b[0], 1, 1).astype(BF16)

        (g1, g1_own, back1, sums2, *rear1) = call(
            mlp_back_body, "back_b",
            [g2, back2, far_back2, s4, s3, *small, slope1, *wd, *wu],
            [full, half_low, full_low, sds((11, width)), *rear_shapes(rear_width_mlp, 2)],
            flops=mlp_flops,
            hold=[*keep_a, s2, n1_own, *fore1[0], *fore1[1], *wq, *wp, *fore3[0], s5, sums3],
        )
        far_back1 = over_ha(back1)
        rear1 = both_rear(rear1)
        streams_b = mlp_streams(SPLIT_B, 0)
        make(
            "wgrad_b", write_mlp, streams_b, n1_own, g1_own, fore1, rear1,
            [*keep_a, s2, *small, *wq, *wp, g1, *late, sums3, sums2],
        )
        send_first(streams_b)

        def window_back_body(
            g_in, part_a, part_b, s_in, small_a, small_b, qkv_ref, probs_ref, wp_a, wp_b,
            g_ref, g_own, sums_ref, *rear_refs,
        ):
            gain = gain_row((small_a, small_b), 1)
            grad = add_norm_back(g_in[...], part_a, part_b, s_in[...], gain, sums_ref)
            g_ref[...] = grad
            low = grad.astype(BF16)
            g_own[...] = low[:, :half]
            put_rear(rear_refs, 0, low[:, half:])
            grad_mixed = project_back(low, wp_a[0], wp_b[0]).astype(BF16)
            attention_part_back(True, grad_mixed, None, qkv_ref, probs_ref, rear_refs)

        (g0, g0_own, sums1, *rear0) = call(
            window_back_body, "back_a",
            [g1, back1, far_back1, s2, *small, qkv0, probs0, *wp],
            [full, half_low, sds((2, width)), *rear_shapes(rear_width_attn, 1)],
            flops=attn_flops, hold=[x0, n0_own, *fore0[0], *fore0[1], s1, *wq, *late, sums3, sums2],
        )
        every = [*streams_d, *streams_c]
        depart = prepare_slot(
            "slot_cd", moving=every, spare=2,
            hold=[x0, n0_own, *fore0[0], *fore0[1], s1, *small, *wq, *late, sums1, sums2, sums3,
                  g0, g0_own, *rear0],
        )
        rear0 = both_rear(later(rear0, streams_d[0].kept))

        keep_0 = [g0, s1, x0, *small, *wq, sums1, sums2, sums3, *rear0[0]]
        streams_a = attn_streams(SPLIT_A, 0)
        make("wgrad_a", write_attn, streams_a, n0_own, g0_own, fore0, rear0, [*late, *keep_0])
        every = [*streams_d, *streams_c, *streams_b, *streams_a]
        send_first(streams_a)
        depart()

        sums_at = -(-rows_in // 16) * 16
        sums_half = sds((sum_rows, half))
        with_sums = sds((sums_at + 2 * sum_rows, half), BF16)

        def put_sums(ref, total):
            high, low = split_low(total)
            ref[sums_at : sums_at + sum_rows, :] = high
            ref[sums_at + sum_rows :, :] = low

        def first_back_body(
            g_in, s_in, x_ref, small_a, small_b, wq_a, wq_b, sums_one, sums_two, sums_three, *refs
        ):
            rear_refs, (kept, sent, sums_own, scratch, sums_ref) = refs[:-5], refs[-5:]
            keep = column_mask(rows)
            packed = [
                get_rear(rear_refs, half + part * heads_width, heads_width) for part in range(3)
            ]
            upstream = jnp.concatenate(qkv_back(packed, 0, wq_a, wq_b), axis=1)
            units, inv_std = norm_stats(s_in[...])
            sums_ref[0:1, :] = jnp.sum(upstream * units, axis=0, keepdims=True)
            sums_ref[1:2, :] = jnp.sum(upstream, axis=0, keepdims=True)
            grad = jnp.where(here("ha") == 0, g_in[...], 0.0)
            grad = grad + norm_back(upstream, units, inv_std, gain_row((small_a, small_b), 0))
            conv_back_into(
                scratch, sums_ref, 2, grad, x_ref[...].astype(F32), (small_a, small_b), 0, keep
            )
            ship(scratch[...], kept, sent)
            sums_ref[11:13, :] = 0.5 * sums_one[...]
            sums_ref[13:24, :] = 0.5 * sums_two[...]
            sums_ref[24:26, :] = 0.5 * sums_three[...]
            sums_ref[26:, :] = jnp.zeros((sum_rows - 26, width), F32)
            sums_own[...] = sums_ref[:, :half]
            put_sums(sent, sums_ref[:, half:])

        token_kept, token_sent, sums_own = call(
            first_back_body, "back_0",
            [g0, s1, x0, *small, *wq, sums1, sums2, sums3, *rear0[0]],
            [shipped[0], with_sums, sums_half],
            scratch=[pltpu.VMEM((rows, width), F32), pltpu.VMEM((sum_rows, width), F32)],
            flops=attn_flops * 3 // 4, hold=late,
        )

        def fold_tokens(kept, both, sums_a, stay, go, sums_ref):
            received = other_core(both)
            fold(kept, received, stay, go)
            total = sums_a[...] + joined(received, sums_at)
            put_sums(go, total)
            sums_ref[...] = joined(go, sums_at)

        token_stay, token_go, sums_chip = call(
            fold_tokens, "fold_tokens",
            [token_kept, lax.all_gather(token_sent, "wa"), sums_own],
            [shipped[0], with_sums, sums_half], hold=late,
        )
        token_got = over_ha(token_go)

        def join_tokens(stay, received, sums_chip, out_ref, sums_ref):
            join(stay, received, out_ref)
            sums_ref[...] = sums_chip[...] + joined(received, sums_at)

        owned = sds((rows_in, half))
        grad_tokens, sums_ha = call(
            join_tokens, "join_tokens", [token_stay, token_got, sums_chip], [owned, sums_half],
            hold=late,
        )
        left_bits = list(range(bits))
        sums = [sums_ha, None, 0, left_bits.pop(0)]
        slot("sums_x", sums=sums, hold=late)
        out_kept, out_sent = call(
            out_body, "out_d", [s5, *fore3[0], *wd], shipped, flops=mlp_flops // 2
        )
        out_both = lax.all_gather(out_sent, "wa")

        def hop():
            if not left_bits:
                return None
            sums[3] = left_bits.pop(0)
            return sums

        turn = 0
        while left_bits or any(stream.step < bits for stream in every):
            turn += 1
            arrived = [s for s in every if s.step == bits and s.final is None]
            first = [*streams_b, *streams_c] if turn > 1 else streams_b
            slot(f"slot_b{turn}", moving=[s for s in first if s.step < bits])
            second = [s for s in [*streams_d, *streams_a] if s.step < bits]
            slot(f"slot_a{turn}", moving=second, ending=arrived, sums=hop())
            if turn == 1:
                out_stay, out_go = call(
                    lambda kept, both, *refs: fold(kept, other_core(both), *refs),
                    "fold_out", [out_kept, out_both], shipped,
                )
                out_got = over_ha(out_go)
        output = call(join, "join_out", [out_stay, out_got], [owned])[0]

        def finish_body(*refs):
            (up, down, qkv, proj, taps_ref, gain_ref, shift_ref) = refs[-7:]
            at = iter(refs)
            total = next(at)[...] + joined(next(at), sums[2])
            for branch, row in enumerate((0, 11, 13, 24)):
                gain_ref[branch : branch + 1, :] = total[row : row + 1]
                shift_ref[branch : branch + 1, :] = total[row + 1 : row + 2]
            for section, row in enumerate((2, 15)):
                for t in range(9):
                    taps_ref[t, section : section + 1, :] = total[row + t : row + t + 1]

            def finished(stream):
                if stream.final is not None:
                    return next(at)[...]
                return last_sum(stream, next(at), next(at))

            for section, streams in enumerate(
                ((*streams_a, *streams_b), (*streams_c, *streams_d))
            ):
                for stream in streams:
                    values, row = finished(stream), 0
                    for piece in stream.pieces:
                        part = values[row : row + piece_rows(piece)]
                        row += piece_rows(piece)
                        if piece == "up":
                            up[section] = part
                        elif piece == "proj":
                            proj[section] = part
                        elif isinstance(piece, tuple):
                            down[section, :, piece[1] * half : (piece[1] + 1) * half] = part
                        else:
                            qkv[section, ("q", "k", "v").index(piece)] = part

        ends = []
        for stream in (*streams_a, *streams_b, *streams_c, *streams_d):
            ends += [stream.kept, stream.got] if stream.final is None else [stream.final]
        up, down, qkv, proj, grad_taps, grad_gain, grad_shift = call(
            finish_body, "finish", [*sums[:2], *ends],
            [sds((2, up_rows, half)), sds((2, down_rows, hidden)), sds((2, 3, qkv_rows, half)),
             sds((2, proj_rows, half)), sds((9, 2, half)), sds((4, half)), sds((4, half))],
        )
        grad_taps = jnp.transpose(grad_taps, (1, 0, 2))
        grad_qkv = jnp.transpose(qkv, (0, 3, 1, 2))
        grad_proj, grad_up, grad_down = (
            jnp.transpose(values, (0, 2, 1)) for values in (proj, up, down)
        )
        return (
            output,
            grad_tokens,
            grad_taps,
            grad_gain,
            grad_shift,
            grad_qkv,
            grad_proj,
            grad_up,
            grad_down,
        )

    placed = (
        P(("dev", "ha"), "wa"),
        P(("dev", "ha"), "wa"),
        P(None, None, "wa"),
        P(None, "wa"),
        P(None, "wa"),
        P(None, "wa", None, "ha"),
        P(None, "ha", "wa"),
        P(None, "wa", "ha"),
        P(None, "ha", "wa"),
        P("dev", None),
    )
    return jax.shard_map(
        on_device,
        mesh=mesh,
        in_specs=placed,
        out_specs=(
            P(("dev", "ha"), "wa"),
            P(("dev", "ha"), "wa"),
            P(None, None, "wa"),
            P(None, "wa"),
            P(None, "wa"),
            P(None, "wa", None, ("ha", "dev")),
            P(None, "ha", ("wa", "dev")),
            P(None, "wa", ("ha", "dev")),
            P(None, "ha", ("wa", "dev")),
        ),
        check_vma=False,
    )
```

```python
from functools import partial

import jax
import jax.numpy as jnp
import numpy as np
from jax import lax
from jax.experimental import pallas as pl
from jax.experimental.pallas import tpu as pltpu
from jax.sharding import PartitionSpec as P

WIN = 7
GRID_COLS = 8
PATCHES = 49
PADDED = WIN * GRID_COLS
HEAD_DIM = 32
LANES = 128
HEADS_TILE = LANES // HEAD_DIM
EPS = 1e-05
NEG = -1e30
SPLIT_D, SPLIT_C, SPLIT_B, SPLIT_A = 0, 2, 0, 4
BF16 = jnp.bfloat16
F32 = jnp.float32
VMEM_LIMIT = 16 * 2**20
TIMES = {"pack_small": 5.0, "choose": 5.0}


def mm(left, right, left_dim, right_dim):
    return lax.dot_general(
        left, right, (((left_dim,), (right_dim,)), ((), ())), preferred_element_type=F32
    )


class Order:
    def __init__(self):
        self.last = None


def kernel_call(
    body, name, ins, outs, order, scratch=(), flops=0, hold=(), reuse=None, carry=None
):
    reuse = reuse or {}
    arrays = list(ins) + list(hold) + ([] if order.last is None else [order.last])
    first_reused = len(arrays)
    aliases = {first_reused + at: out for at, out in enumerate(reuse)}
    arrays += list(reuse.values())
    outs = list(outs) + [sds((8, LANES))]

    def wrapped(*refs):
        out_refs = refs[len(arrays) : len(arrays) + len(outs)]
        for at, out in aliases.items():
            carry(refs[at], out_refs[out])
        body(*refs[: len(ins)], *out_refs[:-1], *refs[len(arrays) + len(outs) :])
        out_refs[-1][...] = jnp.zeros_like(out_refs[-1])

    *results, order.last = pl.pallas_call(
        wrapped,
        in_specs=[pl.BlockSpec(memory_space=pltpu.VMEM)] * len(arrays),
        out_specs=[pl.BlockSpec(memory_space=pltpu.VMEM)] * len(outs),
        out_shape=outs,
        scratch_shapes=list(scratch),
        input_output_aliases=aliases,
        compiler_params=pltpu.CompilerParams(vmem_limit_bytes=VMEM_LIMIT),
        cost_estimate=pl.CostEstimate(
            flops=int(TIMES.get(name, 0) * 1.15e9), bytes_accessed=0, transcendentals=0
        ),
        name=name,
    )(*arrays)
    return results


def sds(shape, dtype=F32):
    return jax.ShapeDtypeStruct(shape, dtype)


def column_mask(rows):
    return (lax.broadcasted_iota(jnp.int32, (rows, 1), 0) % GRID_COLS) < WIN


def placement(images, transposed, begin=0, count=None):
    padded, plain = count or images * PADDED, images * PATCHES
    shape = (plain, padded) if transposed else (padded, plain)
    at = lax.broadcasted_iota(jnp.int32, shape, 1 if transposed else 0) + begin
    image = sum((at >= i * PADDED).astype(jnp.int32) for i in range(1, images))
    inside = at - image * PADDED
    source = image * PATCHES + (inside >> 3) * WIN + (inside & 7)
    other = lax.broadcasted_iota(jnp.int32, shape, 0 if transposed else 1)
    return (((inside & 7) < WIN) & (source == other)).astype(F32).astype(BF16)


def side_shifts(values):
    rows = values.shape[0]
    return (pltpu.roll(values, 1, 0), values, pltpu.roll(values, rows - 1, 0))


def as_grid(values):
    return values.reshape(-1, WIN, GRID_COLS, values.shape[-1])


def move_rows(values, step):
    grid = as_grid(values)
    zeros = jnp.zeros_like(grid[:, :1])
    if step > 0:
        moved = jnp.concatenate([zeros, grid[:, :-1]], axis=1)
    else:
        moved = jnp.concatenate([grid[:, 1:], zeros], axis=1)
    return moved.reshape(values.shape)


def conv_cols(values, taps, keep):
    shifted = side_shifts(values)
    line = [
        sum(shifted[col] * taps[3 * row + col] for col in range(3)) for row in range(3)
    ]
    total = values + line[1] + move_rows(line[0], 1) + move_rows(line[2], -1)
    return jnp.where(keep, total, 0.0)


def tap_sums(grads, values):
    shifted = side_shifts(values)
    grad_grid = as_grid(grads)
    sums = []
    for row in range(3):
        for col in range(3):
            moved = as_grid(shifted[col])
            if row == 0:
                prod = grad_grid[:, 1:] * moved[:, :-1]
            elif row == 1:
                prod = grad_grid * moved
            else:
                prod = grad_grid[:, :-1] * moved[:, 1:]
            flat = prod.reshape(-1, GRID_COLS, prod.shape[-1])
            sums.append(jnp.sum(jnp.sum(flat, axis=0), axis=0, keepdims=True))
    return sums


def norm_stats(stream):
    width = stream.shape[1]
    center = jnp.sum(stream, axis=1, keepdims=True) * (1.0 / width)
    moved = stream - center
    inv_std = lax.rsqrt(jnp.sum(moved * moved, axis=1, keepdims=True) * (1.0 / width) + EPS)
    return moved * inv_std, inv_std


def norm_back(upstream, units, inv_std, gain):
    width = upstream.shape[1]
    scaled = upstream * gain
    first = jnp.sum(scaled, axis=1, keepdims=True) * (1.0 / width)
    second = jnp.sum(scaled * units, axis=1, keepdims=True) * (1.0 / width)
    return inv_std * (scaled - first - units * second)


def gelu_parts(values):
    below = 0.5 + 0.5 * lax.erf(values * float(0.5**0.5))
    bell = jnp.exp2(values * values * float(-0.5 * np.log2(np.e)))
    return below, bell * float(1.0 / np.sqrt(2.0 * np.pi))


def head_mask(index):
    return (lax.broadcasted_iota(jnp.int32, (1, LANES), 1) // HEAD_DIM) == index


def spread_heads(tile):
    return jnp.concatenate(
        [jnp.where(head_mask(j), tile, 0.0) for j in range(HEADS_TILE)], axis=0
    ).astype(BF16)


def gather_heads(stacked):
    rows = stacked.shape[0] // HEADS_TILE
    total = jnp.where(head_mask(0), stacked[:rows], 0.0)
    for j in range(1, HEADS_TILE):
        total = jnp.where(head_mask(j), stacked[j * rows : (j + 1) * rows], total)
    return total


def softmax_rows(scores):
    top = jnp.max(scores, axis=0, keepdims=True)
    weights = jnp.exp(scores - top)
    return weights * (1.0 / jnp.sum(weights, axis=0, keepdims=True))


SCALE = HEAD_DIM**-0.5


def low(tiles):
    return [tile.astype(BF16) for tile in tiles]


def minus_row_sums(probs, grads):
    return [
        (p * (g - jnp.sum(g * p, axis=0, keepdims=True))).astype(BF16)
        for p, g in zip(probs, grads)
    ]


def window_tiles(queries, keys, values):
    keys_ok = column_mask(PADDED)
    scores = [
        mm(k, spread_heads(q), 1, 1) * SCALE for q, k in zip(queries, low(keys))
    ]
    probs = [softmax_rows(jnp.where(keys_ok, score, NEG)) for score in scores]
    mixed = [mm(p, v, 0, 0) for p, v in zip(low(probs), low(values))]
    return probs, [gather_heads(tile) for tile in mixed]


def window_tiles_back(queries, keys, values, probs, grads):
    q_big, g_big = ([spread_heads(tile) for tile in tiles] for tiles in (queries, grads))
    grad_probs = [mm(v, g, 1, 1) for v, g in zip(low(values), g_big)]
    grad_v = [mm(p, g, 1, 0) for p, g in zip(low(probs), g_big)]
    grad_scores = minus_row_sums(probs, grad_probs)
    grad_k = [mm(d, q, 1, 0) * SCALE for d, q in zip(grad_scores, q_big)]
    grad_q = [mm(d, k, 0, 0) for d, k in zip(grad_scores, low(keys))]
    return [gather_heads(tile) * SCALE for tile in grad_q], grad_k, grad_v


def same_head():
    first = lax.broadcasted_iota(jnp.int32, (LANES, LANES), 0) // HEAD_DIM
    second = lax.broadcasted_iota(jnp.int32, (LANES, LANES), 1) // HEAD_DIM
    return first == second


def channel_tiles(queries, keys, values, masks):
    own_head = same_head()
    masked = low([q * mask for q, mask in zip(queries, masks)])
    scores = [mm(k, q, 0, 0) * SCALE for q, k in zip(masked, low(keys))]
    probs = [softmax_rows(jnp.where(own_head, score, NEG)) for score in scores]
    return probs, [mm(v, p, 1, 0) for p, v in zip(low(probs), low(values))]


def channel_tiles_back(queries, keys, values, probs, grads, masks):
    masked = low([q * mask for q, mask in zip(queries, masks)])
    grads = low(grads)
    grad_probs = [mm(v, g, 0, 0) for v, g in zip(low(values), grads)]
    grad_v = [mm(g, p, 1, 1) for g, p in zip(grads, low(probs))]
    grad_scores = minus_row_sums(probs, grad_probs)
    grad_q = [mm(k, d, 1, 0) * SCALE * m for k, d, m in zip(low(keys), grad_scores, masks)]
    grad_k = [mm(q, d, 1, 1) * SCALE for q, d in zip(masked, grad_scores)]
    return grad_q, grad_k, grad_v


def cut_tiles(values, images, tiles):
    return [
        values[image * PADDED : (image + 1) * PADDED, tile * LANES : (tile + 1) * LANES]
        for image in range(images)
        for tile in range(tiles)
    ]


def paste_tiles(parts, images, tiles):
    lines = [
        jnp.concatenate(parts[image * tiles : (image + 1) * tiles], axis=1)
        for image in range(images)
    ]
    return jnp.concatenate(lines, axis=0).astype(BF16)


def solution(mesh):
    n_dev = mesh.shape["dev"]
    bits = n_dev.bit_length() - 1
    assert n_dev == 1 << bits and mesh.shape["ha"] == 2 and mesh.shape["wa"] == 2

    swap = [(0, 1), (1, 0)]

    def over_ha(values):
        return lax.ppermute(values, "ha", swap)

    def over_wa(values):
        return lax.ppermute(values, "wa", swap)

    def over_dev(values, bit):
        return lax.ppermute(values, "dev", [(i, i ^ (1 << bit)) for i in range(n_dev)])

    def on_device(
        tokens, cotangent, conv_taps, norm_gain, norm_shift, w_qkv, w_proj, w_up, w_down, valid
    ):
        rows_in, half = tokens.shape
        images = rows_in // PATCHES
        rows = images * PADDED
        width = 2 * half
        heads_width = w_qkv.shape[3]
        hidden = w_up.shape[2]
        tiles = heads_width // LANES
        assert heads_width == half
        rest = list(range(3, bits))
        orders = [[0, 1, 2, *rest], [1, 0, 2, *rest], [0, 2, 1, *rest], [1, 2, 0, *rest]]

        def here(name):
            return lax.axis_index(name)

        def chunk_at(place, which):
            found = 0
            for step, bit in enumerate(orders[which]):
                found |= ((place >> (bits - 1 - step)) & 1) << bit
            return found ^ here("dev")

        order = Order()
        call = partial(kernel_call, order=order)

        def later(values, event):
            return lax.optimization_barrier((values, event))[0]

        def pack_small(taps_ref, gain_ref, shift_ref, out_ref):
            for section in range(2):
                for t in range(9):
                    at = 9 * section + t
                    out_ref[at : at + 1, :] = taps_ref[t, section : section + 1, :]
            out_ref[18:22, :] = gain_ref[...]
            out_ref[22:26, :] = shift_ref[...]

        def choose(mine, received, own, *others):
            same = here("ha") == here("wa")
            own[...] = jnp.where(same, mine[...], received[...])
            other, at = jnp.where(same, received[...], mine[...]), 0
            for ref in others:
                ref[...] = other[:, at : at + ref.shape[1]]
                at += ref.shape[1]

        wq_own = jnp.transpose(w_qkv, (0, 2, 1, 3))
        wq, wp = (wq_own, over_wa(wq_own)), (w_proj, over_wa(w_proj))
        tokens_in, cot_in = over_ha(tokens), over_ha(cotangent)
        small_own = call(
            pack_small, "pack_small",
            [jnp.transpose(conv_taps, (1, 0, 2)), norm_gain, norm_shift], [sds((26, half))],
            hold=[tokens],
        )[0]
        small = (small_own, over_wa(small_own))
        chosen = [sds((rows_in, columns), BF16) for columns in (half, LANES, half - LANES)]
        tokens_own, *tokens_oth = call(
            choose, "choose", [tokens, tokens_in], chosen, hold=[wq[1], wp[1], small_own]
        )
        token_parts = (tokens_own, *[over_wa(values) for values in tokens_oth])

        def arrive(out_ref):
            out_ref[...] = jnp.zeros_like(out_ref)

        arrived = call(
            arrive, "arrive", [], [sds((8, LANES))],
            hold=[*token_parts, small[1], cot_in, small_own, wq[1], wp[1]],
        )[0]
        wu, wd = ((values, over_wa(later(values, arrived))) for values in (w_up, w_down))

        def unpack(parts, begin=0, count=None):
            values = jnp.concatenate([part[...] for part in parts], axis=1)
            return mm(placement(images, False, begin, count), values, 1, 0)

        def gain_row(refs, branch):
            return jnp.concatenate([ref[18 + branch : 19 + branch, :] for ref in refs], axis=1)

        def shift_row(refs, branch):
            return jnp.concatenate([ref[22 + branch : 23 + branch, :] for ref in refs], axis=1)

        def tap_rows(small_refs, section, col, flipped):
            ref = small_refs[col // half]
            at = col % half
            found = [
                ref[9 * section + t : 9 * section + t + 1, at : at + LANES] for t in range(9)
            ]
            return found[::-1] if flipped else found

        def project_in(normed, first, second):
            return mm(normed[:, :half], first, 1, 0) + mm(normed[:, half:], second, 1, 0)

        def project_back(values, first, second):
            return mm(values[:, :half], first, 1, 1) + mm(values[:, half:], second, 1, 1)

        def to_normed(stream, small_refs, branch):
            units, _ = norm_stats(stream)
            return (units * gain_row(small_refs, branch) + shift_row(small_refs, branch)).astype(
                BF16
            )

        def both_rear(pieces, gather=True):
            pieces = list(pieces)
            if gather:
                return pieces, [lax.all_gather(piece, "wa") for piece in pieces]
            return pieces, [over_wa(piece) for piece in pieces]

        def other_core(ref):
            return ref.at[1 - here("wa")] if len(ref.shape) == 3 else ref

        def put_both(own_ref, oth_ref, values):
            own_ref[...] = values[:, :half]
            oth_ref[:, :half] = values[:, half:]

        def add_parts(stream, part_a, part_b):
            return stream + part_a[...].astype(F32) + part_b[...].astype(F32)

        def attention_part(
            window, section, normed, valid_rows, wq_a, wq_b, qkv_ref, probs_ref, first_image
        ):
            count = normed.shape[0] // PADDED
            packed = [
                project_in(normed, wq_a[section, part], wq_b[section, part]).astype(BF16)
                for part in range(3)
            ]
            begin = first_image * PADDED
            for part in range(3):
                qkv_ref[part, begin : begin + count * PADDED, :] = packed[part]
            q, k, v = (cut_tiles(part.astype(F32), count, tiles) for part in packed)
            if window:
                probs, mixed = window_tiles(q, k, v)
            else:
                masks = [mask for mask in valid_rows for _ in range(tiles)]
                probs, mixed = channel_tiles(q, k, v, masks)
            for at, tile in enumerate(probs):
                probs_ref[first_image * tiles + at] = tile
            return paste_tiles(mixed, count, tiles)

        def attention_part_back(window, grad_mixed, mask_ref, qkv_ref, probs_ref, rear_refs):
            q, k, v = (
                cut_tiles(qkv_ref[part].astype(F32), images, tiles) for part in range(3)
            )
            grads = cut_tiles(grad_mixed.astype(F32), images, tiles)
            probs = [probs_ref[at] for at in range(images * tiles)]
            if window:
                found = window_tiles_back(q, k, v, probs, grads)
            else:
                masks = [
                    mask_ref[image * PADDED : (image + 1) * PADDED, :]
                    for image in range(images)
                    for _ in range(tiles)
                ]
                found = channel_tiles_back(q, k, v, probs, grads, masks)
            packed = [paste_tiles(part, images, tiles) for part in found]
            for part in range(3):
                put_rear(rear_refs, half + part * heads_width, packed[part])
            return packed

        def mul_out(left, section, own_ref, oth_ref, out_ref):
            out_ref[:, :half] = mm(left, own_ref[section], 1, 0).astype(BF16)
            out_ref[:, half:] = mm(left, oth_ref[section], 1, 0).astype(BF16)

        def conv_into(out_ref, rows_at, values, small_refs, section, keep):
            for col in range(0, width, LANES):
                taps = tap_rows(small_refs, section, col, False)
                out_ref[rows_at, col : col + LANES] = conv_cols(
                    values[:, col : col + LANES], taps, keep
                )

        def conv_back_into(out_ref, sums_ref, sums_at, grads, values, small_refs, section, keep):
            for col in range(0, width, LANES):
                lanes_at = slice(col, col + LANES)
                taps = tap_rows(small_refs, section, col, True)
                for t, total in enumerate(tap_sums(grads[:, lanes_at], values[:, lanes_at])):
                    sums_ref[sums_at + t : sums_at + t + 1, lanes_at] = total
                out_ref[:, lanes_at] = conv_cols(grads[:, lanes_at], taps, keep)

        window_probs = sds((images * tiles, PADDED, HEADS_TILE * PADDED))
        channel_probs = sds((images * tiles, LANES, LANES))
        full, full_low = sds((rows, width)), sds((rows, width), BF16)
        half_low = sds((rows, half), BF16)
        hid_low = sds((rows, hidden), BF16)
        qkv_low = sds((3, rows, heads_width), BF16)
        fore_attn = sds((rows, half + heads_width), BF16)
        def cuts(total, count):
            tiles_all = total // LANES
            return [LANES * (-(-tiles_all * (at + 1) // count)) for at in range(count)]

        def rear_shapes(total, count):
            ends = cuts(total, count)
            return [sds((rows, e - b), BF16) for b, e in zip([0, *ends], ends)]

        def rear_ranges(refs, at, size):
            begin = 0
            for ref in refs:
                end = begin + ref.shape[1]
                low, high = max(begin, at), min(end, at + size)
                if low < high:
                    yield ref, low - begin, high - begin, low - at
                begin = end

        def put_rear(refs, at, values, span=slice(None)):
            for ref, low, high, source in rear_ranges(refs, at, values.shape[1]):
                ref[span, low:high] = values[:, source : source + high - low]

        def get_rear(refs, at, size):
            parts = [ref[:, low:high] for ref, low, high, _ in rear_ranges(refs, at, size)]
            return parts[0] if len(parts) == 1 else jnp.concatenate(parts, axis=1)

        rear_width_attn, rear_width_mlp = half + 3 * heads_width, half + hidden
        fore_mlp = sds((rows, rear_width_mlp), BF16)
        attn_flops = 2 * rows * (4 * width * heads_width)
        mlp_flops = 2 * rows * (2 * width * hidden)

        split = (images + 1) // 2
        chunks = [(0, split), (split, images)] if split < images else [(0, images)]
        spans = [slice(begin * PADDED, end * PADDED) for begin, end in chunks]

        def chunk_rows(span):
            return span.stop - span.start

        def part_shape(span):
            return sds((chunk_rows(span), width), BF16)

        def put_normed(own_ref, fore_refs, span, normed):
            own_ref[span, :] = normed[:, :half]
            put_rear(fore_refs, 0, normed[:, half:], span)

        def first_body(chunk, span):
            def body(
                tokens_a, tokens_b, tokens_c, small_a, small_b, wq_a, wq_b, wp_a, wp_b,
                x_ref, s_ref, n_own, fore_ref, qkv_ref, probs_ref, part_ref, *copies,
            ):
                if copies:
                    copies[0][...], copies[1][...] = small_a[...], small_b[...]
                keep = column_mask(chunk_rows(span))
                stream = unpack((tokens_a, tokens_b, tokens_c), span.start, chunk_rows(span))
                x_ref[span, :] = stream.astype(BF16)
                conv_into(s_ref, span, stream, (small_a, small_b), 0, keep)
                normed = to_normed(s_ref[span, :], (small_a, small_b), 0)
                put_normed(n_own, [fore_ref], span, normed)
                mixed = attention_part(
                    True, 0, normed, None, wq_a, wq_b, qkv_ref, probs_ref, chunk[0]
                )
                fore_ref[span, half:] = mixed
                mul_out(mixed, 0, wp_a, wp_b, part_ref)

            return body

        def carry_spans(upto):
            def carry(old, new):
                for chunk, span in zip(chunks[:upto], spans[:upto]):
                    if old.shape[0] == rows:
                        new[span, :] = old[span, :]
                    elif old.shape[1] == rows:
                        new[:, span, :] = old[:, span, :]
                    else:
                        per_image = old.shape[0] // images
                        held = slice(chunk[0] * per_image, chunk[1] * per_image)
                        new[held] = old[held]

            return carry

        def in_chunks(
            name, make_body, ins, shapes, hold, extra=(), between=None, alone=True
        ):
            arrays, parts, fars, more = None, [], [], []
            for at, (chunk, span) in enumerate(zip(chunks, spans)):
                results = call(
                    make_body(chunk, span), f"{name}{at}", ins(at),
                    [*shapes, *([part_shape(span)] if alone else ()), *(extra if at == 0 else ())],
                    hold=[*hold, *more, *parts],
                    reuse=None if arrays is None else dict(enumerate(arrays)),
                    carry=carry_spans(at),
                )
                arrays, rest = results[: len(shapes)], results[len(shapes) :]
                if alone:
                    parts.append(rest[0])
                    fars.append(over_ha(rest[0]))
                more = more or rest[1:]
                if at == 0 and between is not None:
                    between(arrays, more)
            return arrays, parts, fars, more

        small_in, cot_parts = small, []

        def choose_cot(arrays, more):
            own, *others = call(
                choose, "choose_cot", [cotangent, cot_in], chosen,
                hold=[*arrays, *more, *wq, *wp],
            )
            cot_parts.extend([own, *others])

        (x0, s1, n0_own, fore0, qkv0, probs0), part0, far0, small = in_chunks(
            "attn_a", first_body, lambda at: [*token_parts, *small_in, *wq, *wp],
            [full_low, full, half_low, fore_attn, qkv_low, window_probs], [cot_in, arrived],
            [sds((26, half))] * 2, choose_cot,
        )
        keep_a = [x0, n0_own, fore0, qkv0, probs0, s1]

        def mlp_body(chunk, span):
            def body(
                s_in, part_a, part_b, small_a, small_b, wu_a, wu_b, wd_a, wd_b,
                s_ref, n_own, slope_ref, *refs,
            ):
                *fore_refs, part_ref = refs
                s_ref[span, :] = add_parts(s_in[span, :], part_a, part_b)
                normed = to_normed(s_ref[span, :], (small_a, small_b), 1)
                put_normed(n_own, fore_refs, span, normed)
                pre = project_in(normed, wu_a[0], wu_b[0])
                below, bell = gelu_parts(pre)
                hid = (pre * below).astype(BF16)
                put_rear(fore_refs, half, hid, span)
                slope_ref[span, :] = below + pre * bell
                mul_out(hid, 0, wd_a, wd_b, part_ref)

            return body

        (s2, n1_own, slope1, *fore1), part1, far1, _ = in_chunks(
            "mlp_b", mlp_body, lambda at: [s1, part0[at], far0[at], *small, *wu, *wd],
            [full, half_low, sds((rows, hidden)), half_low, hid_low],
            [*keep_a, *wq, *wp, *cot_parts],
        )
        n1_got = over_wa(fore1[0])
        cot_parts[1:] = [over_wa(later(values, part1[0])) for values in cot_parts[1:]]
        keep_b = [s2, n1_own, *fore1, slope1, n1_got]
        weights = [*wq, *wp, *wu, *wd]

        def channel_body(chunk, span):
            def body(
                s_in, part_a, part_b, valid_ref, small_a, small_b, wq_a, wq_b, wp_a, wp_b,
                s_before, s_ref, n_own, qkv_ref, probs_ref, mask_ref, *refs,
            ):
                *fore_refs, part_ref = refs
                keep = column_mask(chunk_rows(span))
                stream = jnp.where(keep, add_parts(s_in[span, :], part_a, part_b), 0.0)
                s_before[span, :] = stream
                conv_into(s_ref, span, stream, (small_a, small_b), 1, keep)
                normed = to_normed(s_ref[span, :], (small_a, small_b), 2)
                put_normed(n_own, fore_refs, span, normed)
                one_image = placement(1, False).astype(F32)
                valid_rows = []
                for image in range(*chunk):
                    line = jnp.where(
                        here("wa") == 0,
                        valid_ref[image : image + 1, :],
                        valid_ref[images + image : images + image + 1, :],
                    ).astype(F32)
                    valid_rows.append(jnp.sum(one_image * line, axis=1, keepdims=True))
                    mask_ref[image * PADDED : (image + 1) * PADDED, :] = valid_rows[-1]
                mixed = attention_part(
                    False, 1, normed, valid_rows, wq_a, wq_b, qkv_ref, probs_ref, chunk[0]
                )
                put_rear(fore_refs, half, mixed, span)
                mul_out(mixed, 1, wp_a, wp_b, part_ref)

            return body

        (s3, s4, n2_own, qkv2, probs2, mask, *fore2), part2, far2, _ = in_chunks(
            "attn_c", channel_body,
            lambda at: [s2, part1[at], far1[at], valid, *small, *wq, *wp],
            [full, full, half_low, qkv_low, channel_probs, sds((rows, 1)), half_low, half_low],
            [*keep_a, *keep_b, *wu, *wd, *cot_parts],
        )
        fore2 = both_rear(fore2, False)
        keep_c = [s3, s4, n2_own, *fore2[0], qkv2, probs2, mask]

        def cot_body(cot_a, cot_b, cot_c, wd_a, wd_b, g_own, g_oth, dhid_ref):
            grad = unpack((cot_a, cot_b, cot_c)).astype(BF16)
            put_both(g_own, g_oth, grad)
            dhid_ref[...] = project_back(grad, wd_a[1], wd_b[1]).astype(BF16)

        g3_own, g3_oth, dhid3 = call(
            cot_body, "cot_d",
            [*cot_parts, *wd],
            [half_low, half_low, hid_low],
            flops=mlp_flops // 2,
            hold=[*keep_a, *keep_b, *keep_c, *small, *wq, *wp, *wu],
        )


        def last_body(chunk, span):
            def body(
                s_in, part_a, part_b, small_a, small_b, dhid_ref, g_oth, wu_a, wu_b,
                s_ref, n_own, fore_ref, *refs,
            ):
                share, *rear_refs = refs
                s_ref[span, :] = add_parts(s_in[span, :], part_a, part_b)
                normed = to_normed(s_ref[span, :], (small_a, small_b), 3)
                put_normed(n_own, [fore_ref], span, normed)
                pre = project_in(normed, wu_a[1], wu_b[1])
                below, bell = gelu_parts(pre)
                fore_ref[span, half:] = (pre * below).astype(BF16)
                dpre = (dhid_ref[span, :].astype(F32) * (below + pre * bell)).astype(BF16)
                put_rear(rear_refs, 0, g_oth[span, :], span)
                put_rear(rear_refs, half, dpre, span)
                share[span, :half] = mm(dpre, wu_a[1], 1, 1).astype(BF16)
                share[span, half:] = mm(dpre, wu_b[1], 1, 1).astype(BF16)

            return body

        (s5, n3_own, fore3, back3, *rear3), _, _, _ = in_chunks(
            "mlp_d", last_body,
            lambda at: [s4, part2[at], far2[at], *small, dhid3, g3_oth, *wu],
            [full, half_low, fore_mlp, full_low, *rear_shapes(rear_width_mlp, 2)],
            [*keep_a, *keep_b, *keep_c, *fore2[1], g3_own, *wq, *wp, *wd], alone=False,
        )
        far_back3 = over_ha(back3)
        fore3 = both_rear([fore3], False)
        keep_c += fore2[1]
        rear3 = both_rear(rear3, False)

        up_rows, down_rows = hidden // n_dev, half // n_dev
        qkv_rows, proj_rows = heads_width // n_dev, half // n_dev
        folds = hidden // half
        cut = n_dev // 2
        sum_rows = 32

        class Stream:
            def __init__(self, which, pieces):
                self.bits, self.which, self.pieces = orders[which], which, pieces
                self.chunk_rows = sum(piece_rows(piece) for piece in pieces)
                self.step, self.kept, self.got, self.at, self.final = 0, None, None, 0, None

        def piece_rows(piece):
            return {"up": up_rows, "q": qkv_rows, "k": qkv_rows, "v": qkv_rows}.get(
                piece, down_rows
            )

        downs = [("down", fold) for fold in range(folds)]

        def two_streams(parts, first, which):
            streams = [Stream(which, parts[:first]), Stream(which + 1, parts[first:])]
            return [stream for stream in streams if stream.pieces]

        def mlp_streams(first, which):
            return two_streams(["up", *downs], 1 + first, which)

        def attn_streams(first, which):
            return two_streams(["q", "k", "v", "proj"], first, which)

        def write_pieces(values, streams, scratches):
            for stream, scratch in zip(streams, scratches):
                at = 0
                for piece in stream.pieces:
                    size = piece_rows(piece)
                    for chunk in range(n_dev):
                        rows_at = slice(chunk * size, (chunk + 1) * size)
                        if isinstance(piece, tuple):
                            columns = slice(piece[1] * half, (piece[1] + 1) * half)
                            part = values["down"][rows_at, columns]
                        else:
                            part = values[piece][rows_at]
                        scratch[chunk, at : at + size, :] = part.astype(BF16)
                    at += size

        def both_sums(n_own, g_own, fore_a, fore_b, rear_a, rear_b):
            def left(at, size):
                return mm(get_rear(rear_a, at, size), n_own[...], 0, 0) + mm(
                    get_rear(rear_b, at, size), get_rear(fore_b, 0, half), 0, 0
                )

            size = sum(ref.shape[1] for ref in fore_a) - half
            right = mm(g_own[...], get_rear(fore_a, half, size), 0, 0) + mm(
                get_rear(rear_b, 0, half), get_rear(fore_b, half, size), 0, 0
            )
            return left, right

        def write_mlp(*refs):
            left, right = both_sums(*refs)
            return {"up": left(half, hidden), "down": right}

        def write_attn(*refs):
            left, right = both_sums(*refs)
            values = {
                name: left(half + part * heads_width, heads_width)
                for part, name in enumerate(("q", "k", "v"))
            }
            return {**values, "proj": right}

        def make(name, write, streams, n_own, g_own, fore, rear, hold):
            outs = [sds((cut * s.chunk_rows, half), BF16) for s in streams for _ in range(2)]
            count = len(rear[0])

            pieces = len(fore[0])

            def body(n_ref, g_ref, *refs):
                fore_a, fore_b, refs = refs[:pieces], refs[pieces : 2 * pieces], refs[2 * pieces :]
                fore_b = [other_core(ref) for ref in fore_b]
                rear_a, rear_b, refs = refs[:count], refs[count : 2 * count], refs[2 * count :]
                rear_b = [other_core(ref) for ref in rear_b]
                out_refs, scratches = refs[: len(outs)], refs[len(outs) :]
                values = write(n_ref, g_ref, fore_a, fore_b, rear_a, rear_b)
                write_pieces(values, streams, scratches)
                for at, (stream, scratch) in enumerate(zip(streams, scratches)):
                    size = stream.chunk_rows
                    for place in range(n_dev):
                        chunk = scratch[chunk_at(place, stream.which)]
                        to = (place % cut) * size
                        out_refs[2 * at + place // cut][to : to + size, :] = chunk

            results = call(
                body, name, [n_own, g_own, *fore[0], *fore[1], *rear[0], *rear[1]], outs, hold=hold,
                scratch=[pltpu.VMEM((n_dev, s.chunk_rows, half), BF16) for s in streams],
            )
            for at, stream in enumerate(streams):
                stream.kept, stream.sent = results[2 * at], results[2 * at + 1]

        def send_first(streams):
            for stream in streams:
                stream.got, stream.step = over_dev(stream.sent, stream.bits[0]), 1

        def sums_in(ref, at):
            return ref[at : at + sum_rows, :].astype(F32)

        def last_sum(stream, kept, got):
            return kept[...].astype(F32) + got[
                stream.at : stream.at + stream.chunk_rows, :
            ].astype(F32)

        def slot(*args, **kwargs):
            prepare_slot(*args, **kwargs)()

        def prepare_slot(
            name, fresh=(), moving=(), ending=(), sums=None, hold=(), spare=None
        ):
            ins, outs, sizes = [], [], {}
            plan_fresh, plan_moving = [], []

            def room(bit, size):
                at = sizes.get(bit, 0)
                sizes[bit] = at + size
                return at

            def place_of(array):
                for at, known in enumerate(ins):
                    if known is array:
                        return at
                ins.append(array)
                return len(ins) - 1

            for stream in fresh:
                size, bit = stream.sent.shape[0], stream.bits[0]
                plan_fresh.append((place_of(stream.sent), size, bit, room(bit, size)))
            for stream in moving:
                size = stream.kept.shape[0] // 2
                bit = stream.bits[stream.step]
                plan_moving.append(
                    (place_of(stream.kept), place_of(stream.got), stream.at, size,
                     len(outs), bit, room(bit, size))
                )
                outs.append(sds((size, half), BF16))
            plan_ending = []
            for stream in ending:
                plan_ending.append(
                    (stream, place_of(stream.kept), place_of(stream.got), len(outs))
                )
                outs.append(sds((stream.chunk_rows, half)))
            if sums is not None:
                total_at = place_of(sums[0])
                sums_got = None if sums[1] is None else place_of(sums[1])
                sums_room = room(sums[3], sum_rows)
                sums_out = len(outs)
                outs.append(sds((sum_rows, half)))
            if spare is not None:
                spare_at = room(*spare)
            bits_used = sorted(sizes)
            buffer_at = {bit: len(outs) + at for at, bit in enumerate(bits_used)}
            outs += [sds((sizes[bit], half), BF16) for bit in bits_used]

            def body(*refs):
                in_refs, out_refs = refs[: len(ins)], refs[len(ins) :]
                for sent_in, size, bit, at in plan_fresh:
                    out_refs[buffer_at[bit]][at : at + size, :] = in_refs[sent_in][...]
                for kept_in, got_in, got_row, size, kept_at, bit, at in plan_moving:
                    kept, got = in_refs[kept_in], in_refs[got_in]
                    out_refs[kept_at][...] = (
                        kept[:size, :].astype(F32) + got[got_row : got_row + size, :].astype(F32)
                    ).astype(BF16)
                    out_refs[buffer_at[bit]][at : at + size, :] = (
                        kept[size:, :].astype(F32)
                        + got[got_row + size : got_row + 2 * size, :].astype(F32)
                    ).astype(BF16)
                if spare is not None:
                    out_refs[buffer_at[spare[0]]][spare_at:, :] = jnp.zeros((spare[1], half), BF16)
                for stream, kept_in, got_in, out_at in plan_ending:
                    out_refs[out_at][...] = last_sum(stream, in_refs[kept_in], in_refs[got_in])
                if sums is not None:
                    total = in_refs[total_at][...]
                    if sums_got is not None:
                        total = total + sums_in(in_refs[sums_got], sums[2])
                    low = total.astype(BF16)
                    out_refs[sums_out][...] = low.astype(F32)
                    out_refs[buffer_at[sums[3]]][sums_room : sums_room + sum_rows, :] = low

            results = call(body, name, ins, outs, hold=hold)
            for stream, _, _, out_at in plan_ending:
                stream.final = results[out_at]
            for stream, (_, _, _, _, kept_at, _, _) in zip(moving, plan_moving):
                stream.kept = results[kept_at]

            def depart():
                received = {bit: over_dev(results[buffer_at[bit]], bit) for bit in bits_used}
                for stream, (_, _, bit, at) in zip(fresh, plan_fresh):
                    stream.got, stream.at, stream.step = received[bit], at, 1
                for stream, (_, _, _, _, _, bit, at) in zip(moving, plan_moving):
                    stream.got, stream.at = received[bit], at
                    stream.step += 1
                if sums is not None:
                    sums[:3] = results[sums_out], received[sums[3]], sums_room

            return depart

        def ship(total, kept, sent):
            packed = mm(placement(images, True), total.astype(BF16), 1, 0).astype(BF16)
            kept[...] = packed[:, :half]
            sent[:rows_in, :] = packed[:, half:]

        shipped = [sds((rows_in, half), BF16)] * 2

        def fold(kept, received, stay, go):
            same = here("ha") == here("wa")
            theirs = received[:rows_in, :]
            stay[...] = jnp.where(same, kept[...], theirs)
            go[:rows_in, :] = jnp.where(same, theirs, kept[...])

        def join(stay, received, out_ref):
            out_ref[...] = stay[...].astype(F32) + received[:rows_in, :].astype(F32)

        def out_body(s_in, fore_ref, wd_a, wd_b, kept, sent):
            hid = fore_ref[:, half:]
            base = jnp.where(here("ha") == 0, s_in[...], 0.0)
            branch = jnp.concatenate([mm(hid, wd_a[1], 1, 0), mm(hid, wd_b[1], 1, 0)], axis=1)
            ship(base + branch, kept, sent)

        streams_d = mlp_streams(SPLIT_D, 0)
        make(
            "wgrad_d", write_mlp, streams_d, n3_own, g3_own, fore3, rear3,
            [*keep_a, *keep_b, *keep_c, *small, *weights, s5],
        )
        send_first(streams_d)

        def add_norm_back(grad, part_a, part_b, stream, gain, sums_ref):
            upstream = part_a[...].astype(F32) + part_b[...].astype(F32)
            units, inv_std = norm_stats(stream)
            sums_ref[0:1, :] = jnp.sum(upstream * units, axis=0, keepdims=True)
            sums_ref[1:2, :] = jnp.sum(upstream, axis=0, keepdims=True)
            return grad + norm_back(upstream, units, inv_std, gain)

        def qkv_back(packed, section, wq_a, wq_b):
            return [
                sum(mm(packed[part], ref[section, part], 1, 1) for part in range(3))
                for ref in (wq_a, wq_b)
            ]

        def channel_back_body(
            g_in_own, g_in_oth, s_in, small_a, small_b, mask_ref, qkv_ref, probs_ref,
            wp_a, wp_b, wq_a, wq_b, *refs,
        ):
            part_a, part_b, g_ref, g_own, part_ref, sums_ref, *rear_refs = refs
            grad = jnp.concatenate([g_in_own[...], g_in_oth[...]], axis=1).astype(F32)
            gain = gain_row((small_a, small_b), 3)
            grad = add_norm_back(grad, part_a, part_b, s_in[...], gain, sums_ref)
            g_ref[...] = grad
            low = grad.astype(BF16)
            g_own[...] = low[:, :half]
            put_rear(rear_refs, 0, low[:, half:])
            grad_mixed = project_back(low, wp_a[1], wp_b[1]).astype(BF16)
            packed = attention_part_back(
                False, grad_mixed, mask_ref, qkv_ref, probs_ref, rear_refs
            )
            own, oth = qkv_back(packed, 1, wq_a, wq_b)
            part_ref[:, :half] = own.astype(BF16)
            part_ref[:, half:] = oth.astype(BF16)

        late = [*fore3[0], *wd, s5]
        (g2, g2_own, back2, sums3, *rear2) = call(
            channel_back_body, "back_c",
            [g3_own, g3_oth, s5, *small, mask, qkv2, probs2, *wp, *wq, back3, far_back3],
            [full, half_low, full_low, sds((2, width)), *rear_shapes(rear_width_attn, 1)],
            flops=attn_flops,
            hold=[*keep_a, *keep_b, s3, s4, n2_own, *fore2[0], *fore2[1], *wu, *wd, *fore3[0]],
        )
        far_back2 = over_ha(back2)
        rear2 = both_rear(rear2, False)
        hid_got, fore0_got = (
            lax.all_gather(later(values, g2), "wa") for values in (fore1[1], fore0)
        )
        fore1, fore0 = (fore1, [n1_got, hid_got]), ([fore0], [fore0_got])
        keep_a.append(fore0_got)
        keep_b.append(hid_got)
        streams_c = attn_streams(SPLIT_C, 2)
        kept_c = [*keep_a, *keep_b, s3, s4, *small, *weights, g2, *late, sums3]
        make("wgrad_c", write_attn, streams_c, n2_own, g2_own, fore2, rear2, kept_c)
        slot(
            "slot_c", fresh=streams_c, moving=streams_d, hold=[*kept_c, back2, far_back2],
        )

        def mlp_back_body(
            g_in, part_a, part_b, s_in, s_before, small_a, small_b, slope_ref,
            wd_a, wd_b, wu_a, wu_b, g_ref, g_own, part_ref, sums_ref, *rear_refs,
        ):
            keep = column_mask(rows)
            gain = gain_row((small_a, small_b), 2)
            grad = add_norm_back(g_in[...], part_a, part_b, s_in[...], gain, sums_ref)
            conv_back_into(g_ref, sums_ref, 2, grad, s_before[...], (small_a, small_b), 1, keep)
            low = g_ref[...].astype(BF16)
            g_own[...] = low[:, :half]
            put_rear(rear_refs, 0, low[:, half:])
            dhid = project_back(low, wd_a[0], wd_b[0]).astype(BF16).astype(F32)
            dpre = (dhid * slope_ref[...]).astype(BF16)
            put_rear(rear_refs, half, dpre)
            part_ref[:, :half] = mm(dpre, wu_a[0], 1, 1).astype(BF16)
            part_ref[:, half:] = mm(dpre, wu_b[0], 1, 1).astype(BF16)

        (g1, g1_own, back1, sums2, *rear1) = call(
            mlp_back_body, "back_b",
            [g2, back2, far_back2, s4, s3, *small, slope1, *wd, *wu],
            [full, half_low, full_low, sds((11, width)), *rear_shapes(rear_width_mlp, 2)],
            flops=mlp_flops,
            hold=[*keep_a, s2, n1_own, *fore1[0], *fore1[1], *wq, *wp, *fore3[0], s5, sums3],
        )
        far_back1 = over_ha(back1)
        rear1 = both_rear(rear1)
        streams_b = mlp_streams(SPLIT_B, 0)
        make(
            "wgrad_b", write_mlp, streams_b, n1_own, g1_own, fore1, rear1,
            [*keep_a, s2, *small, *wq, *wp, g1, *late, sums3, sums2],
        )
        send_first(streams_b)

        def window_back_body(
            g_in, part_a, part_b, s_in, small_a, small_b, qkv_ref, probs_ref, wp_a, wp_b,
            g_ref, g_own, sums_ref, *rear_refs,
        ):
            gain = gain_row((small_a, small_b), 1)
            grad = add_norm_back(g_in[...], part_a, part_b, s_in[...], gain, sums_ref)
            g_ref[...] = grad
            low = grad.astype(BF16)
            g_own[...] = low[:, :half]
            put_rear(rear_refs, 0, low[:, half:])
            grad_mixed = project_back(low, wp_a[0], wp_b[0]).astype(BF16)
            attention_part_back(True, grad_mixed, None, qkv_ref, probs_ref, rear_refs)

        (g0, g0_own, sums1, *rear0) = call(
            window_back_body, "back_a",
            [g1, back1, far_back1, s2, *small, qkv0, probs0, *wp],
            [full, half_low, sds((2, width)), *rear_shapes(rear_width_attn, 1)],
            flops=attn_flops, hold=[x0, n0_own, *fore0[0], *fore0[1], s1, *wq, *late, sums3, sums2],
        )
        every = [*streams_d, *streams_c]
        depart = prepare_slot(
            "slot_cd", moving=every, spare=(2, 16),
            hold=[x0, n0_own, *fore0[0], *fore0[1], s1, *small, *wq, *late, sums1, sums2, sums3,
                  g0, g0_own, *rear0],
        )
        rear0 = both_rear(later(rear0, streams_d[0].kept))

        keep_0 = [g0, s1, x0, *small, *wq, sums1, sums2, sums3, *rear0[0]]
        streams_a = attn_streams(SPLIT_A, 0)
        make("wgrad_a", write_attn, streams_a, n0_own, g0_own, fore0, rear0, [*late, *keep_0])
        every = [*streams_d, *streams_c, *streams_b, *streams_a]
        send_first(streams_a)
        depart()

        sums_at = -(-rows_in // 16) * 16
        sums_half = sds((sum_rows, half))
        with_sums = sds((sums_at + sum_rows, half), BF16)

        def put_sums(ref, total):
            ref[sums_at:, :] = total.astype(BF16)

        def first_back_body(
            g_in, s_in, x_ref, small_a, small_b, wq_a, wq_b, sums_one, sums_two, sums_three, *refs
        ):
            rear_refs, (kept, sent, sums_own, scratch, sums_ref) = refs[:-5], refs[-5:]
            keep = column_mask(rows)
            packed = [
                get_rear(rear_refs, half + part * heads_width, heads_width) for part in range(3)
            ]
            upstream = jnp.concatenate(qkv_back(packed, 0, wq_a, wq_b), axis=1)
            units, inv_std = norm_stats(s_in[...])
            sums_ref[0:1, :] = jnp.sum(upstream * units, axis=0, keepdims=True)
            sums_ref[1:2, :] = jnp.sum(upstream, axis=0, keepdims=True)
            grad = jnp.where(here("ha") == 0, g_in[...], 0.0)
            grad = grad + norm_back(upstream, units, inv_std, gain_row((small_a, small_b), 0))
            conv_back_into(
                scratch, sums_ref, 2, grad, x_ref[...].astype(F32), (small_a, small_b), 0, keep
            )
            ship(scratch[...], kept, sent)
            sums_ref[11:13, :] = 0.5 * sums_one[...]
            sums_ref[13:24, :] = 0.5 * sums_two[...]
            sums_ref[24:26, :] = 0.5 * sums_three[...]
            sums_ref[26:, :] = jnp.zeros((sum_rows - 26, width), F32)
            sums_own[...] = sums_ref[:, :half]
            put_sums(sent, sums_ref[:, half:])

        token_kept, token_sent, sums_own = call(
            first_back_body, "back_0",
            [g0, s1, x0, *small, *wq, sums1, sums2, sums3, *rear0[0]],
            [shipped[0], with_sums, sums_half],
            scratch=[pltpu.VMEM((rows, width), F32), pltpu.VMEM((sum_rows, width), F32)],
            flops=attn_flops * 3 // 4, hold=late,
        )

        def fold_tokens(kept, both, sums_a, stay, go, sums_ref):
            received = other_core(both)
            fold(kept, received, stay, go)
            total = sums_a[...] + sums_in(received, sums_at)
            put_sums(go, total)
            sums_ref[...] = sums_in(go, sums_at)

        token_stay, token_go, sums_chip = call(
            fold_tokens, "fold_tokens",
            [token_kept, lax.all_gather(token_sent, "wa"), sums_own],
            [shipped[0], with_sums, sums_half], hold=late,
        )
        token_got = over_ha(token_go)

        def join_tokens(stay, received, sums_chip, out_ref, sums_ref):
            join(stay, received, out_ref)
            sums_ref[...] = sums_chip[...] + sums_in(received, sums_at)

        owned = sds((rows_in, half))
        grad_tokens, sums_ha = call(
            join_tokens, "join_tokens", [token_stay, token_got, sums_chip], [owned, sums_half],
            hold=late,
        )
        left_bits = list(range(bits))
        sums = [sums_ha, None, 0, left_bits.pop(0)]
        slot("sums_x", sums=sums, spare=(0, 96), hold=late)
        out_kept, out_sent = call(
            out_body, "out_d", [s5, *fore3[0], *wd], shipped, flops=mlp_flops // 2
        )
        out_both = lax.all_gather(out_sent, "wa")

        def hop():
            if not left_bits:
                return None
            sums[3] = left_bits.pop(0)
            return sums

        turn = 0
        while left_bits or any(stream.step < bits for stream in every):
            turn += 1
            arrived = [s for s in every if s.step == bits and s.final is None]
            slot(f"slot_b{turn}", moving=[s for s in streams_b if s.step < bits])
            second = [s for s in [*streams_d, *streams_a] if s.step < bits]
            slot(f"slot_a{turn}", moving=second, ending=arrived, sums=hop())
            if turn > 1:
                slot(f"slot_c{turn}", moving=[s for s in streams_c if s.step < bits])
            if turn == 1:
                out_stay, out_go = call(
                    lambda kept, both, *refs: fold(kept, other_core(both), *refs),
                    "fold_out", [out_kept, out_both], shipped,
                )
                out_got = over_ha(out_go)
        output = call(join, "join_out", [out_stay, out_got], [owned])[0]

        def finish_body(*refs):
            (up, down, qkv, proj, taps_ref, gain_ref, shift_ref) = refs[-7:]
            at = iter(refs)
            total = next(at)[...] + sums_in(next(at), sums[2])
            for branch, row in enumerate((0, 11, 13, 24)):
                gain_ref[branch : branch + 1, :] = total[row : row + 1]
                shift_ref[branch : branch + 1, :] = total[row + 1 : row + 2]
            for section, row in enumerate((2, 15)):
                for t in range(9):
                    taps_ref[t, section : section + 1, :] = total[row + t : row + t + 1]

            def finished(stream):
                if stream.final is not None:
                    return next(at)[...]
                return last_sum(stream, next(at), next(at))

            for section, streams in enumerate(
                ((*streams_a, *streams_b), (*streams_c, *streams_d))
            ):
                for stream in streams:
                    values, row = finished(stream), 0
                    for piece in stream.pieces:
                        part = values[row : row + piece_rows(piece)]
                        row += piece_rows(piece)
                        if piece == "up":
                            up[section] = part
                        elif piece == "proj":
                            proj[section] = part
                        elif isinstance(piece, tuple):
                            down[section, :, piece[1] * half : (piece[1] + 1) * half] = part
                        else:
                            qkv[section, ("q", "k", "v").index(piece)] = part

        ends = []
        for stream in (*streams_a, *streams_b, *streams_c, *streams_d):
            ends += [stream.kept, stream.got] if stream.final is None else [stream.final]
        up, down, qkv, proj, grad_taps, grad_gain, grad_shift = call(
            finish_body, "finish", [*sums[:2], *ends],
            [sds((2, up_rows, half)), sds((2, down_rows, hidden)), sds((2, 3, qkv_rows, half)),
             sds((2, proj_rows, half)), sds((9, 2, half)), sds((4, half)), sds((4, half))],
        )
        grad_taps = jnp.transpose(grad_taps, (1, 0, 2))
        grad_qkv = jnp.transpose(qkv, (0, 3, 1, 2))
        grad_proj, grad_up, grad_down = (
            jnp.transpose(values, (0, 2, 1)) for values in (proj, up, down)
        )
        return (
            output,
            grad_tokens,
            grad_taps,
            grad_gain,
            grad_shift,
            grad_qkv,
            grad_proj,
            grad_up,
            grad_down,
        )

    placed = (
        P(("dev", "ha"), "wa"),
        P(("dev", "ha"), "wa"),
        P(None, None, "wa"),
        P(None, "wa"),
        P(None, "wa"),
        P(None, "wa", None, "ha"),
        P(None, "ha", "wa"),
        P(None, "wa", "ha"),
        P(None, "ha", "wa"),
        P("dev", None),
    )
    return jax.shard_map(
        on_device,
        mesh=mesh,
        in_specs=placed,
        out_specs=(
            P(("dev", "ha"), "wa"),
            P(("dev", "ha"), "wa"),
            P(None, None, "wa"),
            P(None, "wa"),
            P(None, "wa"),
            P(None, "wa", None, ("ha", "dev")),
            P(None, "ha", ("wa", "dev")),
            P(None, "wa", ("ha", "dev")),
            P(None, "ha", ("wa", "dev")),
        ),
        check_vma=False,
    )
```

```python
from functools import partial

import jax
import jax.numpy as jnp
import numpy as np
from jax import lax
from jax.experimental import pallas as pl
from jax.experimental.pallas import tpu as pltpu
from jax.sharding import PartitionSpec as P

WIN = 7
GRID_COLS = 8
PATCHES = 49
PADDED = WIN * GRID_COLS
HEAD_DIM = 32
LANES = 128
HEADS_TILE = LANES // HEAD_DIM
EPS = 1e-05
NEG = -1e30
SPLIT_D, SPLIT_C, SPLIT_B, SPLIT_A = 0, 2, 0, 4
BF16 = jnp.bfloat16
F32 = jnp.float32
VMEM_LIMIT = 16 * 2**20
TIMES = {"pack_small": 5.0, "choose": 5.0}


def mm(left, right, left_dim, right_dim):
    return lax.dot_general(
        left, right, (((left_dim,), (right_dim,)), ((), ())), preferred_element_type=F32
    )


class Order:
    def __init__(self):
        self.last = None


def kernel_call(
    body, name, ins, outs, order, scratch=(), flops=0, hold=(), reuse=None, carry=None
):
    reuse = reuse or {}
    arrays = list(ins) + list(hold) + ([] if order.last is None else [order.last])
    first_reused = len(arrays)
    aliases = {first_reused + at: out for at, out in enumerate(reuse)}
    arrays += list(reuse.values())
    outs = list(outs) + [sds((8, LANES))]

    def wrapped(*refs):
        out_refs = refs[len(arrays) : len(arrays) + len(outs)]
        for at, out in aliases.items():
            carry(refs[at], out_refs[out])
        body(*refs[: len(ins)], *out_refs[:-1], *refs[len(arrays) + len(outs) :])
        out_refs[-1][...] = jnp.zeros_like(out_refs[-1])

    *results, order.last = pl.pallas_call(
        wrapped,
        in_specs=[pl.BlockSpec(memory_space=pltpu.VMEM)] * len(arrays),
        out_specs=[pl.BlockSpec(memory_space=pltpu.VMEM)] * len(outs),
        out_shape=outs,
        scratch_shapes=list(scratch),
        input_output_aliases=aliases,
        compiler_params=pltpu.CompilerParams(vmem_limit_bytes=VMEM_LIMIT),
        cost_estimate=pl.CostEstimate(
            flops=int(TIMES.get(name, 0) * 1.15e9), bytes_accessed=0, transcendentals=0
        ),
        name=name,
    )(*arrays)
    return results


def sds(shape, dtype=F32):
    return jax.ShapeDtypeStruct(shape, dtype)


def column_mask(rows):
    return (lax.broadcasted_iota(jnp.int32, (rows, 1), 0) % GRID_COLS) < WIN


def placement(images, transposed, begin=0, count=None):
    padded, plain = count or images * PADDED, images * PATCHES
    shape = (plain, padded) if transposed else (padded, plain)
    at = lax.broadcasted_iota(jnp.int32, shape, 1 if transposed else 0) + begin
    image = sum((at >= i * PADDED).astype(jnp.int32) for i in range(1, images))
    inside = at - image * PADDED
    source = image * PATCHES + (inside >> 3) * WIN + (inside & 7)
    other = lax.broadcasted_iota(jnp.int32, shape, 0 if transposed else 1)
    return (((inside & 7) < WIN) & (source == other)).astype(F32).astype(BF16)


def side_shifts(values):
    rows = values.shape[0]
    return (pltpu.roll(values, 1, 0), values, pltpu.roll(values, rows - 1, 0))


def as_grid(values):
    return values.reshape(-1, WIN, GRID_COLS, values.shape[-1])


def move_rows(values, step):
    grid = as_grid(values)
    zeros = jnp.zeros_like(grid[:, :1])
    if step > 0:
        moved = jnp.concatenate([zeros, grid[:, :-1]], axis=1)
    else:
        moved = jnp.concatenate([grid[:, 1:], zeros], axis=1)
    return moved.reshape(values.shape)


def conv_cols(values, taps, keep):
    shifted = side_shifts(values)
    line = [
        sum(shifted[col] * taps[3 * row + col] for col in range(3)) for row in range(3)
    ]
    total = values + line[1] + move_rows(line[0], 1) + move_rows(line[2], -1)
    return jnp.where(keep, total, 0.0)


def tap_sums(grads, values):
    shifted = side_shifts(values)
    grad_grid = as_grid(grads)
    sums = []
    for row in range(3):
        for col in range(3):
            moved = as_grid(shifted[col])
            if row == 0:
                prod = grad_grid[:, 1:] * moved[:, :-1]
            elif row == 1:
                prod = grad_grid * moved
            else:
                prod = grad_grid[:, :-1] * moved[:, 1:]
            flat = prod.reshape(-1, GRID_COLS, prod.shape[-1])
            sums.append(jnp.sum(jnp.sum(flat, axis=0), axis=0, keepdims=True))
    return sums


def norm_stats(stream):
    width = stream.shape[1]
    center = jnp.sum(stream, axis=1, keepdims=True) * (1.0 / width)
    moved = stream - center
    inv_std = lax.rsqrt(jnp.sum(moved * moved, axis=1, keepdims=True) * (1.0 / width) + EPS)
    return moved * inv_std, inv_std


def norm_back(upstream, units, inv_std, gain):
    width = upstream.shape[1]
    scaled = upstream * gain
    first = jnp.sum(scaled, axis=1, keepdims=True) * (1.0 / width)
    second = jnp.sum(scaled * units, axis=1, keepdims=True) * (1.0 / width)
    return inv_std * (scaled - first - units * second)


def gelu_parts(values):
    below = 0.5 + 0.5 * lax.erf(values * float(0.5**0.5))
    bell = jnp.exp2(values * values * float(-0.5 * np.log2(np.e)))
    return below, bell * float(1.0 / np.sqrt(2.0 * np.pi))


def head_mask(index):
    return (lax.broadcasted_iota(jnp.int32, (1, LANES), 1) // HEAD_DIM) == index


def spread_heads(tile):
    return jnp.concatenate(
        [jnp.where(head_mask(j), tile, 0.0) for j in range(HEADS_TILE)], axis=0
    ).astype(BF16)


def gather_heads(stacked):
    rows = stacked.shape[0] // HEADS_TILE
    total = jnp.where(head_mask(0), stacked[:rows], 0.0)
    for j in range(1, HEADS_TILE):
        total = jnp.where(head_mask(j), stacked[j * rows : (j + 1) * rows], total)
    return total


def softmax_rows(scores):
    top = jnp.max(scores, axis=0, keepdims=True)
    weights = jnp.exp(scores - top)
    return weights * (1.0 / jnp.sum(weights, axis=0, keepdims=True))


SCALE = HEAD_DIM**-0.5


def low(tiles):
    return [tile.astype(BF16) for tile in tiles]


def minus_row_sums(probs, grads):
    return [
        (p * (g - jnp.sum(g * p, axis=0, keepdims=True))).astype(BF16)
        for p, g in zip(probs, grads)
    ]


def window_tiles(queries, keys, values):
    keys_ok = column_mask(PADDED)
    scores = [
        mm(k, spread_heads(q), 1, 1) * SCALE for q, k in zip(queries, low(keys))
    ]
    probs = [softmax_rows(jnp.where(keys_ok, score, NEG)) for score in scores]
    mixed = [mm(p, v, 0, 0) for p, v in zip(low(probs), low(values))]
    return probs, [gather_heads(tile) for tile in mixed]


def window_tiles_back(queries, keys, values, probs, grads):
    q_big, g_big = ([spread_heads(tile) for tile in tiles] for tiles in (queries, grads))
    grad_probs = [mm(v, g, 1, 1) for v, g in zip(low(values), g_big)]
    grad_v = [mm(p, g, 1, 0) for p, g in zip(low(probs), g_big)]
    grad_scores = minus_row_sums(probs, grad_probs)
    grad_k = [mm(d, q, 1, 0) * SCALE for d, q in zip(grad_scores, q_big)]
    grad_q = [mm(d, k, 0, 0) for d, k in zip(grad_scores, low(keys))]
    return [gather_heads(tile) * SCALE for tile in grad_q], grad_k, grad_v


def same_head():
    first = lax.broadcasted_iota(jnp.int32, (LANES, LANES), 0) // HEAD_DIM
    second = lax.broadcasted_iota(jnp.int32, (LANES, LANES), 1) // HEAD_DIM
    return first == second


def channel_tiles(queries, keys, values, masks):
    own_head = same_head()
    masked = low([q * mask for q, mask in zip(queries, masks)])
    scores = [mm(k, q, 0, 0) * SCALE for q, k in zip(masked, low(keys))]
    probs = [softmax_rows(jnp.where(own_head, score, NEG)) for score in scores]
    return probs, [mm(v, p, 1, 0) for p, v in zip(low(probs), low(values))]


def channel_tiles_back(queries, keys, values, probs, grads, masks):
    masked = low([q * mask for q, mask in zip(queries, masks)])
    grads = low(grads)
    grad_probs = [mm(v, g, 0, 0) for v, g in zip(low(values), grads)]
    grad_v = [mm(g, p, 1, 1) for g, p in zip(grads, low(probs))]
    grad_scores = minus_row_sums(probs, grad_probs)
    grad_q = [mm(k, d, 1, 0) * SCALE * m for k, d, m in zip(low(keys), grad_scores, masks)]
    grad_k = [mm(q, d, 1, 1) * SCALE for q, d in zip(masked, grad_scores)]
    return grad_q, grad_k, grad_v


def cut_tiles(values, images, tiles):
    return [
        values[image * PADDED : (image + 1) * PADDED, tile * LANES : (tile + 1) * LANES]
        for image in range(images)
        for tile in range(tiles)
    ]


def paste_tiles(parts, images, tiles):
    lines = [
        jnp.concatenate(parts[image * tiles : (image + 1) * tiles], axis=1)
        for image in range(images)
    ]
    return jnp.concatenate(lines, axis=0).astype(BF16)


def solution(mesh):
    n_dev = mesh.shape["dev"]
    bits = n_dev.bit_length() - 1
    assert n_dev == 1 << bits and mesh.shape["ha"] == 2 and mesh.shape["wa"] == 2

    swap = [(0, 1), (1, 0)]

    def over_ha(values):
        return lax.ppermute(values, "ha", swap)

    def over_wa(values):
        return lax.ppermute(values, "wa", swap)

    partner = [1 << bit for bit in range(bits)]
    if bits > 2:
        partner[2] = 6

    def over_dev(values, bit):
        return lax.ppermute(values, "dev", [(i, i ^ partner[bit]) for i in range(n_dev)])

    def on_device(
        tokens, cotangent, conv_taps, norm_gain, norm_shift, w_qkv, w_proj, w_up, w_down, valid
    ):
        rows_in, half = tokens.shape
        images = rows_in // PATCHES
        rows = images * PADDED
        width = 2 * half
        heads_width = w_qkv.shape[3]
        hidden = w_up.shape[2]
        tiles = heads_width // LANES
        assert heads_width == half
        rest = list(range(3, bits))
        orders = [[0, 1, 2, *rest], [1, 0, 2, *rest], [0, 2, 1, *rest], [1, 2, 0, *rest]]

        def here(name):
            return lax.axis_index(name)

        def chunk_at(place, which):
            found = 0
            for step, bit in enumerate(orders[which]):
                found ^= ((place >> (bits - 1 - step)) & 1) * partner[bit]
            return found ^ here("dev")

        order = Order()
        call = partial(kernel_call, order=order)

        def later(values, event):
            return lax.optimization_barrier((values, event))[0]

        def pack_small(taps_ref, gain_ref, shift_ref, out_ref):
            for section in range(2):
                for t in range(9):
                    at = 9 * section + t
                    out_ref[at : at + 1, :] = taps_ref[t, section : section + 1, :]
            out_ref[18:22, :] = gain_ref[...]
            out_ref[22:26, :] = shift_ref[...]

        def choose(mine, received, own, *others):
            same = here("ha") == here("wa")
            own[...] = jnp.where(same, mine[...], received[...])
            other, at = jnp.where(same, received[...], mine[...]), 0
            for ref in others:
                ref[...] = other[:, at : at + ref.shape[1]]
                at += ref.shape[1]

        wq_own = jnp.transpose(w_qkv, (0, 2, 1, 3))
        wq, wp = (wq_own, over_wa(wq_own)), (w_proj, over_wa(w_proj))
        tokens_in, cot_in = over_ha(tokens), over_ha(cotangent)
        small_own = call(
            pack_small, "pack_small",
            [jnp.transpose(conv_taps, (1, 0, 2)), norm_gain, norm_shift], [sds((26, half))],
            hold=[tokens],
        )[0]
        small = (small_own, over_wa(small_own))
        chosen = [sds((rows_in, columns), BF16) for columns in (half, LANES, half - LANES)]
        tokens_own, *tokens_oth = call(
            choose, "choose", [tokens, tokens_in], chosen, hold=[wq[1], wp[1], small_own]
        )
        token_parts = (tokens_own, *[over_wa(values) for values in tokens_oth])

        def arrive(out_ref):
            out_ref[...] = jnp.zeros_like(out_ref)

        arrived = call(
            arrive, "arrive", [], [sds((8, LANES))],
            hold=[*token_parts, small[1], cot_in, small_own, wq[1], wp[1]],
        )[0]
        wu, wd = ((values, over_wa(later(values, arrived))) for values in (w_up, w_down))

        def unpack(parts, begin=0, count=None):
            values = jnp.concatenate([part[...] for part in parts], axis=1)
            return mm(placement(images, False, begin, count), values, 1, 0)

        def gain_row(refs, branch):
            return jnp.concatenate([ref[18 + branch : 19 + branch, :] for ref in refs], axis=1)

        def shift_row(refs, branch):
            return jnp.concatenate([ref[22 + branch : 23 + branch, :] for ref in refs], axis=1)

        def tap_rows(small_refs, section, col, flipped):
            ref = small_refs[col // half]
            at = col % half
            found = [
                ref[9 * section + t : 9 * section + t + 1, at : at + LANES] for t in range(9)
            ]
            return found[::-1] if flipped else found

        def project_in(normed, first, second):
            return mm(normed[:, :half], first, 1, 0) + mm(normed[:, half:], second, 1, 0)

        def project_back(values, first, second):
            return mm(values[:, :half], first, 1, 1) + mm(values[:, half:], second, 1, 1)

        def to_normed(stream, small_refs, branch):
            units, _ = norm_stats(stream)
            return (units * gain_row(small_refs, branch) + shift_row(small_refs, branch)).astype(
                BF16
            )

        def both_rear(pieces, gather=True):
            pieces = list(pieces)
            if gather:
                return pieces, [lax.all_gather(piece, "wa") for piece in pieces]
            return pieces, [over_wa(piece) for piece in pieces]

        def other_core(ref):
            return ref.at[1 - here("wa")] if len(ref.shape) == 3 else ref

        def put_both(own_ref, oth_ref, values):
            own_ref[...] = values[:, :half]
            oth_ref[:, :half] = values[:, half:]

        def add_parts(stream, part_a, part_b):
            return stream + part_a[...].astype(F32) + part_b[...].astype(F32)

        def attention_part(
            window, section, normed, valid_rows, wq_a, wq_b, qkv_ref, probs_ref, first_image
        ):
            count = normed.shape[0] // PADDED
            packed = [
                project_in(normed, wq_a[section, part], wq_b[section, part]).astype(BF16)
                for part in range(3)
            ]
            begin = first_image * PADDED
            for part in range(3):
                qkv_ref[part, begin : begin + count * PADDED, :] = packed[part]
            q, k, v = (cut_tiles(part.astype(F32), count, tiles) for part in packed)
            if window:
                probs, mixed = window_tiles(q, k, v)
            else:
                masks = [mask for mask in valid_rows for _ in range(tiles)]
                probs, mixed = channel_tiles(q, k, v, masks)
            for at, tile in enumerate(probs):
                probs_ref[first_image * tiles + at] = tile
            return paste_tiles(mixed, count, tiles)

        def attention_part_back(window, grad_mixed, mask_ref, qkv_ref, probs_ref, rear_refs):
            q, k, v = (
                cut_tiles(qkv_ref[part].astype(F32), images, tiles) for part in range(3)
            )
            grads = cut_tiles(grad_mixed.astype(F32), images, tiles)
            probs = [probs_ref[at] for at in range(images * tiles)]
            if window:
                found = window_tiles_back(q, k, v, probs, grads)
            else:
                masks = [
                    mask_ref[image * PADDED : (image + 1) * PADDED, :]
                    for image in range(images)
                    for _ in range(tiles)
                ]
                found = channel_tiles_back(q, k, v, probs, grads, masks)
            packed = [paste_tiles(part, images, tiles) for part in found]
            for part in range(3):
                put_rear(rear_refs, half + part * heads_width, packed[part])
            return packed

        def mul_out(left, section, own_ref, oth_ref, out_ref):
            out_ref[:, :half] = mm(left, own_ref[section], 1, 0).astype(BF16)
            out_ref[:, half:] = mm(left, oth_ref[section], 1, 0).astype(BF16)

        def conv_into(out_ref, rows_at, values, small_refs, section, keep):
            for col in range(0, width, LANES):
                taps = tap_rows(small_refs, section, col, False)
                out_ref[rows_at, col : col + LANES] = conv_cols(
                    values[:, col : col + LANES], taps, keep
                )

        def conv_back_into(out_ref, sums_ref, sums_at, grads, values, small_refs, section, keep):
            for col in range(0, width, LANES):
                lanes_at = slice(col, col + LANES)
                taps = tap_rows(small_refs, section, col, True)
                for t, total in enumerate(tap_sums(grads[:, lanes_at], values[:, lanes_at])):
                    sums_ref[sums_at + t : sums_at + t + 1, lanes_at] = total
                out_ref[:, lanes_at] = conv_cols(grads[:, lanes_at], taps, keep)

        window_probs = sds((images * tiles, PADDED, HEADS_TILE * PADDED))
        channel_probs = sds((images * tiles, LANES, LANES))
        full, full_low = sds((rows, width)), sds((rows, width), BF16)
        half_low = sds((rows, half), BF16)
        hid_low = sds((rows, hidden), BF16)
        qkv_low = sds((3, rows, heads_width), BF16)
        fore_attn = sds((rows, half + heads_width), BF16)
        def cuts(total, count):
            tiles_all = total // LANES
            return [LANES * (-(-tiles_all * (at + 1) // count)) for at in range(count)]

        def rear_shapes(total, count):
            ends = cuts(total, count)
            return [sds((rows, e - b), BF16) for b, e in zip([0, *ends], ends)]

        def rear_ranges(refs, at, size):
            begin = 0
            for ref in refs:
                end = begin + ref.shape[1]
                low, high = max(begin, at), min(end, at + size)
                if low < high:
                    yield ref, low - begin, high - begin, low - at
                begin = end

        def put_rear(refs, at, values, span=slice(None)):
            for ref, low, high, source in rear_ranges(refs, at, values.shape[1]):
                ref[span, low:high] = values[:, source : source + high - low]

        def get_rear(refs, at, size):
            parts = [ref[:, low:high] for ref, low, high, _ in rear_ranges(refs, at, size)]
            return parts[0] if len(parts) == 1 else jnp.concatenate(parts, axis=1)

        rear_width_attn, rear_width_mlp = half + 3 * heads_width, half + hidden
        fore_mlp = sds((rows, rear_width_mlp), BF16)
        attn_flops = 2 * rows * (4 * width * heads_width)
        mlp_flops = 2 * rows * (2 * width * hidden)

        split = (images + 1) // 2
        chunks = [(0, split), (split, images)] if split < images else [(0, images)]
        spans = [slice(begin * PADDED, end * PADDED) for begin, end in chunks]

        def chunk_rows(span):
            return span.stop - span.start

        def part_shape(span):
            return sds((chunk_rows(span), width), BF16)

        def put_normed(own_ref, fore_refs, span, normed):
            own_ref[span, :] = normed[:, :half]
            put_rear(fore_refs, 0, normed[:, half:], span)

        def first_body(chunk, span):
            def body(
                tokens_a, tokens_b, tokens_c, small_a, small_b, wq_a, wq_b, wp_a, wp_b,
                x_ref, s_ref, n_own, fore_ref, qkv_ref, probs_ref, part_ref, *copies,
            ):
                if copies:
                    copies[0][...], copies[1][...] = small_a[...], small_b[...]
                keep = column_mask(chunk_rows(span))
                stream = unpack((tokens_a, tokens_b, tokens_c), span.start, chunk_rows(span))
                x_ref[span, :] = stream.astype(BF16)
                conv_into(s_ref, span, stream, (small_a, small_b), 0, keep)
                normed = to_normed(s_ref[span, :], (small_a, small_b), 0)
                put_normed(n_own, [fore_ref], span, normed)
                mixed = attention_part(
                    True, 0, normed, None, wq_a, wq_b, qkv_ref, probs_ref, chunk[0]
                )
                fore_ref[span, half:] = mixed
                mul_out(mixed, 0, wp_a, wp_b, part_ref)

            return body

        def carry_spans(upto):
            def carry(old, new):
                for chunk, span in zip(chunks[:upto], spans[:upto]):
                    if old.shape[0] == rows:
                        new[span, :] = old[span, :]
                    elif old.shape[1] == rows:
                        new[:, span, :] = old[:, span, :]
                    else:
                        per_image = old.shape[0] // images
                        held = slice(chunk[0] * per_image, chunk[1] * per_image)
                        new[held] = old[held]

            return carry

        def in_chunks(
            name, make_body, ins, shapes, hold, extra=(), between=None, alone=True
        ):
            arrays, parts, fars, more = None, [], [], []
            for at, (chunk, span) in enumerate(zip(chunks, spans)):
                results = call(
                    make_body(chunk, span), f"{name}{at}", ins(at),
                    [*shapes, *([part_shape(span)] if alone else ()), *(extra if at == 0 else ())],
                    hold=[*hold, *more, *parts],
                    reuse=None if arrays is None else dict(enumerate(arrays)),
                    carry=carry_spans(at),
                )
                arrays, rest = results[: len(shapes)], results[len(shapes) :]
                if alone:
                    parts.append(rest[0])
                    fars.append(over_ha(rest[0]))
                more = more or rest[1:]
                if at == 0 and between is not None:
                    between(arrays, more)
            return arrays, parts, fars, more

        small_in, cot_parts = small, []

        def choose_cot(arrays, more):
            own, *others = call(
                choose, "choose_cot", [cotangent, cot_in], chosen,
                hold=[*arrays, *more, *wq, *wp],
            )
            cot_parts.extend([own, *others])

        (x0, s1, n0_own, fore0, qkv0, probs0), part0, far0, small = in_chunks(
            "attn_a", first_body, lambda at: [*token_parts, *small_in, *wq, *wp],
            [full_low, full, half_low, fore_attn, qkv_low, window_probs], [cot_in, arrived],
            [sds((26, half))] * 2, choose_cot,
        )
        keep_a = [x0, n0_own, fore0, qkv0, probs0, s1]

        def mlp_body(chunk, span):
            def body(
                s_in, part_a, part_b, small_a, small_b, wu_a, wu_b, wd_a, wd_b,
                s_ref, n_own, slope_ref, *refs,
            ):
                *fore_refs, part_ref = refs
                s_ref[span, :] = add_parts(s_in[span, :], part_a, part_b)
                normed = to_normed(s_ref[span, :], (small_a, small_b), 1)
                put_normed(n_own, fore_refs, span, normed)
                pre = project_in(normed, wu_a[0], wu_b[0])
                below, bell = gelu_parts(pre)
                hid = (pre * below).astype(BF16)
                put_rear(fore_refs, half, hid, span)
                slope_ref[span, :] = below + pre * bell
                mul_out(hid, 0, wd_a, wd_b, part_ref)

            return body

        (s2, n1_own, slope1, *fore1), part1, far1, _ = in_chunks(
            "mlp_b", mlp_body, lambda at: [s1, part0[at], far0[at], *small, *wu, *wd],
            [full, half_low, sds((rows, hidden)), half_low, hid_low],
            [*keep_a, *wq, *wp, *cot_parts],
        )
        n1_got = over_wa(fore1[0])
        cot_parts[1:] = [over_wa(later(values, part1[0])) for values in cot_parts[1:]]
        keep_b = [s2, n1_own, *fore1, slope1, n1_got]
        weights = [*wq, *wp, *wu, *wd]

        def channel_body(chunk, span):
            def body(
                s_in, part_a, part_b, valid_ref, small_a, small_b, wq_a, wq_b, wp_a, wp_b,
                s_before, s_ref, n_own, qkv_ref, probs_ref, mask_ref, *refs,
            ):
                *fore_refs, part_ref = refs
                keep = column_mask(chunk_rows(span))
                stream = jnp.where(keep, add_parts(s_in[span, :], part_a, part_b), 0.0)
                s_before[span, :] = stream
                conv_into(s_ref, span, stream, (small_a, small_b), 1, keep)
                normed = to_normed(s_ref[span, :], (small_a, small_b), 2)
                put_normed(n_own, fore_refs, span, normed)
                one_image = placement(1, False).astype(F32)
                valid_rows = []
                for image in range(*chunk):
                    line = jnp.where(
                        here("wa") == 0,
                        valid_ref[image : image + 1, :],
                        valid_ref[images + image : images + image + 1, :],
                    ).astype(F32)
                    valid_rows.append(jnp.sum(one_image * line, axis=1, keepdims=True))
                    mask_ref[image * PADDED : (image + 1) * PADDED, :] = valid_rows[-1]
                mixed = attention_part(
                    False, 1, normed, valid_rows, wq_a, wq_b, qkv_ref, probs_ref, chunk[0]
                )
                put_rear(fore_refs, half, mixed, span)
                mul_out(mixed, 1, wp_a, wp_b, part_ref)

            return body

        (s3, s4, n2_own, qkv2, probs2, mask, *fore2), part2, far2, _ = in_chunks(
            "attn_c", channel_body,
            lambda at: [s2, part1[at], far1[at], valid, *small, *wq, *wp],
            [full, full, half_low, qkv_low, channel_probs, sds((rows, 1)), half_low, half_low],
            [*keep_a, *keep_b, *wu, *wd, *cot_parts],
        )
        fore2 = both_rear(fore2, False)
        keep_c = [s3, s4, n2_own, *fore2[0], qkv2, probs2, mask]

        def cot_body(cot_a, cot_b, cot_c, wd_a, wd_b, g_own, g_oth, dhid_ref):
            grad = unpack((cot_a, cot_b, cot_c)).astype(BF16)
            put_both(g_own, g_oth, grad)
            dhid_ref[...] = project_back(grad, wd_a[1], wd_b[1]).astype(BF16)

        g3_own, g3_oth, dhid3 = call(
            cot_body, "cot_d",
            [*cot_parts, *wd],
            [half_low, half_low, hid_low],
            flops=mlp_flops // 2,
            hold=[*keep_a, *keep_b, *keep_c, *small, *wq, *wp, *wu],
        )


        def last_body(chunk, span):
            def body(
                s_in, part_a, part_b, small_a, small_b, dhid_ref, g_oth, wu_a, wu_b,
                s_ref, n_own, fore_ref, *refs,
            ):
                share, *rear_refs = refs
                s_ref[span, :] = add_parts(s_in[span, :], part_a, part_b)
                normed = to_normed(s_ref[span, :], (small_a, small_b), 3)
                put_normed(n_own, [fore_ref], span, normed)
                pre = project_in(normed, wu_a[1], wu_b[1])
                below, bell = gelu_parts(pre)
                fore_ref[span, half:] = (pre * below).astype(BF16)
                dpre = (dhid_ref[span, :].astype(F32) * (below + pre * bell)).astype(BF16)
                put_rear(rear_refs, 0, g_oth[span, :], span)
                put_rear(rear_refs, half, dpre, span)
                share[span, :half] = mm(dpre, wu_a[1], 1, 1).astype(BF16)
                share[span, half:] = mm(dpre, wu_b[1], 1, 1).astype(BF16)

            return body

        (s5, n3_own, fore3, back3, *rear3), _, _, _ = in_chunks(
            "mlp_d", last_body,
            lambda at: [s4, part2[at], far2[at], *small, dhid3, g3_oth, *wu],
            [full, half_low, fore_mlp, full_low, *rear_shapes(rear_width_mlp, 2)],
            [*keep_a, *keep_b, *keep_c, *fore2[1], g3_own, *wq, *wp, *wd], alone=False,
        )
        far_back3 = over_ha(back3)
        fore3 = both_rear([fore3], False)
        keep_c += fore2[1]
        rear3 = both_rear(rear3, False)

        up_rows, down_rows = hidden // n_dev, half // n_dev
        qkv_rows, proj_rows = heads_width // n_dev, half // n_dev
        folds = hidden // half
        cut = n_dev // 2
        sum_rows = 32

        class Stream:
            def __init__(self, which, pieces):
                self.bits, self.which, self.pieces = orders[which], which, pieces
                self.chunk_rows = sum(piece_rows(piece) for piece in pieces)
                self.step, self.kept, self.got, self.at, self.final = 0, None, None, 0, None

        def piece_rows(piece):
            return {"up": up_rows, "q": qkv_rows, "k": qkv_rows, "v": qkv_rows}.get(
                piece, down_rows
            )

        downs = [("down", fold) for fold in range(folds)]

        def two_streams(parts, first, which):
            streams = [Stream(which, parts[:first]), Stream(which + 1, parts[first:])]
            return [stream for stream in streams if stream.pieces]

        def mlp_streams(first, which):
            return two_streams(["up", *downs], 1 + first, which)

        def attn_streams(first, which):
            return two_streams(["q", "k", "v", "proj"], first, which)

        def write_pieces(values, streams, scratches):
            for stream, scratch in zip(streams, scratches):
                at = 0
                for piece in stream.pieces:
                    size = piece_rows(piece)
                    for chunk in range(n_dev):
                        rows_at = slice(chunk * size, (chunk + 1) * size)
                        if isinstance(piece, tuple):
                            columns = slice(piece[1] * half, (piece[1] + 1) * half)
                            part = values["down"][rows_at, columns]
                        else:
                            part = values[piece][rows_at]
                        scratch[chunk, at : at + size, :] = part.astype(BF16)
                    at += size

        def both_sums(n_own, g_own, fore_a, fore_b, rear_a, rear_b):
            def left(at, size):
                return mm(get_rear(rear_a, at, size), n_own[...], 0, 0) + mm(
                    get_rear(rear_b, at, size), get_rear(fore_b, 0, half), 0, 0
                )

            size = sum(ref.shape[1] for ref in fore_a) - half
            right = mm(g_own[...], get_rear(fore_a, half, size), 0, 0) + mm(
                get_rear(rear_b, 0, half), get_rear(fore_b, half, size), 0, 0
            )
            return left, right

        def write_mlp(*refs):
            left, right = both_sums(*refs)
            return {"up": left(half, hidden), "down": right}

        def write_attn(*refs):
            left, right = both_sums(*refs)
            values = {
                name: left(half + part * heads_width, heads_width)
                for part, name in enumerate(("q", "k", "v"))
            }
            return {**values, "proj": right}

        def make(name, write, streams, n_own, g_own, fore, rear, hold):
            outs = [sds((cut * s.chunk_rows, half), BF16) for s in streams for _ in range(2)]
            count = len(rear[0])

            pieces = len(fore[0])

            def body(n_ref, g_ref, *refs):
                fore_a, fore_b, refs = refs[:pieces], refs[pieces : 2 * pieces], refs[2 * pieces :]
                fore_b = [other_core(ref) for ref in fore_b]
                rear_a, rear_b, refs = refs[:count], refs[count : 2 * count], refs[2 * count :]
                rear_b = [other_core(ref) for ref in rear_b]
                out_refs, scratches = refs[: len(outs)], refs[len(outs) :]
                values = write(n_ref, g_ref, fore_a, fore_b, rear_a, rear_b)
                write_pieces(values, streams, scratches)
                for at, (stream, scratch) in enumerate(zip(streams, scratches)):
                    size = stream.chunk_rows
                    for place in range(n_dev):
                        chunk = scratch[chunk_at(place, stream.which)]
                        to = (place % cut) * size
                        out_refs[2 * at + place // cut][to : to + size, :] = chunk

            results = call(
                body, name, [n_own, g_own, *fore[0], *fore[1], *rear[0], *rear[1]], outs, hold=hold,
                scratch=[pltpu.VMEM((n_dev, s.chunk_rows, half), BF16) for s in streams],
            )
            for at, stream in enumerate(streams):
                stream.kept, stream.sent = results[2 * at], results[2 * at + 1]

        def send_first(streams):
            for stream in streams:
                stream.got, stream.step = over_dev(stream.sent, stream.bits[0]), 1

        def sums_in(ref, at):
            return ref[at : at + sum_rows, :].astype(F32)

        def last_sum(stream, kept, got):
            return kept[...].astype(F32) + got[
                stream.at : stream.at + stream.chunk_rows, :
            ].astype(F32)

        def slot(*args, **kwargs):
            prepare_slot(*args, **kwargs)()

        def prepare_slot(
            name, fresh=(), moving=(), ending=(), sums=None, hold=(), spare=None
        ):
            ins, outs, sizes = [], [], {}
            plan_fresh, plan_moving = [], []

            def room(bit, size):
                at = sizes.get(bit, 0)
                sizes[bit] = at + size
                return at

            def place_of(array):
                for at, known in enumerate(ins):
                    if known is array:
                        return at
                ins.append(array)
                return len(ins) - 1

            for stream in fresh:
                size, bit = stream.sent.shape[0], stream.bits[0]
                plan_fresh.append((place_of(stream.sent), size, bit, room(bit, size)))
            for stream in moving:
                size = stream.kept.shape[0] // 2
                bit = stream.bits[stream.step]
                plan_moving.append(
                    (place_of(stream.kept), place_of(stream.got), stream.at, size,
                     len(outs), bit, room(bit, size))
                )
                outs.append(sds((size, half), BF16))
            plan_ending = []
            for stream in ending:
                plan_ending.append(
                    (stream, place_of(stream.kept), place_of(stream.got), len(outs))
                )
                outs.append(sds((stream.chunk_rows, half)))
            if sums is not None:
                total_at = place_of(sums[0])
                sums_got = None if sums[1] is None else place_of(sums[1])
                sums_room = room(sums[3], sum_rows)
                sums_out = len(outs)
                outs.append(sds((sum_rows, half)))
            if spare is not None:
                spare_at = room(*spare)
            bits_used = sorted(sizes)
            buffer_at = {bit: len(outs) + at for at, bit in enumerate(bits_used)}
            outs += [sds((sizes[bit], half), BF16) for bit in bits_used]

            def body(*refs):
                in_refs, out_refs = refs[: len(ins)], refs[len(ins) :]
                for sent_in, size, bit, at in plan_fresh:
                    out_refs[buffer_at[bit]][at : at + size, :] = in_refs[sent_in][...]
                for kept_in, got_in, got_row, size, kept_at, bit, at in plan_moving:
                    kept, got = in_refs[kept_in], in_refs[got_in]
                    out_refs[kept_at][...] = (
                        kept[:size, :].astype(F32) + got[got_row : got_row + size, :].astype(F32)
                    ).astype(BF16)
                    out_refs[buffer_at[bit]][at : at + size, :] = (
                        kept[size:, :].astype(F32)
                        + got[got_row + size : got_row + 2 * size, :].astype(F32)
                    ).astype(BF16)
                if spare is not None:
                    out_refs[buffer_at[spare[0]]][spare_at:, :] = jnp.zeros((spare[1], half), BF16)
                for stream, kept_in, got_in, out_at in plan_ending:
                    out_refs[out_at][...] = last_sum(stream, in_refs[kept_in], in_refs[got_in])
                if sums is not None:
                    total = in_refs[total_at][...]
                    if sums_got is not None:
                        total = total + sums_in(in_refs[sums_got], sums[2])
                    low = total.astype(BF16)
                    out_refs[sums_out][...] = low.astype(F32)
                    out_refs[buffer_at[sums[3]]][sums_room : sums_room + sum_rows, :] = low

            results = call(body, name, ins, outs, hold=hold)
            for stream, _, _, out_at in plan_ending:
                stream.final = results[out_at]
            for stream, (_, _, _, _, kept_at, _, _) in zip(moving, plan_moving):
                stream.kept = results[kept_at]

            def depart():
                received = {bit: over_dev(results[buffer_at[bit]], bit) for bit in bits_used}
                for stream, (_, _, bit, at) in zip(fresh, plan_fresh):
                    stream.got, stream.at, stream.step = received[bit], at, 1
                for stream, (_, _, _, _, _, bit, at) in zip(moving, plan_moving):
                    stream.got, stream.at = received[bit], at
                    stream.step += 1
                if sums is not None:
                    sums[:3] = results[sums_out], received[sums[3]], sums_room

            return depart

        def ship(total, kept, sent):
            packed = mm(placement(images, True), total.astype(BF16), 1, 0).astype(BF16)
            kept[...] = packed[:, :half]
            sent[:rows_in, :] = packed[:, half:]

        shipped = [sds((rows_in, half), BF16)] * 2

        def fold(kept, received, stay, go):
            same = here("ha") == here("wa")
            theirs = received[:rows_in, :]
            stay[...] = jnp.where(same, kept[...], theirs)
            go[:rows_in, :] = jnp.where(same, theirs, kept[...])

        def join(stay, received, out_ref):
            out_ref[...] = stay[...].astype(F32) + received[:rows_in, :].astype(F32)

        def out_body(s_in, fore_ref, wd_a, wd_b, kept, sent):
            hid = fore_ref[:, half:]
            base = jnp.where(here("ha") == 0, s_in[...], 0.0)
            branch = jnp.concatenate([mm(hid, wd_a[1], 1, 0), mm(hid, wd_b[1], 1, 0)], axis=1)
            ship(base + branch, kept, sent)

        streams_d = mlp_streams(SPLIT_D, 0)
        make(
            "wgrad_d", write_mlp, streams_d, n3_own, g3_own, fore3, rear3,
            [*keep_a, *keep_b, *keep_c, *small, *weights, s5],
        )
        send_first(streams_d)

        def add_norm_back(grad, part_a, part_b, stream, gain, sums_ref):
            upstream = part_a[...].astype(F32) + part_b[...].astype(F32)
            units, inv_std = norm_stats(stream)
            sums_ref[0:1, :] = jnp.sum(upstream * units, axis=0, keepdims=True)
            sums_ref[1:2, :] = jnp.sum(upstream, axis=0, keepdims=True)
            return grad + norm_back(upstream, units, inv_std, gain)

        def qkv_back(packed, section, wq_a, wq_b):
            return [
                sum(mm(packed[part], ref[section, part], 1, 1) for part in range(3))
                for ref in (wq_a, wq_b)
            ]

        def channel_back_body(
            g_in_own, g_in_oth, s_in, small_a, small_b, mask_ref, qkv_ref, probs_ref,
            wp_a, wp_b, wq_a, wq_b, *refs,
        ):
            part_a, part_b, g_ref, g_own, part_ref, sums_ref, *rear_refs = refs
            grad = jnp.concatenate([g_in_own[...], g_in_oth[...]], axis=1).astype(F32)
            gain = gain_row((small_a, small_b), 3)
            grad = add_norm_back(grad, part_a, part_b, s_in[...], gain, sums_ref)
            g_ref[...] = grad
            low = grad.astype(BF16)
            g_own[...] = low[:, :half]
            put_rear(rear_refs, 0, low[:, half:])
            grad_mixed = project_back(low, wp_a[1], wp_b[1]).astype(BF16)
            packed = attention_part_back(
                False, grad_mixed, mask_ref, qkv_ref, probs_ref, rear_refs
            )
            own, oth = qkv_back(packed, 1, wq_a, wq_b)
            part_ref[:, :half] = own.astype(BF16)
            part_ref[:, half:] = oth.astype(BF16)

        late = [*fore3[0], *wd, s5]
        (g2, g2_own, back2, sums3, *rear2) = call(
            channel_back_body, "back_c",
            [g3_own, g3_oth, s5, *small, mask, qkv2, probs2, *wp, *wq, back3, far_back3],
            [full, half_low, full_low, sds((2, width)), *rear_shapes(rear_width_attn, 1)],
            flops=attn_flops,
            hold=[*keep_a, *keep_b, s3, s4, n2_own, *fore2[0], *fore2[1], *wu, *wd, *fore3[0]],
        )
        far_back2 = over_ha(back2)
        rear2 = both_rear(rear2, False)
        hid_got, fore0_got = (
            lax.all_gather(later(values, g2), "wa") for values in (fore1[1], fore0)
        )
        fore1, fore0 = (fore1, [n1_got, hid_got]), ([fore0], [fore0_got])
        keep_a.append(fore0_got)
        keep_b.append(hid_got)
        streams_c = attn_streams(SPLIT_C, 2)
        kept_c = [*keep_a, *keep_b, s3, s4, *small, *weights, g2, *late, sums3]
        make("wgrad_c", write_attn, streams_c, n2_own, g2_own, fore2, rear2, kept_c)
        slot(
            "slot_c", fresh=streams_c, moving=streams_d, hold=[*kept_c, back2, far_back2],
        )

        def mlp_back_body(
            g_in, part_a, part_b, s_in, s_before, small_a, small_b, slope_ref,
            wd_a, wd_b, wu_a, wu_b, g_ref, g_own, part_ref, sums_ref, *rear_refs,
        ):
            keep = column_mask(rows)
            gain = gain_row((small_a, small_b), 2)
            grad = add_norm_back(g_in[...], part_a, part_b, s_in[...], gain, sums_ref)
            conv_back_into(g_ref, sums_ref, 2, grad, s_before[...], (small_a, small_b), 1, keep)
            low = g_ref[...].astype(BF16)
            g_own[...] = low[:, :half]
            put_rear(rear_refs, 0, low[:, half:])
            dhid = project_back(low, wd_a[0], wd_b[0]).astype(BF16).astype(F32)
            dpre = (dhid * slope_ref[...]).astype(BF16)
            put_rear(rear_refs, half, dpre)
            part_ref[:, :half] = mm(dpre, wu_a[0], 1, 1).astype(BF16)
            part_ref[:, half:] = mm(dpre, wu_b[0], 1, 1).astype(BF16)

        (g1, g1_own, back1, sums2, *rear1) = call(
            mlp_back_body, "back_b",
            [g2, back2, far_back2, s4, s3, *small, slope1, *wd, *wu],
            [full, half_low, full_low, sds((11, width)), *rear_shapes(rear_width_mlp, 2)],
            flops=mlp_flops,
            hold=[*keep_a, s2, n1_own, *fore1[0], *fore1[1], *wq, *wp, *fore3[0], s5, sums3],
        )
        far_back1 = over_ha(back1)
        rear1 = both_rear(rear1)
        streams_b = mlp_streams(SPLIT_B, 0)
        make(
            "wgrad_b", write_mlp, streams_b, n1_own, g1_own, fore1, rear1,
            [*keep_a, s2, *small, *wq, *wp, g1, *late, sums3, sums2],
        )
        send_first(streams_b)

        def window_back_body(
            g_in, part_a, part_b, s_in, small_a, small_b, qkv_ref, probs_ref, wp_a, wp_b,
            g_ref, g_own, sums_ref, *rear_refs,
        ):
            gain = gain_row((small_a, small_b), 1)
            grad = add_norm_back(g_in[...], part_a, part_b, s_in[...], gain, sums_ref)
            g_ref[...] = grad
            low = grad.astype(BF16)
            g_own[...] = low[:, :half]
            put_rear(rear_refs, 0, low[:, half:])
            grad_mixed = project_back(low, wp_a[0], wp_b[0]).astype(BF16)
            attention_part_back(True, grad_mixed, None, qkv_ref, probs_ref, rear_refs)

        (g0, g0_own, sums1, *rear0) = call(
            window_back_body, "back_a",
            [g1, back1, far_back1, s2, *small, qkv0, probs0, *wp],
            [full, half_low, sds((2, width)), *rear_shapes(rear_width_attn, 1)],
            flops=attn_flops, hold=[x0, n0_own, *fore0[0], *fore0[1], s1, *wq, *late, sums3, sums2],
        )
        every = [*streams_d, *streams_c]
        depart = prepare_slot(
            "slot_cd", moving=every, spare=(2, 16),
            hold=[x0, n0_own, *fore0[0], *fore0[1], s1, *small, *wq, *late, sums1, sums2, sums3,
                  g0, g0_own, *rear0],
        )
        rear0 = both_rear(later(rear0, streams_d[0].kept))

        keep_0 = [g0, s1, x0, *small, *wq, sums1, sums2, sums3, *rear0[0]]
        streams_a = attn_streams(SPLIT_A, 0)
        make("wgrad_a", write_attn, streams_a, n0_own, g0_own, fore0, rear0, [*late, *keep_0])
        every = [*streams_d, *streams_c, *streams_b, *streams_a]
        send_first(streams_a)
        depart()

        sums_at = -(-rows_in // 16) * 16
        sums_half = sds((sum_rows, half))
        with_sums = sds((sums_at + sum_rows, half), BF16)

        def put_sums(ref, total):
            ref[sums_at:, :] = total.astype(BF16)

        def first_back_body(
            g_in, s_in, x_ref, small_a, small_b, wq_a, wq_b, sums_one, sums_two, sums_three, *refs
        ):
            rear_refs, (kept, sent, sums_own, scratch, sums_ref) = refs[:-5], refs[-5:]
            keep = column_mask(rows)
            packed = [
                get_rear(rear_refs, half + part * heads_width, heads_width) for part in range(3)
            ]
            upstream = jnp.concatenate(qkv_back(packed, 0, wq_a, wq_b), axis=1)
            units, inv_std = norm_stats(s_in[...])
            sums_ref[0:1, :] = jnp.sum(upstream * units, axis=0, keepdims=True)
            sums_ref[1:2, :] = jnp.sum(upstream, axis=0, keepdims=True)
            grad = jnp.where(here("ha") == 0, g_in[...], 0.0)
            grad = grad + norm_back(upstream, units, inv_std, gain_row((small_a, small_b), 0))
            conv_back_into(
                scratch, sums_ref, 2, grad, x_ref[...].astype(F32), (small_a, small_b), 0, keep
            )
            ship(scratch[...], kept, sent)
            sums_ref[11:13, :] = 0.5 * sums_one[...]
            sums_ref[13:24, :] = 0.5 * sums_two[...]
            sums_ref[24:26, :] = 0.5 * sums_three[...]
            sums_ref[26:, :] = jnp.zeros((sum_rows - 26, width), F32)
            sums_own[...] = sums_ref[:, :half]
            put_sums(sent, sums_ref[:, half:])

        token_kept, token_sent, sums_own = call(
            first_back_body, "back_0",
            [g0, s1, x0, *small, *wq, sums1, sums2, sums3, *rear0[0]],
            [shipped[0], with_sums, sums_half],
            scratch=[pltpu.VMEM((rows, width), F32), pltpu.VMEM((sum_rows, width), F32)],
            flops=attn_flops * 3 // 4, hold=late,
        )

        def fold_tokens(kept, both, sums_a, stay, go, sums_ref):
            received = other_core(both)
            fold(kept, received, stay, go)
            total = sums_a[...] + sums_in(received, sums_at)
            put_sums(go, total)
            sums_ref[...] = sums_in(go, sums_at)

        token_stay, token_go, sums_chip = call(
            fold_tokens, "fold_tokens",
            [token_kept, lax.all_gather(token_sent, "wa"), sums_own],
            [shipped[0], with_sums, sums_half], hold=late,
        )
        token_got = over_ha(token_go)

        def join_tokens(stay, received, sums_chip, out_ref, sums_ref):
            join(stay, received, out_ref)
            sums_ref[...] = sums_chip[...] + sums_in(received, sums_at)

        owned = sds((rows_in, half))
        grad_tokens, sums_ha = call(
            join_tokens, "join_tokens", [token_stay, token_got, sums_chip], [owned, sums_half],
            hold=late,
        )
        left_bits = list(range(bits))
        sums = [sums_ha, None, 0, left_bits.pop(0)]
        slot("sums_x", sums=sums, spare=(0, 96), hold=late)
        out_kept, out_sent = call(
            out_body, "out_d", [s5, *fore3[0], *wd], shipped, flops=mlp_flops // 2
        )
        out_both = lax.all_gather(out_sent, "wa")

        def hop():
            if not left_bits:
                return None
            sums[3] = left_bits.pop(0)
            return sums

        turn = 0
        while left_bits or any(stream.step < bits for stream in every):
            turn += 1
            arrived = [s for s in every if s.step == bits and s.final is None]
            slot(f"slot_b{turn}", moving=[s for s in streams_b if s.step < bits])
            second = [s for s in [*streams_d, *streams_a] if s.step < bits]
            slot(f"slot_a{turn}", moving=second, ending=arrived, sums=hop())
            if turn > 1:
                slot(f"slot_c{turn}", moving=[s for s in streams_c if s.step < bits])
            if turn == 1:
                out_stay, out_go = call(
                    lambda kept, both, *refs: fold(kept, other_core(both), *refs),
                    "fold_out", [out_kept, out_both], shipped,
                )
                out_got = over_ha(out_go)
        output = call(join, "join_out", [out_stay, out_got], [owned])[0]

        def finish_body(*refs):
            (up, down, qkv, proj, taps_ref, gain_ref, shift_ref) = refs[-7:]
            at = iter(refs)
            total = next(at)[...] + sums_in(next(at), sums[2])
            for branch, row in enumerate((0, 11, 13, 24)):
                gain_ref[branch : branch + 1, :] = total[row : row + 1]
                shift_ref[branch : branch + 1, :] = total[row + 1 : row + 2]
            for section, row in enumerate((2, 15)):
                for t in range(9):
                    taps_ref[t, section : section + 1, :] = total[row + t : row + t + 1]

            def finished(stream):
                if stream.final is not None:
                    return next(at)[...]
                return last_sum(stream, next(at), next(at))

            for section, streams in enumerate(
                ((*streams_a, *streams_b), (*streams_c, *streams_d))
            ):
                for stream in streams:
                    values, row = finished(stream), 0
                    for piece in stream.pieces:
                        part = values[row : row + piece_rows(piece)]
                        row += piece_rows(piece)
                        if piece == "up":
                            up[section] = part
                        elif piece == "proj":
                            proj[section] = part
                        elif isinstance(piece, tuple):
                            down[section, :, piece[1] * half : (piece[1] + 1) * half] = part
                        else:
                            qkv[section, ("q", "k", "v").index(piece)] = part

        ends = []
        for stream in (*streams_a, *streams_b, *streams_c, *streams_d):
            ends += [stream.kept, stream.got] if stream.final is None else [stream.final]
        up, down, qkv, proj, grad_taps, grad_gain, grad_shift = call(
            finish_body, "finish", [*sums[:2], *ends],
            [sds((2, up_rows, half)), sds((2, down_rows, hidden)), sds((2, 3, qkv_rows, half)),
             sds((2, proj_rows, half)), sds((9, 2, half)), sds((4, half)), sds((4, half))],
        )
        grad_taps = jnp.transpose(grad_taps, (1, 0, 2))
        grad_qkv = jnp.transpose(qkv, (0, 3, 1, 2))
        grad_proj, grad_up, grad_down = (
            jnp.transpose(values, (0, 2, 1)) for values in (proj, up, down)
        )
        return (
            output,
            grad_tokens,
            grad_taps,
            grad_gain,
            grad_shift,
            grad_qkv,
            grad_proj,
            grad_up,
            grad_down,
        )

    placed = (
        P(("dev", "ha"), "wa"),
        P(("dev", "ha"), "wa"),
        P(None, None, "wa"),
        P(None, "wa"),
        P(None, "wa"),
        P(None, "wa", None, "ha"),
        P(None, "ha", "wa"),
        P(None, "wa", "ha"),
        P(None, "ha", "wa"),
        P("dev", None),
    )
    return jax.shard_map(
        on_device,
        mesh=mesh,
        in_specs=placed,
        out_specs=(
            P(("dev", "ha"), "wa"),
            P(("dev", "ha"), "wa"),
            P(None, None, "wa"),
            P(None, "wa"),
            P(None, "wa"),
            P(None, "wa", None, ("ha", "dev")),
            P(None, "ha", ("wa", "dev")),
            P(None, "wa", ("ha", "dev")),
            P(None, "ha", ("wa", "dev")),
        ),
        check_vma=False,
    )
```

```python
from functools import partial

import jax
import jax.numpy as jnp
import numpy as np
from jax import lax
from jax.experimental import pallas as pl
from jax.experimental.pallas import tpu as pltpu
from jax.sharding import PartitionSpec as P

WIN = 7
GRID_COLS = 8
PATCHES = 49
PADDED = WIN * GRID_COLS
HEAD_DIM = 32
LANES = 128
HEADS_TILE = LANES // HEAD_DIM
EPS = 1e-05
NEG = -1e30
SPLIT_D, SPLIT_C, SPLIT_B, SPLIT_A = 0, 2, 0, 4
BF16 = jnp.bfloat16
F32 = jnp.float32
VMEM_LIMIT = 16 * 2**20
TIMES = {"pack_small": 5.0, "choose": 5.0}


def mm(left, right, left_dim, right_dim):
    return lax.dot_general(
        left, right, (((left_dim,), (right_dim,)), ((), ())), preferred_element_type=F32
    )


class Order:
    def __init__(self):
        self.last = None


def kernel_call(
    body, name, ins, outs, order, scratch=(), flops=0, hold=(), reuse=None, carry=None
):
    reuse = reuse or {}
    arrays = list(ins) + list(hold) + ([] if order.last is None else [order.last])
    first_reused = len(arrays)
    aliases = {first_reused + at: out for at, out in enumerate(reuse)}
    arrays += list(reuse.values())
    outs = list(outs) + [sds((8, LANES))]

    def wrapped(*refs):
        out_refs = refs[len(arrays) : len(arrays) + len(outs)]
        for at, out in aliases.items():
            carry(refs[at], out_refs[out])
        body(*refs[: len(ins)], *out_refs[:-1], *refs[len(arrays) + len(outs) :])
        out_refs[-1][...] = jnp.zeros_like(out_refs[-1])

    *results, order.last = pl.pallas_call(
        wrapped,
        in_specs=[pl.BlockSpec(memory_space=pltpu.VMEM)] * len(arrays),
        out_specs=[pl.BlockSpec(memory_space=pltpu.VMEM)] * len(outs),
        out_shape=outs,
        scratch_shapes=list(scratch),
        input_output_aliases=aliases,
        compiler_params=pltpu.CompilerParams(vmem_limit_bytes=VMEM_LIMIT),
        cost_estimate=pl.CostEstimate(
            flops=int(TIMES.get(name, 0) * 1.15e9), bytes_accessed=0, transcendentals=0
        ),
        name=name,
    )(*arrays)
    return results


def sds(shape, dtype=F32):
    return jax.ShapeDtypeStruct(shape, dtype)


def column_mask(rows):
    return (lax.broadcasted_iota(jnp.int32, (rows, 1), 0) % GRID_COLS) < WIN


def placement(images, transposed, begin=0, count=None):
    padded, plain = count or images * PADDED, images * PATCHES
    shape = (plain, padded) if transposed else (padded, plain)
    at = lax.broadcasted_iota(jnp.int32, shape, 1 if transposed else 0) + begin
    image = sum((at >= i * PADDED).astype(jnp.int32) for i in range(1, images))
    inside = at - image * PADDED
    source = image * PATCHES + (inside >> 3) * WIN + (inside & 7)
    other = lax.broadcasted_iota(jnp.int32, shape, 0 if transposed else 1)
    return (((inside & 7) < WIN) & (source == other)).astype(F32).astype(BF16)


def side_shifts(values):
    rows = values.shape[0]
    return (pltpu.roll(values, 1, 0), values, pltpu.roll(values, rows - 1, 0))


def as_grid(values):
    return values.reshape(-1, WIN, GRID_COLS, values.shape[-1])


def move_rows(values, step):
    grid = as_grid(values)
    zeros = jnp.zeros_like(grid[:, :1])
    if step > 0:
        moved = jnp.concatenate([zeros, grid[:, :-1]], axis=1)
    else:
        moved = jnp.concatenate([grid[:, 1:], zeros], axis=1)
    return moved.reshape(values.shape)


def conv_cols(values, taps, keep):
    shifted = side_shifts(values)
    line = [
        sum(shifted[col] * taps[3 * row + col] for col in range(3)) for row in range(3)
    ]
    total = values + line[1] + move_rows(line[0], 1) + move_rows(line[2], -1)
    return jnp.where(keep, total, 0.0)


def tap_sums(grads, values):
    shifted = side_shifts(values)
    grad_grid = as_grid(grads)
    sums = []
    for row in range(3):
        for col in range(3):
            moved = as_grid(shifted[col])
            if row == 0:
                prod = grad_grid[:, 1:] * moved[:, :-1]
            elif row == 1:
                prod = grad_grid * moved
            else:
                prod = grad_grid[:, :-1] * moved[:, 1:]
            flat = prod.reshape(-1, GRID_COLS, prod.shape[-1])
            sums.append(jnp.sum(jnp.sum(flat, axis=0), axis=0, keepdims=True))
    return sums


def norm_stats(stream):
    width = stream.shape[1]
    center = jnp.sum(stream, axis=1, keepdims=True) * (1.0 / width)
    moved = stream - center
    inv_std = lax.rsqrt(jnp.sum(moved * moved, axis=1, keepdims=True) * (1.0 / width) + EPS)
    return moved * inv_std, inv_std


def norm_back(upstream, units, inv_std, gain):
    width = upstream.shape[1]
    scaled = upstream * gain
    first = jnp.sum(scaled, axis=1, keepdims=True) * (1.0 / width)
    second = jnp.sum(scaled * units, axis=1, keepdims=True) * (1.0 / width)
    return inv_std * (scaled - first - units * second)


def gelu_parts(values):
    below = 0.5 + 0.5 * lax.erf(values * float(0.5**0.5))
    bell = jnp.exp2(values * values * float(-0.5 * np.log2(np.e)))
    return below, bell * float(1.0 / np.sqrt(2.0 * np.pi))


def head_mask(index):
    return (lax.broadcasted_iota(jnp.int32, (1, LANES), 1) // HEAD_DIM) == index


def spread_heads(tile):
    return jnp.concatenate(
        [jnp.where(head_mask(j), tile, 0.0) for j in range(HEADS_TILE)], axis=0
    ).astype(BF16)


def gather_heads(stacked):
    rows = stacked.shape[0] // HEADS_TILE
    total = jnp.where(head_mask(0), stacked[:rows], 0.0)
    for j in range(1, HEADS_TILE):
        total = jnp.where(head_mask(j), stacked[j * rows : (j + 1) * rows], total)
    return total


def softmax_rows(scores):
    top = jnp.max(scores, axis=0, keepdims=True)
    weights = jnp.exp(scores - top)
    return weights * (1.0 / jnp.sum(weights, axis=0, keepdims=True))


SCALE = HEAD_DIM**-0.5


def low(tiles):
    return [tile.astype(BF16) for tile in tiles]


def minus_row_sums(probs, grads):
    return [
        (p * (g - jnp.sum(g * p, axis=0, keepdims=True))).astype(BF16)
        for p, g in zip(probs, grads)
    ]


def window_tiles(queries, keys, values):
    keys_ok = column_mask(PADDED)
    scores = [
        mm(k, spread_heads(q), 1, 1) * SCALE for q, k in zip(queries, low(keys))
    ]
    probs = [softmax_rows(jnp.where(keys_ok, score, NEG)) for score in scores]
    mixed = [mm(p, v, 0, 0) for p, v in zip(low(probs), low(values))]
    return probs, [gather_heads(tile) for tile in mixed]


def window_tiles_back(queries, keys, values, probs, grads):
    q_big, g_big = ([spread_heads(tile) for tile in tiles] for tiles in (queries, grads))
    grad_probs = [mm(v, g, 1, 1) for v, g in zip(low(values), g_big)]
    grad_v = [mm(p, g, 1, 0) for p, g in zip(low(probs), g_big)]
    grad_scores = minus_row_sums(probs, grad_probs)
    grad_k = [mm(d, q, 1, 0) * SCALE for d, q in zip(grad_scores, q_big)]
    grad_q = [mm(d, k, 0, 0) for d, k in zip(grad_scores, low(keys))]
    return [gather_heads(tile) * SCALE for tile in grad_q], grad_k, grad_v


def same_head():
    first = lax.broadcasted_iota(jnp.int32, (LANES, LANES), 0) // HEAD_DIM
    second = lax.broadcasted_iota(jnp.int32, (LANES, LANES), 1) // HEAD_DIM
    return first == second


def channel_tiles(queries, keys, values, masks):
    own_head = same_head()
    masked = low([q * mask for q, mask in zip(queries, masks)])
    scores = [mm(k, q, 0, 0) * SCALE for q, k in zip(masked, low(keys))]
    probs = [softmax_rows(jnp.where(own_head, score, NEG)) for score in scores]
    return probs, [mm(v, p, 1, 0) for p, v in zip(low(probs), low(values))]


def channel_tiles_back(queries, keys, values, probs, grads, masks):
    masked = low([q * mask for q, mask in zip(queries, masks)])
    grads = low(grads)
    grad_probs = [mm(v, g, 0, 0) for v, g in zip(low(values), grads)]
    grad_v = [mm(g, p, 1, 1) for g, p in zip(grads, low(probs))]
    grad_scores = minus_row_sums(probs, grad_probs)
    grad_q = [mm(k, d, 1, 0) * SCALE * m for k, d, m in zip(low(keys), grad_scores, masks)]
    grad_k = [mm(q, d, 1, 1) * SCALE for q, d in zip(masked, grad_scores)]
    return grad_q, grad_k, grad_v


def cut_tiles(values, images, tiles):
    return [
        values[image * PADDED : (image + 1) * PADDED, tile * LANES : (tile + 1) * LANES]
        for image in range(images)
        for tile in range(tiles)
    ]


def paste_tiles(parts, images, tiles):
    lines = [
        jnp.concatenate(parts[image * tiles : (image + 1) * tiles], axis=1)
        for image in range(images)
    ]
    return jnp.concatenate(lines, axis=0).astype(BF16)


def solution(mesh):
    n_dev = mesh.shape["dev"]
    bits = n_dev.bit_length() - 1
    assert n_dev == 1 << bits and mesh.shape["ha"] == 2 and mesh.shape["wa"] == 2

    swap = [(0, 1), (1, 0)]

    def over_ha(values):
        return lax.ppermute(values, "ha", swap)

    def over_wa(values):
        return lax.ppermute(values, "wa", swap)

    partner = [1 << bit for bit in range(bits)]
    if bits > 2:
        partner[2] = 6

    def over_dev(values, bit):
        return lax.ppermute(values, "dev", [(i, i ^ partner[bit]) for i in range(n_dev)])

    def on_device(
        tokens, cotangent, conv_taps, norm_gain, norm_shift, w_qkv, w_proj, w_up, w_down, valid
    ):
        rows_in, half = tokens.shape
        images = rows_in // PATCHES
        rows = images * PADDED
        width = 2 * half
        heads_width = w_qkv.shape[3]
        hidden = w_up.shape[2]
        tiles = heads_width // LANES
        assert heads_width == half
        rest = list(range(3, bits))
        orders = [[0, 1, 2, *rest], [1, 0, 2, *rest], [0, 2, 1, *rest], [1, 2, 0, *rest]]

        def here(name):
            return lax.axis_index(name)

        def chunk_at(place, which):
            found = 0
            for step, bit in enumerate(orders[which]):
                found ^= ((place >> (bits - 1 - step)) & 1) * partner[bit]
            return found ^ here("dev")

        order = Order()
        call = partial(kernel_call, order=order)

        def later(values, event):
            return lax.optimization_barrier((values, event))[0]

        def pack_small(taps_ref, gain_ref, shift_ref, out_ref):
            for section in range(2):
                for t in range(9):
                    at = 9 * section + t
                    out_ref[at : at + 1, :] = taps_ref[t, section : section + 1, :]
            out_ref[18:22, :] = gain_ref[...]
            out_ref[22:26, :] = shift_ref[...]

        def choose(mine, received, own, *others):
            same = here("ha") == here("wa")
            own[...] = jnp.where(same, mine[...], received[...])
            other, at = jnp.where(same, received[...], mine[...]), 0
            for ref in others:
                ref[...] = other[:, at : at + ref.shape[1]]
                at += ref.shape[1]

        wq_own = jnp.transpose(w_qkv, (0, 2, 1, 3))
        wq, wp = (wq_own, over_wa(wq_own)), (w_proj, over_wa(w_proj))
        tokens_in, cot_in = over_ha(tokens), over_ha(cotangent)
        small_own = call(
            pack_small, "pack_small",
            [jnp.transpose(conv_taps, (1, 0, 2)), norm_gain, norm_shift], [sds((26, half))],
            hold=[tokens],
        )[0]
        small = (small_own, over_wa(small_own))
        chosen = [sds((rows_in, columns), BF16) for columns in (half, LANES, half - LANES)]
        tokens_own, *tokens_oth = call(
            choose, "choose", [tokens, tokens_in], chosen, hold=[wq[1], wp[1], small_own]
        )
        token_parts = (tokens_own, *[over_wa(values) for values in tokens_oth])

        def arrive(out_ref):
            out_ref[...] = jnp.zeros_like(out_ref)

        arrived = call(
            arrive, "arrive", [], [sds((8, LANES))],
            hold=[*token_parts, small[1], cot_in, small_own, wq[1], wp[1]],
        )[0]
        wu, wd = ((values, over_wa(later(values, arrived))) for values in (w_up, w_down))

        def unpack(parts, begin=0, count=None):
            values = jnp.concatenate([part[...] for part in parts], axis=1)
            return mm(placement(images, False, begin, count), values, 1, 0)

        def gain_row(refs, branch):
            return jnp.concatenate([ref[18 + branch : 19 + branch, :] for ref in refs], axis=1)

        def shift_row(refs, branch):
            return jnp.concatenate([ref[22 + branch : 23 + branch, :] for ref in refs], axis=1)

        def tap_rows(small_refs, section, col, flipped):
            ref = small_refs[col // half]
            at = col % half
            found = [
                ref[9 * section + t : 9 * section + t + 1, at : at + LANES] for t in range(9)
            ]
            return found[::-1] if flipped else found

        def project_in(normed, first, second):
            return mm(normed[:, :half], first, 1, 0) + mm(normed[:, half:], second, 1, 0)

        def project_back(values, first, second):
            return mm(values[:, :half], first, 1, 1) + mm(values[:, half:], second, 1, 1)

        def to_normed(stream, small_refs, branch):
            units, _ = norm_stats(stream)
            return (units * gain_row(small_refs, branch) + shift_row(small_refs, branch)).astype(
                BF16
            )

        def both_rear(pieces, gather=True):
            pieces = list(pieces)
            if gather:
                return pieces, [lax.all_gather(piece, "wa") for piece in pieces]
            return pieces, [over_wa(piece) for piece in pieces]

        def other_core(ref):
            return ref.at[1 - here("wa")] if len(ref.shape) == 3 else ref

        def put_both(own_ref, oth_ref, values):
            own_ref[...] = values[:, :half]
            oth_ref[:, :half] = values[:, half:]

        def add_parts(stream, part_a, part_b):
            return stream + part_a[...].astype(F32) + part_b[...].astype(F32)

        def attention_part(
            window, section, normed, valid_rows, wq_a, wq_b, qkv_ref, probs_ref, first_image
        ):
            count = normed.shape[0] // PADDED
            packed = [
                project_in(normed, wq_a[section, part], wq_b[section, part]).astype(BF16)
                for part in range(3)
            ]
            begin = first_image * PADDED
            for part in range(3):
                qkv_ref[part, begin : begin + count * PADDED, :] = packed[part]
            q, k, v = (cut_tiles(part.astype(F32), count, tiles) for part in packed)
            if window:
                probs, mixed = window_tiles(q, k, v)
            else:
                masks = [mask for mask in valid_rows for _ in range(tiles)]
                probs, mixed = channel_tiles(q, k, v, masks)
            for at, tile in enumerate(probs):
                probs_ref[first_image * tiles + at] = tile
            return paste_tiles(mixed, count, tiles)

        def attention_part_back(window, grad_mixed, mask_ref, qkv_ref, probs_ref, rear_refs):
            q, k, v = (
                cut_tiles(qkv_ref[part].astype(F32), images, tiles) for part in range(3)
            )
            grads = cut_tiles(grad_mixed.astype(F32), images, tiles)
            probs = [probs_ref[at] for at in range(images * tiles)]
            if window:
                found = window_tiles_back(q, k, v, probs, grads)
            else:
                masks = [
                    mask_ref[image * PADDED : (image + 1) * PADDED, :]
                    for image in range(images)
                    for _ in range(tiles)
                ]
                found = channel_tiles_back(q, k, v, probs, grads, masks)
            packed = [paste_tiles(part, images, tiles) for part in found]
            for part in range(3):
                put_rear(rear_refs, half + part * heads_width, packed[part])
            return packed

        def mul_out(left, section, own_ref, oth_ref, out_ref):
            out_ref[:, :half] = mm(left, own_ref[section], 1, 0).astype(BF16)
            out_ref[:, half:] = mm(left, oth_ref[section], 1, 0).astype(BF16)

        def conv_into(out_ref, rows_at, values, small_refs, section, keep):
            for col in range(0, width, LANES):
                taps = tap_rows(small_refs, section, col, False)
                out_ref[rows_at, col : col + LANES] = conv_cols(
                    values[:, col : col + LANES], taps, keep
                )

        def conv_back_into(out_ref, sums_ref, sums_at, grads, values, small_refs, section, keep):
            for col in range(0, width, LANES):
                lanes_at = slice(col, col + LANES)
                taps = tap_rows(small_refs, section, col, True)
                for t, total in enumerate(tap_sums(grads[:, lanes_at], values[:, lanes_at])):
                    sums_ref[sums_at + t : sums_at + t + 1, lanes_at] = total
                out_ref[:, lanes_at] = conv_cols(grads[:, lanes_at], taps, keep)

        window_probs = sds((images * tiles, PADDED, HEADS_TILE * PADDED))
        channel_probs = sds((images * tiles, LANES, LANES))
        full, full_low = sds((rows, width)), sds((rows, width), BF16)
        half_low = sds((rows, half), BF16)
        hid_low = sds((rows, hidden), BF16)
        qkv_low = sds((3, rows, heads_width), BF16)
        fore_attn = sds((rows, half + heads_width), BF16)
        def cuts(total, count):
            tiles_all = total // LANES
            return [LANES * (-(-tiles_all * (at + 1) // count)) for at in range(count)]

        def rear_shapes(total, count):
            ends = cuts(total, count)
            return [sds((rows, e - b), BF16) for b, e in zip([0, *ends], ends)]

        def rear_ranges(refs, at, size):
            begin = 0
            for ref in refs:
                end = begin + ref.shape[1]
                low, high = max(begin, at), min(end, at + size)
                if low < high:
                    yield ref, low - begin, high - begin, low - at
                begin = end

        def put_rear(refs, at, values, span=slice(None)):
            for ref, low, high, source in rear_ranges(refs, at, values.shape[1]):
                ref[span, low:high] = values[:, source : source + high - low]

        def get_rear(refs, at, size):
            parts = [ref[:, low:high] for ref, low, high, _ in rear_ranges(refs, at, size)]
            return parts[0] if len(parts) == 1 else jnp.concatenate(parts, axis=1)

        rear_width_attn, rear_width_mlp = half + 3 * heads_width, half + hidden
        fore_mlp = sds((rows, rear_width_mlp), BF16)
        attn_flops = 2 * rows * (4 * width * heads_width)
        mlp_flops = 2 * rows * (2 * width * hidden)

        split = (images + 1) // 2
        chunks = [(0, split), (split, images)] if split < images else [(0, images)]
        spans = [slice(begin * PADDED, end * PADDED) for begin, end in chunks]

        def chunk_rows(span):
            return span.stop - span.start

        def part_shape(span):
            return sds((chunk_rows(span), width), BF16)

        def put_normed(own_ref, fore_refs, span, normed):
            own_ref[span, :] = normed[:, :half]
            put_rear(fore_refs, 0, normed[:, half:], span)

        def first_body(chunk, span):
            def body(
                tokens_a, tokens_b, tokens_c, small_a, small_b, wq_a, wq_b, wp_a, wp_b,
                x_ref, s_ref, n_own, fore_ref, qkv_ref, probs_ref, part_ref, *copies,
            ):
                if copies:
                    copies[0][...], copies[1][...] = small_a[...], small_b[...]
                keep = column_mask(chunk_rows(span))
                stream = unpack((tokens_a, tokens_b, tokens_c), span.start, chunk_rows(span))
                x_ref[span, :] = stream.astype(BF16)
                conv_into(s_ref, span, stream, (small_a, small_b), 0, keep)
                normed = to_normed(s_ref[span, :], (small_a, small_b), 0)
                put_normed(n_own, [fore_ref], span, normed)
                mixed = attention_part(
                    True, 0, normed, None, wq_a, wq_b, qkv_ref, probs_ref, chunk[0]
                )
                fore_ref[span, half:] = mixed
                mul_out(mixed, 0, wp_a, wp_b, part_ref)

            return body

        def carry_spans(upto):
            def carry(old, new):
                for chunk, span in zip(chunks[:upto], spans[:upto]):
                    if old.shape[0] == rows:
                        new[span, :] = old[span, :]
                    elif old.shape[1] == rows:
                        new[:, span, :] = old[:, span, :]
                    else:
                        per_image = old.shape[0] // images
                        held = slice(chunk[0] * per_image, chunk[1] * per_image)
                        new[held] = old[held]

            return carry

        def in_chunks(
            name, make_body, ins, shapes, hold, extra=(), between=None, alone=True
        ):
            arrays, parts, fars, more = None, [], [], []
            for at, (chunk, span) in enumerate(zip(chunks, spans)):
                results = call(
                    make_body(chunk, span), f"{name}{at}", ins(at),
                    [*shapes, *([part_shape(span)] if alone else ()), *(extra if at == 0 else ())],
                    hold=[*hold, *more, *parts],
                    reuse=None if arrays is None else dict(enumerate(arrays)),
                    carry=carry_spans(at),
                )
                arrays, rest = results[: len(shapes)], results[len(shapes) :]
                if alone:
                    parts.append(rest[0])
                    fars.append(over_ha(rest[0]))
                more = more or rest[1:]
                if at == 0 and between is not None:
                    between(arrays, more)
            return arrays, parts, fars, more

        small_in, cot_parts = small, []

        def choose_cot(arrays, more):
            own, *others = call(
                choose, "choose_cot", [cotangent, cot_in], chosen,
                hold=[*arrays, *more, *wq, *wp],
            )
            cot_parts.extend([own, *others])

        (x0, s1, n0_own, fore0, qkv0, probs0), part0, far0, small = in_chunks(
            "attn_a", first_body, lambda at: [*token_parts, *small_in, *wq, *wp],
            [full_low, full, half_low, fore_attn, qkv_low, window_probs], [cot_in, arrived],
            [sds((26, half))] * 2, choose_cot,
        )
        keep_a = [x0, n0_own, fore0, qkv0, probs0, s1]

        def mlp_body(chunk, span):
            def body(
                s_in, part_a, part_b, small_a, small_b, wu_a, wu_b, wd_a, wd_b,
                s_ref, n_own, slope_ref, *refs,
            ):
                *fore_refs, part_ref = refs
                s_ref[span, :] = add_parts(s_in[span, :], part_a, part_b)
                normed = to_normed(s_ref[span, :], (small_a, small_b), 1)
                put_normed(n_own, fore_refs, span, normed)
                pre = project_in(normed, wu_a[0], wu_b[0])
                below, bell = gelu_parts(pre)
                hid = (pre * below).astype(BF16)
                put_rear(fore_refs, half, hid, span)
                slope_ref[span, :] = below + pre * bell
                mul_out(hid, 0, wd_a, wd_b, part_ref)

            return body

        (s2, n1_own, slope1, *fore1), part1, far1, _ = in_chunks(
            "mlp_b", mlp_body, lambda at: [s1, part0[at], far0[at], *small, *wu, *wd],
            [full, half_low, sds((rows, hidden)), half_low, hid_low],
            [*keep_a, *wq, *wp, *cot_parts],
        )
        n1_got = over_wa(fore1[0])
        cot_parts[1:] = [over_wa(later(values, part1[0])) for values in cot_parts[1:]]
        keep_b = [s2, n1_own, *fore1, slope1, n1_got]
        weights = [*wq, *wp, *wu, *wd]

        def channel_body(chunk, span):
            def body(
                s_in, part_a, part_b, valid_ref, small_a, small_b, wq_a, wq_b, wp_a, wp_b,
                s_before, s_ref, n_own, qkv_ref, probs_ref, mask_ref, *refs,
            ):
                *fore_refs, part_ref = refs
                keep = column_mask(chunk_rows(span))
                stream = jnp.where(keep, add_parts(s_in[span, :], part_a, part_b), 0.0)
                s_before[span, :] = stream
                conv_into(s_ref, span, stream, (small_a, small_b), 1, keep)
                normed = to_normed(s_ref[span, :], (small_a, small_b), 2)
                put_normed(n_own, fore_refs, span, normed)
                one_image = placement(1, False).astype(F32)
                valid_rows = []
                for image in range(*chunk):
                    line = jnp.where(
                        here("wa") == 0,
                        valid_ref[image : image + 1, :],
                        valid_ref[images + image : images + image + 1, :],
                    ).astype(F32)
                    valid_rows.append(jnp.sum(one_image * line, axis=1, keepdims=True))
                    mask_ref[image * PADDED : (image + 1) * PADDED, :] = valid_rows[-1]
                mixed = attention_part(
                    False, 1, normed, valid_rows, wq_a, wq_b, qkv_ref, probs_ref, chunk[0]
                )
                put_rear(fore_refs, half, mixed, span)
                mul_out(mixed, 1, wp_a, wp_b, part_ref)

            return body

        (s3, s4, n2_own, qkv2, probs2, mask, *fore2), part2, far2, _ = in_chunks(
            "attn_c", channel_body,
            lambda at: [s2, part1[at], far1[at], valid, *small, *wq, *wp],
            [full, full, half_low, qkv_low, channel_probs, sds((rows, 1)), half_low, half_low],
            [*keep_a, *keep_b, *wu, *wd, *cot_parts],
        )
        fore2 = both_rear(fore2, False)
        keep_c = [s3, s4, n2_own, *fore2[0], qkv2, probs2, mask]

        def cot_body(cot_a, cot_b, cot_c, wd_a, wd_b, g_own, g_oth, dhid_ref):
            grad = unpack((cot_a, cot_b, cot_c)).astype(BF16)
            put_both(g_own, g_oth, grad)
            dhid_ref[...] = project_back(grad, wd_a[1], wd_b[1]).astype(BF16)

        g3_own, g3_oth, dhid3 = call(
            cot_body, "cot_d",
            [*cot_parts, *wd],
            [half_low, half_low, hid_low],
            flops=mlp_flops // 2,
            hold=[*keep_a, *keep_b, *keep_c, *small, *wq, *wp, *wu],
        )


        def last_body(chunk, span):
            def body(
                s_in, part_a, part_b, small_a, small_b, dhid_ref, g_oth, wu_a, wu_b,
                s_ref, n_own, fore_ref, *refs,
            ):
                share, *rear_refs = refs
                s_ref[span, :] = add_parts(s_in[span, :], part_a, part_b)
                normed = to_normed(s_ref[span, :], (small_a, small_b), 3)
                put_normed(n_own, [fore_ref], span, normed)
                pre = project_in(normed, wu_a[1], wu_b[1])
                below, bell = gelu_parts(pre)
                fore_ref[span, half:] = (pre * below).astype(BF16)
                dpre = (dhid_ref[span, :].astype(F32) * (below + pre * bell)).astype(BF16)
                put_rear(rear_refs, 0, g_oth[span, :], span)
                put_rear(rear_refs, half, dpre, span)
                share[span, :half] = mm(dpre, wu_a[1], 1, 1).astype(BF16)
                share[span, half:] = mm(dpre, wu_b[1], 1, 1).astype(BF16)

            return body

        (s5, n3_own, fore3, back3, *rear3), _, _, _ = in_chunks(
            "mlp_d", last_body,
            lambda at: [s4, part2[at], far2[at], *small, dhid3, g3_oth, *wu],
            [full, half_low, fore_mlp, full_low, *rear_shapes(rear_width_mlp, 2)],
            [*keep_a, *keep_b, *keep_c, *fore2[1], g3_own, *wq, *wp, *wd], alone=False,
        )
        far_back3 = over_ha(back3)
        fore3 = both_rear([fore3], False)
        keep_c += fore2[1]
        rear3 = both_rear(rear3, False)

        up_rows, down_rows = hidden // n_dev, half // n_dev
        qkv_rows, proj_rows = heads_width // n_dev, half // n_dev
        folds = hidden // half
        cut = n_dev // 2
        sum_rows = 32

        class Stream:
            def __init__(self, which, pieces):
                self.bits, self.which, self.pieces = orders[which], which, pieces
                self.chunk_rows = sum(piece_rows(piece) for piece in pieces)
                self.step, self.kept, self.got, self.at, self.final = 0, None, None, 0, None

        def piece_rows(piece):
            return {"up": up_rows, "q": qkv_rows, "k": qkv_rows, "v": qkv_rows}.get(
                piece, down_rows
            )

        downs = [("down", fold) for fold in range(folds)]

        def two_streams(parts, first, which):
            streams = [Stream(which, parts[:first]), Stream(which + 1, parts[first:])]
            return [stream for stream in streams if stream.pieces]

        def mlp_streams(first, which):
            return two_streams(["up", *downs], 1 + first, which)

        def attn_streams(first, which):
            return two_streams(["q", "k", "v", "proj"], first, which)

        def write_pieces(values, streams, scratches):
            for stream, scratch in zip(streams, scratches):
                at = 0
                for piece in stream.pieces:
                    size = piece_rows(piece)
                    for chunk in range(n_dev):
                        rows_at = slice(chunk * size, (chunk + 1) * size)
                        if isinstance(piece, tuple):
                            columns = slice(piece[1] * half, (piece[1] + 1) * half)
                            part = values["down"][rows_at, columns]
                        else:
                            part = values[piece][rows_at]
                        scratch[chunk, at : at + size, :] = part.astype(BF16)
                    at += size

        def both_sums(n_own, g_own, fore_a, fore_b, rear_a, rear_b):
            def left(at, size):
                return mm(get_rear(rear_a, at, size), n_own[...], 0, 0) + mm(
                    get_rear(rear_b, at, size), get_rear(fore_b, 0, half), 0, 0
                )

            size = sum(ref.shape[1] for ref in fore_a) - half
            right = mm(g_own[...], get_rear(fore_a, half, size), 0, 0) + mm(
                get_rear(rear_b, 0, half), get_rear(fore_b, half, size), 0, 0
            )
            return left, right

        def write_mlp(*refs):
            left, right = both_sums(*refs)
            return {"up": left(half, hidden), "down": right}

        def write_attn(*refs):
            left, right = both_sums(*refs)
            values = {
                name: left(half + part * heads_width, heads_width)
                for part, name in enumerate(("q", "k", "v"))
            }
            return {**values, "proj": right}

        def make(name, write, streams, n_own, g_own, fore, rear, hold):
            outs = [sds((cut * s.chunk_rows, half), BF16) for s in streams for _ in range(2)]
            count = len(rear[0])

            pieces = len(fore[0])

            def body(n_ref, g_ref, *refs):
                fore_a, fore_b, refs = refs[:pieces], refs[pieces : 2 * pieces], refs[2 * pieces :]
                fore_b = [other_core(ref) for ref in fore_b]
                rear_a, rear_b, refs = refs[:count], refs[count : 2 * count], refs[2 * count :]
                rear_b = [other_core(ref) for ref in rear_b]
                out_refs, scratches = refs[: len(outs)], refs[len(outs) :]
                values = write(n_ref, g_ref, fore_a, fore_b, rear_a, rear_b)
                write_pieces(values, streams, scratches)
                for at, (stream, scratch) in enumerate(zip(streams, scratches)):
                    size = stream.chunk_rows
                    for place in range(n_dev):
                        chunk = scratch[chunk_at(place, stream.which)]
                        to = (place % cut) * size
                        out_refs[2 * at + place // cut][to : to + size, :] = chunk

            results = call(
                body, name, [n_own, g_own, *fore[0], *fore[1], *rear[0], *rear[1]], outs, hold=hold,
                scratch=[pltpu.VMEM((n_dev, s.chunk_rows, half), BF16) for s in streams],
            )
            for at, stream in enumerate(streams):
                stream.kept, stream.sent = results[2 * at], results[2 * at + 1]

        def send_first(streams):
            for stream in streams:
                stream.got, stream.step = over_dev(stream.sent, stream.bits[0]), 1

        def sums_in(ref, at):
            return ref[at : at + sum_rows, :].astype(F32)

        def last_sum(stream, kept, got):
            return kept[...].astype(F32) + got[
                stream.at : stream.at + stream.chunk_rows, :
            ].astype(F32)

        def slot(*args, **kwargs):
            prepare_slot(*args, **kwargs)()

        def prepare_slot(
            name, fresh=(), moving=(), ending=(), sums=None, hold=(), spare=None
        ):
            ins, outs, sizes = [], [], {}
            plan_fresh, plan_moving = [], []

            def room(bit, size):
                at = sizes.get(bit, 0)
                sizes[bit] = at + size
                return at

            def place_of(array):
                for at, known in enumerate(ins):
                    if known is array:
                        return at
                ins.append(array)
                return len(ins) - 1

            for stream in fresh:
                size, bit = stream.sent.shape[0], stream.bits[0]
                plan_fresh.append((place_of(stream.sent), size, bit, room(bit, size)))
            for stream in moving:
                size = stream.kept.shape[0] // 2
                bit = stream.bits[stream.step]
                plan_moving.append(
                    (place_of(stream.kept), place_of(stream.got), stream.at, size,
                     len(outs), bit, room(bit, size))
                )
                outs.append(sds((size, half), BF16))
            plan_ending = []
            for stream in ending:
                plan_ending.append(
                    (stream, place_of(stream.kept), place_of(stream.got), len(outs))
                )
                outs.append(sds((stream.chunk_rows, half)))
            if sums is not None:
                total_at = place_of(sums[0])
                sums_got = None if sums[1] is None else place_of(sums[1])
                sums_room = room(sums[3], sum_rows)
                sums_out = len(outs)
                outs.append(sds((sum_rows, half)))
            if spare is not None:
                spare_at = room(*spare)
            bits_used = sorted(sizes)
            buffer_at = {bit: len(outs) + at for at, bit in enumerate(bits_used)}
            outs += [sds((sizes[bit], half), BF16) for bit in bits_used]

            def body(*refs):
                in_refs, out_refs = refs[: len(ins)], refs[len(ins) :]
                for sent_in, size, bit, at in plan_fresh:
                    out_refs[buffer_at[bit]][at : at + size, :] = in_refs[sent_in][...]
                for kept_in, got_in, got_row, size, kept_at, bit, at in plan_moving:
                    kept, got = in_refs[kept_in], in_refs[got_in]
                    out_refs[kept_at][...] = (
                        kept[:size, :].astype(F32) + got[got_row : got_row + size, :].astype(F32)
                    ).astype(BF16)
                    out_refs[buffer_at[bit]][at : at + size, :] = (
                        kept[size:, :].astype(F32)
                        + got[got_row + size : got_row + 2 * size, :].astype(F32)
                    ).astype(BF16)
                if spare is not None:
                    out_refs[buffer_at[spare[0]]][spare_at:, :] = jnp.zeros((spare[1], half), BF16)
                for stream, kept_in, got_in, out_at in plan_ending:
                    out_refs[out_at][...] = last_sum(stream, in_refs[kept_in], in_refs[got_in])
                if sums is not None:
                    total = in_refs[total_at][...]
                    if sums_got is not None:
                        total = total + sums_in(in_refs[sums_got], sums[2])
                    low = total.astype(BF16)
                    out_refs[sums_out][...] = low.astype(F32)
                    out_refs[buffer_at[sums[3]]][sums_room : sums_room + sum_rows, :] = low

            results = call(body, name, ins, outs, hold=hold)
            for stream, _, _, out_at in plan_ending:
                stream.final = results[out_at]
            for stream, (_, _, _, _, kept_at, _, _) in zip(moving, plan_moving):
                stream.kept = results[kept_at]

            def depart(event=None):
                buffers = {bit: results[buffer_at[bit]] for bit in bits_used}
                if event is not None:
                    buffers = later(buffers, event)
                received = {bit: over_dev(buffers[bit], bit) for bit in bits_used}
                for stream, (_, _, bit, at) in zip(fresh, plan_fresh):
                    stream.got, stream.at, stream.step = received[bit], at, 1
                for stream, (_, _, _, _, _, bit, at) in zip(moving, plan_moving):
                    stream.got, stream.at = received[bit], at
                    stream.step += 1
                if sums is not None:
                    sums[:3] = results[sums_out], received[sums[3]], sums_room

            return depart

        def ship(total, kept, sent):
            packed = mm(placement(images, True), total.astype(BF16), 1, 0).astype(BF16)
            kept[...] = packed[:, :half]
            sent[:rows_in, :] = packed[:, half:]

        shipped = [sds((rows_in, half), BF16)] * 2

        def fold(kept, received, stay, go):
            same = here("ha") == here("wa")
            theirs = received[:rows_in, :]
            stay[...] = jnp.where(same, kept[...], theirs)
            go[:rows_in, :] = jnp.where(same, theirs, kept[...])

        def join(stay, received, out_ref):
            out_ref[...] = stay[...].astype(F32) + received[:rows_in, :].astype(F32)

        def out_body(s_in, fore_ref, wd_a, wd_b, kept, sent):
            hid = fore_ref[:, half:]
            base = jnp.where(here("ha") == 0, s_in[...], 0.0)
            branch = jnp.concatenate([mm(hid, wd_a[1], 1, 0), mm(hid, wd_b[1], 1, 0)], axis=1)
            ship(base + branch, kept, sent)

        streams_d = mlp_streams(SPLIT_D, 0)
        make(
            "wgrad_d", write_mlp, streams_d, n3_own, g3_own, fore3, rear3,
            [*keep_a, *keep_b, *keep_c, *small, *weights, s5],
        )
        send_first(streams_d)

        def add_norm_back(grad, part_a, part_b, stream, gain, sums_ref):
            upstream = part_a[...].astype(F32) + part_b[...].astype(F32)
            units, inv_std = norm_stats(stream)
            sums_ref[0:1, :] = jnp.sum(upstream * units, axis=0, keepdims=True)
            sums_ref[1:2, :] = jnp.sum(upstream, axis=0, keepdims=True)
            return grad + norm_back(upstream, units, inv_std, gain)

        def qkv_back(packed, section, wq_a, wq_b):
            return [
                sum(mm(packed[part], ref[section, part], 1, 1) for part in range(3))
                for ref in (wq_a, wq_b)
            ]

        def channel_back_body(
            g_in_own, g_in_oth, s_in, small_a, small_b, mask_ref, qkv_ref, probs_ref,
            wp_a, wp_b, wq_a, wq_b, *refs,
        ):
            part_a, part_b, g_ref, g_own, part_ref, sums_ref, *rear_refs = refs
            grad = jnp.concatenate([g_in_own[...], g_in_oth[...]], axis=1).astype(F32)
            gain = gain_row((small_a, small_b), 3)
            grad = add_norm_back(grad, part_a, part_b, s_in[...], gain, sums_ref)
            g_ref[...] = grad
            low = grad.astype(BF16)
            g_own[...] = low[:, :half]
            put_rear(rear_refs, 0, low[:, half:])
            grad_mixed = project_back(low, wp_a[1], wp_b[1]).astype(BF16)
            packed = attention_part_back(
                False, grad_mixed, mask_ref, qkv_ref, probs_ref, rear_refs
            )
            own, oth = qkv_back(packed, 1, wq_a, wq_b)
            part_ref[:, :half] = own.astype(BF16)
            part_ref[:, half:] = oth.astype(BF16)

        late = [*fore3[0], *wd, s5]
        (g2, g2_own, back2, sums3, *rear2) = call(
            channel_back_body, "back_c",
            [g3_own, g3_oth, s5, *small, mask, qkv2, probs2, *wp, *wq, back3, far_back3],
            [full, half_low, full_low, sds((2, width)), *rear_shapes(rear_width_attn, 1)],
            flops=attn_flops,
            hold=[*keep_a, *keep_b, s3, s4, n2_own, *fore2[0], *fore2[1], *wu, *wd, *fore3[0]],
        )
        far_back2 = over_ha(back2)
        rear2 = both_rear(rear2, False)
        hid_got, fore0_got = (
            lax.all_gather(later(values, g2), "wa") for values in (fore1[1], fore0)
        )
        fore1, fore0 = (fore1, [n1_got, hid_got]), ([fore0], [fore0_got])
        keep_a.append(fore0_got)
        keep_b.append(hid_got)
        streams_c = attn_streams(SPLIT_C, 2)
        kept_c = [*keep_a, *keep_b, s3, s4, *small, *weights, g2, *late, sums3]
        make("wgrad_c", write_attn, streams_c, n2_own, g2_own, fore2, rear2, kept_c)
        slot(
            "slot_c", fresh=streams_c, moving=streams_d, hold=[*kept_c, back2, far_back2],
        )

        def mlp_back_body(
            g_in, part_a, part_b, s_in, s_before, small_a, small_b, slope_ref,
            wd_a, wd_b, wu_a, wu_b, g_ref, g_own, part_ref, sums_ref, *rear_refs,
        ):
            keep = column_mask(rows)
            gain = gain_row((small_a, small_b), 2)
            grad = add_norm_back(g_in[...], part_a, part_b, s_in[...], gain, sums_ref)
            conv_back_into(g_ref, sums_ref, 2, grad, s_before[...], (small_a, small_b), 1, keep)
            low = g_ref[...].astype(BF16)
            g_own[...] = low[:, :half]
            put_rear(rear_refs, 0, low[:, half:])
            dhid = project_back(low, wd_a[0], wd_b[0]).astype(BF16).astype(F32)
            dpre = (dhid * slope_ref[...]).astype(BF16)
            put_rear(rear_refs, half, dpre)
            part_ref[:, :half] = mm(dpre, wu_a[0], 1, 1).astype(BF16)
            part_ref[:, half:] = mm(dpre, wu_b[0], 1, 1).astype(BF16)

        (g1, g1_own, back1, sums2, *rear1) = call(
            mlp_back_body, "back_b",
            [g2, back2, far_back2, s4, s3, *small, slope1, *wd, *wu],
            [full, half_low, full_low, sds((11, width)), *rear_shapes(rear_width_mlp, 2)],
            flops=mlp_flops,
            hold=[*keep_a, s2, n1_own, *fore1[0], *fore1[1], *wq, *wp, *fore3[0], s5, sums3],
        )
        far_back1 = over_ha(back1)
        rear1 = both_rear(rear1)
        streams_b = mlp_streams(SPLIT_B, 0)
        make(
            "wgrad_b", write_mlp, streams_b, n1_own, g1_own, fore1, rear1,
            [*keep_a, s2, *small, *wq, *wp, g1, *late, sums3, sums2],
        )
        send_first(streams_b)

        def window_back_body(
            g_in, part_a, part_b, s_in, small_a, small_b, qkv_ref, probs_ref, wp_a, wp_b,
            g_ref, g_own, sums_ref, *rear_refs,
        ):
            gain = gain_row((small_a, small_b), 1)
            grad = add_norm_back(g_in[...], part_a, part_b, s_in[...], gain, sums_ref)
            g_ref[...] = grad
            low = grad.astype(BF16)
            g_own[...] = low[:, :half]
            put_rear(rear_refs, 0, low[:, half:])
            grad_mixed = project_back(low, wp_a[0], wp_b[0]).astype(BF16)
            attention_part_back(True, grad_mixed, None, qkv_ref, probs_ref, rear_refs)

        (g0, g0_own, sums1, *rear0) = call(
            window_back_body, "back_a",
            [g1, back1, far_back1, s2, *small, qkv0, probs0, *wp],
            [full, half_low, sds((2, width)), *rear_shapes(rear_width_attn, 1)],
            flops=attn_flops, hold=[x0, n0_own, *fore0[0], *fore0[1], s1, *wq, *late, sums3, sums2],
        )
        every = [*streams_d, *streams_c]
        depart = prepare_slot(
            "slot_cd", moving=every, spare=(2, 16),
            hold=[x0, n0_own, *fore0[0], *fore0[1], s1, *small, *wq, *late, sums1, sums2, sums3,
                  g0, g0_own, *rear0],
        )
        rear0 = both_rear(later(rear0, streams_d[0].kept))

        keep_0 = [g0, s1, x0, *small, *wq, sums1, sums2, sums3, *rear0[0]]
        streams_a = attn_streams(SPLIT_A, 0)
        make("wgrad_a", write_attn, streams_a, n0_own, g0_own, fore0, rear0, [*late, *keep_0])
        every = [*streams_d, *streams_c, *streams_b, *streams_a]
        send_first(streams_a)
        depart()

        sums_at = -(-rows_in // 16) * 16
        sums_half = sds((sum_rows, half))
        with_sums = sds((sums_at + sum_rows, half), BF16)

        def put_sums(ref, total):
            ref[sums_at:, :] = total.astype(BF16)

        def first_back_body(
            g_in, s_in, x_ref, small_a, small_b, wq_a, wq_b, sums_one, sums_two, sums_three, *refs
        ):
            rear_refs, (kept, sent, sums_own, scratch, sums_ref) = refs[:-5], refs[-5:]
            keep = column_mask(rows)
            packed = [
                get_rear(rear_refs, half + part * heads_width, heads_width) for part in range(3)
            ]
            upstream = jnp.concatenate(qkv_back(packed, 0, wq_a, wq_b), axis=1)
            units, inv_std = norm_stats(s_in[...])
            sums_ref[0:1, :] = jnp.sum(upstream * units, axis=0, keepdims=True)
            sums_ref[1:2, :] = jnp.sum(upstream, axis=0, keepdims=True)
            grad = jnp.where(here("ha") == 0, g_in[...], 0.0)
            grad = grad + norm_back(upstream, units, inv_std, gain_row((small_a, small_b), 0))
            conv_back_into(
                scratch, sums_ref, 2, grad, x_ref[...].astype(F32), (small_a, small_b), 0, keep
            )
            ship(scratch[...], kept, sent)
            sums_ref[11:13, :] = 0.5 * sums_one[...]
            sums_ref[13:24, :] = 0.5 * sums_two[...]
            sums_ref[24:26, :] = 0.5 * sums_three[...]
            sums_ref[26:, :] = jnp.zeros((sum_rows - 26, width), F32)
            sums_own[...] = sums_ref[:, :half]
            put_sums(sent, sums_ref[:, half:])

        token_kept, token_sent, sums_own = call(
            first_back_body, "back_0",
            [g0, s1, x0, *small, *wq, sums1, sums2, sums3, *rear0[0]],
            [shipped[0], with_sums, sums_half],
            scratch=[pltpu.VMEM((rows, width), F32), pltpu.VMEM((sum_rows, width), F32)],
            flops=attn_flops * 3 // 4, hold=late,
        )

        def fold_tokens(kept, both, sums_a, stay, go, sums_ref):
            received = other_core(both)
            fold(kept, received, stay, go)
            total = sums_a[...] + sums_in(received, sums_at)
            put_sums(go, total)
            sums_ref[...] = sums_in(go, sums_at)

        token_stay, token_go, sums_chip = call(
            fold_tokens, "fold_tokens",
            [token_kept, lax.all_gather(token_sent, "wa"), sums_own],
            [shipped[0], with_sums, sums_half], hold=late,
        )
        token_got = over_ha(token_go)

        def join_tokens(stay, received, sums_chip, out_ref, sums_ref):
            join(stay, received, out_ref)
            sums_ref[...] = sums_chip[...] + sums_in(received, sums_at)

        owned = sds((rows_in, half))
        grad_tokens, sums_ha = call(
            join_tokens, "join_tokens", [token_stay, token_got, sums_chip], [owned, sums_half],
            hold=late,
        )
        left_bits = list(range(bits))
        sums = [sums_ha, None, 0, left_bits.pop(0)]
        slot("sums_x", sums=sums, spare=(0, 96), hold=late)
        out_kept, out_sent = call(
            out_body, "out_d", [s5, *fore3[0], *wd], shipped, flops=mlp_flops // 2
        )
        def hop():
            if not left_bits:
                return None
            sums[3] = left_bits.pop(0)
            return sums

        turn = 0
        while left_bits or any(stream.step < bits for stream in every):
            turn += 1
            arrived = [s for s in every if s.step == bits and s.final is None]
            slot(f"slot_b{turn}", moving=[s for s in streams_b if s.step < bits])
            second = [s for s in [*streams_d, *streams_a] if s.step < bits]
            depart = prepare_slot(f"slot_a{turn}", moving=second, ending=arrived, sums=hop())
            if turn > 1:
                depart()
                slot(f"slot_c{turn}", moving=[s for s in streams_c if s.step < bits])
                continue
            out_both = lax.all_gather(later(out_sent, streams_a[0].kept), "wa")
            out_stay, out_go = call(
                lambda kept, both, *refs: fold(kept, other_core(both), *refs),
                "fold_out", [out_kept, out_both], shipped,
            )
            depart(out_stay)
            out_got = over_ha(out_go)
        output = call(join, "join_out", [out_stay, out_got], [owned])[0]

        def finish_body(*refs):
            (up, down, qkv, proj, taps_ref, gain_ref, shift_ref) = refs[-7:]
            at = iter(refs)
            total = next(at)[...] + sums_in(next(at), sums[2])
            for branch, row in enumerate((0, 11, 13, 24)):
                gain_ref[branch : branch + 1, :] = total[row : row + 1]
                shift_ref[branch : branch + 1, :] = total[row + 1 : row + 2]
            for section, row in enumerate((2, 15)):
                for t in range(9):
                    taps_ref[t, section : section + 1, :] = total[row + t : row + t + 1]

            def finished(stream):
                if stream.final is not None:
                    return next(at)[...]
                return last_sum(stream, next(at), next(at))

            for section, streams in enumerate(
                ((*streams_a, *streams_b), (*streams_c, *streams_d))
            ):
                for stream in streams:
                    values, row = finished(stream), 0
                    for piece in stream.pieces:
                        part = values[row : row + piece_rows(piece)]
                        row += piece_rows(piece)
                        if piece == "up":
                            up[section] = part
                        elif piece == "proj":
                            proj[section] = part
                        elif isinstance(piece, tuple):
                            down[section, :, piece[1] * half : (piece[1] + 1) * half] = part
                        else:
                            qkv[section, ("q", "k", "v").index(piece)] = part

        ends = []
        for stream in (*streams_a, *streams_b, *streams_c, *streams_d):
            ends += [stream.kept, stream.got] if stream.final is None else [stream.final]
        up, down, qkv, proj, grad_taps, grad_gain, grad_shift = call(
            finish_body, "finish", [*sums[:2], *ends],
            [sds((2, up_rows, half)), sds((2, down_rows, hidden)), sds((2, 3, qkv_rows, half)),
             sds((2, proj_rows, half)), sds((9, 2, half)), sds((4, half)), sds((4, half))],
        )
        grad_taps = jnp.transpose(grad_taps, (1, 0, 2))
        grad_qkv = jnp.transpose(qkv, (0, 3, 1, 2))
        grad_proj, grad_up, grad_down = (
            jnp.transpose(values, (0, 2, 1)) for values in (proj, up, down)
        )
        return (
            output,
            grad_tokens,
            grad_taps,
            grad_gain,
            grad_shift,
            grad_qkv,
            grad_proj,
            grad_up,
            grad_down,
        )

    placed = (
        P(("dev", "ha"), "wa"),
        P(("dev", "ha"), "wa"),
        P(None, None, "wa"),
        P(None, "wa"),
        P(None, "wa"),
        P(None, "wa", None, "ha"),
        P(None, "ha", "wa"),
        P(None, "wa", "ha"),
        P(None, "ha", "wa"),
        P("dev", None),
    )
    return jax.shard_map(
        on_device,
        mesh=mesh,
        in_specs=placed,
        out_specs=(
            P(("dev", "ha"), "wa"),
            P(("dev", "ha"), "wa"),
            P(None, None, "wa"),
            P(None, "wa"),
            P(None, "wa"),
            P(None, "wa", None, ("ha", "dev")),
            P(None, "ha", ("wa", "dev")),
            P(None, "wa", ("ha", "dev")),
            P(None, "ha", ("wa", "dev")),
        ),
        check_vma=False,
    )
```

```python
from functools import partial

import jax
import jax.numpy as jnp
import numpy as np
from jax import lax
from jax.experimental import pallas as pl
from jax.experimental.pallas import tpu as pltpu
from jax.sharding import PartitionSpec as P

WIN = 7
GRID_COLS = 8
PATCHES = 49
PADDED = WIN * GRID_COLS
HEAD_DIM = 32
LANES = 128
HEADS_TILE = LANES // HEAD_DIM
EPS = 1e-05
NEG = -1e30
SPLIT_D, SPLIT_C, SPLIT_B, SPLIT_A = 0, 2, 0, 4
BF16 = jnp.bfloat16
F32 = jnp.float32
VMEM_LIMIT = 16 * 2**20
TIMES = {"pack_small": 5.0, "choose": 5.0}


def mm(left, right, left_dim, right_dim):
    return lax.dot_general(
        left, right, (((left_dim,), (right_dim,)), ((), ())), preferred_element_type=F32
    )


class Order:
    def __init__(self):
        self.last = None


def kernel_call(
    body, name, ins, outs, order, scratch=(), flops=0, hold=(), reuse=None, carry=None
):
    reuse = reuse or {}
    arrays = list(ins) + list(hold) + ([] if order.last is None else [order.last])
    first_reused = len(arrays)
    aliases = {first_reused + at: out for at, out in enumerate(reuse)}
    arrays += list(reuse.values())
    outs = list(outs) + [sds((8, LANES))]

    def wrapped(*refs):
        out_refs = refs[len(arrays) : len(arrays) + len(outs)]
        for at, out in aliases.items():
            carry(refs[at], out_refs[out])
        body(*refs[: len(ins)], *out_refs[:-1], *refs[len(arrays) + len(outs) :])
        out_refs[-1][...] = jnp.zeros_like(out_refs[-1])

    *results, order.last = pl.pallas_call(
        wrapped,
        in_specs=[pl.BlockSpec(memory_space=pltpu.VMEM)] * len(arrays),
        out_specs=[pl.BlockSpec(memory_space=pltpu.VMEM)] * len(outs),
        out_shape=outs,
        scratch_shapes=list(scratch),
        input_output_aliases=aliases,
        compiler_params=pltpu.CompilerParams(vmem_limit_bytes=VMEM_LIMIT),
        cost_estimate=pl.CostEstimate(
            flops=int(TIMES.get(name, 0) * 1.15e9), bytes_accessed=0, transcendentals=0
        ),
        name=name,
    )(*arrays)
    return results


def sds(shape, dtype=F32):
    return jax.ShapeDtypeStruct(shape, dtype)


def column_mask(rows):
    return (lax.broadcasted_iota(jnp.int32, (rows, 1), 0) % GRID_COLS) < WIN


def placement(images, transposed, begin=0, count=None):
    padded, plain = count or images * PADDED, images * PATCHES
    shape = (plain, padded) if transposed else (padded, plain)
    at = lax.broadcasted_iota(jnp.int32, shape, 1 if transposed else 0) + begin
    image = sum((at >= i * PADDED).astype(jnp.int32) for i in range(1, images))
    inside = at - image * PADDED
    source = image * PATCHES + (inside >> 3) * WIN + (inside & 7)
    other = lax.broadcasted_iota(jnp.int32, shape, 0 if transposed else 1)
    return (((inside & 7) < WIN) & (source == other)).astype(F32).astype(BF16)


def side_shifts(values):
    rows = values.shape[0]
    return (pltpu.roll(values, 1, 0), values, pltpu.roll(values, rows - 1, 0))


def as_grid(values):
    return values.reshape(-1, WIN, GRID_COLS, values.shape[-1])


def move_rows(values, step):
    grid = as_grid(values)
    zeros = jnp.zeros_like(grid[:, :1])
    if step > 0:
        moved = jnp.concatenate([zeros, grid[:, :-1]], axis=1)
    else:
        moved = jnp.concatenate([grid[:, 1:], zeros], axis=1)
    return moved.reshape(values.shape)


def conv_cols(values, taps, keep):
    shifted = side_shifts(values)
    line = [
        sum(shifted[col] * taps[3 * row + col] for col in range(3)) for row in range(3)
    ]
    total = values + line[1] + move_rows(line[0], 1) + move_rows(line[2], -1)
    return jnp.where(keep, total, 0.0)


def tap_sums(grads, values):
    shifted = side_shifts(values)
    grad_grid = as_grid(grads)
    sums = []
    for row in range(3):
        for col in range(3):
            moved = as_grid(shifted[col])
            if row == 0:
                prod = grad_grid[:, 1:] * moved[:, :-1]
            elif row == 1:
                prod = grad_grid * moved
            else:
                prod = grad_grid[:, :-1] * moved[:, 1:]
            flat = prod.reshape(-1, GRID_COLS, prod.shape[-1])
            sums.append(jnp.sum(jnp.sum(flat, axis=0), axis=0, keepdims=True))
    return sums


def norm_stats(stream):
    width = stream.shape[1]
    center = jnp.sum(stream, axis=1, keepdims=True) * (1.0 / width)
    moved = stream - center
    inv_std = lax.rsqrt(jnp.sum(moved * moved, axis=1, keepdims=True) * (1.0 / width) + EPS)
    return moved * inv_std, inv_std


def norm_back(upstream, units, inv_std, gain):
    width = upstream.shape[1]
    scaled = upstream * gain
    first = jnp.sum(scaled, axis=1, keepdims=True) * (1.0 / width)
    second = jnp.sum(scaled * units, axis=1, keepdims=True) * (1.0 / width)
    return inv_std * (scaled - first - units * second)


def gelu_parts(values):
    below = 0.5 + 0.5 * lax.erf(values * float(0.5**0.5))
    bell = jnp.exp2(values * values * float(-0.5 * np.log2(np.e)))
    return below, bell * float(1.0 / np.sqrt(2.0 * np.pi))


def head_mask(index):
    return (lax.broadcasted_iota(jnp.int32, (1, LANES), 1) // HEAD_DIM) == index


def spread_heads(tile):
    return jnp.concatenate(
        [jnp.where(head_mask(j), tile, 0.0) for j in range(HEADS_TILE)], axis=0
    ).astype(BF16)


def gather_heads(stacked):
    rows = stacked.shape[0] // HEADS_TILE
    total = jnp.where(head_mask(0), stacked[:rows], 0.0)
    for j in range(1, HEADS_TILE):
        total = jnp.where(head_mask(j), stacked[j * rows : (j + 1) * rows], total)
    return total


def softmax_rows(scores):
    top = jnp.max(scores, axis=0, keepdims=True)
    weights = jnp.exp(scores - top)
    return weights * (1.0 / jnp.sum(weights, axis=0, keepdims=True))


SCALE = HEAD_DIM**-0.5


def low(tiles):
    return [tile.astype(BF16) for tile in tiles]


def minus_row_sums(probs, grads):
    return [
        (p * (g - jnp.sum(g * p, axis=0, keepdims=True))).astype(BF16)
        for p, g in zip(probs, grads)
    ]


def window_tiles(queries, keys, values):
    keys_ok = column_mask(PADDED)
    scores = [
        mm(k, spread_heads(q), 1, 1) * SCALE for q, k in zip(queries, low(keys))
    ]
    probs = [softmax_rows(jnp.where(keys_ok, score, NEG)) for score in scores]
    mixed = [mm(p, v, 0, 0) for p, v in zip(low(probs), low(values))]
    return probs, [gather_heads(tile) for tile in mixed]


def window_tiles_back(queries, keys, values, probs, grads):
    q_big, g_big = ([spread_heads(tile) for tile in tiles] for tiles in (queries, grads))
    grad_probs = [mm(v, g, 1, 1) for v, g in zip(low(values), g_big)]
    grad_v = [mm(p, g, 1, 0) for p, g in zip(low(probs), g_big)]
    grad_scores = minus_row_sums(probs, grad_probs)
    grad_k = [mm(d, q, 1, 0) * SCALE for d, q in zip(grad_scores, q_big)]
    grad_q = [mm(d, k, 0, 0) for d, k in zip(grad_scores, low(keys))]
    return [gather_heads(tile) * SCALE for tile in grad_q], grad_k, grad_v


def same_head():
    first = lax.broadcasted_iota(jnp.int32, (LANES, LANES), 0) // HEAD_DIM
    second = lax.broadcasted_iota(jnp.int32, (LANES, LANES), 1) // HEAD_DIM
    return first == second


def channel_tiles(queries, keys, values, masks):
    own_head = same_head()
    masked = low([q * mask for q, mask in zip(queries, masks)])
    scores = [mm(k, q, 0, 0) * SCALE for q, k in zip(masked, low(keys))]
    probs = [softmax_rows(jnp.where(own_head, score, NEG)) for score in scores]
    return probs, [mm(v, p, 1, 0) for p, v in zip(low(probs), low(values))]


def channel_tiles_back(queries, keys, values, probs, grads, masks):
    masked = low([q * mask for q, mask in zip(queries, masks)])
    grads = low(grads)
    grad_probs = [mm(v, g, 0, 0) for v, g in zip(low(values), grads)]
    grad_v = [mm(g, p, 1, 1) for g, p in zip(grads, low(probs))]
    grad_scores = minus_row_sums(probs, grad_probs)
    grad_q = [mm(k, d, 1, 0) * SCALE * m for k, d, m in zip(low(keys), grad_scores, masks)]
    grad_k = [mm(q, d, 1, 1) * SCALE for q, d in zip(masked, grad_scores)]
    return grad_q, grad_k, grad_v


def cut_tiles(values, images, tiles):
    return [
        values[image * PADDED : (image + 1) * PADDED, tile * LANES : (tile + 1) * LANES]
        for image in range(images)
        for tile in range(tiles)
    ]


def paste_tiles(parts, images, tiles):
    lines = [
        jnp.concatenate(parts[image * tiles : (image + 1) * tiles], axis=1)
        for image in range(images)
    ]
    return jnp.concatenate(lines, axis=0).astype(BF16)


def solution(mesh):
    n_dev = mesh.shape["dev"]
    bits = n_dev.bit_length() - 1
    assert n_dev == 1 << bits and mesh.shape["ha"] == 2 and mesh.shape["wa"] == 2

    swap = [(0, 1), (1, 0)]

    def over_ha(values):
        return lax.ppermute(values, "ha", swap)

    def over_wa(values):
        return lax.ppermute(values, "wa", swap)

    partner = [1 << bit for bit in range(bits)]
    if bits > 2:
        partner[2] = 6

    def over_dev(values, bit):
        return lax.ppermute(values, "dev", [(i, i ^ partner[bit]) for i in range(n_dev)])

    def on_device(
        tokens, cotangent, conv_taps, norm_gain, norm_shift, w_qkv, w_proj, w_up, w_down, valid
    ):
        rows_in, half = tokens.shape
        images = rows_in // PATCHES
        rows = images * PADDED
        width = 2 * half
        heads_width = w_qkv.shape[3]
        hidden = w_up.shape[2]
        tiles = heads_width // LANES
        assert heads_width == half
        rest = list(range(3, bits))
        orders = [[0, 1, 2, *rest], [1, 0, 2, *rest], [0, 2, 1, *rest], [1, 2, 0, *rest]]

        def here(name):
            return lax.axis_index(name)

        def chunk_at(place, which):
            found = 0
            for step, bit in enumerate(orders[which]):
                found ^= ((place >> (bits - 1 - step)) & 1) * partner[bit]
            return found ^ here("dev")

        order = Order()
        call = partial(kernel_call, order=order)

        def later(values, event):
            return lax.optimization_barrier((values, event))[0]

        def pack_small(taps_ref, gain_ref, shift_ref, out_ref):
            for section in range(2):
                for t in range(9):
                    at = 9 * section + t
                    out_ref[at : at + 1, :] = taps_ref[t, section : section + 1, :]
            out_ref[18:22, :] = gain_ref[...]
            out_ref[22:26, :] = shift_ref[...]

        def choose(mine, received, own, *others):
            same = here("ha") == here("wa")
            own[...] = jnp.where(same, mine[...], received[...])
            other, at = jnp.where(same, received[...], mine[...]), 0
            for ref in others:
                ref[...] = other[:, at : at + ref.shape[1]]
                at += ref.shape[1]

        wq_own = jnp.transpose(w_qkv, (0, 2, 1, 3))
        wq, wp = (wq_own, over_wa(wq_own)), (w_proj, over_wa(w_proj))
        tokens_in, cot_in = over_ha(tokens), over_ha(cotangent)
        small_own = call(
            pack_small, "pack_small",
            [jnp.transpose(conv_taps, (1, 0, 2)), norm_gain, norm_shift], [sds((26, half))],
            hold=[tokens],
        )[0]
        small = (small_own, over_wa(small_own))
        chosen = [sds((rows_in, columns), BF16) for columns in (half, LANES, half - LANES)]
        tokens_own, *tokens_oth = call(
            choose, "choose", [tokens, tokens_in], chosen, hold=[wq[1], wp[1], small_own]
        )
        token_parts = (tokens_own, *[over_wa(values) for values in tokens_oth])

        def arrive(out_ref):
            out_ref[...] = jnp.zeros_like(out_ref)

        arrived = call(
            arrive, "arrive", [], [sds((8, LANES))],
            hold=[*token_parts, small[1], cot_in, small_own, wq[1], wp[1]],
        )[0]
        wu, wd = ((values, over_wa(later(values, arrived))) for values in (w_up, w_down))

        def unpack(parts, begin=0, count=None):
            values = jnp.concatenate([part[...] for part in parts], axis=1)
            return mm(placement(images, False, begin, count), values, 1, 0)

        def gain_row(refs, branch):
            return jnp.concatenate([ref[18 + branch : 19 + branch, :] for ref in refs], axis=1)

        def shift_row(refs, branch):
            return jnp.concatenate([ref[22 + branch : 23 + branch, :] for ref in refs], axis=1)

        def tap_rows(small_refs, section, col, flipped):
            ref = small_refs[col // half]
            at = col % half
            found = [
                ref[9 * section + t : 9 * section + t + 1, at : at + LANES] for t in range(9)
            ]
            return found[::-1] if flipped else found

        def project_in(normed, first, second):
            return mm(normed[:, :half], first, 1, 0) + mm(normed[:, half:], second, 1, 0)

        def project_back(values, first, second):
            return mm(values[:, :half], first, 1, 1) + mm(values[:, half:], second, 1, 1)

        def to_normed(stream, small_refs, branch):
            units, _ = norm_stats(stream)
            return (units * gain_row(small_refs, branch) + shift_row(small_refs, branch)).astype(
                BF16
            )

        def both_rear(pieces, gather=True):
            pieces = list(pieces)
            if gather:
                return pieces, [lax.all_gather(piece, "wa") for piece in pieces]
            return pieces, [over_wa(piece) for piece in pieces]

        def other_core(ref):
            return ref.at[1 - here("wa")] if len(ref.shape) == 3 else ref

        def put_both(own_ref, oth_ref, values):
            own_ref[...] = values[:, :half]
            oth_ref[:, :half] = values[:, half:]

        def add_parts(stream, part_a, part_b):
            return stream + part_a[...].astype(F32) + part_b[...].astype(F32)

        def attention_part(
            window, section, normed, valid_rows, wq_a, wq_b, qkv_ref, probs_ref, first_image
        ):
            count = normed.shape[0] // PADDED
            packed = [
                project_in(normed, wq_a[section, part], wq_b[section, part]).astype(BF16)
                for part in range(3)
            ]
            begin = first_image * PADDED
            for part in range(3):
                qkv_ref[part, begin : begin + count * PADDED, :] = packed[part]
            q, k, v = (cut_tiles(part.astype(F32), count, tiles) for part in packed)
            if window:
                probs, mixed = window_tiles(q, k, v)
            else:
                masks = [mask for mask in valid_rows for _ in range(tiles)]
                probs, mixed = channel_tiles(q, k, v, masks)
            for at, tile in enumerate(probs):
                probs_ref[first_image * tiles + at] = tile
            return paste_tiles(mixed, count, tiles)

        def attention_part_back(window, grad_mixed, mask_ref, qkv_ref, probs_ref, rear_refs):
            q, k, v = (
                cut_tiles(qkv_ref[part].astype(F32), images, tiles) for part in range(3)
            )
            grads = cut_tiles(grad_mixed.astype(F32), images, tiles)
            probs = [probs_ref[at] for at in range(images * tiles)]
            if window:
                found = window_tiles_back(q, k, v, probs, grads)
            else:
                masks = [
                    mask_ref[image * PADDED : (image + 1) * PADDED, :]
                    for image in range(images)
                    for _ in range(tiles)
                ]
                found = channel_tiles_back(q, k, v, probs, grads, masks)
            packed = [paste_tiles(part, images, tiles) for part in found]
            for part in range(3):
                put_rear(rear_refs, half + part * heads_width, packed[part])
            return packed

        def mul_out(left, section, own_ref, oth_ref, out_ref):
            out_ref[:, :half] = mm(left, own_ref[section], 1, 0).astype(BF16)
            out_ref[:, half:] = mm(left, oth_ref[section], 1, 0).astype(BF16)

        def conv_into(out_ref, rows_at, values, small_refs, section, keep):
            for col in range(0, width, LANES):
                taps = tap_rows(small_refs, section, col, False)
                out_ref[rows_at, col : col + LANES] = conv_cols(
                    values[:, col : col + LANES], taps, keep
                )

        def conv_back_into(out_ref, sums_ref, sums_at, grads, values, small_refs, section, keep):
            for col in range(0, width, LANES):
                lanes_at = slice(col, col + LANES)
                taps = tap_rows(small_refs, section, col, True)
                for t, total in enumerate(tap_sums(grads[:, lanes_at], values[:, lanes_at])):
                    sums_ref[sums_at + t : sums_at + t + 1, lanes_at] = total
                out_ref[:, lanes_at] = conv_cols(grads[:, lanes_at], taps, keep)

        window_probs = sds((images * tiles, PADDED, HEADS_TILE * PADDED))
        channel_probs = sds((images * tiles, LANES, LANES))
        full, full_low = sds((rows, width)), sds((rows, width), BF16)
        half_low = sds((rows, half), BF16)
        hid_low = sds((rows, hidden), BF16)
        qkv_low = sds((3, rows, heads_width), BF16)
        fore_attn = sds((rows, half + heads_width), BF16)
        def cuts(total, count):
            tiles_all = total // LANES
            return [LANES * (-(-tiles_all * (at + 1) // count)) for at in range(count)]

        def rear_shapes(total, count):
            ends = cuts(total, count)
            return [sds((rows, e - b), BF16) for b, e in zip([0, *ends], ends)]

        def rear_ranges(refs, at, size):
            begin = 0
            for ref in refs:
                end = begin + ref.shape[1]
                low, high = max(begin, at), min(end, at + size)
                if low < high:
                    yield ref, low - begin, high - begin, low - at
                begin = end

        def put_rear(refs, at, values, span=slice(None)):
            for ref, low, high, source in rear_ranges(refs, at, values.shape[1]):
                ref[span, low:high] = values[:, source : source + high - low]

        def get_rear(refs, at, size):
            parts = [ref[:, low:high] for ref, low, high, _ in rear_ranges(refs, at, size)]
            return parts[0] if len(parts) == 1 else jnp.concatenate(parts, axis=1)

        rear_width_attn, rear_width_mlp = half + 3 * heads_width, half + hidden
        fore_mlp = sds((rows, rear_width_mlp), BF16)
        attn_flops = 2 * rows * (4 * width * heads_width)
        mlp_flops = 2 * rows * (2 * width * hidden)

        split = (images + 1) // 2
        chunks = [(0, split), (split, images)] if split < images else [(0, images)]
        spans = [slice(begin * PADDED, end * PADDED) for begin, end in chunks]

        def chunk_rows(span):
            return span.stop - span.start

        def part_shape(span):
            return sds((chunk_rows(span), width), BF16)

        def put_normed(own_ref, fore_refs, span, normed):
            own_ref[span, :] = normed[:, :half]
            put_rear(fore_refs, 0, normed[:, half:], span)

        def first_body(chunk, span):
            def body(
                tokens_a, tokens_b, tokens_c, small_a, small_b, wq_a, wq_b, wp_a, wp_b,
                x_ref, s_ref, n_own, fore_ref, qkv_ref, probs_ref, part_ref, *copies,
            ):
                if copies:
                    copies[0][...], copies[1][...] = small_a[...], small_b[...]
                keep = column_mask(chunk_rows(span))
                stream = unpack((tokens_a, tokens_b, tokens_c), span.start, chunk_rows(span))
                x_ref[span, :] = stream.astype(BF16)
                conv_into(s_ref, span, stream, (small_a, small_b), 0, keep)
                normed = to_normed(s_ref[span, :], (small_a, small_b), 0)
                put_normed(n_own, [fore_ref], span, normed)
                mixed = attention_part(
                    True, 0, normed, None, wq_a, wq_b, qkv_ref, probs_ref, chunk[0]
                )
                fore_ref[span, half:] = mixed
                mul_out(mixed, 0, wp_a, wp_b, part_ref)

            return body

        def carry_spans(upto):
            def carry(old, new):
                for chunk, span in zip(chunks[:upto], spans[:upto]):
                    if old.shape[0] == rows:
                        new[span, :] = old[span, :]
                    elif old.shape[1] == rows:
                        new[:, span, :] = old[:, span, :]
                    else:
                        per_image = old.shape[0] // images
                        held = slice(chunk[0] * per_image, chunk[1] * per_image)
                        new[held] = old[held]

            return carry

        def in_chunks(
            name, make_body, ins, shapes, hold, extra=(), between=None, alone=True
        ):
            arrays, parts, fars, more = None, [], [], []
            for at, (chunk, span) in enumerate(zip(chunks, spans)):
                results = call(
                    make_body(chunk, span), f"{name}{at}", ins(at),
                    [*shapes, *([part_shape(span)] if alone else ()), *(extra if at == 0 else ())],
                    hold=[*hold, *more, *parts],
                    reuse=None if arrays is None else dict(enumerate(arrays)),
                    carry=carry_spans(at),
                )
                arrays, rest = results[: len(shapes)], results[len(shapes) :]
                if alone:
                    parts.append(rest[0])
                    fars.append(over_ha(rest[0]))
                more = more or rest[1:]
                if at == 0 and between is not None:
                    between(arrays, more)
            return arrays, parts, fars, more

        small_in, cot_parts = small, []

        def choose_cot(arrays, more):
            own, *others = call(
                choose, "choose_cot", [cotangent, cot_in], chosen,
                hold=[*arrays, *more, *wq, *wp],
            )
            cot_parts.extend([own, *others])

        (x0, s1, n0_own, fore0, qkv0, probs0), part0, far0, small = in_chunks(
            "attn_a", first_body, lambda at: [*token_parts, *small_in, *wq, *wp],
            [full_low, full, half_low, fore_attn, qkv_low, window_probs], [cot_in, arrived],
            [sds((26, half))] * 2, choose_cot,
        )
        keep_a = [x0, n0_own, fore0, qkv0, probs0, s1]

        def mlp_body(chunk, span):
            def body(
                s_in, part_a, part_b, small_a, small_b, wu_a, wu_b, wd_a, wd_b,
                s_ref, n_own, slope_ref, *refs,
            ):
                *fore_refs, part_ref = refs
                s_ref[span, :] = add_parts(s_in[span, :], part_a, part_b)
                normed = to_normed(s_ref[span, :], (small_a, small_b), 1)
                put_normed(n_own, fore_refs, span, normed)
                pre = project_in(normed, wu_a[0], wu_b[0])
                below, bell = gelu_parts(pre)
                hid = (pre * below).astype(BF16)
                put_rear(fore_refs, half, hid, span)
                slope_ref[span, :] = below + pre * bell
                mul_out(hid, 0, wd_a, wd_b, part_ref)

            return body

        (s2, n1_own, slope1, *fore1), part1, far1, _ = in_chunks(
            "mlp_b", mlp_body, lambda at: [s1, part0[at], far0[at], *small, *wu, *wd],
            [full, half_low, sds((rows, hidden)), half_low, hid_low],
            [*keep_a, *wq, *wp, *cot_parts],
        )
        n1_got = over_wa(fore1[0])
        cot_parts[1:] = [over_wa(later(values, part1[0])) for values in cot_parts[1:]]
        keep_b = [s2, n1_own, *fore1, slope1, n1_got]
        weights = [*wq, *wp, *wu, *wd]

        def channel_body(chunk, span):
            def body(
                s_in, part_a, part_b, valid_ref, small_a, small_b, wq_a, wq_b, wp_a, wp_b,
                s_before, s_ref, n_own, qkv_ref, probs_ref, mask_ref, *refs,
            ):
                *fore_refs, part_ref = refs
                keep = column_mask(chunk_rows(span))
                stream = jnp.where(keep, add_parts(s_in[span, :], part_a, part_b), 0.0)
                s_before[span, :] = stream
                conv_into(s_ref, span, stream, (small_a, small_b), 1, keep)
                normed = to_normed(s_ref[span, :], (small_a, small_b), 2)
                put_normed(n_own, fore_refs, span, normed)
                one_image = placement(1, False).astype(F32)
                valid_rows = []
                for image in range(*chunk):
                    line = jnp.where(
                        here("wa") == 0,
                        valid_ref[image : image + 1, :],
                        valid_ref[images + image : images + image + 1, :],
                    ).astype(F32)
                    valid_rows.append(jnp.sum(one_image * line, axis=1, keepdims=True))
                    mask_ref[image * PADDED : (image + 1) * PADDED, :] = valid_rows[-1]
                mixed = attention_part(
                    False, 1, normed, valid_rows, wq_a, wq_b, qkv_ref, probs_ref, chunk[0]
                )
                put_rear(fore_refs, half, mixed, span)
                mul_out(mixed, 1, wp_a, wp_b, part_ref)

            return body

        (s3, s4, n2_own, qkv2, probs2, mask, *fore2), part2, far2, _ = in_chunks(
            "attn_c", channel_body,
            lambda at: [s2, part1[at], far1[at], valid, *small, *wq, *wp],
            [full, full, half_low, qkv_low, channel_probs, sds((rows, 1)), half_low, half_low],
            [*keep_a, *keep_b, *wu, *wd, *cot_parts],
        )
        fore2 = both_rear(fore2, False)
        keep_c = [s3, s4, n2_own, *fore2[0], qkv2, probs2, mask]

        def cot_body(cot_a, cot_b, cot_c, wd_a, wd_b, g_own, g_oth, dhid_ref):
            grad = unpack((cot_a, cot_b, cot_c)).astype(BF16)
            put_both(g_own, g_oth, grad)
            dhid_ref[...] = project_back(grad, wd_a[1], wd_b[1]).astype(BF16)

        g3_own, g3_oth, dhid3 = call(
            cot_body, "cot_d",
            [*cot_parts, *wd],
            [half_low, half_low, hid_low],
            flops=mlp_flops // 2,
            hold=[*keep_a, *keep_b, *keep_c, *small, *wq, *wp, *wu],
        )


        def last_body(chunk, span):
            def body(
                s_in, part_a, part_b, small_a, small_b, dhid_ref, g_oth, wu_a, wu_b,
                s_ref, n_own, fore_ref, *refs,
            ):
                share, *rear_refs = refs
                s_ref[span, :] = add_parts(s_in[span, :], part_a, part_b)
                normed = to_normed(s_ref[span, :], (small_a, small_b), 3)
                put_normed(n_own, [fore_ref], span, normed)
                pre = project_in(normed, wu_a[1], wu_b[1])
                below, bell = gelu_parts(pre)
                fore_ref[span, half:] = (pre * below).astype(BF16)
                dpre = (dhid_ref[span, :].astype(F32) * (below + pre * bell)).astype(BF16)
                put_rear(rear_refs, 0, g_oth[span, :], span)
                put_rear(rear_refs, half, dpre, span)
                share[span, :half] = mm(dpre, wu_a[1], 1, 1).astype(BF16)
                share[span, half:] = mm(dpre, wu_b[1], 1, 1).astype(BF16)

            return body

        (s5, n3_own, fore3, back3, *rear3), _, _, _ = in_chunks(
            "mlp_d", last_body,
            lambda at: [s4, part2[at], far2[at], *small, dhid3, g3_oth, *wu],
            [full, half_low, fore_mlp, full_low, *rear_shapes(rear_width_mlp, 2)],
            [*keep_a, *keep_b, *keep_c, *fore2[1], g3_own, *wq, *wp, *wd], alone=False,
        )
        far_back3 = over_ha(back3)
        fore3 = both_rear([fore3], False)
        keep_c += fore2[1]
        rear3 = both_rear(rear3, False)

        up_rows, down_rows = hidden // n_dev, half // n_dev
        qkv_rows, proj_rows = heads_width // n_dev, half // n_dev
        folds = hidden // half
        cut = n_dev // 2
        sum_rows = 32

        class Stream:
            def __init__(self, which, pieces):
                self.bits, self.which, self.pieces = orders[which], which, pieces
                self.chunk_rows = sum(piece_rows(piece) for piece in pieces)
                self.step, self.kept, self.got, self.at, self.final = 0, None, None, 0, None

        def piece_rows(piece):
            return {"up": up_rows, "q": qkv_rows, "k": qkv_rows, "v": qkv_rows}.get(
                piece, down_rows
            )

        downs = [("down", fold) for fold in range(folds)]

        def two_streams(parts, first, which):
            streams = [Stream(which, parts[:first]), Stream(which + 1, parts[first:])]
            return [stream for stream in streams if stream.pieces]

        def mlp_streams(first, which):
            return two_streams(["up", *downs], 1 + first, which)

        def attn_streams(first, which):
            return two_streams(["q", "k", "v", "proj"], first, which)

        def write_pieces(values, streams, scratches):
            for stream, scratch in zip(streams, scratches):
                at = 0
                for piece in stream.pieces:
                    size = piece_rows(piece)
                    for chunk in range(n_dev):
                        rows_at = slice(chunk * size, (chunk + 1) * size)
                        if isinstance(piece, tuple):
                            columns = slice(piece[1] * half, (piece[1] + 1) * half)
                            part = values["down"][rows_at, columns]
                        else:
                            part = values[piece][rows_at]
                        scratch[chunk, at : at + size, :] = part.astype(BF16)
                    at += size

        def both_sums(n_own, g_own, fore_a, fore_b, rear_a, rear_b):
            def left(at, size):
                return mm(get_rear(rear_a, at, size), n_own[...], 0, 0) + mm(
                    get_rear(rear_b, at, size), get_rear(fore_b, 0, half), 0, 0
                )

            size = sum(ref.shape[1] for ref in fore_a) - half
            right = mm(g_own[...], get_rear(fore_a, half, size), 0, 0) + mm(
                get_rear(rear_b, 0, half), get_rear(fore_b, half, size), 0, 0
            )
            return left, right

        def write_mlp(*refs):
            left, right = both_sums(*refs)
            return {"up": left(half, hidden), "down": right}

        def write_attn(*refs):
            left, right = both_sums(*refs)
            values = {
                name: left(half + part * heads_width, heads_width)
                for part, name in enumerate(("q", "k", "v"))
            }
            return {**values, "proj": right}

        def make(name, write, streams, n_own, g_own, fore, rear, hold):
            outs = [sds((cut * s.chunk_rows, half), BF16) for s in streams for _ in range(2)]
            count = len(rear[0])

            pieces = len(fore[0])

            def body(n_ref, g_ref, *refs):
                fore_a, fore_b, refs = refs[:pieces], refs[pieces : 2 * pieces], refs[2 * pieces :]
                fore_b = [other_core(ref) for ref in fore_b]
                rear_a, rear_b, refs = refs[:count], refs[count : 2 * count], refs[2 * count :]
                rear_b = [other_core(ref) for ref in rear_b]
                out_refs, scratches = refs[: len(outs)], refs[len(outs) :]
                values = write(n_ref, g_ref, fore_a, fore_b, rear_a, rear_b)
                write_pieces(values, streams, scratches)
                for at, (stream, scratch) in enumerate(zip(streams, scratches)):
                    size = stream.chunk_rows
                    for place in range(n_dev):
                        chunk = scratch[chunk_at(place, stream.which)]
                        to = (place % cut) * size
                        out_refs[2 * at + place // cut][to : to + size, :] = chunk

            results = call(
                body, name, [n_own, g_own, *fore[0], *fore[1], *rear[0], *rear[1]], outs, hold=hold,
                scratch=[pltpu.VMEM((n_dev, s.chunk_rows, half), BF16) for s in streams],
            )
            for at, stream in enumerate(streams):
                stream.kept, stream.sent = results[2 * at], results[2 * at + 1]

        def send_first(streams):
            for stream in streams:
                stream.got, stream.step = over_dev(stream.sent, stream.bits[0]), 1

        def sums_in(ref, at):
            return ref[at : at + sum_rows, :].astype(F32)

        def last_sum(stream, kept, got):
            return kept[...].astype(F32) + got[
                stream.at : stream.at + stream.chunk_rows, :
            ].astype(F32)

        def slot(*args, **kwargs):
            prepare_slot(*args, **kwargs)()

        def prepare_slot(
            name, fresh=(), moving=(), ending=(), sums=None, hold=(), spare=None
        ):
            ins, outs, sizes = [], [], {}
            plan_fresh, plan_moving = [], []

            def room(bit, size):
                at = sizes.get(bit, 0)
                sizes[bit] = at + size
                return at

            def place_of(array):
                for at, known in enumerate(ins):
                    if known is array:
                        return at
                ins.append(array)
                return len(ins) - 1

            for stream in fresh:
                size, bit = stream.sent.shape[0], stream.bits[0]
                plan_fresh.append((place_of(stream.sent), size, bit, room(bit, size)))
            for stream in moving:
                size = stream.kept.shape[0] // 2
                bit = stream.bits[stream.step]
                plan_moving.append(
                    (place_of(stream.kept), place_of(stream.got), stream.at, size,
                     len(outs), bit, room(bit, size))
                )
                outs.append(sds((size, half), BF16))
            plan_ending = []
            for stream in ending:
                plan_ending.append(
                    (stream, place_of(stream.kept), place_of(stream.got), len(outs))
                )
                outs.append(sds((stream.chunk_rows, half)))
            if sums is not None:
                total_at = place_of(sums[0])
                sums_got = None if sums[1] is None else place_of(sums[1])
                sums_room = room(sums[3], sum_rows)
                sums_out = len(outs)
                outs.append(sds((sum_rows, half)))
            if spare is not None:
                spare_at = room(*spare)
            bits_used = sorted(sizes)
            buffer_at = {bit: len(outs) + at for at, bit in enumerate(bits_used)}
            outs += [sds((sizes[bit], half), BF16) for bit in bits_used]

            def body(*refs):
                in_refs, out_refs = refs[: len(ins)], refs[len(ins) :]
                for sent_in, size, bit, at in plan_fresh:
                    out_refs[buffer_at[bit]][at : at + size, :] = in_refs[sent_in][...]
                for kept_in, got_in, got_row, size, kept_at, bit, at in plan_moving:
                    kept, got = in_refs[kept_in], in_refs[got_in]
                    out_refs[kept_at][...] = (
                        kept[:size, :].astype(F32) + got[got_row : got_row + size, :].astype(F32)
                    ).astype(BF16)
                    out_refs[buffer_at[bit]][at : at + size, :] = (
                        kept[size:, :].astype(F32)
                        + got[got_row + size : got_row + 2 * size, :].astype(F32)
                    ).astype(BF16)
                if spare is not None:
                    out_refs[buffer_at[spare[0]]][spare_at:, :] = jnp.zeros((spare[1], half), BF16)
                for stream, kept_in, got_in, out_at in plan_ending:
                    out_refs[out_at][...] = last_sum(stream, in_refs[kept_in], in_refs[got_in])
                if sums is not None:
                    total = in_refs[total_at][...]
                    if sums_got is not None:
                        total = total + sums_in(in_refs[sums_got], sums[2])
                    low = total.astype(BF16)
                    out_refs[sums_out][...] = low.astype(F32)
                    out_refs[buffer_at[sums[3]]][sums_room : sums_room + sum_rows, :] = low

            results = call(body, name, ins, outs, hold=hold)
            for stream, _, _, out_at in plan_ending:
                stream.final = results[out_at]
            for stream, (_, _, _, _, kept_at, _, _) in zip(moving, plan_moving):
                stream.kept = results[kept_at]

            def depart(event=None):
                buffers = {bit: results[buffer_at[bit]] for bit in bits_used}
                if event is not None:
                    buffers = later(buffers, event)
                received = {bit: over_dev(buffers[bit], bit) for bit in bits_used}
                for stream, (_, _, bit, at) in zip(fresh, plan_fresh):
                    stream.got, stream.at, stream.step = received[bit], at, 1
                for stream, (_, _, _, _, _, bit, at) in zip(moving, plan_moving):
                    stream.got, stream.at = received[bit], at
                    stream.step += 1
                if sums is not None:
                    sums[:3] = results[sums_out], received[sums[3]], sums_room

            return depart

        def ship(total, kept, sent):
            packed = mm(placement(images, True), total.astype(BF16), 1, 0).astype(BF16)
            kept[...] = packed[:, :half]
            sent[:rows_in, :] = packed[:, half:]

        shipped = [sds((rows_in, half), BF16)] * 2

        def fold(kept, received, stay, go):
            same = here("ha") == here("wa")
            theirs = received[:rows_in, :]
            stay[...] = jnp.where(same, kept[...], theirs)
            go[:rows_in, :] = jnp.where(same, theirs, kept[...])

        def join(stay, received, out_ref):
            out_ref[...] = stay[...].astype(F32) + received[:rows_in, :].astype(F32)

        def out_body(s_in, fore_ref, wd_a, wd_b, kept, sent):
            hid = fore_ref[:, half:]
            base = jnp.where(here("ha") == 0, s_in[...], 0.0)
            branch = jnp.concatenate([mm(hid, wd_a[1], 1, 0), mm(hid, wd_b[1], 1, 0)], axis=1)
            ship(base + branch, kept, sent)

        streams_d = mlp_streams(SPLIT_D, 0)
        make(
            "wgrad_d", write_mlp, streams_d, n3_own, g3_own, fore3, rear3,
            [*keep_a, *keep_b, *keep_c, *small, *weights, s5],
        )
        send_first(streams_d)

        def add_norm_back(grad, part_a, part_b, stream, gain, sums_ref):
            upstream = part_a[...].astype(F32) + part_b[...].astype(F32)
            units, inv_std = norm_stats(stream)
            sums_ref[0:1, :] = jnp.sum(upstream * units, axis=0, keepdims=True)
            sums_ref[1:2, :] = jnp.sum(upstream, axis=0, keepdims=True)
            return grad + norm_back(upstream, units, inv_std, gain)

        def qkv_back(packed, section, wq_a, wq_b):
            return [
                sum(mm(packed[part], ref[section, part], 1, 1) for part in range(3))
                for ref in (wq_a, wq_b)
            ]

        def channel_back_body(
            g_in_own, g_in_oth, s_in, small_a, small_b, mask_ref, qkv_ref, probs_ref,
            wp_a, wp_b, wq_a, wq_b, *refs,
        ):
            part_a, part_b, g_ref, g_own, part_ref, sums_ref, *rear_refs = refs
            grad = jnp.concatenate([g_in_own[...], g_in_oth[...]], axis=1).astype(F32)
            gain = gain_row((small_a, small_b), 3)
            grad = add_norm_back(grad, part_a, part_b, s_in[...], gain, sums_ref)
            g_ref[...] = grad
            low = grad.astype(BF16)
            g_own[...] = low[:, :half]
            put_rear(rear_refs, 0, low[:, half:])
            grad_mixed = project_back(low, wp_a[1], wp_b[1]).astype(BF16)
            packed = attention_part_back(
                False, grad_mixed, mask_ref, qkv_ref, probs_ref, rear_refs
            )
            own, oth = qkv_back(packed, 1, wq_a, wq_b)
            part_ref[:, :half] = own.astype(BF16)
            part_ref[:, half:] = oth.astype(BF16)

        late = [*fore3[0], *wd, s5]
        (g2, g2_own, back2, sums3, *rear2) = call(
            channel_back_body, "back_c",
            [g3_own, g3_oth, s5, *small, mask, qkv2, probs2, *wp, *wq, back3, far_back3],
            [full, half_low, full_low, sds((2, width)), *rear_shapes(rear_width_attn, 1)],
            flops=attn_flops,
            hold=[*keep_a, *keep_b, s3, s4, n2_own, *fore2[0], *fore2[1], *wu, *wd, *fore3[0]],
        )
        far_back2 = over_ha(back2)
        rear2 = both_rear(rear2, False)
        hid_got, fore0_got = (
            lax.all_gather(later(values, g2), "wa") for values in (fore1[1], fore0)
        )
        fore1, fore0 = (fore1, [n1_got, hid_got]), ([fore0], [fore0_got])
        keep_a.append(fore0_got)
        keep_b.append(hid_got)
        streams_c = attn_streams(SPLIT_C, 2)
        kept_c = [*keep_a, *keep_b, s3, s4, *small, *weights, g2, *late, sums3]
        make("wgrad_c", write_attn, streams_c, n2_own, g2_own, fore2, rear2, kept_c)
        slot(
            "slot_c", fresh=streams_c, moving=streams_d, hold=[*kept_c, back2, far_back2],
        )

        def mlp_back_body(
            g_in, part_a, part_b, s_in, s_before, small_a, small_b, slope_ref,
            wd_a, wd_b, wu_a, wu_b, g_ref, g_own, part_ref, sums_ref, *rear_refs,
        ):
            keep = column_mask(rows)
            gain = gain_row((small_a, small_b), 2)
            grad = add_norm_back(g_in[...], part_a, part_b, s_in[...], gain, sums_ref)
            conv_back_into(g_ref, sums_ref, 2, grad, s_before[...], (small_a, small_b), 1, keep)
            low = g_ref[...].astype(BF16)
            g_own[...] = low[:, :half]
            put_rear(rear_refs, 0, low[:, half:])
            dhid = project_back(low, wd_a[0], wd_b[0]).astype(BF16).astype(F32)
            dpre = (dhid * slope_ref[...]).astype(BF16)
            put_rear(rear_refs, half, dpre)
            part_ref[:, :half] = mm(dpre, wu_a[0], 1, 1).astype(BF16)
            part_ref[:, half:] = mm(dpre, wu_b[0], 1, 1).astype(BF16)

        (g1, g1_own, back1, sums2, *rear1) = call(
            mlp_back_body, "back_b",
            [g2, back2, far_back2, s4, s3, *small, slope1, *wd, *wu],
            [full, half_low, full_low, sds((11, width)), *rear_shapes(rear_width_mlp, 2)],
            flops=mlp_flops,
            hold=[*keep_a, s2, n1_own, *fore1[0], *fore1[1], *wq, *wp, *fore3[0], s5, sums3],
        )
        far_back1 = over_ha(back1)
        rear1 = both_rear(rear1)
        streams_b = mlp_streams(SPLIT_B, 0)
        make(
            "wgrad_b", write_mlp, streams_b, n1_own, g1_own, fore1, rear1,
            [*keep_a, s2, *small, *wq, *wp, g1, *late, sums3, sums2],
        )
        send_first(streams_b)

        def window_back_body(
            g_in, part_a, part_b, s_in, small_a, small_b, qkv_ref, probs_ref, wp_a, wp_b,
            g_ref, g_own, sums_ref, *rear_refs,
        ):
            gain = gain_row((small_a, small_b), 1)
            grad = add_norm_back(g_in[...], part_a, part_b, s_in[...], gain, sums_ref)
            g_ref[...] = grad
            low = grad.astype(BF16)
            g_own[...] = low[:, :half]
            put_rear(rear_refs, 0, low[:, half:])
            grad_mixed = project_back(low, wp_a[0], wp_b[0]).astype(BF16)
            attention_part_back(True, grad_mixed, None, qkv_ref, probs_ref, rear_refs)

        (g0, g0_own, sums1, *rear0) = call(
            window_back_body, "back_a",
            [g1, back1, far_back1, s2, *small, qkv0, probs0, *wp],
            [full, half_low, sds((2, width)), *rear_shapes(rear_width_attn, 1)],
            flops=attn_flops, hold=[x0, n0_own, *fore0[0], *fore0[1], s1, *wq, *late, sums3, sums2],
        )
        every = [*streams_d, *streams_c]
        depart = prepare_slot(
            "slot_cd", moving=every, spare=(2, 16),
            hold=[x0, n0_own, *fore0[0], *fore0[1], s1, *small, *wq, *late, sums1, sums2, sums3,
                  g0, g0_own, *rear0],
        )
        rear0 = both_rear(later(rear0, streams_d[0].kept))

        keep_0 = [g0, s1, x0, *small, *wq, sums1, sums2, sums3, *rear0[0]]
        streams_a = attn_streams(SPLIT_A, 0)
        make("wgrad_a", write_attn, streams_a, n0_own, g0_own, fore0, rear0, [*late, *keep_0])
        every = [*streams_d, *streams_c, *streams_b, *streams_a]
        send_first(streams_a)
        depart()

        sums_at = -(-rows_in // 16) * 16
        sums_half = sds((sum_rows, half))
        with_sums = sds((sums_at + sum_rows, half), BF16)

        def put_sums(ref, total):
            ref[sums_at:, :] = total.astype(BF16)

        def first_back_body(
            g_in, s_in, x_ref, small_a, small_b, wq_a, wq_b, sums_one, sums_two, sums_three, *refs
        ):
            rear_refs, (kept, sent, sums_own, scratch, sums_ref) = refs[:-5], refs[-5:]
            keep = column_mask(rows)
            packed = [
                get_rear(rear_refs, half + part * heads_width, heads_width) for part in range(3)
            ]
            upstream = jnp.concatenate(qkv_back(packed, 0, wq_a, wq_b), axis=1)
            units, inv_std = norm_stats(s_in[...])
            sums_ref[0:1, :] = jnp.sum(upstream * units, axis=0, keepdims=True)
            sums_ref[1:2, :] = jnp.sum(upstream, axis=0, keepdims=True)
            grad = jnp.where(here("ha") == 0, g_in[...], 0.0)
            grad = grad + norm_back(upstream, units, inv_std, gain_row((small_a, small_b), 0))
            conv_back_into(
                scratch, sums_ref, 2, grad, x_ref[...].astype(F32), (small_a, small_b), 0, keep
            )
            ship(scratch[...], kept, sent)
            sums_ref[11:13, :] = 0.5 * sums_one[...]
            sums_ref[13:24, :] = 0.5 * sums_two[...]
            sums_ref[24:26, :] = 0.5 * sums_three[...]
            sums_ref[26:, :] = jnp.zeros((sum_rows - 26, width), F32)
            sums_own[...] = sums_ref[:, :half]
            put_sums(sent, sums_ref[:, half:])

        token_kept, token_sent, sums_own = call(
            first_back_body, "back_0",
            [g0, s1, x0, *small, *wq, sums1, sums2, sums3, *rear0[0]],
            [shipped[0], with_sums, sums_half],
            scratch=[pltpu.VMEM((rows, width), F32), pltpu.VMEM((sum_rows, width), F32)],
            flops=attn_flops * 3 // 4, hold=late,
        )

        def fold_tokens(kept, both, sums_a, stay, go, sums_ref):
            received = other_core(both)
            fold(kept, received, stay, go)
            total = sums_a[...] + sums_in(received, sums_at)
            put_sums(go, total)
            sums_ref[...] = sums_in(go, sums_at)

        token_stay, token_go, sums_chip = call(
            fold_tokens, "fold_tokens",
            [token_kept, lax.all_gather(token_sent, "wa"), sums_own],
            [shipped[0], with_sums, sums_half], hold=late,
        )
        token_got = over_ha(token_go)

        def join_tokens(stay, received, sums_chip, out_ref, sums_ref):
            join(stay, received, out_ref)
            sums_ref[...] = sums_chip[...] + sums_in(received, sums_at)

        owned = sds((rows_in, half))
        grad_tokens, sums_ha = call(
            join_tokens, "join_tokens", [token_stay, token_got, sums_chip], [owned, sums_half],
            hold=late,
        )
        left_bits = list(range(bits))
        sums = [sums_ha, None, 0, left_bits.pop(0)]
        slot("sums_x", sums=sums, spare=(0, 96), hold=late)
        def hop():
            if not left_bits:
                return None
            sums[3] = left_bits.pop(0)
            return sums

        turn = 0
        while left_bits or any(stream.step < bits for stream in every):
            turn += 1
            arrived = [s for s in every if s.step == bits and s.final is None]
            slot(
                f"slot_b{turn}", moving=[s for s in streams_b if s.step < bits],
                hold=late if turn == 1 else (),
            )
            if turn == 1:
                out_kept, out_sent = call(
                    out_body, "out_d", [s5, *fore3[0], *wd], shipped, flops=mlp_flops // 2
                )
            second = [s for s in [*streams_d, *streams_a] if s.step < bits]
            depart = prepare_slot(f"slot_a{turn}", moving=second, ending=arrived, sums=hop())
            if turn > 1:
                depart()
                slot(f"slot_c{turn}", moving=[s for s in streams_c if s.step < bits])
                continue
            out_both = lax.all_gather(later(out_sent, streams_a[0].kept), "wa")
            out_stay, out_go = call(
                lambda kept, both, *refs: fold(kept, other_core(both), *refs),
                "fold_out", [out_kept, out_both], shipped,
            )
            depart(out_stay)
            out_got = over_ha(out_go)
        output = call(join, "join_out", [out_stay, out_got], [owned])[0]

        def finish_body(*refs):
            (up, down, qkv, proj, taps_ref, gain_ref, shift_ref) = refs[-7:]
            at = iter(refs)
            total = next(at)[...] + sums_in(next(at), sums[2])
            for branch, row in enumerate((0, 11, 13, 24)):
                gain_ref[branch : branch + 1, :] = total[row : row + 1]
                shift_ref[branch : branch + 1, :] = total[row + 1 : row + 2]
            for section, row in enumerate((2, 15)):
                for t in range(9):
                    taps_ref[t, section : section + 1, :] = total[row + t : row + t + 1]

            def finished(stream):
                if stream.final is not None:
                    return next(at)[...]
                return last_sum(stream, next(at), next(at))

            for section, streams in enumerate(
                ((*streams_a, *streams_b), (*streams_c, *streams_d))
            ):
                for stream in streams:
                    values, row = finished(stream), 0
                    for piece in stream.pieces:
                        part = values[row : row + piece_rows(piece)]
                        row += piece_rows(piece)
                        if piece == "up":
                            up[section] = part
                        elif piece == "proj":
                            proj[section] = part
                        elif isinstance(piece, tuple):
                            down[section, :, piece[1] * half : (piece[1] + 1) * half] = part
                        else:
                            qkv[section, ("q", "k", "v").index(piece)] = part

        ends = []
        for stream in (*streams_a, *streams_b, *streams_c, *streams_d):
            ends += [stream.kept, stream.got] if stream.final is None else [stream.final]
        up, down, qkv, proj, grad_taps, grad_gain, grad_shift = call(
            finish_body, "finish", [*sums[:2], *ends],
            [sds((2, up_rows, half)), sds((2, down_rows, hidden)), sds((2, 3, qkv_rows, half)),
             sds((2, proj_rows, half)), sds((9, 2, half)), sds((4, half)), sds((4, half))],
        )
        grad_taps = jnp.transpose(grad_taps, (1, 0, 2))
        grad_qkv = jnp.transpose(qkv, (0, 3, 1, 2))
        grad_proj, grad_up, grad_down = (
            jnp.transpose(values, (0, 2, 1)) for values in (proj, up, down)
        )
        return (
            output,
            grad_tokens,
            grad_taps,
            grad_gain,
            grad_shift,
            grad_qkv,
            grad_proj,
            grad_up,
            grad_down,
        )

    placed = (
        P(("dev", "ha"), "wa"),
        P(("dev", "ha"), "wa"),
        P(None, None, "wa"),
        P(None, "wa"),
        P(None, "wa"),
        P(None, "wa", None, "ha"),
        P(None, "ha", "wa"),
        P(None, "wa", "ha"),
        P(None, "ha", "wa"),
        P("dev", None),
    )
    return jax.shard_map(
        on_device,
        mesh=mesh,
        in_specs=placed,
        out_specs=(
            P(("dev", "ha"), "wa"),
            P(("dev", "ha"), "wa"),
            P(None, None, "wa"),
            P(None, "wa"),
            P(None, "wa"),
            P(None, "wa", None, ("ha", "dev")),
            P(None, "ha", ("wa", "dev")),
            P(None, "wa", ("ha", "dev")),
            P(None, "ha", ("wa", "dev")),
        ),
        check_vma=False,
    )
```
